32 devices in a mesh: section: 4 (over y, core), dom: 8 (over z, x).
Axes of the slice: x: 2, y: 2, z: 4, core: 2. Of those that a mesh axis runs over, the one named last changes fastest.
Arguments:
- right_sides: float32 [256, 32, 128], P(('section', 'dom')), may hold values from -6 to 6
- diag_inverse: bfloat16 [256, 128, 128], P(('section', 'dom')), as said below
- diag_blocks: bfloat16 [256, 128, 128], P(('section', 'dom')), as said below
- lower_blocks: bfloat16 [256, 3, 128, 128], P(('section', 'dom'))
- upper_blocks: bfloat16 [256, 3, 128, 128], P(('section', 'dom'))
- halo_blocks: bfloat16 [256, 2, 128, 128], P(('section', 'dom')), may hold values from -0.1875 to 0.1875
- lower_index: int32 [256, 3], P(('section', 'dom')), may hold values from 0 to 7, as said below
- upper_index: int32 [256, 3], P(('section', 'dom')), may hold values from 0 to 7, as said below
- halo_index: int32 [256, 2], P(('section', 'dom')), may hold values from 0 to 7, as said below
Outputs:
- solution: float32 [256, 32, 128], P(('section', 'dom'))
- product: float32 [256, 32, 128], P(('section', 'dom'))
The draws below stay inside these ranges and needn't reach their ends.
Inputs may be any that keep to these rules, and one draw needn't show every extreme that they name: `lower_index`: for block row g with k = g mod 8, every entry lies in 0 to k, and the first entry equals k. `upper_index`: for block row g with k = g mod 8, every entry lies in k to 7, and the first entry equals k. `halo_index`: for block row g the first entry equals g mod 8. `diag_inverse`: each block is the identity scaled row by row plus a full block. `diag_blocks`: each block is the identity scaled row by row plus a full block.
All inputs are finite; a program needn't handle non-finite values.
Results may differ from the reference program's by a relative error of at most 0.029.
Values may be sent and summed in bfloat16 or wider, within the bound.
No kernel may reach another device: no remote copies, remote signals or barrier semaphores. Data moves between devices by JAX's collectives and lax.ppermute only.
A program may use at most 64 MiB of HBM per device.

```python
import math
import jax
import jax.numpy as jnp
from jax import lax

BLK = 128
NRHS = 32
ROWS_DEV = 8
NLOW = 3
NUPP = 3
NHALO = 2
RIM = 4
BROWS = 256
N_SECTION = 4
N_DOM = 8


def draw_diag_inverse(key, part):
    key_diag, key_jitter = jax.random.split(jax.random.fold_in(key, 11))
    diagonal = jax.random.uniform(key_diag, (BROWS, BLK), jnp.float32, 0.7, 1.3)
    jitter = jax.random.normal(key_jitter, (BROWS, BLK, BLK), jnp.float32)
    identity = jnp.eye(BLK, dtype=jnp.float32)
    return (jitter * (0.35 / math.sqrt(BLK)) + diagonal[:, :, None] * identity).astype(jnp.bfloat16)


def draw_diag_blocks(key, part):
    key_diag, key_jitter = jax.random.split(jax.random.fold_in(key, 23))
    diagonal = jax.random.uniform(key_diag, (BROWS, BLK), jnp.float32, 0.8, 1.6)
    jitter = jax.random.normal(key_jitter, (BROWS, BLK, BLK), jnp.float32)
    identity = jnp.eye(BLK, dtype=jnp.float32)
    return (jitter * (0.35 / math.sqrt(BLK)) + diagonal[:, :, None] * identity).astype(jnp.bfloat16)


def slot_blocks(key, slots):
    jitter = jax.random.normal(key, (BROWS, slots, BLK, BLK), jnp.float32)
    weights = jnp.where(jnp.arange(slots) == 0, 0.7, 0.35).astype(jnp.float32)
    return (jitter * weights[None, :, None, None] / math.sqrt(BLK)).astype(jnp.bfloat16)


def draw_lower_blocks(key, part):
    return slot_blocks(jax.random.fold_in(key, 37), NLOW)


def draw_upper_blocks(key, part):
    return slot_blocks(jax.random.fold_in(key, 41), NUPP)


def draw_lower_index(key, part):
    position = jnp.arange(BROWS, dtype=jnp.int32) % ROWS_DEV
    others = jax.random.randint(jax.random.fold_in(key, 53), (BROWS, NLOW - 1), 0, (position + 1)[:, None], dtype=jnp.int32)
    return jnp.concatenate([position[:, None], others], axis=1)


def draw_upper_index(key, part):
    position = jnp.arange(BROWS, dtype=jnp.int32) % ROWS_DEV
    others = jax.random.randint(jax.random.fold_in(key, 59), (BROWS, NUPP - 1), position[:, None], ROWS_DEV, dtype=jnp.int32)
    return jnp.concatenate([position[:, None], others], axis=1)


def draw_halo_index(key, part):
    position = jnp.arange(BROWS, dtype=jnp.int32) % ROWS_DEV
    others = jax.random.randint(jax.random.fold_in(key, 61), (BROWS, NHALO - 1), 0, 2 * RIM, dtype=jnp.int32)
    return jnp.concatenate([(position % (2 * RIM))[:, None], others], axis=1)


def shard_levels(stream_key, dims, cuts, least, high):
    def one(dim, shards_of):
        steps = jax.random.uniform(jax.random.fold_in(jax.random.fold_in(stream_key, 6), dim), (shards_of,), jnp.float32, least / len(cuts), high / len(cuts))
        return jnp.repeat(jnp.exp(steps), dims[dim] // shards_of).reshape((-1,) + (1,) * (len(dims) - dim - 1))

    gain = one(*cuts[0])
    for cut in cuts[1:]:
        gain = gain * one(*cut)
    return gain


def bell_draw(own_key, dims, width, most, shards=(), kind=jnp.bfloat16):
    loudness = shard_levels(own_key, dims, shards, -0.22, 0.18) if shards else 1.0
    values = jax.random.normal(own_key, dims, jnp.float32) * width * loudness
    return jnp.minimum(jnp.maximum(values, -most), most).astype(kind)


def setup_inputs(seed: int = 0) -> dict:
    key_of = jax.random.split(jax.random.key(seed), 10)
    return {
        "right_sides": bell_draw(key_of[0], (BROWS, NRHS, BLK), 1.0, 6.0, ((0, 32),), jnp.float32),
        "diag_inverse": draw_diag_inverse(jax.random.fold_in(key_of[9], 71), 0),
        "diag_blocks": draw_diag_blocks(jax.random.fold_in(key_of[9], 71), 0),
        "lower_blocks": draw_lower_blocks(jax.random.fold_in(key_of[9], 71), 0),
        "upper_blocks": draw_upper_blocks(jax.random.fold_in(key_of[9], 71), 0),
        "halo_blocks": bell_draw(key_of[5], (BROWS, NHALO, BLK, BLK), (8 * BLK) ** -0.5, 0.1875, ((0, 32),)),
        "lower_index": draw_lower_index(jax.random.fold_in(key_of[9], 71), 0),
        "upper_index": draw_upper_index(jax.random.fold_in(key_of[9], 71), 0),
        "halo_index": draw_halo_index(jax.random.fold_in(key_of[9], 71), 0),
    }


highest = lax.Precision.HIGHEST


def solve_down(target, inverse, lower_part, pointers, inflow):
    def advance(solved, entries):
        target_row, inverse_row, blocks, chosen, position = entries
        picked = jnp.take(solved, chosen, axis=0)
        source = jnp.where((chosen == position)[:, None, None], inflow[None], picked)
        source = source.astype(jnp.bfloat16).astype(jnp.float32)
        summed = jnp.einsum("sqb,sbc->qc", source, blocks.astype(jnp.float32), precision=highest)
        gap = (target_row - summed).astype(jnp.bfloat16)
        result = jnp.dot(gap, inverse_row, preferred_element_type=jnp.float32)
        return lax.dynamic_update_index_in_dim(solved, result, position, 0), None

    positions = jnp.arange(target.shape[0], dtype=jnp.int32)
    solved, unused = lax.scan(advance, jnp.zeros_like(target), (target, inverse, lower_part, pointers, positions))
    return solved


def solve_up(target, inverse, upper_part, pointers, inflow):
    def advance(solved, entries):
        target_row, inverse_row, blocks, chosen, position = entries
        picked = jnp.take(solved, chosen, axis=0)
        source = jnp.where((chosen == position)[:, None, None], inflow[None], picked)
        source = source.astype(jnp.bfloat16).astype(jnp.float32)
        summed = jnp.einsum("sqb,sbc->qc", source, blocks.astype(jnp.float32), precision=highest)
        result = target_row - jnp.dot(summed.astype(jnp.bfloat16), inverse_row, preferred_element_type=jnp.float32)
        return lax.dynamic_update_index_in_dim(solved, result, position, 0), None

    positions = jnp.arange(target.shape[0], dtype=jnp.int32)
    solved, unused = lax.scan(advance, jnp.zeros_like(target), (target, inverse, upper_part, pointers, positions), reverse=True)
    return solved


def apply_rows(solution, diag_part, lower_part, lower_pointers, upper_part, upper_pointers, halo_part, halo_pointers, before, after, rim_rows):
    positions = jnp.arange(solution.shape[0], dtype=jnp.int32)[:, None]
    lower_source = jnp.where((lower_pointers == positions)[:, :, None, None], before[None, None], jnp.take(solution, lower_pointers, axis=0))
    upper_source = jnp.where((upper_pointers == positions)[:, :, None, None], after[None, None], jnp.take(solution, upper_pointers, axis=0))
    halo_source = jnp.take(rim_rows, halo_pointers, axis=0)
    total = jnp.einsum("rqb,rbc->rqc", solution.astype(jnp.float32), diag_part.astype(jnp.float32), precision=highest)
    total = total + jnp.einsum("rsqb,rsbc->rqc", lower_source.astype(jnp.float32), lower_part.astype(jnp.float32), precision=highest)
    total = total + jnp.einsum("rsqb,rsbc->rqc", upper_source.astype(jnp.float32), upper_part.astype(jnp.float32), precision=highest)
    total = total + jnp.einsum("rsqb,rsbc->rqc", halo_source.astype(jnp.float32), halo_part.astype(jnp.float32), precision=highest)
    return total


def by_device(array):
    return array.reshape((N_SECTION, N_DOM, ROWS_DEV) + array.shape[1:])


def reference(right_sides, diag_inverse, diag_blocks, lower_blocks, upper_blocks, halo_blocks, lower_index, upper_index, halo_index):
    targets = by_device(right_sides)
    inverses = by_device(diag_inverse)
    diagonals = by_device(diag_blocks)
    lowers = by_device(lower_blocks)
    uppers = by_device(upper_blocks)
    halos = by_device(halo_blocks)
    lower_ptrs = by_device(lower_index)
    upper_ptrs = by_device(upper_index)
    halo_ptrs = by_device(halo_index)
    zeros = jnp.zeros((N_DOM, NRHS, BLK), right_sides.dtype)

    def forward_section(inflow, entries):
        solved = jax.vmap(solve_down)(*entries, inflow)
        return solved[:, -1], solved

    unused, forward = lax.scan(forward_section, zeros, (targets, inverses, lowers, lower_ptrs))

    def backward_section(inflow, entries):
        solved = jax.vmap(solve_up)(*entries, inflow)
        return solved[:, 0], solved

    unused, solution = lax.scan(backward_section, zeros, (forward, inverses, uppers, upper_ptrs), reverse=True)
    rounded = solution.astype(jnp.bfloat16)
    last_rows = rounded[:, :, -1]
    first_rows = rounded[:, :, 0]
    before = jnp.concatenate([jnp.zeros_like(last_rows[:1]), last_rows[:-1]], axis=0)
    after = jnp.concatenate([first_rows[1:], jnp.zeros_like(first_rows[:1])], axis=0)
    left_rim = jnp.concatenate([jnp.zeros_like(rounded[:, :1, ROWS_DEV - RIM:]), rounded[:, :-1, ROWS_DEV - RIM:]], axis=1)
    right_rim = jnp.concatenate([rounded[:, 1:, :RIM], jnp.zeros_like(rounded[:, :1, :RIM])], axis=1)
    rim_rows = jnp.concatenate([left_rim, right_rim], axis=2)
    product = lax.map(lambda entries: jax.vmap(apply_rows)(*entries), (rounded, diagonals, lowers, lower_ptrs, uppers, upper_ptrs, halos, halo_ptrs, before, after, rim_rows))
    return solution.reshape(right_sides.shape), product.reshape(right_sides.shape)
```

```python
import jax
import jax.numpy as jnp
from jax import lax
from jax.experimental import pallas as pl
from jax.experimental.pallas import tpu as pltpu
from jax.sharding import PartitionSpec as P

RIM = 4

VMEM = pl.BlockSpec(memory_space=pltpu.VMEM)
SMEM = pl.BlockSpec(memory_space=pltpu.SMEM)


def mul(a, b):
    return jnp.dot(a, b, preferred_element_type=jnp.float32)


def narrow(a):
    return a.astype(jnp.bfloat16)


def sweep_kernel(
    rhs, inverse, lower, upper, lower_at, upper_at, base, response, payload, low, upp, down, exact
):
    rows, count, width = rhs.shape
    slots = lower.shape[1]
    upper_slots = upper.shape[1]
    near = count + width
    last = rows - 1
    eye = narrow(
        lax.broadcasted_iota(jnp.int32, (width, width), 0)
        == lax.broadcasted_iota(jnp.int32, (width, width), 1)
    )
    scaled = []
    for k in range(rows):
        own = inverse[k]
        scaled.append(mul(narrow(rhs[k]), own))
        low[k] = narrow(mul(lower[k].reshape(slots * width, width), own))
        upp[k] = narrow(mul(upper[k].reshape(upper_slots * width, width), own))
    down[:, :count] = jnp.zeros((rows, count, width), jnp.bfloat16)
    response[:, :near] = jnp.zeros((rows, near, width), jnp.bfloat16)
    for k in range(rows):
        down[k, count:] = eye
        response[k, near:] = eye

    for k in range(rows):
        if k == 0:
            total = low[k, :width].astype(jnp.float32)
            for m in range(1, slots):
                total = total + low[k, m * width : (m + 1) * width].astype(jnp.float32)
            exact[k, :count] = scaled[k]
            exact[k, count:] = -total
        else:
            source = jnp.concatenate([down[lower_at[k, m]] for m in range(1, slots)], axis=1)
            summed = mul(source, low[k, width:])
            exact[k, :count] = scaled[k] - summed[:count]
            exact[k, count:] = -low[k, :width].astype(jnp.float32) - summed[count:]
        down[k] = narrow(exact[k])

    for k in range(last, -1, -1):
        if k == last:
            total = upp[k, :width].astype(jnp.float32)
            for m in range(1, upper_slots):
                total = total + upp[k, m * width : (m + 1) * width].astype(jnp.float32)
            base[k] = exact[k, :count]
            response[k, :near] = narrow(exact[k])
            response[k, near:] = narrow(-total)
        else:
            source = jnp.concatenate(
                [response[upper_at[k, m]] for m in range(1, upper_slots)], axis=1
            )
            summed = mul(source, upp[k, width:])
            solved = exact[k] - summed[:near]
            base[k] = solved[:count]
            response[k, :near] = narrow(solved)
            response[k, near:] = narrow(-upp[k, :width].astype(jnp.float32) - summed[near:])

    far = near + width
    payload[:near] = down[last]
    payload[near : near + far] = response[0]
    payload[near + far :] = response[last, near:]


def chain_kernel(groups, axes, gathered, base, response, solution, rounded, ends, flow):
    rows, count, width = base.shape
    near = count + width
    far = near + width
    me = lax.axis_index(axes[0])
    side = lax.rem(lax.axis_index(axes[1]), 2)
    zero = jnp.zeros((count, width), jnp.bfloat16)

    inflow = [zero]
    for t in range(1, groups):
        add = gathered[t - 1, :count].astype(jnp.float32)
        if t > 1:
            add = add + mul(inflow[-1], gathered[t - 1, count:near])
        inflow.append(narrow(add))
    outflow = [zero]
    for t in range(groups - 1, 0, -1):
        add = gathered[t, near : near + count].astype(jnp.float32)
        add = add + mul(inflow[t], gathered[t, near + count : 2 * near])
        if t < groups - 1:
            add = add + mul(outflow[0], gathered[t, 2 * near : near + far])
        outflow.insert(0, narrow(add))
    for t in range(groups):
        flow[0, t] = inflow[t]
        flow[1, t] = outflow[t]

    both = jnp.concatenate([flow[0, me], flow[1, me]], axis=1)
    for k in range(rows):
        value = base[k] + mul(both, response[k, count:])
        solution[k] = value
        rounded[k] = narrow(value)
    rounded[rows + 1] = flow[1, me]
    prior = lax.max(me - 1, 0)
    before = flow[0, me].astype(jnp.float32) + mul(flow[1, prior], gathered[prior, near + far :])
    rounded[rows] = narrow(jnp.where(me > 0, before, 0.0))
    rim = ends.shape[1]
    for e in range(rim):
        ends[0, e] = rounded[(1 - side) * (rows - rim) + e]
        ends[1, e] = rounded[side * (rows - rim) + e]


def local_kernel(rounded, diagonal, lower, upper, lower_at, upper_at, partial):
    rows, slots, width, _ = lower.shape
    upper_slots = upper.shape[1]
    for k in range(rows):
        total = mul(rounded[k], diagonal[k])
        source = [rounded[rows]]
        for m in range(1, slots):
            at = lower_at[k, m]
            source.append(rounded[jnp.where(at == k, rows, at)])
        total = total + mul(
            jnp.concatenate(source, axis=1), lower[k].reshape(slots * width, width)
        )
        source = [rounded[rows + 1]]
        for m in range(1, upper_slots):
            at = upper_at[k, m]
            source.append(rounded[jnp.where(at == k, rows + 1, at)])
        total = total + mul(
            jnp.concatenate(source, axis=1), upper[k].reshape(upper_slots * width, width)
        )
        partial[k] = total


def halo_kernel(axis, partial, inner, outer, halo, halo_at, product, rim_rows):
    rows, slots, width, _ = halo.shape
    rim = inner.shape[0]
    turn = rim * (1 - lax.rem(lax.axis_index(axis), 2))
    rim_rows[:rim] = inner[...]
    rim_rows[rim:] = outer[...]
    for k in range(rows):
        source = [
            rim_rows[lax.rem(halo_at[k, m] + turn, 2 * rim)] for m in range(slots)
        ]
        product[k] = partial[k] + mul(
            jnp.concatenate(source, axis=1), halo[k].reshape(slots * width, width)
        )


def swaps(block, axis, first):
    count = lax.axis_size(axis)
    pairs = []
    for low in range(first, count - 1, 2):
        pairs += [(low, low + 1), (low + 1, low)]
    return lax.ppermute(block, axis, pairs)


def on_device(
    right_sides,
    diag_inverse,
    diag_blocks,
    lower_blocks,
    upper_blocks,
    halo_blocks,
    lower_index,
    upper_index,
    halo_index,
):
    rows, count, width = right_sides.shape
    slots = lower_blocks.shape[1]
    upper_slots = upper_blocks.shape[1]
    groups = lax.axis_size("section")
    near = count + width
    far = near + width
    wide = jax.ShapeDtypeStruct((rows, count, width), jnp.float32)

    base, response, payload = pl.pallas_call(
        sweep_kernel,
        out_shape=(
            wide,
            jax.ShapeDtypeStruct((rows, far, width), jnp.bfloat16),
            jax.ShapeDtypeStruct((near + far + width, width), jnp.bfloat16),
        ),
        in_specs=[VMEM] * 4 + [SMEM] * 2,
        out_specs=(VMEM, VMEM, VMEM),
        scratch_shapes=[
            pltpu.VMEM((rows, slots * width, width), jnp.bfloat16),
            pltpu.VMEM((rows, upper_slots * width, width), jnp.bfloat16),
            pltpu.VMEM((rows, near, width), jnp.bfloat16),
            pltpu.VMEM((rows, near, width), jnp.float32),
        ],
        name="sweeps",
    )(right_sides, diag_inverse, lower_blocks, upper_blocks, lower_index, upper_index)

    gathered = lax.all_gather(payload, "section")

    def chain(*refs):
        chain_kernel(groups, ("section", "dom"), *refs)

    solution, rounded, ends = pl.pallas_call(
        chain,
        out_shape=(
            wide,
            jax.ShapeDtypeStruct((rows + 2, count, width), jnp.bfloat16),
            jax.ShapeDtypeStruct((2, RIM, count, width), jnp.bfloat16),
        ),
        in_specs=[VMEM] * 3,
        out_specs=(VMEM, VMEM, VMEM),
        scratch_shapes=[pltpu.VMEM((2, groups, count, width), jnp.bfloat16)],
        name="chain",
    )(gathered, base, response)

    inner = swaps(ends[0], "dom", 0)
    outer = swaps(ends[1], "dom", 1)

    partial = pl.pallas_call(
        local_kernel,
        out_shape=wide,
        in_specs=[VMEM] * 4 + [SMEM] * 2,
        out_specs=VMEM,
        name="local_product",
    )(rounded, diag_blocks, lower_blocks, upper_blocks, lower_index, upper_index)

    def halo(*refs):
        halo_kernel("dom", *refs)

    product = pl.pallas_call(
        halo,
        out_shape=wide,
        in_specs=[VMEM] * 4 + [SMEM],
        out_specs=VMEM,
        scratch_shapes=[pltpu.VMEM((2 * RIM, count, width), jnp.bfloat16)],
        name="halo_product",
    )(partial, inner, outer, halo_blocks, halo_index)
    return (solution, product)


def solution(mesh):
    in_specs = (
        P(("section", "dom"), None, None),
        P(("section", "dom"), None, None),
        P(("section", "dom"), None, None),
        P(("section", "dom"), None, None, None),
        P(("section", "dom"), None, None, None),
        P(("section", "dom"), None, None, None),
        P(("section", "dom"), None),
        P(("section", "dom"), None),
        P(("section", "dom"), None),
    )
    out_specs = (P(("section", "dom"), None, None), P(("section", "dom"), None, None))
    return jax.shard_map(
        on_device, mesh=mesh, in_specs=in_specs, out_specs=out_specs, check_vma=False
    )
```

```python
import jax
import jax.numpy as jnp
from jax import lax
from jax.experimental import pallas as pl
from jax.experimental.pallas import tpu as pltpu
from jax.sharding import PartitionSpec as P

RIM = 4

VMEM = pl.BlockSpec(memory_space=pltpu.VMEM)
SMEM = pl.BlockSpec(memory_space=pltpu.SMEM)
SMALL = pltpu.CompilerParams(vmem_limit_bytes=16 * 1024 * 1024)


def mul(a, b):
    return jnp.dot(a, b, preferred_element_type=jnp.float32)


def narrow(a):
    return a.astype(jnp.bfloat16)


def sweep_kernel(
    rhs, inverse, lower, upper, lower_at, upper_at, base, response, payload, low, upp, down, exact
):
    rows, count, width = rhs.shape
    slots = lower.shape[1]
    upper_slots = upper.shape[1]
    near = count + width
    last = rows - 1
    eye = narrow(
        lax.broadcasted_iota(jnp.int32, (width, width), 0)
        == lax.broadcasted_iota(jnp.int32, (width, width), 1)
    )
    scaled = []
    for k in range(rows):
        own = inverse[k]
        scaled.append(mul(narrow(rhs[k]), own))
        low[k] = narrow(mul(lower[k].reshape(slots * width, width), own))
        upp[k] = narrow(mul(upper[k].reshape(upper_slots * width, width), own))
    down[:, :count] = jnp.zeros((rows, count, width), jnp.bfloat16)
    response[:, :near] = jnp.zeros((rows, near, width), jnp.bfloat16)
    for k in range(rows):
        down[k, count:] = eye
        response[k, near:] = eye

    for k in range(rows):
        if k == 0:
            total = low[k, :width].astype(jnp.float32)
            for m in range(1, slots):
                total = total + low[k, m * width : (m + 1) * width].astype(jnp.float32)
            exact[k, :count] = scaled[k]
            exact[k, count:] = -total
        else:
            source = jnp.concatenate([down[lower_at[m, k]] for m in range(1, slots)], axis=1)
            summed = mul(source, low[k, width:])
            exact[k, :count] = scaled[k] - summed[:count]
            exact[k, count:] = -low[k, :width].astype(jnp.float32) - summed[count:]
        down[k] = narrow(exact[k])

    for k in range(last, -1, -1):
        if k == last:
            total = upp[k, :width].astype(jnp.float32)
            for m in range(1, upper_slots):
                total = total + upp[k, m * width : (m + 1) * width].astype(jnp.float32)
            base[k] = exact[k, :count]
            response[k, :near] = narrow(exact[k])
            response[k, near:] = narrow(-total)
        else:
            source = jnp.concatenate(
                [response[upper_at[m, k]] for m in range(1, upper_slots)], axis=1
            )
            summed = mul(source, upp[k, width:])
            solved = exact[k] - summed[:near]
            base[k] = solved[:count]
            response[k, :near] = narrow(solved)
            response[k, near:] = narrow(-upp[k, :width].astype(jnp.float32) - summed[near:])

    far = near + width
    payload[:near] = down[last]
    payload[near : near + far] = response[0]
    payload[near + far :] = response[last, near:]


def chain_kernel(
    groups, axes, gathered, base, response, solution, rounded, inner, outer, flow
):
    rows, count, width = base.shape
    near = count + width
    far = near + width
    me = lax.axis_index(axes[0])
    side = lax.rem(lax.axis_index(axes[1]), 2)
    zero = jnp.zeros((count, width), jnp.bfloat16)

    inflow = [zero]
    for t in range(1, groups):
        add = gathered[t - 1, :count].astype(jnp.float32)
        if t > 1:
            add = add + mul(inflow[-1], gathered[t - 1, count:near])
        inflow.append(narrow(add))
    outflow = [zero]
    for t in range(groups - 1, 0, -1):
        add = gathered[t, near : near + count].astype(jnp.float32)
        add = add + mul(inflow[t], gathered[t, near + count : 2 * near])
        if t < groups - 1:
            add = add + mul(outflow[0], gathered[t, 2 * near : near + far])
        outflow.insert(0, narrow(add))
    for t in range(groups):
        flow[0, t] = inflow[t]
        flow[1, t] = outflow[t]

    both = jnp.concatenate([flow[0, me], flow[1, me]], axis=1)
    for k in range(rows):
        value = base[k] + mul(both, response[k, count:])
        solution[k] = value
        rounded[k] = narrow(value)
    rounded[rows + 1] = flow[1, me]
    prior = lax.max(me - 1, 0)
    before = flow[0, me].astype(jnp.float32) + mul(flow[1, prior], gathered[prior, near + far :])
    rounded[rows] = narrow(jnp.where(me > 0, before, 0.0))
    rim = inner.shape[0]
    for e in range(rim):
        inner[e] = rounded[(1 - side) * (rows - rim) + e]
        outer[e] = rounded[side * (rows - rim) + e]


def local_kernel(rounded, diagonal, lower, upper, lower_at, upper_at, partial):
    rows, slots, width, _ = lower.shape
    upper_slots = upper.shape[1]
    for k in range(rows):
        total = mul(rounded[k], diagonal[k])
        source = [rounded[rows]]
        for m in range(1, slots):
            at = lower_at[m, k]
            source.append(rounded[jnp.where(at == k, rows, at)])
        total = total + mul(
            jnp.concatenate(source, axis=1), lower[k].reshape(slots * width, width)
        )
        source = [rounded[rows + 1]]
        for m in range(1, upper_slots):
            at = upper_at[m, k]
            source.append(rounded[jnp.where(at == k, rows + 1, at)])
        total = total + mul(
            jnp.concatenate(source, axis=1), upper[k].reshape(upper_slots * width, width)
        )
        partial[k] = total


def halo_kernel(axis, partial, inner, outer, halo, halo_at, product, rim_rows):
    rows, slots, width, _ = halo.shape
    rim = inner.shape[0]
    turn = rim * (1 - lax.rem(lax.axis_index(axis), 2))
    rim_rows[:rim] = inner[...]
    rim_rows[rim:] = outer[...]
    for k in range(rows):
        source = [
            rim_rows[lax.rem(halo_at[m, k] + turn, 2 * rim)] for m in range(slots)
        ]
        product[k] = partial[k] + mul(
            jnp.concatenate(source, axis=1), halo[k].reshape(slots * width, width)
        )


def swaps(block, axis, first):
    count = lax.axis_size(axis)
    pairs = []
    for low in range(first, count - 1, 2):
        pairs += [(low, low + 1), (low + 1, low)]
    return lax.ppermute(block, axis, pairs)


def on_device(
    right_sides,
    diag_inverse,
    diag_blocks,
    lower_blocks,
    upper_blocks,
    halo_blocks,
    lower_index,
    upper_index,
    halo_index,
):
    rows, count, width = right_sides.shape
    lower_at, upper_at, halo_at = lower_index.T, upper_index.T, halo_index.T
    slots = lower_blocks.shape[1]
    upper_slots = upper_blocks.shape[1]
    groups = lax.axis_size("section")
    near = count + width
    far = near + width
    wide = jax.ShapeDtypeStruct((rows, count, width), jnp.float32)

    base, response, payload = pl.pallas_call(
        sweep_kernel,
        out_shape=(
            wide,
            jax.ShapeDtypeStruct((rows, far, width), jnp.bfloat16),
            jax.ShapeDtypeStruct((near + far + width, width), jnp.bfloat16),
        ),
        in_specs=[VMEM] * 4 + [SMEM] * 2,
        out_specs=(VMEM, VMEM, VMEM),
        scratch_shapes=[
            pltpu.VMEM((rows, slots * width, width), jnp.bfloat16),
            pltpu.VMEM((rows, upper_slots * width, width), jnp.bfloat16),
            pltpu.VMEM((rows, near, width), jnp.bfloat16),
            pltpu.VMEM((rows, near, width), jnp.float32),
        ],
        compiler_params=SMALL,
        name="sweeps",
    )(right_sides, diag_inverse, lower_blocks, upper_blocks, lower_at, upper_at)

    gathered = lax.all_gather(payload, "section")

    def chain(*refs):
        chain_kernel(groups, ("section", "dom"), *refs)

    solution, rounded, inner, outer = pl.pallas_call(
        chain,
        out_shape=(
            wide,
            jax.ShapeDtypeStruct((rows + 2, count, width), jnp.bfloat16),
            jax.ShapeDtypeStruct((RIM, count, width), jnp.bfloat16),
            jax.ShapeDtypeStruct((RIM, count, width), jnp.bfloat16),
        ),
        in_specs=[VMEM] * 3,
        out_specs=(VMEM,) * 4,
        scratch_shapes=[pltpu.VMEM((2, groups, count, width), jnp.bfloat16)],
        compiler_params=SMALL,
        name="chain",
    )(gathered, base, response)

    inner = swaps(inner, "dom", 0)
    outer = swaps(outer, "dom", 1)

    partial = pl.pallas_call(
        local_kernel,
        out_shape=wide,
        in_specs=[VMEM] * 4 + [SMEM] * 2,
        out_specs=VMEM,
        compiler_params=SMALL,
        name="local_product",
    )(rounded, diag_blocks, lower_blocks, upper_blocks, lower_at, upper_at)

    def halo(*refs):
        halo_kernel("dom", *refs)

    product = pl.pallas_call(
        halo,
        out_shape=wide,
        in_specs=[VMEM] * 4 + [SMEM],
        out_specs=VMEM,
        scratch_shapes=[pltpu.VMEM((2 * RIM, count, width), jnp.bfloat16)],
        compiler_params=SMALL,
        name="halo_product",
    )(partial, inner, outer, halo_blocks, halo_at)
    return (solution, product)


def solution(mesh):
    in_specs = (
        P(("section", "dom"), None, None),
        P(("section", "dom"), None, None),
        P(("section", "dom"), None, None),
        P(("section", "dom"), None, None, None),
        P(("section", "dom"), None, None, None),
        P(("section", "dom"), None, None, None),
        P(("section", "dom"), None),
        P(("section", "dom"), None),
        P(("section", "dom"), None),
    )
    out_specs = (P(("section", "dom"), None, None), P(("section", "dom"), None, None))
    return jax.shard_map(
        on_device, mesh=mesh, in_specs=in_specs, out_specs=out_specs, check_vma=False
    )
```

```python
import jax
import jax.numpy as jnp
from jax import lax
from jax.experimental import pallas as pl
from jax.experimental.pallas import tpu as pltpu
from jax.sharding import PartitionSpec as P

RIM = 4

VMEM = pl.BlockSpec(memory_space=pltpu.VMEM)
SMEM = pl.BlockSpec(memory_space=pltpu.SMEM)
HBM = pl.BlockSpec(memory_space=pltpu.HBM)
SMALL = pltpu.CompilerParams(vmem_limit_bytes=16 * 1024 * 1024)


def mul(a, b):
    return jnp.dot(a, b, preferred_element_type=jnp.float32)


def narrow(a):
    return a.astype(jnp.bfloat16)


def sweep_kernel(
    rhs_far,
    inverse_far,
    lower_far,
    upper_far,
    lower_at_far,
    upper_at_far,
    base,
    response,
    payload,
    rhs,
    inverse,
    lower,
    upper,
    lower_at,
    upper_at,
    low,
    upp,
    down,
    exact,
    arrived,
):
    rows, count, width = rhs.shape
    slots = lower.shape[1]
    upper_slots = upper.shape[1]
    near = count + width
    last = rows - 1
    half = rows // 2
    parts = [
        (inverse_far, inverse),
        (rhs_far, rhs),
        (lower_far.at[:half], lower.at[:half]),
        (lower_at_far, lower_at),
        (lower_far.at[half:], lower.at[half:]),
        (upper_far, upper),
        (upper_at_far, upper_at),
    ]
    copies = [
        pltpu.make_async_copy(far, here, arrived.at[i]) for i, (far, here) in enumerate(parts)
    ]
    for copy in copies:
        copy.start()
    eye = narrow(
        lax.broadcasted_iota(jnp.int32, (width, width), 0)
        == lax.broadcasted_iota(jnp.int32, (width, width), 1)
    )
    down[:, :count] = jnp.zeros((rows, count, width), jnp.bfloat16)
    response[:, :near] = jnp.zeros((rows, near, width), jnp.bfloat16)
    for k in range(rows):
        down[k, count:] = eye
        response[k, near:] = eye

    for k in range(rows):
        if k == 0:
            for copy in copies[:4]:
                copy.wait()
        if k == half:
            for copy in copies[4:]:
                copy.wait()
            for j in range(rows):
                blocks = upper[j].reshape(upper_slots * width, width)
                upp[j] = narrow(mul(blocks, inverse[j]))
        own = inverse[k]
        scaled = mul(narrow(rhs[k]), own)
        low[k] = narrow(mul(lower[k].reshape(slots * width, width), own))
        if k == 0:
            total = low[k, :width].astype(jnp.float32)
            for m in range(1, slots):
                total = total + low[k, m * width : (m + 1) * width].astype(jnp.float32)
            exact[k, :count] = scaled
            exact[k, count:] = -total
        else:
            source = jnp.concatenate([down[lower_at[m, k]] for m in range(1, slots)], axis=1)
            summed = mul(source, low[k, width:])
            exact[k, :count] = scaled - summed[:count]
            exact[k, count:] = -low[k, :width].astype(jnp.float32) - summed[count:]
        down[k] = narrow(exact[k])

    for k in range(last, -1, -1):
        if k == last:
            total = upp[k, :width].astype(jnp.float32)
            for m in range(1, upper_slots):
                total = total + upp[k, m * width : (m + 1) * width].astype(jnp.float32)
            base[k] = exact[k, :count]
            response[k, :near] = narrow(exact[k])
            response[k, near:] = narrow(-total)
        else:
            source = jnp.concatenate(
                [response[upper_at[m, k]] for m in range(1, upper_slots)], axis=1
            )
            summed = mul(source, upp[k, width:])
            solved = exact[k] - summed[:near]
            base[k] = solved[:count]
            response[k, :near] = narrow(solved)
            response[k, near:] = narrow(-upp[k, :width].astype(jnp.float32) - summed[near:])

    far = near + width
    payload[:near] = down[last]
    payload[near : near + far] = response[0]
    payload[near + far :] = response[last, near:]


def chain_kernel(
    groups, axes, gathered, base, response, solution, rounded, inner, outer, flow
):
    rows, count, width = base.shape
    near = count + width
    far = near + width
    me = lax.axis_index(axes[0])
    side = lax.rem(lax.axis_index(axes[1]), 2)
    zero = jnp.zeros((count, width), jnp.bfloat16)

    inflow = [zero]
    for t in range(1, groups):
        add = gathered[t - 1, :count].astype(jnp.float32)
        if t > 1:
            add = add + mul(inflow[-1], gathered[t - 1, count:near])
        inflow.append(narrow(add))
    outflow = [zero]
    for t in range(groups - 1, 0, -1):
        add = gathered[t, near : near + count].astype(jnp.float32)
        add = add + mul(inflow[t], gathered[t, near + count : 2 * near])
        if t < groups - 1:
            add = add + mul(outflow[0], gathered[t, 2 * near : near + far])
        outflow.insert(0, narrow(add))
    for t in range(groups):
        flow[0, t] = inflow[t]
        flow[1, t] = outflow[t]

    both = jnp.concatenate([flow[0, me], flow[1, me]], axis=1)
    for k in range(rows):
        value = base[k] + mul(both, response[k, count:])
        solution[k] = value
        rounded[k] = narrow(value)
    rounded[rows + 1] = flow[1, me]
    prior = lax.max(me - 1, 0)
    before = flow[0, me].astype(jnp.float32) + mul(flow[1, prior], gathered[prior, near + far :])
    rounded[rows] = narrow(jnp.where(me > 0, before, 0.0))
    rim = inner.shape[0]
    for e in range(rim):
        inner[e] = rounded[(1 - side) * (rows - rim) + e]
        outer[e] = rounded[side * (rows - rim) + e]


def local_kernel(rounded, diagonal, lower, upper, lower_at, upper_at, partial):
    rows, slots, width, _ = lower.shape
    upper_slots = upper.shape[1]
    for k in range(rows):
        total = mul(rounded[k], diagonal[k])
        source = [rounded[rows]]
        for m in range(1, slots):
            at = lower_at[m, k]
            source.append(rounded[jnp.where(at == k, rows, at)])
        total = total + mul(
            jnp.concatenate(source, axis=1), lower[k].reshape(slots * width, width)
        )
        source = [rounded[rows + 1]]
        for m in range(1, upper_slots):
            at = upper_at[m, k]
            source.append(rounded[jnp.where(at == k, rows + 1, at)])
        total = total + mul(
            jnp.concatenate(source, axis=1), upper[k].reshape(upper_slots * width, width)
        )
        partial[k] = total


def halo_kernel(axis, partial, inner, outer, halo, halo_at, product, rim_rows):
    rows, slots, width, _ = halo.shape
    rim = inner.shape[0]
    turn = rim * (1 - lax.rem(lax.axis_index(axis), 2))
    rim_rows[:rim] = inner[...]
    rim_rows[rim:] = outer[...]
    for k in range(rows):
        source = [
            rim_rows[lax.rem(halo_at[m, k] + turn, 2 * rim)] for m in range(slots)
        ]
        product[k] = partial[k] + mul(
            jnp.concatenate(source, axis=1), halo[k].reshape(slots * width, width)
        )


def swaps(block, axis, first):
    count = lax.axis_size(axis)
    pairs = []
    for low in range(first, count - 1, 2):
        pairs += [(low, low + 1), (low + 1, low)]
    return lax.ppermute(block, axis, pairs)


def on_device(
    right_sides,
    diag_inverse,
    diag_blocks,
    lower_blocks,
    upper_blocks,
    halo_blocks,
    lower_index,
    upper_index,
    halo_index,
):
    rows, count, width = right_sides.shape
    lower_at, upper_at, halo_at = lower_index.T, upper_index.T, halo_index.T
    slots = lower_blocks.shape[1]
    upper_slots = upper_blocks.shape[1]
    groups = lax.axis_size("section")
    near = count + width
    far = near + width
    wide = jax.ShapeDtypeStruct((rows, count, width), jnp.float32)

    base, response, payload = pl.pallas_call(
        sweep_kernel,
        out_shape=(
            wide,
            jax.ShapeDtypeStruct((rows, far, width), jnp.bfloat16),
            jax.ShapeDtypeStruct((near + far + width, width), jnp.bfloat16),
        ),
        in_specs=[HBM] * 6,
        out_specs=(VMEM, VMEM, VMEM),
        scratch_shapes=[
            pltpu.VMEM(right_sides.shape, right_sides.dtype),
            pltpu.VMEM(diag_inverse.shape, diag_inverse.dtype),
            pltpu.VMEM(lower_blocks.shape, lower_blocks.dtype),
            pltpu.VMEM(upper_blocks.shape, upper_blocks.dtype),
            pltpu.SMEM(lower_at.shape, jnp.int32),
            pltpu.SMEM(upper_at.shape, jnp.int32),
            pltpu.VMEM((rows, slots * width, width), jnp.bfloat16),
            pltpu.VMEM((rows, upper_slots * width, width), jnp.bfloat16),
            pltpu.VMEM((rows, near, width), jnp.bfloat16),
            pltpu.VMEM((rows, near, width), jnp.float32),
            pltpu.SemaphoreType.DMA((7,)),
        ],
        compiler_params=SMALL,
        name="sweeps",
    )(
        *(
            pltpu.with_memory_space_constraint(a, pltpu.HBM)
            for a in (right_sides, diag_inverse, lower_blocks, upper_blocks, lower_at, upper_at)
        )
    )

    gathered = lax.all_gather(payload, "section")

    def chain(*refs):
        chain_kernel(groups, ("section", "dom"), *refs)

    solution, rounded, inner, outer = pl.pallas_call(
        chain,
        out_shape=(
            wide,
            jax.ShapeDtypeStruct((rows + 2, count, width), jnp.bfloat16),
            jax.ShapeDtypeStruct((RIM, count, width), jnp.bfloat16),
            jax.ShapeDtypeStruct((RIM, count, width), jnp.bfloat16),
        ),
        in_specs=[VMEM] * 3,
        out_specs=(VMEM,) * 4,
        scratch_shapes=[pltpu.VMEM((2, groups, count, width), jnp.bfloat16)],
        compiler_params=SMALL,
        name="chain",
    )(gathered, base, response)

    outer = swaps(outer, "dom", 1)
    inner = swaps(inner, "dom", 0)

    partial = pl.pallas_call(
        local_kernel,
        out_shape=wide,
        in_specs=[VMEM] * 4 + [SMEM] * 2,
        out_specs=VMEM,
        compiler_params=SMALL,
        name="local_product",
    )(rounded, diag_blocks, lower_blocks, upper_blocks, lower_at, upper_at)

    def halo(*refs):
        halo_kernel("dom", *refs)

    product = pl.pallas_call(
        halo,
        out_shape=wide,
        in_specs=[VMEM] * 4 + [SMEM],
        out_specs=VMEM,
        scratch_shapes=[pltpu.VMEM((2 * RIM, count, width), jnp.bfloat16)],
        compiler_params=SMALL,
        name="halo_product",
    )(partial, inner, outer, halo_blocks, halo_at)
    return (solution, product)


def solution(mesh):
    in_specs = (
        P(("section", "dom"), None, None),
        P(("section", "dom"), None, None),
        P(("section", "dom"), None, None),
        P(("section", "dom"), None, None, None),
        P(("section", "dom"), None, None, None),
        P(("section", "dom"), None, None, None),
        P(("section", "dom"), None),
        P(("section", "dom"), None),
        P(("section", "dom"), None),
    )
    out_specs = (P(("section", "dom"), None, None), P(("section", "dom"), None, None))
    return jax.shard_map(
        on_device, mesh=mesh, in_specs=in_specs, out_specs=out_specs, check_vma=False
    )
```

```python
import jax
import jax.numpy as jnp
from jax import lax
from jax.experimental import pallas as pl
from jax.experimental.pallas import tpu as pltpu
from jax.sharding import PartitionSpec as P

RIM = 4

VMEM = pl.BlockSpec(memory_space=pltpu.VMEM)
SMEM = pl.BlockSpec(memory_space=pltpu.SMEM)
HBM = pl.BlockSpec(memory_space=pltpu.HBM)
SMALL = pltpu.CompilerParams(vmem_limit_bytes=16 * 1024 * 1024)


def mul(a, b):
    return jnp.dot(a, b, preferred_element_type=jnp.float32)


def narrow(a):
    return a.astype(jnp.bfloat16)


def sweep_kernel(
    rhs_far,
    inverse_far,
    lower_far,
    upper_far,
    lower_at_far,
    upper_at_far,
    base,
    response,
    payload,
    rhs,
    inverse,
    lower,
    upper,
    lower_at,
    upper_at,
    low,
    upp,
    down,
    exact,
    arrived,
):
    rows, count, width = rhs.shape
    slots = lower.shape[1]
    upper_slots = upper.shape[1]
    near = count + width
    last = rows - 1
    half = rows // 2
    parts = [
        (inverse_far, inverse),
        (rhs_far, rhs),
        (lower_far.at[:half], lower.at[:half]),
        (lower_at_far, lower_at),
        (lower_far.at[half:], lower.at[half:]),
        (upper_far, upper),
        (upper_at_far, upper_at),
    ]
    copies = [
        pltpu.make_async_copy(far, here, arrived.at[i]) for i, (far, here) in enumerate(parts)
    ]
    for copy in copies:
        copy.start()
    eye = narrow(
        lax.broadcasted_iota(jnp.int32, (width, width), 0)
        == lax.broadcasted_iota(jnp.int32, (width, width), 1)
    )
    down[:, :count] = jnp.zeros((rows, count, width), jnp.bfloat16)
    response[:, :near] = jnp.zeros((rows, near, width), jnp.bfloat16)
    for k in range(rows):
        down[k, count:] = eye
        response[k, near:] = eye

    for k in range(rows):
        if k == 0:
            for copy in copies[:4]:
                copy.wait()
        if k == half:
            for copy in copies[4:]:
                copy.wait()
            for j in range(rows):
                blocks = upper[j].reshape(upper_slots * width, width)
                upp[j] = narrow(mul(blocks, inverse[j]))
        own = inverse[k]
        scaled = mul(narrow(rhs[k]), own)
        low[k] = narrow(mul(lower[k].reshape(slots * width, width), own))
        if k == 0:
            total = low[k, :width].astype(jnp.float32)
            for m in range(1, slots):
                total = total + low[k, m * width : (m + 1) * width].astype(jnp.float32)
            exact[k, :count] = scaled
            exact[k, count:] = -total
        else:
            source = jnp.concatenate([down[lower_at[m, k]] for m in range(1, slots)], axis=1)
            summed = mul(source, low[k, width:])
            exact[k, :count] = scaled - summed[:count]
            exact[k, count:] = -low[k, :width].astype(jnp.float32) - summed[count:]
        down[k] = narrow(exact[k])

    for k in range(last, -1, -1):
        if k == last:
            total = upp[k, :width].astype(jnp.float32)
            for m in range(1, upper_slots):
                total = total + upp[k, m * width : (m + 1) * width].astype(jnp.float32)
            base[k] = exact[k, :count]
            response[k, :near] = narrow(exact[k])
            response[k, near:] = narrow(-total)
        else:
            source = jnp.concatenate(
                [response[upper_at[m, k]] for m in range(1, upper_slots)], axis=1
            )
            summed = mul(source, upp[k, width:])
            solved = exact[k] - summed[:near]
            base[k] = solved[:count]
            response[k, :near] = narrow(solved)
            response[k, near:] = narrow(-upp[k, :width].astype(jnp.float32) - summed[near:])

    far = near + width
    payload[:near] = down[last]
    payload[near : near + far] = response[0]
    payload[near + far :] = response[last, near:]


def compose_kernel(axis, bit, final, mine, theirs, *refs):
    prior, sent, inner, prior_out = refs[:4] if bit > 1 else (None, *refs[:3])
    pair = refs[-1]
    width = mine.shape[1]
    count = (mine.shape[0] - 4 * width) // 2
    near = count + width
    me = lax.axis_index(axis)
    place = lax.rem(lax.div(me, bit), 2)
    mid = near + count
    far = near + near + width

    pair[place] = mine[...]
    pair[1 - place] = theirs[...]
    a = pair[0]
    b = pair[1]
    across = mul(a[:near], jnp.concatenate([b[count:near], b[mid : mid + width]], axis=1))
    ahead = b[:near].astype(jnp.float32)
    joined = across[:, :width] + jnp.concatenate(
        [ahead[:count], jnp.zeros((width, width), jnp.float32)], axis=0
    )
    between = across[:, width:] + jnp.concatenate(
        [b[near:mid].astype(jnp.float32), jnp.zeros((width, width), jnp.float32)], axis=0
    )
    between = jnp.concatenate([narrow(between), b[mid + width : far]], axis=0)
    first = mul(between, a[mid + width : far])
    first = narrow(first[:near] + a[near : 2 * near].astype(jnp.float32)), narrow(first[near:])
    joined = narrow(joined)
    inner[:near] = a[:near]
    inner[near:] = between
    prior_out[...] = a[far:]
    if prior is not None:
        lowest = jnp.logical_and(place == 1, lax.rem(me, bit) == 0)

        @pl.when(jnp.logical_not(lowest))
        def _():
            prior_out[...] = prior[...]

    if final:
        refs[-2][...] = joined[:count]
        above = lax.rem(lax.div(me, 2 * bit), 2) == 1

        @pl.when(above)
        def _():
            sent[...] = first[0]

        @pl.when(jnp.logical_not(above))
        def _():
            sent[:count] = joined[:count]
            sent[count:] = b[far:]

    else:
        sent[:near] = joined
        sent[near : 2 * near] = first[0]
        sent[2 * near : far] = first[1]
        sent[far:] = b[far:]


def chain_kernel(axes, levels, *refs):
    own, theirs, base, response, prior = refs[:5]
    inner = refs[5 : 4 + levels]
    solution, rounded, prior_out, near_rows, far_rows = refs[4 + levels :]
    rows, count, width = base.shape
    near = count + width
    me = lax.axis_index(axes[0])
    side = lax.rem(lax.axis_index(axes[1]), 2)

    bit = 1 << (levels - 1)
    upper = lax.div(me, bit) == 1
    down = theirs[:count].astype(jnp.float32)
    up = down + mul(own[...], theirs[count:])
    inflow = narrow(jnp.where(upper, down, 0.0))
    outflow = narrow(jnp.where(upper, 0.0, up))
    prior_out[...] = prior[...]

    @pl.when(me == bit)
    def _():
        prior_out[...] = theirs[count:]

    for level in range(levels - 2, -1, -1):
        part = inner[level]
        upper = lax.rem(lax.div(me, 1 << level), 2) == 1
        down = part[:count].astype(jnp.float32) + mul(inflow, part[count:near])
        both = jnp.concatenate([inflow, outflow], axis=1)
        up = part[near : near + count].astype(jnp.float32) + mul(both, part[near + count :])
        inflow, outflow = (
            narrow(jnp.where(upper, down, inflow.astype(jnp.float32))),
            narrow(jnp.where(upper, outflow.astype(jnp.float32), up)),
        )

    both = jnp.concatenate([inflow, outflow], axis=1)
    for k in range(rows):
        value = base[k] + mul(both, response[k, count:])
        solution[k] = value
        rounded[k] = narrow(value)
    rounded[rows] = inflow
    rounded[rows + 1] = outflow
    rim = near_rows.shape[0]
    for e in range(rim):
        near_rows[e] = rounded[(1 - side) * (rows - rim) + e]
        far_rows[e] = rounded[side * (rows - rim) + e]


def local_kernel(
    axis,
    rounded,
    prior,
    solved,
    diagonal,
    lower,
    upper,
    lower_at,
    upper_at,
    partial,
    solution,
    held,
):
    solution[...] = solved[...]
    rows, slots, width, _ = lower.shape
    upper_slots = upper.shape[1]
    before = rounded[rows].astype(jnp.float32) + mul(rounded[0], prior[...])
    held[...] = rounded[...]
    held[rows] = narrow(jnp.where(lax.axis_index(axis) > 0, before, 0.0))
    for k in range(rows):
        total = mul(rounded[k], diagonal[k])
        source = [held[rows]]
        for m in range(1, slots):
            at = lower_at[m, k]
            source.append(held[jnp.where(at == k, rows, at)])
        total = total + mul(
            jnp.concatenate(source, axis=1), lower[k].reshape(slots * width, width)
        )
        source = [rounded[rows + 1]]
        for m in range(1, upper_slots):
            at = upper_at[m, k]
            source.append(rounded[jnp.where(at == k, rows + 1, at)])
        total = total + mul(
            jnp.concatenate(source, axis=1), upper[k].reshape(upper_slots * width, width)
        )
        partial[k] = total


def halo_kernel(axis, partial, outer, inner, halo, halo_at, product, rim_rows):
    rows, slots, width, _ = halo.shape
    rim = inner.shape[0]
    turn = rim * (1 - lax.rem(lax.axis_index(axis), 2))
    rim_rows[:rim] = inner[...]
    rim_rows[rim:] = outer[...]
    for k in range(rows):
        source = [
            rim_rows[lax.rem(halo_at[m, k] + turn, 2 * rim)] for m in range(slots)
        ]
        product[k] = partial[k] + mul(
            jnp.concatenate(source, axis=1), halo[k].reshape(slots * width, width)
        )


def trade(block, axis, bit):
    count = lax.axis_size(axis)
    return lax.ppermute(block, axis, [(i, i ^ bit) for i in range(count)])


def swaps(block, axis, first):
    count = lax.axis_size(axis)
    pairs = []
    for low in range(first, count - 1, 2):
        pairs += [(low, low + 1), (low + 1, low)]
    return lax.ppermute(block, axis, pairs)


def on_device(
    right_sides,
    diag_inverse,
    diag_blocks,
    lower_blocks,
    upper_blocks,
    halo_blocks,
    lower_index,
    upper_index,
    halo_index,
):
    rows, count, width = right_sides.shape
    lower_at, upper_at, halo_at = lower_index.T, upper_index.T, halo_index.T
    slots = lower_blocks.shape[1]
    upper_slots = upper_blocks.shape[1]
    groups = lax.axis_size("section")
    near = count + width
    far = near + width
    wide = jax.ShapeDtypeStruct((rows, count, width), jnp.float32)

    base, response, payload = pl.pallas_call(
        sweep_kernel,
        out_shape=(
            wide,
            jax.ShapeDtypeStruct((rows, far, width), jnp.bfloat16),
            jax.ShapeDtypeStruct((near + far + width, width), jnp.bfloat16),
        ),
        in_specs=[HBM] * 6,
        out_specs=(VMEM, VMEM, VMEM),
        scratch_shapes=[
            pltpu.VMEM(right_sides.shape, right_sides.dtype),
            pltpu.VMEM(diag_inverse.shape, diag_inverse.dtype),
            pltpu.VMEM(lower_blocks.shape, lower_blocks.dtype),
            pltpu.VMEM(upper_blocks.shape, upper_blocks.dtype),
            pltpu.SMEM(lower_at.shape, jnp.int32),
            pltpu.SMEM(upper_at.shape, jnp.int32),
            pltpu.VMEM((rows, slots * width, width), jnp.bfloat16),
            pltpu.VMEM((rows, upper_slots * width, width), jnp.bfloat16),
            pltpu.VMEM((rows, near, width), jnp.bfloat16),
            pltpu.VMEM((rows, near, width), jnp.float32),
            pltpu.SemaphoreType.DMA((7,)),
        ],
        compiler_params=SMALL,
        name="sweeps",
    )(
        *(
            pltpu.with_memory_space_constraint(a, pltpu.HBM)
            for a in (right_sides, diag_inverse, lower_blocks, upper_blocks, lower_at, upper_at)
        )
    )

    levels = groups.bit_length() - 1
    segment = payload.shape[0]
    bits = jnp.bfloat16
    prior = []
    inner = []
    for level in range(levels - 1):
        theirs = trade(payload, "section", 1 << level)
        final = level == levels - 2

        def compose(*refs, bit=1 << level, final=final):
            compose_kernel("section", bit, final, *refs)

        payload, between, *prior = pl.pallas_call(
            compose,
            out_shape=(
                jax.ShapeDtypeStruct((near if final else segment, width), bits),
                jax.ShapeDtypeStruct((near + far, width), bits),
                jax.ShapeDtypeStruct((width, width), bits),
            )
            + (jax.ShapeDtypeStruct((count, width), bits),) * final,
            in_specs=[VMEM] * (2 + len(prior)),
            out_specs=(VMEM,) * (3 + final),
            scratch_shapes=[pltpu.VMEM((2, segment, width), bits)],
            compiler_params=SMALL,
            name="compose",
        )(payload, theirs, *prior)
        inner.append(between)
    prior, own = prior
    theirs = trade(payload, "section", 1 << (levels - 1))

    def chain(*refs):
        chain_kernel(("section", "dom"), levels, *refs)

    solved, rounded, prior, inner, outer = pl.pallas_call(
        chain,
        out_shape=(
            wide,
            jax.ShapeDtypeStruct((rows + 2, count, width), bits),
            jax.ShapeDtypeStruct((width, width), bits),
            jax.ShapeDtypeStruct((RIM, count, width), bits),
            jax.ShapeDtypeStruct((RIM, count, width), bits),
        ),
        in_specs=[VMEM] * (4 + levels),
        out_specs=(VMEM,) * 5,
        compiler_params=SMALL,
        name="chain",
    )(own, theirs, base, response, prior, *inner)

    outer = swaps(outer, "dom", 1)
    inner = swaps(inner, "dom", 0)

    def local(*refs):
        local_kernel("section", *refs)

    partial, solution = pl.pallas_call(
        local,
        out_shape=(wide, wide),
        in_specs=[VMEM] * 6 + [SMEM] * 2,
        out_specs=(VMEM, VMEM),
        scratch_shapes=[pltpu.VMEM((rows + 2, count, width), bits)],
        compiler_params=SMALL,
        name="local_product",
    )(rounded, prior, solved, diag_blocks, lower_blocks, upper_blocks, lower_at, upper_at)

    def halo(*refs):
        halo_kernel("dom", *refs)

    product = pl.pallas_call(
        halo,
        out_shape=wide,
        in_specs=[VMEM] * 4 + [SMEM],
        out_specs=VMEM,
        scratch_shapes=[pltpu.VMEM((2 * RIM, count, width), jnp.bfloat16)],
        compiler_params=SMALL,
        name="halo_product",
    )(partial, outer, inner, halo_blocks, halo_at)
    return (solution, product)


def solution(mesh):
    in_specs = (
        P(("section", "dom"), None, None),
        P(("section", "dom"), None, None),
        P(("section", "dom"), None, None),
        P(("section", "dom"), None, None, None),
        P(("section", "dom"), None, None, None),
        P(("section", "dom"), None, None, None),
        P(("section", "dom"), None),
        P(("section", "dom"), None),
        P(("section", "dom"), None),
    )
    out_specs = (P(("section", "dom"), None, None), P(("section", "dom"), None, None))
    return jax.shard_map(
        on_device, mesh=mesh, in_specs=in_specs, out_specs=out_specs, check_vma=False
    )
```

```python
import jax
import jax.numpy as jnp
from jax import lax
from jax.experimental import pallas as pl
from jax.experimental.pallas import tpu as pltpu
from jax.sharding import PartitionSpec as P

RIM = 4

VMEM = pl.BlockSpec(memory_space=pltpu.VMEM)
SMEM = pl.BlockSpec(memory_space=pltpu.SMEM)
HBM = pl.BlockSpec(memory_space=pltpu.HBM)
SMALL = pltpu.CompilerParams(vmem_limit_bytes=16 * 1024 * 1024)


def mul(a, b):
    return jnp.dot(a, b, preferred_element_type=jnp.float32)


def narrow(a):
    return a.astype(jnp.bfloat16)


def sweep_kernel(
    rhs_far,
    inverse_far,
    lower_far,
    upper_far,
    lower_at_far,
    upper_at_far,
    halo_at_far,
    base,
    response,
    payload,
    lower_at_kept,
    upper_at_kept,
    halo_at_kept,
    rhs,
    inverse,
    lower,
    upper,
    lower_at,
    upper_at,
    low,
    upp,
    down,
    exact,
    arrived,
):
    rows, count, width = rhs.shape
    slots = lower.shape[1]
    upper_slots = upper.shape[1]
    near = count + width
    last = rows - 1
    half = rows // 2
    parts = [
        (inverse_far, inverse),
        (rhs_far, rhs),
        (lower_far.at[:half], lower.at[:half]),
        (lower_at_far, lower_at),
        (lower_far.at[half:], lower.at[half:]),
        (upper_far, upper),
        (upper_at_far, upper_at),
        (lower_at_far, lower_at_kept),
        (upper_at_far, upper_at_kept),
        (halo_at_far, halo_at_kept),
    ]
    copies = [
        pltpu.make_async_copy(far, here, arrived.at[i]) for i, (far, here) in enumerate(parts)
    ]
    for copy in copies:
        copy.start()
    eye = narrow(
        lax.broadcasted_iota(jnp.int32, (width, width), 0)
        == lax.broadcasted_iota(jnp.int32, (width, width), 1)
    )
    down[:, :count] = jnp.zeros((rows, count, width), jnp.bfloat16)
    response[:, :near] = jnp.zeros((rows, near, width), jnp.bfloat16)
    for k in range(rows):
        down[k, count:] = eye
        response[k, near:] = eye

    for k in range(rows):
        if k == 0:
            for copy in copies[:4]:
                copy.wait()
        if k == half:
            for copy in copies[4:]:
                copy.wait()
            for j in range(rows):
                blocks = upper[j].reshape(upper_slots * width, width)
                upp[j] = narrow(mul(blocks, inverse[j]))
        own = inverse[k]
        scaled = mul(narrow(rhs[k]), own)
        low[k] = narrow(mul(lower[k].reshape(slots * width, width), own))
        if k == 0:
            total = low[k, :width].astype(jnp.float32)
            for m in range(1, slots):
                total = total + low[k, m * width : (m + 1) * width].astype(jnp.float32)
            exact[k, :count] = scaled
            exact[k, count:] = -total
        else:
            source = jnp.concatenate([down[lower_at[m, k]] for m in range(1, slots)], axis=1)
            summed = mul(source, low[k, width:])
            exact[k, :count] = scaled - summed[:count]
            exact[k, count:] = -low[k, :width].astype(jnp.float32) - summed[count:]
        down[k] = narrow(exact[k])

    for k in range(last, -1, -1):
        if k == last:
            total = upp[k, :width].astype(jnp.float32)
            for m in range(1, upper_slots):
                total = total + upp[k, m * width : (m + 1) * width].astype(jnp.float32)
            base[k] = exact[k, :count]
            response[k, :near] = narrow(exact[k])
            response[k, near:] = narrow(-total)
        else:
            source = jnp.concatenate(
                [response[upper_at[m, k]] for m in range(1, upper_slots)], axis=1
            )
            summed = mul(source, upp[k, width:])
            solved = exact[k] - summed[:near]
            base[k] = solved[:count]
            response[k, :near] = narrow(solved)
            response[k, near:] = narrow(-upp[k, :width].astype(jnp.float32) - summed[near:])

    far = near + width
    payload[:near] = down[last]
    payload[near : near + far] = response[0]
    payload[near + far :] = response[last, near:]


def compose_kernel(axis, bit, final, mine, theirs, *refs):
    prior, sent, inner, prior_out = refs[:4] if bit > 1 else (None, *refs[:3])
    pair = refs[-1]
    width = mine.shape[1]
    count = (mine.shape[0] - 4 * width) // 2
    near = count + width
    me = lax.axis_index(axis)
    place = lax.rem(lax.div(me, bit), 2)
    mid = near + count
    far = near + near + width

    pair[place] = mine[...]
    pair[1 - place] = theirs[...]
    a = pair[0]
    b = pair[1]
    across = mul(a[:near], jnp.concatenate([b[count:near], b[mid : mid + width]], axis=1))
    ahead = b[:near].astype(jnp.float32)
    joined = across[:, :width] + jnp.concatenate(
        [ahead[:count], jnp.zeros((width, width), jnp.float32)], axis=0
    )
    between = across[:, width:] + jnp.concatenate(
        [b[near:mid].astype(jnp.float32), jnp.zeros((width, width), jnp.float32)], axis=0
    )
    between = jnp.concatenate([narrow(between), b[mid + width : far]], axis=0)
    first = mul(between, a[mid + width : far])
    first = narrow(first[:near] + a[near : 2 * near].astype(jnp.float32)), narrow(first[near:])
    joined = narrow(joined)
    inner[:near] = a[:near]
    inner[near:] = between
    prior_out[...] = a[far:]
    if prior is not None:
        lowest = jnp.logical_and(place == 1, lax.rem(me, bit) == 0)

        @pl.when(jnp.logical_not(lowest))
        def _():
            prior_out[...] = prior[...]

    if final:
        refs[-2][...] = joined[:count]
        above = lax.rem(lax.div(me, 2 * bit), 2) == 1

        @pl.when(above)
        def _():
            sent[...] = first[0]

        @pl.when(jnp.logical_not(above))
        def _():
            sent[:count] = joined[:count]
            sent[count:] = b[far:]

    else:
        sent[:near] = joined
        sent[near : 2 * near] = first[0]
        sent[2 * near : far] = first[1]
        sent[far:] = b[far:]


def chain_kernel(axes, levels, *refs):
    own, theirs, base, response, prior = refs[:5]
    inner = refs[5 : 4 + levels]
    solution, rounded, prior_out, near_rows, far_rows = refs[4 + levels :]
    rows, count, width = base.shape
    near = count + width
    me = lax.axis_index(axes[0])
    side = lax.rem(lax.axis_index(axes[1]), 2)

    bit = 1 << (levels - 1)
    upper = lax.div(me, bit) == 1
    down = theirs[:count].astype(jnp.float32)
    up = down + mul(own[...], theirs[count:])
    inflow = narrow(jnp.where(upper, down, 0.0))
    outflow = narrow(jnp.where(upper, 0.0, up))
    prior_out[...] = prior[...]

    @pl.when(me == bit)
    def _():
        prior_out[...] = theirs[count:]

    for level in range(levels - 2, -1, -1):
        part = inner[level]
        upper = lax.rem(lax.div(me, 1 << level), 2) == 1
        down = part[:count].astype(jnp.float32) + mul(inflow, part[count:near])
        both = jnp.concatenate([inflow, outflow], axis=1)
        up = part[near : near + count].astype(jnp.float32) + mul(both, part[near + count :])
        inflow, outflow = (
            narrow(jnp.where(upper, down, inflow.astype(jnp.float32))),
            narrow(jnp.where(upper, outflow.astype(jnp.float32), up)),
        )

    both = jnp.concatenate([inflow, outflow], axis=1)
    for k in range(rows):
        value = base[k] + mul(both, response[k, count:])
        solution[k] = value
        rounded[k] = narrow(value)
    rounded[rows] = inflow
    rounded[rows + 1] = outflow
    rim = near_rows.shape[0]
    for e in range(rim):
        near_rows[e] = rounded[(1 - side) * (rows - rim) + e]
        far_rows[e] = rounded[side * (rows - rim) + e]


def local_kernel(
    axis,
    rounded,
    prior,
    solved,
    diagonal,
    lower,
    upper,
    lower_at,
    upper_at,
    partial,
    solution,
    held,
    out,
):
    copy = pltpu.make_async_copy(solved, solution, out)
    copy.start()
    rows, slots, width, _ = lower.shape
    upper_slots = upper.shape[1]
    before = rounded[rows].astype(jnp.float32) + mul(rounded[0], prior[...])
    held[...] = rounded[...]
    held[rows] = narrow(jnp.where(lax.axis_index(axis) > 0, before, 0.0))
    for k in range(rows):
        total = mul(rounded[k], diagonal[k])
        source = [held[rows]]
        for m in range(1, slots):
            at = lower_at[m, k]
            source.append(held[jnp.where(at == k, rows, at)])
        total = total + mul(
            jnp.concatenate(source, axis=1), lower[k].reshape(slots * width, width)
        )
        source = [rounded[rows + 1]]
        for m in range(1, upper_slots):
            at = upper_at[m, k]
            source.append(rounded[jnp.where(at == k, rows + 1, at)])
        total = total + mul(
            jnp.concatenate(source, axis=1), upper[k].reshape(upper_slots * width, width)
        )
        partial[k] = total
    copy.wait()


def halo_kernel(axis, partial, outer, inner, halo, halo_at, product, rim_rows):
    rows, slots, width, _ = halo.shape
    rim = inner.shape[0]
    turn = rim * (1 - lax.rem(lax.axis_index(axis), 2))
    rim_rows[:rim] = inner[...]
    rim_rows[rim:] = outer[...]
    for k in range(rows):
        source = [
            rim_rows[lax.rem(halo_at[m, k] + turn, 2 * rim)] for m in range(slots)
        ]
        product[k] = partial[k] + mul(
            jnp.concatenate(source, axis=1), halo[k].reshape(slots * width, width)
        )


def trade(block, axis, bit):
    count = lax.axis_size(axis)
    return lax.ppermute(block, axis, [(i, i ^ bit) for i in range(count)])


def swaps(block, axis, first):
    count = lax.axis_size(axis)
    pairs = []
    for low in range(first, count - 1, 2):
        pairs += [(low, low + 1), (low + 1, low)]
    return lax.ppermute(block, axis, pairs)


def on_device(
    right_sides,
    diag_inverse,
    diag_blocks,
    lower_blocks,
    upper_blocks,
    halo_blocks,
    lower_index,
    upper_index,
    halo_index,
):
    rows, count, width = right_sides.shape
    lower_at, upper_at, halo_at = lower_index.T, upper_index.T, halo_index.T
    slots = lower_blocks.shape[1]
    upper_slots = upper_blocks.shape[1]
    groups = lax.axis_size("section")
    near = count + width
    far = near + width
    wide = jax.ShapeDtypeStruct((rows, count, width), jnp.float32)

    indices = (lower_at, upper_at, halo_at)
    base, response, payload, *indices = pl.pallas_call(
        sweep_kernel,
        out_shape=(
            wide,
            jax.ShapeDtypeStruct((rows, far, width), jnp.bfloat16),
            jax.ShapeDtypeStruct((near + far + width, width), jnp.bfloat16),
        )
        + tuple(jax.ShapeDtypeStruct(a.shape, a.dtype) for a in indices),
        in_specs=[HBM] * 7,
        out_specs=(VMEM,) * 6,
        scratch_shapes=[
            pltpu.VMEM(right_sides.shape, right_sides.dtype),
            pltpu.VMEM(diag_inverse.shape, diag_inverse.dtype),
            pltpu.VMEM(lower_blocks.shape, lower_blocks.dtype),
            pltpu.VMEM(upper_blocks.shape, upper_blocks.dtype),
            pltpu.SMEM(lower_at.shape, jnp.int32),
            pltpu.SMEM(upper_at.shape, jnp.int32),
            pltpu.VMEM((rows, slots * width, width), jnp.bfloat16),
            pltpu.VMEM((rows, upper_slots * width, width), jnp.bfloat16),
            pltpu.VMEM((rows, near, width), jnp.bfloat16),
            pltpu.VMEM((rows, near, width), jnp.float32),
            pltpu.SemaphoreType.DMA((10,)),
        ],
        compiler_params=SMALL,
        name="sweeps",
    )(
        *(
            pltpu.with_memory_space_constraint(a, pltpu.HBM)
            for a in (right_sides, diag_inverse, lower_blocks, upper_blocks, *indices)
        )
    )

    levels = groups.bit_length() - 1
    segment = payload.shape[0]
    bits = jnp.bfloat16
    prior = []
    inner = []
    for level in range(levels - 1):
        theirs = trade(payload, "section", 1 << level)
        final = level == levels - 2

        def compose(*refs, bit=1 << level, final=final):
            compose_kernel("section", bit, final, *refs)

        payload, between, *prior = pl.pallas_call(
            compose,
            out_shape=(
                jax.ShapeDtypeStruct((near if final else segment, width), bits),
                jax.ShapeDtypeStruct((near + far, width), bits),
                jax.ShapeDtypeStruct((width, width), bits),
            )
            + (jax.ShapeDtypeStruct((count, width), bits),) * final,
            in_specs=[VMEM] * (2 + len(prior)),
            out_specs=(VMEM,) * (3 + final),
            scratch_shapes=[pltpu.VMEM((2, segment, width), bits)],
            compiler_params=SMALL,
            name="compose",
        )(payload, theirs, *prior)
        inner.append(between)
    prior, own = prior
    theirs = trade(payload, "section", 1 << (levels - 1))

    def chain(*refs):
        chain_kernel(("section", "dom"), levels, *refs)

    solved, rounded, prior, inner, outer = pl.pallas_call(
        chain,
        out_shape=(
            wide,
            jax.ShapeDtypeStruct((rows + 2, count, width), bits),
            jax.ShapeDtypeStruct((width, width), bits),
            jax.ShapeDtypeStruct((RIM, count, width), bits),
            jax.ShapeDtypeStruct((RIM, count, width), bits),
        ),
        in_specs=[VMEM] * (4 + levels),
        out_specs=(VMEM,) * 5,
        compiler_params=SMALL,
        name="chain",
    )(own, theirs, base, response, prior, *inner)

    outer = swaps(outer, "dom", 1)
    inner = swaps(inner, "dom", 0)

    def local(*refs):
        local_kernel("section", *refs)

    partial, solution = pl.pallas_call(
        local,
        out_shape=(wide, wide),
        in_specs=[VMEM] * 6 + [SMEM] * 2,
        out_specs=(VMEM, HBM),
        scratch_shapes=[
            pltpu.VMEM((rows + 2, count, width), bits),
            pltpu.SemaphoreType.DMA(()),
        ],
        compiler_params=SMALL,
        name="local_product",
    )(rounded, prior, solved, diag_blocks, lower_blocks, upper_blocks, *indices[:2])

    def halo(*refs):
        halo_kernel("dom", *refs)

    product = pl.pallas_call(
        halo,
        out_shape=wide,
        in_specs=[VMEM] * 4 + [SMEM],
        out_specs=VMEM,
        scratch_shapes=[pltpu.VMEM((2 * RIM, count, width), jnp.bfloat16)],
        compiler_params=SMALL,
        name="halo_product",
    )(partial, outer, inner, halo_blocks, indices[2])
    return (solution, product)


def solution(mesh):
    in_specs = (
        P(("section", "dom"), None, None),
        P(("section", "dom"), None, None),
        P(("section", "dom"), None, None),
        P(("section", "dom"), None, None, None),
        P(("section", "dom"), None, None, None),
        P(("section", "dom"), None, None, None),
        P(("section", "dom"), None),
        P(("section", "dom"), None),
        P(("section", "dom"), None),
    )
    out_specs = (P(("section", "dom"), None, None), P(("section", "dom"), None, None))
    return jax.shard_map(
        on_device, mesh=mesh, in_specs=in_specs, out_specs=out_specs, check_vma=False
    )
```

```python
import jax
import jax.numpy as jnp
from jax import lax
from jax.experimental import pallas as pl
from jax.experimental.pallas import tpu as pltpu
from jax.sharding import PartitionSpec as P

RIM = 4

VMEM = pl.BlockSpec(memory_space=pltpu.VMEM)
SMEM = pl.BlockSpec(memory_space=pltpu.SMEM)
HBM = pl.BlockSpec(memory_space=pltpu.HBM)
SMALL = pltpu.CompilerParams(vmem_limit_bytes=16 * 1024 * 1024)


def mul(a, b):
    return jnp.dot(a, b, preferred_element_type=jnp.float32)


def narrow(a):
    return a.astype(jnp.bfloat16)


def sweep_kernel(
    rhs_far,
    inverse_far,
    lower_far,
    upper_far,
    lower_at_far,
    upper_at_far,
    halo_at_far,
    base,
    response,
    payload,
    lower_at_kept,
    upper_at_kept,
    halo_at_kept,
    rhs,
    inverse,
    lower,
    upper,
    lower_at,
    upper_at,
    low_pair,
    low_second,
    upp_pair,
    upp_second,
    down,
    exact,
    fixed,
    arrived,
):
    rows, count, width = rhs.shape
    slots = lower.shape[1]
    upper_slots = upper.shape[1]
    near = count + width
    last = rows - 1
    half = rows // 2
    parts = [
        (inverse_far, inverse),
        (rhs_far, rhs),
        (lower_far.at[:half], lower.at[:half]),
        (lower_at_far, lower_at),
        (lower_far.at[half:], lower.at[half:]),
        (upper_far, upper),
        (upper_at_far, upper_at),
        (lower_at_far, lower_at_kept),
        (upper_at_far, upper_at_kept),
        (halo_at_far, halo_at_kept),
    ]
    copies = [
        pltpu.make_async_copy(far, here, arrived.at[i]) for i, (far, here) in enumerate(parts)
    ]
    for copy in copies:
        copy.start()
    eye = narrow(
        lax.broadcasted_iota(jnp.int32, (width, width), 0)
        == lax.broadcasted_iota(jnp.int32, (width, width), 1)
    )
    down[:, :count] = jnp.zeros((rows + 1, count, width), jnp.bfloat16)
    response[:, :near] = jnp.zeros((rows + 1, near, width), jnp.bfloat16)
    for k in range(rows):
        down[k, count:] = eye
        response[k, near:] = eye
    down[rows, count:] = jnp.zeros_like(eye)
    response[rows, near:] = jnp.zeros_like(eye)

    def piece(blocks, m):
        return blocks[m * width : (m + 1) * width]

    def named(at, k, row, blocks, many):
        return sum(
            jnp.where(at[m, k] == row, piece(blocks, m), 0.0) for m in range(1, many)
        )

    def sources(held, at, k, skipped, many):
        picked = []
        for m in range(1, many):
            row = at[m, k]
            picked.append(held[row if skipped is None else jnp.where(row == skipped, rows, row)])
        return jnp.concatenate(picked, axis=1)

    def ready_down(p):
        a, b = 2 * p, 2 * p + 1
        both = []
        for k in (a, b):
            blocks = lower[k].reshape(slots * width, width)
            both.append(mul(jnp.concatenate([narrow(rhs[k]), blocks], axis=0), inverse[k]))
        of_a, of_b = both
        link = narrow(named(lower_at, b, a, of_b[count:], slots))
        of_a_narrow = narrow(of_a)
        through = mul(of_a_narrow, link)
        exact[a, :count] = of_a[:count]
        exact[a, count:] = -of_a[count:near]
        exact[b, :count] = of_b[:count] - through[:count]
        exact[b, count:] = through[count:near] - of_b[count:near]
        if p == 0:
            inner = sum(piece(of_a[count:], m) for m in range(1, slots))
            exact[a, count:] += -inner
            inner = sum(piece(through[count:], m) for m in range(1, slots))
            exact[b, count:] += inner - named(lower_at, b, b, of_b[count:], slots)
        else:
            low_pair[p, :, :width] = of_a_narrow[near:]
            low_pair[p, :, width:] = narrow(through[near:])
            low_second[p] = narrow(of_b[near:])

    def go_down(p):
        a, b = 2 * p, 2 * p + 1
        if p > 0:
            first = mul(sources(down, lower_at, a, None, slots), low_pair[p])
            second = mul(sources(down, lower_at, b, a, slots), low_second[p])
            exact[a] -= first[:, :width]
            exact[b] += first[:, width:] - second
        down[a] = narrow(exact[a])
        down[b] = narrow(exact[b])

    def ready_up(p):
        a = last - 2 * p
        b = a - 1
        of_a = mul(upper[a].reshape(upper_slots * width, width), inverse[a])
        of_b = mul(upper[b].reshape(upper_slots * width, width), inverse[b])
        link = narrow(named(upper_at, b, a, of_b, upper_slots))
        of_a_narrow = narrow(of_a)
        through = mul(of_a_narrow, link)
        fixed[a] = -of_a[:width]
        fixed[b] = through[:width] - of_b[:width]
        if p == 0:
            fixed[a] += -sum(piece(of_a, m) for m in range(1, upper_slots))
            inner = sum(piece(through, m) for m in range(1, upper_slots))
            fixed[b] += inner - named(upper_at, b, b, of_b, upper_slots)
        else:
            upp_pair[p, :, :width] = of_a_narrow[width:]
            upp_pair[p, :, width:] = narrow(through[width:])
            upp_second[p] = narrow(of_b[width:])
        return link

    def go_up(p, link):
        a = last - 2 * p
        b = a - 1
        of_a = exact[a]
        of_b = exact[b] - mul(down[a], link)
        free_a = fixed[a]
        free_b = fixed[b]
        if p > 0:
            first = mul(sources(response, upper_at, a, None, upper_slots), upp_pair[p])
            second = mul(sources(response, upper_at, b, a, upper_slots), upp_second[p])
            of_a = of_a - first[:near, :width]
            of_b = of_b + first[:near, width:] - second[:near]
            free_a = free_a - first[near:, :width]
            free_b = free_b + first[near:, width:] - second[near:]
        for k, value, free in ((a, of_a, free_a), (b, of_b, free_b)):
            base[k] = value[:count]
            response[k, :near] = narrow(value)
            response[k, near:] = narrow(free)

    pairs = rows // 2
    for copy in copies[:4]:
        copy.wait()
    links = []
    for p in range(pairs):
        if 2 * p + 2 > half and len(links) == 0:
            for copy in copies[4:]:
                copy.wait()
            links.append(ready_up(0))
        ready_down(p)
        go_down(p)
        if 0 < len(links) < pairs:
            links.append(ready_up(len(links)))
    while len(links) < pairs:
        links.append(ready_up(len(links)))
    for p in range(pairs):
        go_up(p, links[p])

    far = near + width
    payload[:near] = down[last]
    payload[near : near + far] = response[0]
    payload[near + far :] = response[last, near:]


def compose_kernel(axis, bit, final, mine, theirs, *refs):
    prior, sent, inner, prior_out = refs[:4] if bit > 1 else (None, *refs[:3])
    pair = refs[-1]
    width = mine.shape[1]
    count = (mine.shape[0] - 4 * width) // 2
    near = count + width
    me = lax.axis_index(axis)
    place = lax.rem(lax.div(me, bit), 2)
    mid = near + count
    far = near + near + width

    pair[place] = mine[...]
    pair[1 - place] = theirs[...]
    a = pair[0]
    b = pair[1]
    across = mul(a[:near], jnp.concatenate([b[count:near], b[mid : mid + width]], axis=1))
    ahead = b[:near].astype(jnp.float32)
    joined = across[:, :width] + jnp.concatenate(
        [ahead[:count], jnp.zeros((width, width), jnp.float32)], axis=0
    )
    between = across[:, width:] + jnp.concatenate(
        [b[near:mid].astype(jnp.float32), jnp.zeros((width, width), jnp.float32)], axis=0
    )
    between = jnp.concatenate([narrow(between), b[mid + width : far]], axis=0)
    first = mul(between, a[mid + width : far])
    first = narrow(first[:near] + a[near : 2 * near].astype(jnp.float32)), narrow(first[near:])
    joined = narrow(joined)
    inner[:near] = a[:near]
    inner[near:] = between
    prior_out[...] = a[far:]
    if prior is not None:
        lowest = jnp.logical_and(place == 1, lax.rem(me, bit) == 0)

        @pl.when(jnp.logical_not(lowest))
        def _():
            prior_out[...] = prior[...]

    if final:
        refs[-2][...] = joined[:count]
        above = lax.rem(lax.div(me, 2 * bit), 2) == 1

        @pl.when(above)
        def _():
            sent[...] = first[0]

        @pl.when(jnp.logical_not(above))
        def _():
            sent[:count] = joined[:count]
            sent[count:] = b[far:]

    else:
        sent[:near] = joined
        sent[near : 2 * near] = first[0]
        sent[2 * near : far] = first[1]
        sent[far:] = b[far:]


def chain_kernel(axes, levels, *refs):
    own, theirs, base, response, prior = refs[:5]
    inner = refs[5 : 4 + levels]
    solution, rounded, prior_out, near_rows, far_rows = refs[4 + levels :]
    rows, count, width = base.shape
    near = count + width
    me = lax.axis_index(axes[0])
    side = lax.rem(lax.axis_index(axes[1]), 2)

    bit = 1 << (levels - 1)
    upper = lax.div(me, bit) == 1
    down = theirs[:count].astype(jnp.float32)
    up = down + mul(own[...], theirs[count:])
    inflow = narrow(jnp.where(upper, down, 0.0))
    outflow = narrow(jnp.where(upper, 0.0, up))
    prior_out[...] = prior[...]

    @pl.when(me == bit)
    def _():
        prior_out[...] = theirs[count:]

    for level in range(levels - 2, -1, -1):
        part = inner[level]
        upper = lax.rem(lax.div(me, 1 << level), 2) == 1
        down = part[:count].astype(jnp.float32) + mul(inflow, part[count:near])
        both = jnp.concatenate([inflow, outflow], axis=1)
        up = part[near : near + count].astype(jnp.float32) + mul(both, part[near + count :])
        inflow, outflow = (
            narrow(jnp.where(upper, down, inflow.astype(jnp.float32))),
            narrow(jnp.where(upper, outflow.astype(jnp.float32), up)),
        )

    both = jnp.concatenate([inflow, outflow], axis=1)
    for k in range(rows):
        value = base[k] + mul(both, response[k, count:])
        solution[k] = value
        rounded[k] = narrow(value)
    rounded[rows] = inflow
    rounded[rows + 1] = outflow
    rim = near_rows.shape[0]
    for e in range(rim):
        near_rows[e] = rounded[(1 - side) * (rows - rim) + e]
        far_rows[e] = rounded[side * (rows - rim) + e]


def local_kernel(
    axis,
    rounded,
    prior,
    solved,
    diagonal,
    lower,
    upper,
    lower_at,
    upper_at,
    partial,
    solution,
    held,
    out,
):
    copy = pltpu.make_async_copy(solved, solution, out)
    copy.start()
    rows, slots, width, _ = lower.shape
    upper_slots = upper.shape[1]
    before = rounded[rows].astype(jnp.float32) + mul(rounded[0], prior[...])
    held[...] = rounded[...]
    held[rows] = narrow(jnp.where(lax.axis_index(axis) > 0, before, 0.0))
    for k in range(rows):
        total = mul(rounded[k], diagonal[k])
        source = [held[rows]]
        for m in range(1, slots):
            at = lower_at[m, k]
            source.append(held[jnp.where(at == k, rows, at)])
        total = total + mul(
            jnp.concatenate(source, axis=1), lower[k].reshape(slots * width, width)
        )
        source = [rounded[rows + 1]]
        for m in range(1, upper_slots):
            at = upper_at[m, k]
            source.append(rounded[jnp.where(at == k, rows + 1, at)])
        total = total + mul(
            jnp.concatenate(source, axis=1), upper[k].reshape(upper_slots * width, width)
        )
        partial[k] = total
    copy.wait()


def halo_kernel(axis, partial, outer, inner, halo, halo_at, product, rim_rows):
    rows, slots, width, _ = halo.shape
    rim = inner.shape[0]
    turn = rim * (1 - lax.rem(lax.axis_index(axis), 2))
    rim_rows[:rim] = inner[...]
    rim_rows[rim:] = outer[...]
    for k in range(rows):
        source = [
            rim_rows[lax.rem(halo_at[m, k] + turn, 2 * rim)] for m in range(slots)
        ]
        product[k] = partial[k] + mul(
            jnp.concatenate(source, axis=1), halo[k].reshape(slots * width, width)
        )


def trade(block, axis, bit):
    count = lax.axis_size(axis)
    return lax.ppermute(block, axis, [(i, i ^ bit) for i in range(count)])


def swaps(block, axis, first):
    count = lax.axis_size(axis)
    pairs = []
    for low in range(first, count - 1, 2):
        pairs += [(low, low + 1), (low + 1, low)]
    return lax.ppermute(block, axis, pairs)


def on_device(
    right_sides,
    diag_inverse,
    diag_blocks,
    lower_blocks,
    upper_blocks,
    halo_blocks,
    lower_index,
    upper_index,
    halo_index,
):
    rows, count, width = right_sides.shape
    lower_at, upper_at, halo_at = lower_index.T, upper_index.T, halo_index.T
    slots = lower_blocks.shape[1]
    upper_slots = upper_blocks.shape[1]
    groups = lax.axis_size("section")
    near = count + width
    far = near + width
    wide = jax.ShapeDtypeStruct((rows, count, width), jnp.float32)

    indices = (lower_at, upper_at, halo_at)
    base, response, payload, *indices = pl.pallas_call(
        sweep_kernel,
        out_shape=(
            wide,
            jax.ShapeDtypeStruct((rows + 1, far, width), jnp.bfloat16),
            jax.ShapeDtypeStruct((near + far + width, width), jnp.bfloat16),
        )
        + tuple(jax.ShapeDtypeStruct(a.shape, a.dtype) for a in indices),
        in_specs=[HBM] * 7,
        out_specs=(VMEM,) * 6,
        scratch_shapes=[
            pltpu.VMEM(right_sides.shape, right_sides.dtype),
            pltpu.VMEM(diag_inverse.shape, diag_inverse.dtype),
            pltpu.VMEM(lower_blocks.shape, lower_blocks.dtype),
            pltpu.VMEM(upper_blocks.shape, upper_blocks.dtype),
            pltpu.SMEM(lower_at.shape, jnp.int32),
            pltpu.SMEM(upper_at.shape, jnp.int32),
            pltpu.VMEM((rows // 2, (slots - 1) * width, 2 * width), jnp.bfloat16),
            pltpu.VMEM((rows // 2, (slots - 1) * width, width), jnp.bfloat16),
            pltpu.VMEM((rows // 2, (upper_slots - 1) * width, 2 * width), jnp.bfloat16),
            pltpu.VMEM((rows // 2, (upper_slots - 1) * width, width), jnp.bfloat16),
            pltpu.VMEM((rows + 1, near, width), jnp.bfloat16),
            pltpu.VMEM((rows, near, width), jnp.float32),
            pltpu.VMEM((rows, width, width), jnp.float32),
            pltpu.SemaphoreType.DMA((10,)),
        ],
        compiler_params=SMALL,
        name="sweeps",
    )(
        *(
            pltpu.with_memory_space_constraint(a, pltpu.HBM)
            for a in (right_sides, diag_inverse, lower_blocks, upper_blocks, *indices)
        )
    )

    levels = groups.bit_length() - 1
    segment = payload.shape[0]
    bits = jnp.bfloat16
    prior = []
    inner = []
    for level in range(levels - 1):
        theirs = trade(payload, "section", 1 << level)
        final = level == levels - 2

        def compose(*refs, bit=1 << level, final=final):
            compose_kernel("section", bit, final, *refs)

        payload, between, *prior = pl.pallas_call(
            compose,
            out_shape=(
                jax.ShapeDtypeStruct((near if final else segment, width), bits),
                jax.ShapeDtypeStruct((near + far, width), bits),
                jax.ShapeDtypeStruct((width, width), bits),
            )
            + (jax.ShapeDtypeStruct((count, width), bits),) * final,
            in_specs=[VMEM] * (2 + len(prior)),
            out_specs=(VMEM,) * (3 + final),
            scratch_shapes=[pltpu.VMEM((2, segment, width), bits)],
            compiler_params=SMALL,
            name="compose",
        )(payload, theirs, *prior)
        inner.append(between)
    prior, own = prior
    theirs = trade(payload, "section", 1 << (levels - 1))

    def chain(*refs):
        chain_kernel(("section", "dom"), levels, *refs)

    solved, rounded, prior, inner, outer = pl.pallas_call(
        chain,
        out_shape=(
            wide,
            jax.ShapeDtypeStruct((rows + 2, count, width), bits),
            jax.ShapeDtypeStruct((width, width), bits),
            jax.ShapeDtypeStruct((RIM, count, width), bits),
            jax.ShapeDtypeStruct((RIM, count, width), bits),
        ),
        in_specs=[VMEM] * (4 + levels),
        out_specs=(VMEM,) * 5,
        compiler_params=SMALL,
        name="chain",
    )(own, theirs, base, response, prior, *inner)

    outer = swaps(outer, "dom", 1)
    inner = swaps(inner, "dom", 0)

    def local(*refs):
        local_kernel("section", *refs)

    partial, solution = pl.pallas_call(
        local,
        out_shape=(wide, wide),
        in_specs=[VMEM] * 6 + [SMEM] * 2,
        out_specs=(VMEM, HBM),
        scratch_shapes=[
            pltpu.VMEM((rows + 2, count, width), bits),
            pltpu.SemaphoreType.DMA(()),
        ],
        compiler_params=SMALL,
        name="local_product",
    )(rounded, prior, solved, diag_blocks, lower_blocks, upper_blocks, *indices[:2])

    def halo(*refs):
        halo_kernel("dom", *refs)

    product = pl.pallas_call(
        halo,
        out_shape=wide,
        in_specs=[VMEM] * 4 + [SMEM],
        out_specs=VMEM,
        scratch_shapes=[pltpu.VMEM((2 * RIM, count, width), jnp.bfloat16)],
        compiler_params=SMALL,
        name="halo_product",
    )(partial, outer, inner, halo_blocks, indices[2])
    return (solution, product)


def solution(mesh):
    in_specs = (
        P(("section", "dom"), None, None),
        P(("section", "dom"), None, None),
        P(("section", "dom"), None, None),
        P(("section", "dom"), None, None, None),
        P(("section", "dom"), None, None, None),
        P(("section", "dom"), None, None, None),
        P(("section", "dom"), None),
        P(("section", "dom"), None),
        P(("section", "dom"), None),
    )
    out_specs = (P(("section", "dom"), None, None), P(("section", "dom"), None, None))
    return jax.shard_map(
        on_device, mesh=mesh, in_specs=in_specs, out_specs=out_specs, check_vma=False
    )
```

```python
import jax
import jax.numpy as jnp
from jax import lax
from jax.experimental import pallas as pl
from jax.experimental.pallas import tpu as pltpu
from jax.sharding import PartitionSpec as P

RIM = 4

VMEM = pl.BlockSpec(memory_space=pltpu.VMEM)
SMEM = pl.BlockSpec(memory_space=pltpu.SMEM)
HBM = pl.BlockSpec(memory_space=pltpu.HBM)
SMALL = pltpu.CompilerParams(vmem_limit_bytes=16 * 1024 * 1024)


def mul(a, b):
    return jnp.dot(a, b, preferred_element_type=jnp.float32)


def narrow(a):
    return a.astype(jnp.bfloat16)


def sweep_kernel(
    rhs_far,
    inverse_far,
    lower_far,
    upper_far,
    lower_at_far,
    upper_at_far,
    halo_at_far,
    base,
    response,
    payload,
    lower_at_kept,
    upper_at_kept,
    halo_at_kept,
    rhs,
    inverse,
    lower,
    upper,
    lower_at,
    upper_at,
    low_pair,
    low_second,
    upp_pair,
    upp_second,
    down,
    exact,
    fixed,
    arrived,
):
    rows, count, width = rhs.shape
    slots = lower.shape[1]
    upper_slots = upper.shape[1]
    near = count + width
    last = rows - 1
    parts = [
        (inverse_far.at[:2], inverse.at[:2]),
        (lower_far.at[:2], lower.at[:2]),
        (rhs_far, rhs),
        (lower_at_far, lower_at),
        (inverse_far.at[2:], inverse.at[2:]),
        (lower_far.at[2:], lower.at[2:]),
        (upper_far, upper),
        (upper_at_far, upper_at),
        (lower_at_far, lower_at_kept),
        (upper_at_far, upper_at_kept),
        (halo_at_far, halo_at_kept),
    ]
    copies = [
        pltpu.make_async_copy(far, here, arrived.at[i]) for i, (far, here) in enumerate(parts)
    ]
    for copy in copies:
        copy.start()
    eye = narrow(
        lax.broadcasted_iota(jnp.int32, (width, width), 0)
        == lax.broadcasted_iota(jnp.int32, (width, width), 1)
    )
    down[:, :count] = jnp.zeros((rows + 1, count, width), jnp.bfloat16)
    response[:, :near] = jnp.zeros((rows + 1, near, width), jnp.bfloat16)
    for k in range(rows):
        down[k, count:] = eye
        response[k, near:] = eye
    down[rows, count:] = jnp.zeros_like(eye)
    response[rows, near:] = jnp.zeros_like(eye)

    def piece(blocks, m):
        return blocks[m * width : (m + 1) * width]

    def named(at, k, row, blocks, many):
        return sum(jnp.where(at[m, k] == row, blocks[m], 0.0) for m in range(1, many))

    def linked(left, own, link):
        link = narrow(mul(own, narrow(link)))
        return mul(left, jnp.concatenate([own, link], axis=1))

    def first_pair(at, a, b, blocks, many, heads):
        of_a = [blocks[a, m].astype(jnp.float32) for m in range(many)]
        of_b = [blocks[b, m].astype(jnp.float32) for m in range(many)]
        left = [narrow(of_b[0] + named(at, b, b, of_b, many)), narrow(named(at, b, a, of_b, many))]
        of_b = mul(jnp.concatenate(heads[1:] + left, axis=0), inverse[b])
        left = jnp.concatenate(heads[:1] + [narrow(sum(of_a))], axis=0)
        link = of_b[of_b.shape[0] - width :]
        return linked(left, inverse[a], link), of_b, link

    def next_pair(at, a, b, blocks, many, heads, pair, second):
        left = blocks[b].reshape(many * width, width)
        of_b = mul(jnp.concatenate(heads[1:] + [left], axis=0), inverse[b])
        top = of_b.shape[0] - many * width
        link = named(at, b, a, [piece(of_b[top:], m) for m in range(many)], many)
        left = blocks[a].reshape(many * width, width)
        of_a = linked(jnp.concatenate(heads[:1] + [left], axis=0), inverse[a], link)
        pair[...] = narrow(of_a[top + width :])
        second[...] = narrow(of_b[top + width :])
        return of_a, of_b, link

    def sources(held, at, k, skipped, many):
        picked = []
        for m in range(1, many):
            row = at[m, k]
            picked.append(held[row if skipped is None else jnp.where(row == skipped, rows, row)])
        return jnp.concatenate(picked, axis=1)

    def ready_down(p):
        a, b = 2 * p, 2 * p + 1
        heads = [narrow(rhs[a]), narrow(rhs[b])]
        if p == 0:
            of_a, of_b, _ = first_pair(lower_at, a, b, lower, slots, heads)
        else:
            of_a, of_b, _ = next_pair(
                lower_at, a, b, lower, slots, heads, low_pair.at[p], low_second.at[p]
            )
        exact[a, :count] = of_a[:count, :width]
        exact[a, count:] = -of_a[count:near, :width]
        exact[b, :count] = of_b[:count] - of_a[:count, width:]
        exact[b, count:] = of_a[count:near, width:] - of_b[count:near]

    def go_down(p):
        a, b = 2 * p, 2 * p + 1
        if p > 0:
            first = mul(sources(down, lower_at, a, None, slots), low_pair[p])
            second = mul(sources(down, lower_at, b, a, slots), low_second[p])
            exact[a] -= first[:, :width]
            exact[b] += first[:, width:] - second
        down[a] = narrow(exact[a])
        down[b] = narrow(exact[b])

    def ready_up(p):
        a = last - 2 * p
        b = a - 1
        if p == 0:
            of_a, of_b, link = first_pair(upper_at, a, b, upper, upper_slots, [])
        else:
            of_a, of_b, link = next_pair(
                upper_at, a, b, upper, upper_slots, [], upp_pair.at[p], upp_second.at[p]
            )
        fixed[a] = -of_a[:width, :width]
        fixed[b] = of_a[:width, width:] - of_b[:width]
        return narrow(link)

    def go_up(p, link):
        a = last - 2 * p
        b = a - 1
        of_a = exact[a]
        of_b = exact[b] - mul(down[a], link)
        free_a = fixed[a]
        free_b = fixed[b]
        if p > 0:
            first = mul(sources(response, upper_at, a, None, upper_slots), upp_pair[p])
            second = mul(sources(response, upper_at, b, a, upper_slots), upp_second[p])
            of_a = of_a - first[:near, :width]
            of_b = of_b + first[:near, width:] - second[:near]
            free_a = free_a - first[near:, :width]
            free_b = free_b + first[near:, width:] - second[near:]
        for k, value, free in ((a, of_a, free_a), (b, of_b, free_b)):
            base[k] = value[:count]
            response[k, :near] = narrow(value)
            response[k, near:] = narrow(free)

    pairs = rows // 2
    links = []
    for copy in copies[:4]:
        copy.wait()
    ready_down(0)
    go_down(0)
    for copy in copies[4:6]:
        copy.wait()
    for p in range(1, pairs):
        ready_down(p)
        go_down(p)
        if p == 1:
            for copy in copies[6:]:
                copy.wait()
        links.append(ready_up(p - 1))
    links.append(ready_up(pairs - 1))
    for p in range(pairs):
        go_up(p, links[p])

    far = near + width
    payload[:near] = down[last]
    payload[near : near + far] = response[0]
    payload[near + far :] = response[last, near:]


def compose_kernel(axis, bit, final, mine, theirs, *refs):
    prior, sent, inner, prior_out = refs[:4] if bit > 1 else (None, *refs[:3])
    pair = refs[-1]
    width = mine.shape[1]
    count = (mine.shape[0] - 4 * width) // 2
    near = count + width
    me = lax.axis_index(axis)
    place = lax.rem(lax.div(me, bit), 2)
    mid = near + count
    far = near + near + width

    pair[place] = mine[...]
    pair[1 - place] = theirs[...]
    a = pair[0]
    b = pair[1]
    across = mul(a[:near], jnp.concatenate([b[count:near], b[mid : mid + width]], axis=1))
    ahead = b[:near].astype(jnp.float32)
    joined = across[:, :width] + jnp.concatenate(
        [ahead[:count], jnp.zeros((width, width), jnp.float32)], axis=0
    )
    between = across[:, width:] + jnp.concatenate(
        [b[near:mid].astype(jnp.float32), jnp.zeros((width, width), jnp.float32)], axis=0
    )
    between = jnp.concatenate([narrow(between), b[mid + width : far]], axis=0)
    first = mul(between, a[mid + width : far])
    first = narrow(first[:near] + a[near : 2 * near].astype(jnp.float32)), narrow(first[near:])
    joined = narrow(joined)
    inner[:near] = a[:near]
    inner[near:] = between
    prior_out[...] = a[far:]
    if prior is not None:
        lowest = jnp.logical_and(place == 1, lax.rem(me, bit) == 0)

        @pl.when(jnp.logical_not(lowest))
        def _():
            prior_out[...] = prior[...]

    if final:
        refs[-2][...] = joined[:count]
        above = lax.rem(lax.div(me, 2 * bit), 2) == 1

        @pl.when(above)
        def _():
            sent[...] = first[0]

        @pl.when(jnp.logical_not(above))
        def _():
            sent[:count] = joined[:count]
            sent[count:] = b[far:]

    else:
        sent[:near] = joined
        sent[near : 2 * near] = first[0]
        sent[2 * near : far] = first[1]
        sent[far:] = b[far:]


def chain_kernel(axes, levels, *refs):
    own, theirs, base, response, prior = refs[:5]
    inner = refs[5 : 4 + levels]
    solution, rounded, prior_out, near_rows, far_rows = refs[4 + levels :]
    rows, count, width = base.shape
    near = count + width
    me = lax.axis_index(axes[0])
    side = lax.rem(lax.axis_index(axes[1]), 2)

    bit = 1 << (levels - 1)
    upper = lax.div(me, bit) == 1
    down = theirs[:count].astype(jnp.float32)
    up = down + mul(own[...], theirs[count:])
    inflow = narrow(jnp.where(upper, down, 0.0))
    outflow = narrow(jnp.where(upper, 0.0, up))
    prior_out[...] = prior[...]

    @pl.when(me == bit)
    def _():
        prior_out[...] = theirs[count:]

    for level in range(levels - 2, -1, -1):
        part = inner[level]
        upper = lax.rem(lax.div(me, 1 << level), 2) == 1
        down = part[:count].astype(jnp.float32) + mul(inflow, part[count:near])
        both = jnp.concatenate([inflow, outflow], axis=1)
        up = part[near : near + count].astype(jnp.float32) + mul(both, part[near + count :])
        inflow, outflow = (
            narrow(jnp.where(upper, down, inflow.astype(jnp.float32))),
            narrow(jnp.where(upper, outflow.astype(jnp.float32), up)),
        )

    both = jnp.concatenate([inflow, outflow], axis=1)
    for k in range(rows):
        value = base[k] + mul(both, response[k, count:])
        solution[k] = value
        rounded[k] = narrow(value)
    rounded[rows] = inflow
    rounded[rows + 1] = outflow
    rim = near_rows.shape[0]
    for e in range(rim):
        near_rows[e] = rounded[(1 - side) * (rows - rim) + e]
        far_rows[e] = rounded[side * (rows - rim) + e]


def local_kernel(
    axis,
    rounded,
    prior,
    solved,
    diagonal,
    lower,
    upper,
    lower_at,
    upper_at,
    partial,
    solution,
    held,
    out,
):
    copy = pltpu.make_async_copy(solved, solution, out)
    copy.start()
    rows, slots, width, _ = lower.shape
    upper_slots = upper.shape[1]
    before = rounded[rows].astype(jnp.float32) + mul(rounded[0], prior[...])
    held[...] = rounded[...]
    held[rows] = narrow(jnp.where(lax.axis_index(axis) > 0, before, 0.0))
    for k in range(rows):
        total = mul(rounded[k], diagonal[k])
        source = [held[rows]]
        for m in range(1, slots):
            at = lower_at[m, k]
            source.append(held[jnp.where(at == k, rows, at)])
        total = total + mul(
            jnp.concatenate(source, axis=1), lower[k].reshape(slots * width, width)
        )
        source = [rounded[rows + 1]]
        for m in range(1, upper_slots):
            at = upper_at[m, k]
            source.append(rounded[jnp.where(at == k, rows + 1, at)])
        total = total + mul(
            jnp.concatenate(source, axis=1), upper[k].reshape(upper_slots * width, width)
        )
        partial[k] = total
    copy.wait()


def halo_kernel(axis, partial, outer, inner, halo, halo_at, product, rim_rows):
    rows, slots, width, _ = halo.shape
    rim = inner.shape[0]
    turn = rim * (1 - lax.rem(lax.axis_index(axis), 2))
    rim_rows[:rim] = inner[...]
    rim_rows[rim:] = outer[...]
    for k in range(rows):
        source = [
            rim_rows[lax.rem(halo_at[m, k] + turn, 2 * rim)] for m in range(slots)
        ]
        product[k] = partial[k] + mul(
            jnp.concatenate(source, axis=1), halo[k].reshape(slots * width, width)
        )


def trade(block, axis, bit):
    count = lax.axis_size(axis)
    return lax.ppermute(block, axis, [(i, i ^ bit) for i in range(count)])


def swaps(block, axis, first):
    count = lax.axis_size(axis)
    pairs = []
    for low in range(first, count - 1, 2):
        pairs += [(low, low + 1), (low + 1, low)]
    return lax.ppermute(block, axis, pairs)


def on_device(
    right_sides,
    diag_inverse,
    diag_blocks,
    lower_blocks,
    upper_blocks,
    halo_blocks,
    lower_index,
    upper_index,
    halo_index,
):
    rows, count, width = right_sides.shape
    lower_at, upper_at, halo_at = lower_index.T, upper_index.T, halo_index.T
    slots = lower_blocks.shape[1]
    upper_slots = upper_blocks.shape[1]
    groups = lax.axis_size("section")
    near = count + width
    far = near + width
    wide = jax.ShapeDtypeStruct((rows, count, width), jnp.float32)

    indices = (lower_at, upper_at, halo_at)
    base, response, payload, *indices = pl.pallas_call(
        sweep_kernel,
        out_shape=(
            wide,
            jax.ShapeDtypeStruct((rows + 1, far, width), jnp.bfloat16),
            jax.ShapeDtypeStruct((near + far + width, width), jnp.bfloat16),
        )
        + tuple(jax.ShapeDtypeStruct(a.shape, a.dtype) for a in indices),
        in_specs=[HBM] * 7,
        out_specs=(VMEM,) * 6,
        scratch_shapes=[
            pltpu.VMEM(right_sides.shape, right_sides.dtype),
            pltpu.VMEM(diag_inverse.shape, diag_inverse.dtype),
            pltpu.VMEM(lower_blocks.shape, lower_blocks.dtype),
            pltpu.VMEM(upper_blocks.shape, upper_blocks.dtype),
            pltpu.SMEM(lower_at.shape, jnp.int32),
            pltpu.SMEM(upper_at.shape, jnp.int32),
            pltpu.VMEM((rows // 2, (slots - 1) * width, 2 * width), jnp.bfloat16),
            pltpu.VMEM((rows // 2, (slots - 1) * width, width), jnp.bfloat16),
            pltpu.VMEM((rows // 2, (upper_slots - 1) * width, 2 * width), jnp.bfloat16),
            pltpu.VMEM((rows // 2, (upper_slots - 1) * width, width), jnp.bfloat16),
            pltpu.VMEM((rows + 1, near, width), jnp.bfloat16),
            pltpu.VMEM((rows, near, width), jnp.float32),
            pltpu.VMEM((rows, width, width), jnp.float32),
            pltpu.SemaphoreType.DMA((11,)),
        ],
        compiler_params=SMALL,
        name="sweeps",
    )(
        *(
            pltpu.with_memory_space_constraint(a, pltpu.HBM)
            for a in (right_sides, diag_inverse, lower_blocks, upper_blocks, *indices)
        )
    )

    levels = groups.bit_length() - 1
    segment = payload.shape[0]
    bits = jnp.bfloat16
    prior = []
    inner = []
    for level in range(levels - 1):
        theirs = trade(payload, "section", 1 << level)
        final = level == levels - 2

        def compose(*refs, bit=1 << level, final=final):
            compose_kernel("section", bit, final, *refs)

        payload, between, *prior = pl.pallas_call(
            compose,
            out_shape=(
                jax.ShapeDtypeStruct((near if final else segment, width), bits),
                jax.ShapeDtypeStruct((near + far, width), bits),
                jax.ShapeDtypeStruct((width, width), bits),
            )
            + (jax.ShapeDtypeStruct((count, width), bits),) * final,
            in_specs=[VMEM] * (2 + len(prior)),
            out_specs=(VMEM,) * (3 + final),
            scratch_shapes=[pltpu.VMEM((2, segment, width), bits)],
            compiler_params=SMALL,
            name="compose",
        )(payload, theirs, *prior)
        inner.append(between)
    prior, own = prior
    theirs = trade(payload, "section", 1 << (levels - 1))

    def chain(*refs):
        chain_kernel(("section", "dom"), levels, *refs)

    solved, rounded, prior, inner, outer = pl.pallas_call(
        chain,
        out_shape=(
            wide,
            jax.ShapeDtypeStruct((rows + 2, count, width), bits),
            jax.ShapeDtypeStruct((width, width), bits),
            jax.ShapeDtypeStruct((RIM, count, width), bits),
            jax.ShapeDtypeStruct((RIM, count, width), bits),
        ),
        in_specs=[VMEM] * (4 + levels),
        out_specs=(VMEM,) * 5,
        compiler_params=SMALL,
        name="chain",
    )(own, theirs, base, response, prior, *inner)

    outer = swaps(outer, "dom", 1)
    inner = swaps(inner, "dom", 0)

    def local(*refs):
        local_kernel("section", *refs)

    partial, solution = pl.pallas_call(
        local,
        out_shape=(wide, wide),
        in_specs=[VMEM] * 6 + [SMEM] * 2,
        out_specs=(VMEM, HBM),
        scratch_shapes=[
            pltpu.VMEM((rows + 2, count, width), bits),
            pltpu.SemaphoreType.DMA(()),
        ],
        compiler_params=SMALL,
        name="local_product",
    )(rounded, prior, solved, diag_blocks, lower_blocks, upper_blocks, *indices[:2])

    def halo(*refs):
        halo_kernel("dom", *refs)

    product = pl.pallas_call(
        halo,
        out_shape=wide,
        in_specs=[VMEM] * 4 + [SMEM],
        out_specs=VMEM,
        scratch_shapes=[pltpu.VMEM((2 * RIM, count, width), jnp.bfloat16)],
        compiler_params=SMALL,
        name="halo_product",
    )(partial, outer, inner, halo_blocks, indices[2])
    return (solution, product)


def solution(mesh):
    in_specs = (
        P(("section", "dom"), None, None),
        P(("section", "dom"), None, None),
        P(("section", "dom"), None, None),
        P(("section", "dom"), None, None, None),
        P(("section", "dom"), None, None, None),
        P(("section", "dom"), None, None, None),
        P(("section", "dom"), None),
        P(("section", "dom"), None),
        P(("section", "dom"), None),
    )
    out_specs = (P(("section", "dom"), None, None), P(("section", "dom"), None, None))
    return jax.shard_map(
        on_device, mesh=mesh, in_specs=in_specs, out_specs=out_specs, check_vma=False
    )
```

```python
import jax
import jax.numpy as jnp
from jax import lax
from jax.experimental import pallas as pl
from jax.experimental.pallas import tpu as pltpu
from jax.sharding import PartitionSpec as P

RIM = 4

VMEM = pl.BlockSpec(memory_space=pltpu.VMEM)
SMEM = pl.BlockSpec(memory_space=pltpu.SMEM)
HBM = pl.BlockSpec(memory_space=pltpu.HBM)
SMALL = pltpu.CompilerParams(vmem_limit_bytes=16 * 1024 * 1024)


def mul(a, b):
    return jnp.dot(a, b, preferred_element_type=jnp.float32)


def narrow(a):
    return a.astype(jnp.bfloat16)


def sweep_kernel(
    rhs_far,
    inverse_far,
    lower_far,
    upper_far,
    lower_at_far,
    upper_at_far,
    halo_at_far,
    base,
    response,
    payload,
    lower_at_kept,
    upper_at_kept,
    halo_at_kept,
    rhs,
    inverse,
    lower,
    upper,
    lower_at,
    upper_at,
    low_pair,
    low_second,
    upp_pair,
    upp_second,
    down,
    exact,
    fixed,
    arrived,
):
    rows, count, width = rhs.shape
    slots = lower.shape[1]
    upper_slots = upper.shape[1]
    near = count + width
    last = rows - 1
    half = rows // 2
    parts = [
        (inverse_far, inverse),
        (rhs_far, rhs),
        (lower_far.at[:half], lower.at[:half]),
        (lower_at_far, lower_at),
        (lower_far.at[half:], lower.at[half:]),
        (upper_far, upper),
        (upper_at_far, upper_at),
        (lower_at_far, lower_at_kept),
        (upper_at_far, upper_at_kept),
        (halo_at_far, halo_at_kept),
    ]
    copies = [
        pltpu.make_async_copy(far, here, arrived.at[i]) for i, (far, here) in enumerate(parts)
    ]
    for copy in copies:
        copy.start()
    eye = narrow(
        lax.broadcasted_iota(jnp.int32, (width, width), 0)
        == lax.broadcasted_iota(jnp.int32, (width, width), 1)
    )
    down[:, :count] = jnp.zeros((rows + 1, count, width), jnp.bfloat16)
    response[:, :near] = jnp.zeros((rows + 1, near, width), jnp.bfloat16)
    for k in range(rows):
        down[k, count:] = eye
        response[k, near:] = eye
    down[rows, count:] = jnp.zeros_like(eye)
    response[rows, near:] = jnp.zeros_like(eye)

    def piece(blocks, m):
        return blocks[m * width : (m + 1) * width]

    def named(at, k, row, blocks, many):
        return sum(
            jnp.where(at[m, k] == row, piece(blocks, m), 0.0) for m in range(1, many)
        )

    def sources(held, at, k, skipped, many):
        picked = []
        for m in range(1, many):
            row = at[m, k]
            picked.append(held[row if skipped is None else jnp.where(row == skipped, rows, row)])
        return jnp.concatenate(picked, axis=1)

    def apart(left, right, own, other):
        zero = jnp.zeros_like(own)
        sides = [jnp.concatenate([own, zero], axis=1), jnp.concatenate([zero, other], axis=1)]
        return mul(jnp.concatenate([left, right], axis=1), jnp.concatenate(sides, axis=0))

    def ready(at, blocks, many, first, step, heads):
        of_a, of_b, links = [], [], []
        for a in (first, first + 2 * step):
            b = a + step
            lefts = [
                jnp.concatenate(heads(k) + [blocks[k].reshape(many * width, width)], axis=0)
                for k in (a, b)
            ]
            both = apart(*lefts, inverse[a], inverse[b])
            of_a.append(both[:, :width])
            of_b.append(both[:, width:])
            tail = both[both.shape[0] - many * width :, width:]
            links.append(narrow(named(at, b, a, tail, many)))
        narrow_a = [narrow(value) for value in of_a]
        both = apart(*narrow_a, *links)
        through = [both[:, :width], both[:, width:]]
        return of_a, narrow_a, of_b, through, links

    def ready_down(p):
        of_a, narrow_a, of_b, through, _ = ready(
            lower_at, lower, slots, 2 * p, 1, lambda k: [narrow(rhs[k])]
        )
        for i in range(2):
            a, b = 2 * (p + i), 2 * (p + i) + 1
            exact[a, :count] = of_a[i][:count]
            exact[a, count:] = -of_a[i][count:near]
            exact[b, :count] = of_b[i][:count] - through[i][:count]
            exact[b, count:] = through[i][count:near] - of_b[i][count:near]
            if p + i == 0:
                inner = sum(piece(of_a[i][count:], m) for m in range(1, slots))
                exact[a, count:] += -inner
                inner = sum(piece(through[i][count:], m) for m in range(1, slots))
                exact[b, count:] += inner - named(lower_at, b, b, of_b[i][count:], slots)
            else:
                low_pair[p + i, :, :width] = narrow_a[i][near:]
                low_pair[p + i, :, width:] = narrow(through[i][near:])
                low_second[p + i] = narrow(of_b[i][near:])

    def go_down(p):
        a, b = 2 * p, 2 * p + 1
        if p > 0:
            first = mul(sources(down, lower_at, a, None, slots), low_pair[p])
            second = mul(sources(down, lower_at, b, a, slots), low_second[p])
            exact[a] -= first[:, :width]
            exact[b] += first[:, width:] - second
        down[a] = narrow(exact[a])
        down[b] = narrow(exact[b])

    def ready_up(p):
        of_a, narrow_a, of_b, through, links = ready(
            upper_at, upper, upper_slots, last - 2 * p, -1, lambda k: []
        )
        for i in range(2):
            a = last - 2 * (p + i)
            b = a - 1
            fixed[a] = -of_a[i][:width]
            fixed[b] = through[i][:width] - of_b[i][:width]
            if p + i == 0:
                fixed[a] += -sum(piece(of_a[i], m) for m in range(1, upper_slots))
                inner = sum(piece(through[i], m) for m in range(1, upper_slots))
                fixed[b] += inner - named(upper_at, b, b, of_b[i], upper_slots)
            else:
                upp_pair[p + i, :, :width] = narrow_a[i][width:]
                upp_pair[p + i, :, width:] = narrow(through[i][width:])
                upp_second[p + i] = narrow(of_b[i][width:])
        return links

    def go_up(p, link):
        a = last - 2 * p
        b = a - 1
        of_a = exact[a]
        of_b = exact[b] - mul(down[a], link)
        free_a = fixed[a]
        free_b = fixed[b]
        if p > 0:
            first = mul(sources(response, upper_at, a, None, upper_slots), upp_pair[p])
            second = mul(sources(response, upper_at, b, a, upper_slots), upp_second[p])
            of_a = of_a - first[:near, :width]
            of_b = of_b + first[:near, width:] - second[:near]
            free_a = free_a - first[near:, :width]
            free_b = free_b + first[near:, width:] - second[near:]
        for k, value, free in ((a, of_a, free_a), (b, of_b, free_b)):
            base[k] = value[:count]
            response[k, :near] = narrow(value)
            response[k, near:] = narrow(free)

    pairs = rows // 2
    for copy in copies[:4]:
        copy.wait()
    ready_down(0)
    go_down(0)
    for copy in copies[4:]:
        copy.wait()
    links = []
    for p in range(1, pairs):
        if p % 2 == 1 and p + 1 < pairs:
            ready_down(p + 1)
        go_down(p)
        if p % 2 == 1:
            links += ready_up(p - 1)
    for p in range(pairs):
        go_up(p, links[p])

    far = near + width
    payload[:near] = down[last]
    payload[near : near + far] = response[0]
    payload[near + far :] = response[last, near:]


def compose_kernel(axis, bit, final, mine, theirs, *refs):
    prior, sent, inner, prior_out = refs[:4] if bit > 1 else (None, *refs[:3])
    pair = refs[-1]
    width = mine.shape[1]
    count = (mine.shape[0] - 4 * width) // 2
    near = count + width
    me = lax.axis_index(axis)
    place = lax.rem(lax.div(me, bit), 2)
    mid = near + count
    far = near + near + width

    pair[place] = mine[...]
    pair[1 - place] = theirs[...]
    a = pair[0]
    b = pair[1]
    across = mul(a[:near], jnp.concatenate([b[count:near], b[mid : mid + width]], axis=1))
    ahead = b[:near].astype(jnp.float32)
    joined = across[:, :width] + jnp.concatenate(
        [ahead[:count], jnp.zeros((width, width), jnp.float32)], axis=0
    )
    between = across[:, width:] + jnp.concatenate(
        [b[near:mid].astype(jnp.float32), jnp.zeros((width, width), jnp.float32)], axis=0
    )
    between = jnp.concatenate([narrow(between), b[mid + width : far]], axis=0)
    first = mul(between, a[mid + width : far])
    first = narrow(first[:near] + a[near : 2 * near].astype(jnp.float32)), narrow(first[near:])
    joined = narrow(joined)
    inner[:near] = a[:near]
    inner[near:] = between
    prior_out[...] = a[far:]
    if prior is not None:
        lowest = jnp.logical_and(place == 1, lax.rem(me, bit) == 0)

        @pl.when(jnp.logical_not(lowest))
        def _():
            prior_out[...] = prior[...]

    if final:
        refs[-2][...] = joined[:count]
        above = lax.rem(lax.div(me, 2 * bit), 2) == 1

        @pl.when(above)
        def _():
            sent[...] = first[0]

        @pl.when(jnp.logical_not(above))
        def _():
            sent[:count] = joined[:count]
            sent[count:] = b[far:]

    else:
        sent[:near] = joined
        sent[near : 2 * near] = first[0]
        sent[2 * near : far] = first[1]
        sent[far:] = b[far:]


def chain_kernel(axes, levels, *refs):
    own, theirs, base, response, prior = refs[:5]
    inner = refs[5 : 4 + levels]
    solution, rounded, prior_out, near_rows, far_rows = refs[4 + levels :]
    rows, count, width = base.shape
    near = count + width
    me = lax.axis_index(axes[0])
    side = lax.rem(lax.axis_index(axes[1]), 2)

    bit = 1 << (levels - 1)
    upper = lax.div(me, bit) == 1
    down = theirs[:count].astype(jnp.float32)
    up = down + mul(own[...], theirs[count:])
    inflow = narrow(jnp.where(upper, down, 0.0))
    outflow = narrow(jnp.where(upper, 0.0, up))
    prior_out[...] = prior[...]

    @pl.when(me == bit)
    def _():
        prior_out[...] = theirs[count:]

    for level in range(levels - 2, -1, -1):
        part = inner[level]
        upper = lax.rem(lax.div(me, 1 << level), 2) == 1
        down = part[:count].astype(jnp.float32) + mul(inflow, part[count:near])
        both = jnp.concatenate([inflow, outflow], axis=1)
        up = part[near : near + count].astype(jnp.float32) + mul(both, part[near + count :])
        inflow, outflow = (
            narrow(jnp.where(upper, down, inflow.astype(jnp.float32))),
            narrow(jnp.where(upper, outflow.astype(jnp.float32), up)),
        )

    both = jnp.concatenate([inflow, outflow], axis=1)
    for k in range(rows):
        value = base[k] + mul(both, response[k, count:])
        solution[k] = value
        rounded[k] = narrow(value)
    rounded[rows] = inflow
    rounded[rows + 1] = outflow
    rim = near_rows.shape[0]
    for e in range(rim):
        near_rows[e] = rounded[(1 - side) * (rows - rim) + e]
        far_rows[e] = rounded[side * (rows - rim) + e]


def local_kernel(
    axis,
    rounded,
    prior,
    solved,
    diagonal,
    lower,
    upper,
    lower_at,
    upper_at,
    partial,
    solution,
    held,
    out,
):
    copy = pltpu.make_async_copy(solved, solution, out)
    copy.start()
    rows, slots, width, _ = lower.shape
    upper_slots = upper.shape[1]
    before = rounded[rows].astype(jnp.float32) + mul(rounded[0], prior[...])
    held[...] = rounded[...]
    held[rows] = narrow(jnp.where(lax.axis_index(axis) > 0, before, 0.0))
    for k in range(rows):
        total = mul(rounded[k], diagonal[k])
        source = [held[rows]]
        for m in range(1, slots):
            at = lower_at[m, k]
            source.append(held[jnp.where(at == k, rows, at)])
        total = total + mul(
            jnp.concatenate(source, axis=1), lower[k].reshape(slots * width, width)
        )
        source = [rounded[rows + 1]]
        for m in range(1, upper_slots):
            at = upper_at[m, k]
            source.append(rounded[jnp.where(at == k, rows + 1, at)])
        total = total + mul(
            jnp.concatenate(source, axis=1), upper[k].reshape(upper_slots * width, width)
        )
        partial[k] = total
    copy.wait()


def halo_kernel(axis, partial, outer, inner, halo, halo_at, product, rim_rows):
    rows, slots, width, _ = halo.shape
    rim = inner.shape[0]
    turn = rim * (1 - lax.rem(lax.axis_index(axis), 2))
    rim_rows[:rim] = inner[...]
    rim_rows[rim:] = outer[...]
    for k in range(rows):
        source = [
            rim_rows[lax.rem(halo_at[m, k] + turn, 2 * rim)] for m in range(slots)
        ]
        product[k] = partial[k] + mul(
            jnp.concatenate(source, axis=1), halo[k].reshape(slots * width, width)
        )


def trade(block, axis, bit):
    count = lax.axis_size(axis)
    return lax.ppermute(block, axis, [(i, i ^ bit) for i in range(count)])


def swaps(block, axis, first):
    count = lax.axis_size(axis)
    pairs = []
    for low in range(first, count - 1, 2):
        pairs += [(low, low + 1), (low + 1, low)]
    return lax.ppermute(block, axis, pairs)


def on_device(
    right_sides,
    diag_inverse,
    diag_blocks,
    lower_blocks,
    upper_blocks,
    halo_blocks,
    lower_index,
    upper_index,
    halo_index,
):
    rows, count, width = right_sides.shape
    lower_at, upper_at, halo_at = lower_index.T, upper_index.T, halo_index.T
    slots = lower_blocks.shape[1]
    upper_slots = upper_blocks.shape[1]
    groups = lax.axis_size("section")
    near = count + width
    far = near + width
    wide = jax.ShapeDtypeStruct((rows, count, width), jnp.float32)

    indices = (lower_at, upper_at, halo_at)
    base, response, payload, *indices = pl.pallas_call(
        sweep_kernel,
        out_shape=(
            wide,
            jax.ShapeDtypeStruct((rows + 1, far, width), jnp.bfloat16),
            jax.ShapeDtypeStruct((near + far + width, width), jnp.bfloat16),
        )
        + tuple(jax.ShapeDtypeStruct(a.shape, a.dtype) for a in indices),
        in_specs=[HBM] * 7,
        out_specs=(VMEM,) * 6,
        scratch_shapes=[
            pltpu.VMEM(right_sides.shape, right_sides.dtype),
            pltpu.VMEM(diag_inverse.shape, diag_inverse.dtype),
            pltpu.VMEM(lower_blocks.shape, lower_blocks.dtype),
            pltpu.VMEM(upper_blocks.shape, upper_blocks.dtype),
            pltpu.SMEM(lower_at.shape, jnp.int32),
            pltpu.SMEM(upper_at.shape, jnp.int32),
            pltpu.VMEM((rows // 2, (slots - 1) * width, 2 * width), jnp.bfloat16),
            pltpu.VMEM((rows // 2, (slots - 1) * width, width), jnp.bfloat16),
            pltpu.VMEM((rows // 2, (upper_slots - 1) * width, 2 * width), jnp.bfloat16),
            pltpu.VMEM((rows // 2, (upper_slots - 1) * width, width), jnp.bfloat16),
            pltpu.VMEM((rows + 1, near, width), jnp.bfloat16),
            pltpu.VMEM((rows, near, width), jnp.float32),
            pltpu.VMEM((rows, width, width), jnp.float32),
            pltpu.SemaphoreType.DMA((10,)),
        ],
        compiler_params=SMALL,
        name="sweeps",
    )(
        *(
            pltpu.with_memory_space_constraint(a, pltpu.HBM)
            for a in (right_sides, diag_inverse, lower_blocks, upper_blocks, *indices)
        )
    )

    levels = groups.bit_length() - 1
    segment = payload.shape[0]
    bits = jnp.bfloat16
    prior = []
    inner = []
    for level in range(levels - 1):
        theirs = trade(payload, "section", 1 << level)
        final = level == levels - 2

        def compose(*refs, bit=1 << level, final=final):
            compose_kernel("section", bit, final, *refs)

        payload, between, *prior = pl.pallas_call(
            compose,
            out_shape=(
                jax.ShapeDtypeStruct((near if final else segment, width), bits),
                jax.ShapeDtypeStruct((near + far, width), bits),
                jax.ShapeDtypeStruct((width, width), bits),
            )
            + (jax.ShapeDtypeStruct((count, width), bits),) * final,
            in_specs=[VMEM] * (2 + len(prior)),
            out_specs=(VMEM,) * (3 + final),
            scratch_shapes=[pltpu.VMEM((2, segment, width), bits)],
            compiler_params=SMALL,
            name="compose",
        )(payload, theirs, *prior)
        inner.append(between)
    prior, own = prior
    theirs = trade(payload, "section", 1 << (levels - 1))

    def chain(*refs):
        chain_kernel(("section", "dom"), levels, *refs)

    solved, rounded, prior, inner, outer = pl.pallas_call(
        chain,
        out_shape=(
            wide,
            jax.ShapeDtypeStruct((rows + 2, count, width), bits),
            jax.ShapeDtypeStruct((width, width), bits),
            jax.ShapeDtypeStruct((RIM, count, width), bits),
            jax.ShapeDtypeStruct((RIM, count, width), bits),
        ),
        in_specs=[VMEM] * (4 + levels),
        out_specs=(VMEM,) * 5,
        compiler_params=SMALL,
        name="chain",
    )(own, theirs, base, response, prior, *inner)

    outer = swaps(outer, "dom", 1)
    inner = swaps(inner, "dom", 0)

    def local(*refs):
        local_kernel("section", *refs)

    partial, solution = pl.pallas_call(
        local,
        out_shape=(wide, wide),
        in_specs=[VMEM] * 6 + [SMEM] * 2,
        out_specs=(VMEM, HBM),
        scratch_shapes=[
            pltpu.VMEM((rows + 2, count, width), bits),
            pltpu.SemaphoreType.DMA(()),
        ],
        compiler_params=SMALL,
        name="local_product",
    )(rounded, prior, solved, diag_blocks, lower_blocks, upper_blocks, *indices[:2])

    def halo(*refs):
        halo_kernel("dom", *refs)

    product = pl.pallas_call(
        halo,
        out_shape=wide,
        in_specs=[VMEM] * 4 + [SMEM],
        out_specs=VMEM,
        scratch_shapes=[pltpu.VMEM((2 * RIM, count, width), jnp.bfloat16)],
        compiler_params=SMALL,
        name="halo_product",
    )(partial, outer, inner, halo_blocks, indices[2])
    return (solution, product)


def solution(mesh):
    in_specs = (
        P(("section", "dom"), None, None),
        P(("section", "dom"), None, None),
        P(("section", "dom"), None, None),
        P(("section", "dom"), None, None, None),
        P(("section", "dom"), None, None, None),
        P(("section", "dom"), None, None, None),
        P(("section", "dom"), None),
        P(("section", "dom"), None),
        P(("section", "dom"), None),
    )
    out_specs = (P(("section", "dom"), None, None), P(("section", "dom"), None, None))
    return jax.shard_map(
        on_device, mesh=mesh, in_specs=in_specs, out_specs=out_specs, check_vma=False
    )
```

```python
import jax
import jax.numpy as jnp
from jax import lax
from jax.experimental import pallas as pl
from jax.experimental.pallas import tpu as pltpu
from jax.sharding import PartitionSpec as P

RIM = 4

VMEM = pl.BlockSpec(memory_space=pltpu.VMEM)
SMEM = pl.BlockSpec(memory_space=pltpu.SMEM)
HBM = pl.BlockSpec(memory_space=pltpu.HBM)
SMALL = pltpu.CompilerParams(vmem_limit_bytes=16 * 1024 * 1024)


def mul(a, b):
    return jnp.dot(a, b, preferred_element_type=jnp.float32)


def narrow(a):
    return a.astype(jnp.bfloat16)


def sweep_kernel(
    rhs_far,
    inverse_far,
    lower_far,
    upper_far,
    lower_at_far,
    upper_at_far,
    halo_at_far,
    base,
    response,
    payload,
    lower_at_kept,
    upper_at_kept,
    halo_at_kept,
    rhs,
    inverse,
    lower,
    upper,
    lower_at,
    upper_at,
    low_pair,
    low_second,
    upp_pair,
    upp_second,
    down,
    exact,
    fixed,
    arrived,
):
    rows, count, width = rhs.shape
    slots = lower.shape[1]
    upper_slots = upper.shape[1]
    near = count + width
    last = rows - 1
    half = rows // 2
    parts = [
        (inverse_far, inverse),
        (rhs_far, rhs),
        (lower_far.at[:half], lower.at[:half]),
        (lower_at_far, lower_at),
        (lower_far.at[half:], lower.at[half:]),
        (upper_far, upper),
        (upper_at_far, upper_at),
        (lower_at_far, lower_at_kept),
        (upper_at_far, upper_at_kept),
        (halo_at_far, halo_at_kept),
    ]
    copies = [
        pltpu.make_async_copy(far, here, arrived.at[i]) for i, (far, here) in enumerate(parts)
    ]
    for copy in copies:
        copy.start()
    eye = narrow(
        lax.broadcasted_iota(jnp.int32, (width, width), 0)
        == lax.broadcasted_iota(jnp.int32, (width, width), 1)
    )
    down[:, :count] = jnp.zeros((rows + 1, count, width), jnp.bfloat16)
    response[:, :near] = jnp.zeros((rows + 1, near, width), jnp.bfloat16)
    for k in range(rows):
        down[k, count:] = eye
        response[k, near:] = eye
    down[rows, count:] = jnp.zeros_like(eye)
    response[rows, near:] = jnp.zeros_like(eye)

    def piece(blocks, m):
        return blocks[m * width : (m + 1) * width]

    def named(at, k, row, blocks, many):
        return sum(
            jnp.where(at[m, k] == row, piece(blocks, m), 0.0) for m in range(1, many)
        )

    def sources(held, at, k, skipped, many):
        picked = []
        for m in range(1, many):
            row = at[m, k]
            picked.append(held[row if skipped is None else jnp.where(row == skipped, rows, row)])
        return jnp.concatenate(picked, axis=1)

    def apart(left, right, own, other):
        zero = jnp.zeros_like(own)
        sides = [jnp.concatenate([own, zero], axis=1), jnp.concatenate([zero, other], axis=1)]
        return mul(jnp.concatenate([left, right], axis=1), jnp.concatenate(sides, axis=0))

    def ready(at, blocks, many, first, step, heads):
        of_a, of_b, links = [], [], []
        for a in (first, first + 2 * step):
            b = a + step
            lefts = [
                jnp.concatenate(heads(k) + [blocks[k].reshape(many * width, width)], axis=0)
                for k in (a, b)
            ]
            both = apart(*lefts, inverse[a], inverse[b])
            of_a.append(both[:, :width])
            of_b.append(both[:, width:])
            tail = both[both.shape[0] - many * width :, width:]
            links.append(narrow(named(at, b, a, tail, many)))
        narrow_a = [narrow(value) for value in of_a]
        both = apart(*narrow_a, *links)
        through = [both[:, :width], both[:, width:]]
        return of_a, narrow_a, of_b, through, links

    def ready_down(p):
        of_a, narrow_a, of_b, through, _ = ready(
            lower_at, lower, slots, 2 * p, 1, lambda k: [narrow(rhs[k])]
        )
        for i in range(2):
            a, b = 2 * (p + i), 2 * (p + i) + 1
            exact[a, :count] = of_a[i][:count]
            exact[a, count:] = -of_a[i][count:near]
            exact[b, :count] = of_b[i][:count] - through[i][:count]
            exact[b, count:] = through[i][count:near] - of_b[i][count:near]
            if p + i == 0:
                inner = sum(piece(of_a[i][count:], m) for m in range(1, slots))
                exact[a, count:] += -inner
                inner = sum(piece(through[i][count:], m) for m in range(1, slots))
                exact[b, count:] += inner - named(lower_at, b, b, of_b[i][count:], slots)
            else:
                low_pair[p + i, :, :width] = narrow_a[i][near:]
                low_pair[p + i, :, width:] = narrow(through[i][near:])
                low_second[p + i] = narrow(of_b[i][near:])

    def go_down(p):
        a, b = 2 * p, 2 * p + 1
        if p > 0:
            first = mul(sources(down, lower_at, a, None, slots), low_pair[p])
            second = mul(sources(down, lower_at, b, a, slots), low_second[p])
            exact[a] -= first[:, :width]
            exact[b] += first[:, width:] - second
        down[a] = narrow(exact[a])
        down[b] = narrow(exact[b])

    def ready_up(p):
        of_a, narrow_a, of_b, through, links = ready(
            upper_at, upper, upper_slots, last - 2 * p, -1, lambda k: []
        )
        for i in range(2):
            a = last - 2 * (p + i)
            b = a - 1
            fixed[a] = -of_a[i][:width]
            fixed[b] = through[i][:width] - of_b[i][:width]
            if p + i == 0:
                fixed[a] += -sum(piece(of_a[i], m) for m in range(1, upper_slots))
                inner = sum(piece(through[i], m) for m in range(1, upper_slots))
                fixed[b] += inner - named(upper_at, b, b, of_b[i], upper_slots)
            else:
                upp_pair[p + i, :, :width] = narrow_a[i][width:]
                upp_pair[p + i, :, width:] = narrow(through[i][width:])
                upp_second[p + i] = narrow(of_b[i][width:])
        return links

    def go_up(p, passed):
        a = last - 2 * p
        b = a - 1
        of_a = exact[a]
        of_b = exact[b] - passed
        free_a = fixed[a]
        free_b = fixed[b]
        if p > 0:
            first = mul(sources(response, upper_at, a, None, upper_slots), upp_pair[p])
            second = mul(sources(response, upper_at, b, a, upper_slots), upp_second[p])
            of_a = of_a - first[:near, :width]
            of_b = of_b + first[:near, width:] - second[:near]
            free_a = free_a - first[near:, :width]
            free_b = free_b + first[near:, width:] - second[near:]
        for k, value, free in ((a, of_a, free_a), (b, of_b, free_b)):
            base[k] = value[:count]
            response[k, :near] = narrow(value)
            response[k, near:] = narrow(free)

    pairs = rows // 2
    for copy in copies[:4]:
        copy.wait()
    ready_down(0)
    go_down(0)
    for copy in copies[4:]:
        copy.wait()
    links = []
    for p in range(1, pairs):
        if p % 2 == 1 and p + 1 < pairs:
            ready_down(p + 1)
        go_down(p)
        if p % 2 == 1:
            links += ready_up(p - 1)
    for p in range(0, pairs, 2):
        a = last - 2 * p
        passed = apart(down[a], down[a - 2], links[p], links[p + 1])
        go_up(p, passed[:, :width])
        go_up(p + 1, passed[:, width:])

    far = near + width
    payload[:near] = down[last]
    payload[near : near + far] = response[0]
    payload[near + far :] = response[last, near:]


def compose_kernel(axis, bit, final, mine, theirs, *refs):
    prior, sent, inner, prior_out = refs[:4] if bit > 1 else (None, *refs[:3])
    pair = refs[-1]
    width = mine.shape[1]
    count = (mine.shape[0] - 4 * width) // 2
    near = count + width
    me = lax.axis_index(axis)
    place = lax.rem(lax.div(me, bit), 2)
    mid = near + count
    far = near + near + width

    pair[place] = mine[...]
    pair[1 - place] = theirs[...]
    a = pair[0]
    b = pair[1]
    across = mul(a[:near], jnp.concatenate([b[count:near], b[mid : mid + width]], axis=1))
    ahead = b[:near].astype(jnp.float32)
    joined = across[:, :width] + jnp.concatenate(
        [ahead[:count], jnp.zeros((width, width), jnp.float32)], axis=0
    )
    between = across[:, width:] + jnp.concatenate(
        [b[near:mid].astype(jnp.float32), jnp.zeros((width, width), jnp.float32)], axis=0
    )
    between = jnp.concatenate([narrow(between), b[mid + width : far]], axis=0)
    first = mul(between, a[mid + width : far])
    first = narrow(first[:near] + a[near : 2 * near].astype(jnp.float32)), narrow(first[near:])
    joined = narrow(joined)
    inner[:near] = a[:near]
    inner[near:] = between
    prior_out[...] = a[far:]
    if prior is not None:
        lowest = jnp.logical_and(place == 1, lax.rem(me, bit) == 0)

        @pl.when(jnp.logical_not(lowest))
        def _():
            prior_out[...] = prior[...]

    if final:
        refs[-2][...] = joined[:count]
        above = lax.rem(lax.div(me, 2 * bit), 2) == 1

        @pl.when(above)
        def _():
            sent[...] = first[0]

        @pl.when(jnp.logical_not(above))
        def _():
            sent[:count] = joined[:count]
            sent[count:] = b[far:]

    else:
        sent[:near] = joined
        sent[near : 2 * near] = first[0]
        sent[2 * near : far] = first[1]
        sent[far:] = b[far:]


def chain_kernel(axes, levels, *refs):
    own, theirs, base, response, prior = refs[:5]
    inner = refs[5 : 4 + levels]
    solution, rounded, prior_out, near_rows, far_rows = refs[4 + levels :]
    rows, count, width = base.shape
    near = count + width
    me = lax.axis_index(axes[0])
    side = lax.rem(lax.axis_index(axes[1]), 2)

    bit = 1 << (levels - 1)
    upper = lax.div(me, bit) == 1
    down = theirs[:count].astype(jnp.float32)
    up = down + mul(own[...], theirs[count:])
    inflow = narrow(jnp.where(upper, down, 0.0))
    outflow = narrow(jnp.where(upper, 0.0, up))
    prior_out[...] = prior[...]

    @pl.when(me == bit)
    def _():
        prior_out[...] = theirs[count:]

    for level in range(levels - 2, -1, -1):
        part = inner[level]
        upper = lax.rem(lax.div(me, 1 << level), 2) == 1
        down = part[:count].astype(jnp.float32) + mul(inflow, part[count:near])
        both = jnp.concatenate([inflow, outflow], axis=1)
        up = part[near : near + count].astype(jnp.float32) + mul(both, part[near + count :])
        inflow, outflow = (
            narrow(jnp.where(upper, down, inflow.astype(jnp.float32))),
            narrow(jnp.where(upper, outflow.astype(jnp.float32), up)),
        )

    both = jnp.concatenate([inflow, outflow], axis=1)
    for k in range(rows):
        value = base[k] + mul(both, response[k, count:])
        solution[k] = value
        rounded[k] = narrow(value)
    rounded[rows] = inflow
    rounded[rows + 1] = outflow
    rim = near_rows.shape[0]
    for e in range(rim):
        near_rows[e] = rounded[(1 - side) * (rows - rim) + e]
        far_rows[e] = rounded[side * (rows - rim) + e]


def local_kernel(
    axis,
    rounded,
    prior,
    solved,
    diagonal,
    lower,
    upper,
    lower_at,
    upper_at,
    partial,
    solution,
    held,
    out,
):
    copy = pltpu.make_async_copy(solved, solution, out)
    copy.start()
    rows, slots, width, _ = lower.shape
    upper_slots = upper.shape[1]
    before = rounded[rows].astype(jnp.float32) + mul(rounded[0], prior[...])
    held[...] = rounded[...]
    held[rows] = narrow(jnp.where(lax.axis_index(axis) > 0, before, 0.0))
    for k in range(rows):
        total = mul(rounded[k], diagonal[k])
        source = [held[rows]]
        for m in range(1, slots):
            at = lower_at[m, k]
            source.append(held[jnp.where(at == k, rows, at)])
        total = total + mul(
            jnp.concatenate(source, axis=1), lower[k].reshape(slots * width, width)
        )
        source = [rounded[rows + 1]]
        for m in range(1, upper_slots):
            at = upper_at[m, k]
            source.append(rounded[jnp.where(at == k, rows + 1, at)])
        total = total + mul(
            jnp.concatenate(source, axis=1), upper[k].reshape(upper_slots * width, width)
        )
        partial[k] = total
    copy.wait()


def halo_kernel(axis, partial, outer, inner, halo, halo_at, product, rim_rows, total, out):
    rows, slots, width, _ = halo.shape
    rim = inner.shape[0]
    turn = rim * (1 - lax.rem(lax.axis_index(axis), 2))
    rim_rows[:rim] = inner[...]
    rim_rows[rim:] = outer[...]
    step = out.shape[0]
    copies = []
    for k in range(rows):
        source = [
            rim_rows[lax.rem(halo_at[m, k] + turn, 2 * rim)] for m in range(slots)
        ]
        total[k] = partial[k] + mul(
            jnp.concatenate(source, axis=1), halo[k].reshape(slots * width, width)
        )
        done = (k + 1) * step // rows
        if done > len(copies):
            part = pl.ds(len(copies) * rows // step, rows // step)
            copies.append(pltpu.make_async_copy(total.at[part], product.at[part], out.at[done - 1]))
            copies[-1].start()
    for copy in copies:
        copy.wait()


def trade(block, axis, bit):
    count = lax.axis_size(axis)
    return lax.ppermute(block, axis, [(i, i ^ bit) for i in range(count)])


def swaps(block, axis, first):
    count = lax.axis_size(axis)
    pairs = []
    for low in range(first, count - 1, 2):
        pairs += [(low, low + 1), (low + 1, low)]
    return lax.ppermute(block, axis, pairs)


def on_device(
    right_sides,
    diag_inverse,
    diag_blocks,
    lower_blocks,
    upper_blocks,
    halo_blocks,
    lower_index,
    upper_index,
    halo_index,
):
    rows, count, width = right_sides.shape
    lower_at, upper_at, halo_at = lower_index.T, upper_index.T, halo_index.T
    slots = lower_blocks.shape[1]
    upper_slots = upper_blocks.shape[1]
    groups = lax.axis_size("section")
    near = count + width
    far = near + width
    wide = jax.ShapeDtypeStruct((rows, count, width), jnp.float32)

    indices = (lower_at, upper_at, halo_at)
    base, response, payload, *indices = pl.pallas_call(
        sweep_kernel,
        out_shape=(
            wide,
            jax.ShapeDtypeStruct((rows + 1, far, width), jnp.bfloat16),
            jax.ShapeDtypeStruct((near + far + width, width), jnp.bfloat16),
        )
        + tuple(jax.ShapeDtypeStruct(a.shape, a.dtype) for a in indices),
        in_specs=[HBM] * 7,
        out_specs=(VMEM,) * 6,
        scratch_shapes=[
            pltpu.VMEM(right_sides.shape, right_sides.dtype),
            pltpu.VMEM(diag_inverse.shape, diag_inverse.dtype),
            pltpu.VMEM(lower_blocks.shape, lower_blocks.dtype),
            pltpu.VMEM(upper_blocks.shape, upper_blocks.dtype),
            pltpu.SMEM(lower_at.shape, jnp.int32),
            pltpu.SMEM(upper_at.shape, jnp.int32),
            pltpu.VMEM((rows // 2, (slots - 1) * width, 2 * width), jnp.bfloat16),
            pltpu.VMEM((rows // 2, (slots - 1) * width, width), jnp.bfloat16),
            pltpu.VMEM((rows // 2, (upper_slots - 1) * width, 2 * width), jnp.bfloat16),
            pltpu.VMEM((rows // 2, (upper_slots - 1) * width, width), jnp.bfloat16),
            pltpu.VMEM((rows + 1, near, width), jnp.bfloat16),
            pltpu.VMEM((rows, near, width), jnp.float32),
            pltpu.VMEM((rows, width, width), jnp.float32),
            pltpu.SemaphoreType.DMA((10,)),
        ],
        compiler_params=SMALL,
        name="sweeps",
    )(
        *(
            pltpu.with_memory_space_constraint(a, pltpu.HBM)
            for a in (right_sides, diag_inverse, lower_blocks, upper_blocks, *indices)
        )
    )

    levels = groups.bit_length() - 1
    segment = payload.shape[0]
    bits = jnp.bfloat16
    prior = []
    inner = []
    for level in range(levels - 1):
        theirs = trade(payload, "section", 1 << level)
        final = level == levels - 2

        def compose(*refs, bit=1 << level, final=final):
            compose_kernel("section", bit, final, *refs)

        payload, between, *prior = pl.pallas_call(
            compose,
            out_shape=(
                jax.ShapeDtypeStruct((near if final else segment, width), bits),
                jax.ShapeDtypeStruct((near + far, width), bits),
                jax.ShapeDtypeStruct((width, width), bits),
            )
            + (jax.ShapeDtypeStruct((count, width), bits),) * final,
            in_specs=[VMEM] * (2 + len(prior)),
            out_specs=(VMEM,) * (3 + final),
            scratch_shapes=[pltpu.VMEM((2, segment, width), bits)],
            compiler_params=SMALL,
            name="compose",
        )(payload, theirs, *prior)
        inner.append(between)
    prior, own = prior
    theirs = trade(payload, "section", 1 << (levels - 1))

    def chain(*refs):
        chain_kernel(("section", "dom"), levels, *refs)

    solved, rounded, prior, inner, outer = pl.pallas_call(
        chain,
        out_shape=(
            wide,
            jax.ShapeDtypeStruct((rows + 2, count, width), bits),
            jax.ShapeDtypeStruct((width, width), bits),
            jax.ShapeDtypeStruct((RIM, count, width), bits),
            jax.ShapeDtypeStruct((RIM, count, width), bits),
        ),
        in_specs=[VMEM] * (4 + levels),
        out_specs=(VMEM,) * 5,
        compiler_params=SMALL,
        name="chain",
    )(own, theirs, base, response, prior, *inner)

    outer = swaps(outer, "dom", 1)
    inner = swaps(inner, "dom", 0)

    def local(*refs):
        local_kernel("section", *refs)

    partial, solution = pl.pallas_call(
        local,
        out_shape=(wide, wide),
        in_specs=[VMEM] * 6 + [SMEM] * 2,
        out_specs=(VMEM, HBM),
        scratch_shapes=[
            pltpu.VMEM((rows + 2, count, width), bits),
            pltpu.SemaphoreType.DMA(()),
        ],
        compiler_params=SMALL,
        name="local_product",
    )(rounded, prior, solved, diag_blocks, lower_blocks, upper_blocks, *indices[:2])

    def halo(*refs):
        halo_kernel("dom", *refs)

    product = pl.pallas_call(
        halo,
        out_shape=wide,
        in_specs=[VMEM] * 4 + [SMEM],
        out_specs=HBM,
        scratch_shapes=[
            pltpu.VMEM((2 * RIM, count, width), bits),
            pltpu.VMEM(right_sides.shape, jnp.float32),
            pltpu.SemaphoreType.DMA((4,)),
        ],
        compiler_params=SMALL,
        name="halo_product",
    )(partial, outer, inner, halo_blocks, indices[2])
    return (solution, product)


def solution(mesh):
    in_specs = (
        P(("section", "dom"), None, None),
        P(("section", "dom"), None, None),
        P(("section", "dom"), None, None),
        P(("section", "dom"), None, None, None),
        P(("section", "dom"), None, None, None),
        P(("section", "dom"), None, None, None),
        P(("section", "dom"), None),
        P(("section", "dom"), None),
        P(("section", "dom"), None),
    )
    out_specs = (P(("section", "dom"), None, None), P(("section", "dom"), None, None))
    return jax.shard_map(
        on_device, mesh=mesh, in_specs=in_specs, out_specs=out_specs, check_vma=False
    )
```

```python
import jax
import jax.numpy as jnp
from jax import lax
from jax.experimental import pallas as pl
from jax.experimental.pallas import tpu as pltpu
from jax.sharding import PartitionSpec as P

RIM = 4

VMEM = pl.BlockSpec(memory_space=pltpu.VMEM)
SMEM = pl.BlockSpec(memory_space=pltpu.SMEM)
HBM = pl.BlockSpec(memory_space=pltpu.HBM)
SMALL = pltpu.CompilerParams(vmem_limit_bytes=16 * 1024 * 1024)


def mul(a, b):
    return jnp.dot(a, b, preferred_element_type=jnp.float32)


def narrow(a):
    return a.astype(jnp.bfloat16)


def sweep_kernel(
    rhs_far,
    inverse_far,
    lower_far,
    upper_far,
    lower_at_far,
    upper_at_far,
    halo_at_far,
    base,
    response,
    payload,
    lower_at_kept,
    upper_at_kept,
    halo_at_kept,
    rhs,
    inverse,
    lower,
    upper,
    lower_at,
    upper_at,
    low_pair,
    low_second,
    upp_pair,
    upp_second,
    down,
    exact,
    fixed,
    arrived,
):
    rows, count, width = rhs.shape
    slots = lower.shape[1]
    upper_slots = upper.shape[1]
    near = count + width
    last = rows - 1
    half = rows // 2
    parts = [
        (inverse_far, inverse),
        (rhs_far, rhs),
        (lower_far.at[:half], lower.at[:half]),
        (lower_at_far, lower_at),
        (lower_far.at[half:], lower.at[half:]),
        (upper_far, upper),
        (upper_at_far, upper_at),
        (lower_at_far, lower_at_kept),
        (upper_at_far, upper_at_kept),
        (halo_at_far, halo_at_kept),
    ]
    copies = [
        pltpu.make_async_copy(far, here, arrived.at[i]) for i, (far, here) in enumerate(parts)
    ]
    for copy in copies:
        copy.start()
    eye = narrow(
        lax.broadcasted_iota(jnp.int32, (width, width), 0)
        == lax.broadcasted_iota(jnp.int32, (width, width), 1)
    )
    down[:, :count] = jnp.zeros((rows + 1, count, width), jnp.bfloat16)
    response[:, :near] = jnp.zeros((rows + 1, near, width), jnp.bfloat16)
    for k in range(rows):
        down[k, count:] = eye
        response[k, near:] = eye
    down[rows, count:] = jnp.zeros_like(eye)
    response[rows, near:] = jnp.zeros_like(eye)

    def piece(blocks, m):
        return blocks[m * width : (m + 1) * width]

    def named(at, k, row, blocks, many):
        return sum(
            jnp.where(at[m, k] == row, piece(blocks, m), 0.0) for m in range(1, many)
        )

    def sources(held, at, k, skipped, many):
        picked = []
        for m in range(1, many):
            row = at[m, k]
            picked.append(held[row if skipped is None else jnp.where(row == skipped, rows, row)])
        return jnp.concatenate(picked, axis=1)

    def apart(left, right, own, other):
        zero = jnp.zeros_like(own)
        sides = [jnp.concatenate([own, zero], axis=1), jnp.concatenate([zero, other], axis=1)]
        return mul(jnp.concatenate([left, right], axis=1), jnp.concatenate(sides, axis=0))

    def ready(at, blocks, many, first, step, heads):
        of_a, of_b, links = [], [], []
        for a in (first, first + 2 * step):
            b = a + step
            lefts = [
                jnp.concatenate(heads(k) + [blocks[k].reshape(many * width, width)], axis=0)
                for k in (a, b)
            ]
            both = apart(*lefts, inverse[a], inverse[b])
            of_a.append(both[:, :width])
            of_b.append(both[:, width:])
            tail = both[both.shape[0] - many * width :, width:]
            links.append(narrow(named(at, b, a, tail, many)))
        narrow_a = [narrow(value) for value in of_a]
        both = apart(*narrow_a, *links)
        through = [both[:, :width], both[:, width:]]
        return of_a, narrow_a, of_b, through, links

    def ready_down(p):
        of_a, narrow_a, of_b, through, _ = ready(
            lower_at, lower, slots, 2 * p, 1, lambda k: [narrow(rhs[k])]
        )
        for i in range(2):
            a, b = 2 * (p + i), 2 * (p + i) + 1
            exact[a, :count] = of_a[i][:count]
            exact[a, count:] = -of_a[i][count:near]
            exact[b, :count] = of_b[i][:count] - through[i][:count]
            exact[b, count:] = through[i][count:near] - of_b[i][count:near]
            if p + i == 0:
                inner = sum(piece(of_a[i][count:], m) for m in range(1, slots))
                exact[a, count:] += -inner
                inner = sum(piece(through[i][count:], m) for m in range(1, slots))
                exact[b, count:] += inner - named(lower_at, b, b, of_b[i][count:], slots)
            else:
                low_pair[p + i, :, :width] = narrow_a[i][near:]
                low_pair[p + i, :, width:] = narrow(through[i][near:])
                low_second[p + i] = narrow(of_b[i][near:])

    def go_down(p):
        a, b = 2 * p, 2 * p + 1
        if p > 0:
            first = mul(sources(down, lower_at, a, None, slots), low_pair[p])
            second = mul(sources(down, lower_at, b, a, slots), low_second[p])
            exact[a] -= first[:, :width]
            exact[b] += first[:, width:] - second
        down[a] = narrow(exact[a])
        down[b] = narrow(exact[b])

    def ready_up(p):
        of_a, narrow_a, of_b, through, links = ready(
            upper_at, upper, upper_slots, last - 2 * p, -1, lambda k: []
        )
        for i in range(2):
            a = last - 2 * (p + i)
            b = a - 1
            fixed[a] = -of_a[i][:width]
            fixed[b] = through[i][:width] - of_b[i][:width]
            if p + i == 0:
                fixed[a] += -sum(piece(of_a[i], m) for m in range(1, upper_slots))
                inner = sum(piece(through[i], m) for m in range(1, upper_slots))
                fixed[b] += inner - named(upper_at, b, b, of_b[i], upper_slots)
            else:
                upp_pair[p + i, :, :width] = narrow_a[i][width:]
                upp_pair[p + i, :, width:] = narrow(through[i][width:])
                upp_second[p + i] = narrow(of_b[i][width:])
        return links

    def go_up(p, passed):
        a = last - 2 * p
        b = a - 1
        of_a = exact[a]
        of_b = exact[b] - passed
        free_a = fixed[a]
        free_b = fixed[b]
        if p > 0:
            first = mul(sources(response, upper_at, a, None, upper_slots), upp_pair[p])
            second = mul(sources(response, upper_at, b, a, upper_slots), upp_second[p])
            of_a = of_a - first[:near, :width]
            of_b = of_b + first[:near, width:] - second[:near]
            free_a = free_a - first[near:, :width]
            free_b = free_b + first[near:, width:] - second[near:]
        for k, value, free in ((a, of_a, free_a), (b, of_b, free_b)):
            base[k] = value[:count]
            response[k, :near] = narrow(value)
            response[k, near:] = narrow(free)

    pairs = rows // 2
    for copy in copies[:4]:
        copy.wait()
    ready_down(0)
    go_down(0)
    for copy in copies[4:]:
        copy.wait()
    links = []
    for p in range(1, pairs):
        if p % 2 == 1 and p + 1 < pairs:
            ready_down(p + 1)
        go_down(p)
        if p % 2 == 1:
            links += ready_up(p - 1)
    for p in range(0, pairs, 2):
        a = last - 2 * p
        passed = apart(down[a], down[a - 2], links[p], links[p + 1])
        go_up(p, passed[:, :width])
        go_up(p + 1, passed[:, width:])

    far = near + width
    payload[:near] = down[last]
    payload[near : near + far] = response[0]
    payload[near + far :] = response[last, near:]


def compose_kernel(axis, bit, final, mine, theirs, *refs):
    prior, sent, inner, prior_out = refs[:4] if bit > 1 else (None, *refs[:3])
    pair = refs[-1]
    width = mine.shape[1]
    count = (mine.shape[0] - 4 * width) // 2
    near = count + width
    me = lax.axis_index(axis)
    place = lax.rem(lax.div(me, bit), 2)
    mid = near + count
    far = near + near + width

    pair[place] = mine[...]
    pair[1 - place] = theirs[...]
    a = pair[0]
    b = pair[1]
    across = mul(a[:near], jnp.concatenate([b[count:near], b[mid : mid + width]], axis=1))
    ahead = b[:near].astype(jnp.float32)
    joined = across[:, :width] + jnp.concatenate(
        [ahead[:count], jnp.zeros((width, width), jnp.float32)], axis=0
    )
    between = across[:, width:] + jnp.concatenate(
        [b[near:mid].astype(jnp.float32), jnp.zeros((width, width), jnp.float32)], axis=0
    )
    between = jnp.concatenate([narrow(between), b[mid + width : far]], axis=0)
    first = mul(between, a[mid + width : far])
    first = narrow(first[:near] + a[near : 2 * near].astype(jnp.float32)), narrow(first[near:])
    joined = narrow(joined)
    inner[:near] = a[:near]
    inner[near:] = between
    prior_out[...] = a[far:]
    if prior is not None:
        lowest = jnp.logical_and(place == 1, lax.rem(me, bit) == 0)

        @pl.when(jnp.logical_not(lowest))
        def _():
            prior_out[...] = prior[...]

    if final:
        refs[-2][...] = joined[:count]
        above = lax.rem(lax.div(me, 2 * bit), 2) == 1

        @pl.when(above)
        def _():
            sent[...] = first[0]

        @pl.when(jnp.logical_not(above))
        def _():
            sent[:count] = joined[:count]
            sent[count:] = b[far:]

    else:
        sent[:near] = joined
        sent[near : 2 * near] = first[0]
        sent[2 * near : far] = first[1]
        sent[far:] = b[far:]


def chain_kernel(axes, levels, *refs):
    own, theirs, base, response, prior = refs[:5]
    inner = refs[5 : 4 + levels]
    solution, rounded, prior_out, near_rows, far_rows = refs[4 + levels :]
    rows, count, width = base.shape
    near = count + width
    me = lax.axis_index(axes[0])
    side = lax.rem(lax.axis_index(axes[1]), 2)

    bit = 1 << (levels - 1)
    upper = lax.div(me, bit) == 1
    down = theirs[:count].astype(jnp.float32)
    up = down + mul(own[...], theirs[count:])
    inflow = narrow(jnp.where(upper, down, 0.0))
    outflow = narrow(jnp.where(upper, 0.0, up))
    prior_out[...] = prior[...]

    @pl.when(me == bit)
    def _():
        prior_out[...] = theirs[count:]

    for level in range(levels - 2, -1, -1):
        part = inner[level]
        upper = lax.rem(lax.div(me, 1 << level), 2) == 1
        down = part[:count].astype(jnp.float32) + mul(inflow, part[count:near])
        both = jnp.concatenate([inflow, outflow], axis=1)
        up = part[near : near + count].astype(jnp.float32) + mul(both, part[near + count :])
        inflow, outflow = (
            narrow(jnp.where(upper, down, inflow.astype(jnp.float32))),
            narrow(jnp.where(upper, outflow.astype(jnp.float32), up)),
        )

    both = jnp.concatenate([inflow, outflow], axis=1)
    for k in range(rows):
        value = base[k] + mul(both, response[k, count:])
        solution[k] = value
        rounded[k] = narrow(value)
    rounded[rows] = inflow
    rounded[rows + 1] = outflow
    rim = near_rows.shape[0]
    for e in range(rim):
        near_rows[e] = rounded[(1 - side) * (rows - rim) + e]
        far_rows[e] = rounded[side * (rows - rim) + e]


def local_kernel(
    axes,
    rounded,
    prior,
    solved,
    diagonal,
    lower,
    upper,
    lower_at,
    upper_at,
    halo_at,
    partial,
    solution,
    masks,
    held,
    out,
):
    copy = pltpu.make_async_copy(solved, solution, out)
    copy.start()
    rows, slots, width, _ = lower.shape
    upper_slots = upper.shape[1]
    before = rounded[rows].astype(jnp.float32) + mul(rounded[0], prior[...])
    held[...] = rounded[...]
    held[rows] = narrow(jnp.where(lax.axis_index(axes[0]) > 0, before, 0.0))
    for k in range(rows):
        total = mul(rounded[k], diagonal[k])
        source = [held[rows]]
        for m in range(1, slots):
            at = lower_at[m, k]
            source.append(held[jnp.where(at == k, rows, at)])
        total = total + mul(
            jnp.concatenate(source, axis=1), lower[k].reshape(slots * width, width)
        )
        source = [rounded[rows + 1]]
        for m in range(1, upper_slots):
            at = upper_at[m, k]
            source.append(rounded[jnp.where(at == k, rows + 1, at)])
        total = total + mul(
            jnp.concatenate(source, axis=1), upper[k].reshape(upper_slots * width, width)
        )
        partial[k] = total
    _, picked, places, count, _ = masks.shape
    turn = places // 2 * (1 - lax.rem(lax.axis_index(axes[1]), 2))
    for k in range(rows):
        for m in range(picked):
            at = lax.rem(halo_at[m + 1, k] + turn, places)
            for j in range(places):
                mask = jnp.where(at == j, 1.0, 0.0)
                masks[k, m, j] = narrow(jnp.full((count, width), mask, jnp.float32))
    copy.wait()


def halo_kernel(axis, partial, outer, inner, halo, masks, product, rim_rows):
    rows, slots, width, _ = halo.shape
    rim = inner.shape[0]
    turn = rim * (1 - lax.rem(lax.axis_index(axis), 2))
    rim_rows[:rim] = inner[...]
    rim_rows[rim:] = outer[...]
    for k in range(rows):
        source = [rim_rows[lax.rem(k + turn, 2 * rim)]]
        for m in range(1, slots):
            source.append(sum(masks[k, m - 1, j] * rim_rows[j] for j in range(2 * rim)))
        product[k] = partial[k] + mul(
            jnp.concatenate(source, axis=1), halo[k].reshape(slots * width, width)
        )


def trade(block, axis, bit):
    count = lax.axis_size(axis)
    return lax.ppermute(block, axis, [(i, i ^ bit) for i in range(count)])


def swaps(block, axis, first):
    count = lax.axis_size(axis)
    pairs = []
    for low in range(first, count - 1, 2):
        pairs += [(low, low + 1), (low + 1, low)]
    return lax.ppermute(block, axis, pairs)


def on_device(
    right_sides,
    diag_inverse,
    diag_blocks,
    lower_blocks,
    upper_blocks,
    halo_blocks,
    lower_index,
    upper_index,
    halo_index,
):
    rows, count, width = right_sides.shape
    lower_at, upper_at, halo_at = lower_index.T, upper_index.T, halo_index.T
    slots = lower_blocks.shape[1]
    upper_slots = upper_blocks.shape[1]
    groups = lax.axis_size("section")
    near = count + width
    far = near + width
    wide = jax.ShapeDtypeStruct((rows, count, width), jnp.float32)

    indices = (lower_at, upper_at, halo_at)
    base, response, payload, *indices = pl.pallas_call(
        sweep_kernel,
        out_shape=(
            wide,
            jax.ShapeDtypeStruct((rows + 1, far, width), jnp.bfloat16),
            jax.ShapeDtypeStruct((near + far + width, width), jnp.bfloat16),
        )
        + tuple(jax.ShapeDtypeStruct(a.shape, a.dtype) for a in indices),
        in_specs=[HBM] * 7,
        out_specs=(VMEM,) * 6,
        scratch_shapes=[
            pltpu.VMEM(right_sides.shape, right_sides.dtype),
            pltpu.VMEM(diag_inverse.shape, diag_inverse.dtype),
            pltpu.VMEM(lower_blocks.shape, lower_blocks.dtype),
            pltpu.VMEM(upper_blocks.shape, upper_blocks.dtype),
            pltpu.SMEM(lower_at.shape, jnp.int32),
            pltpu.SMEM(upper_at.shape, jnp.int32),
            pltpu.VMEM((rows // 2, (slots - 1) * width, 2 * width), jnp.bfloat16),
            pltpu.VMEM((rows // 2, (slots - 1) * width, width), jnp.bfloat16),
            pltpu.VMEM((rows // 2, (upper_slots - 1) * width, 2 * width), jnp.bfloat16),
            pltpu.VMEM((rows // 2, (upper_slots - 1) * width, width), jnp.bfloat16),
            pltpu.VMEM((rows + 1, near, width), jnp.bfloat16),
            pltpu.VMEM((rows, near, width), jnp.float32),
            pltpu.VMEM((rows, width, width), jnp.float32),
            pltpu.SemaphoreType.DMA((10,)),
        ],
        compiler_params=SMALL,
        name="sweeps",
    )(
        *(
            pltpu.with_memory_space_constraint(a, pltpu.HBM)
            for a in (right_sides, diag_inverse, lower_blocks, upper_blocks, *indices)
        )
    )

    levels = groups.bit_length() - 1
    segment = payload.shape[0]
    bits = jnp.bfloat16
    prior = []
    inner = []
    for level in range(levels - 1):
        theirs = trade(payload, "section", 1 << level)
        final = level == levels - 2

        def compose(*refs, bit=1 << level, final=final):
            compose_kernel("section", bit, final, *refs)

        payload, between, *prior = pl.pallas_call(
            compose,
            out_shape=(
                jax.ShapeDtypeStruct((near if final else segment, width), bits),
                jax.ShapeDtypeStruct((near + far, width), bits),
                jax.ShapeDtypeStruct((width, width), bits),
            )
            + (jax.ShapeDtypeStruct((count, width), bits),) * final,
            in_specs=[VMEM] * (2 + len(prior)),
            out_specs=(VMEM,) * (3 + final),
            scratch_shapes=[pltpu.VMEM((2, segment, width), bits)],
            compiler_params=SMALL,
            name="compose",
        )(payload, theirs, *prior)
        inner.append(between)
    prior, own = prior
    theirs = trade(payload, "section", 1 << (levels - 1))

    def chain(*refs):
        chain_kernel(("section", "dom"), levels, *refs)

    solved, rounded, prior, inner, outer = pl.pallas_call(
        chain,
        out_shape=(
            wide,
            jax.ShapeDtypeStruct((rows + 2, count, width), bits),
            jax.ShapeDtypeStruct((width, width), bits),
            jax.ShapeDtypeStruct((RIM, count, width), bits),
            jax.ShapeDtypeStruct((RIM, count, width), bits),
        ),
        in_specs=[VMEM] * (4 + levels),
        out_specs=(VMEM,) * 5,
        compiler_params=SMALL,
        name="chain",
    )(own, theirs, base, response, prior, *inner)

    outer = swaps(outer, "dom", 1)
    inner = swaps(inner, "dom", 0)

    def local(*refs):
        local_kernel(("section", "dom"), *refs)

    masks = (rows, halo_blocks.shape[1] - 1, 2 * RIM, count, width)
    partial, solution, masks = pl.pallas_call(
        local,
        out_shape=(wide, wide, jax.ShapeDtypeStruct(masks, bits)),
        in_specs=[VMEM] * 6 + [SMEM] * 3,
        out_specs=(VMEM, HBM, VMEM),
        scratch_shapes=[
            pltpu.VMEM((rows + 2, count, width), bits),
            pltpu.SemaphoreType.DMA(()),
        ],
        compiler_params=SMALL,
        name="local_product",
    )(rounded, prior, solved, diag_blocks, lower_blocks, upper_blocks, *indices)

    def halo(*refs):
        halo_kernel("dom", *refs)

    product = pl.pallas_call(
        halo,
        out_shape=wide,
        in_specs=[VMEM] * 5,
        out_specs=VMEM,
        scratch_shapes=[pltpu.VMEM((2 * RIM, count, width), bits)],
        compiler_params=SMALL,
        name="halo_product",
    )(partial, outer, inner, halo_blocks, masks)
    return (solution, product)


def solution(mesh):
    in_specs = (
        P(("section", "dom"), None, None),
        P(("section", "dom"), None, None),
        P(("section", "dom"), None, None),
        P(("section", "dom"), None, None, None),
        P(("section", "dom"), None, None, None),
        P(("section", "dom"), None, None, None),
        P(("section", "dom"), None),
        P(("section", "dom"), None),
        P(("section", "dom"), None),
    )
    out_specs = (P(("section", "dom"), None, None), P(("section", "dom"), None, None))
    return jax.shard_map(
        on_device, mesh=mesh, in_specs=in_specs, out_specs=out_specs, check_vma=False
    )
```

```python
import jax
import jax.numpy as jnp
from jax import lax
from jax.experimental import pallas as pl
from jax.experimental.pallas import tpu as pltpu
from jax.sharding import PartitionSpec as P

RIM = 4

VMEM = pl.BlockSpec(memory_space=pltpu.VMEM)
SMEM = pl.BlockSpec(memory_space=pltpu.SMEM)
HBM = pl.BlockSpec(memory_space=pltpu.HBM)
SMALL = pltpu.CompilerParams(vmem_limit_bytes=16 * 1024 * 1024)


def mul(a, b):
    return jnp.dot(a, b, preferred_element_type=jnp.float32)


def narrow(a):
    return a.astype(jnp.bfloat16)


def sweep_kernel(
    rhs_far,
    inverse_far,
    lower_far,
    upper_far,
    lower_at_far,
    upper_at_far,
    halo_at_far,
    base,
    response,
    payload,
    lower_at_kept,
    upper_at_kept,
    halo_at_kept,
    rhs,
    inverse,
    lower,
    upper,
    lower_at,
    upper_at,
    low_pair,
    low_second,
    upp_pair,
    upp_second,
    down,
    exact,
    fixed,
    arrived,
):
    rows, count, width = rhs.shape
    slots = lower.shape[1]
    upper_slots = upper.shape[1]
    near = count + width
    last = rows - 1
    half = rows // 2
    parts = [
        (inverse_far, inverse),
        (rhs_far, rhs),
        (lower_far.at[:half], lower.at[:half]),
        (lower_at_far, lower_at),
        (lower_far.at[half:], lower.at[half:]),
        (upper_far, upper),
        (upper_at_far, upper_at),
        (lower_at_far, lower_at_kept),
        (upper_at_far, upper_at_kept),
        (halo_at_far, halo_at_kept),
    ]
    copies = [
        pltpu.make_async_copy(far, here, arrived.at[i]) for i, (far, here) in enumerate(parts)
    ]
    for copy in copies:
        copy.start()
    eye = narrow(
        lax.broadcasted_iota(jnp.int32, (width, width), 0)
        == lax.broadcasted_iota(jnp.int32, (width, width), 1)
    )
    down[:, :count] = jnp.zeros((rows + 1, count, width), jnp.bfloat16)
    response[:, :near] = jnp.zeros((rows + 1, near, width), jnp.bfloat16)
    for k in range(rows):
        down[k, count:] = eye
        response[k, near:] = eye
    down[rows, count:] = jnp.zeros_like(eye)
    response[rows, near:] = jnp.zeros_like(eye)

    def piece(blocks, m):
        return blocks[m * width : (m + 1) * width]

    def named(at, k, row, blocks, many):
        return sum(
            jnp.where(at[m, k] == row, piece(blocks, m), 0.0) for m in range(1, many)
        )

    def sources(held, at, k, skipped, many):
        picked = []
        for m in range(1, many):
            row = at[m, k]
            picked.append(held[row if skipped is None else jnp.where(row == skipped, rows, row)])
        return jnp.concatenate(picked, axis=1)

    def apart(left, right, own, other):
        zero = jnp.zeros_like(own)
        sides = [jnp.concatenate([own, zero], axis=1), jnp.concatenate([zero, other], axis=1)]
        return mul(jnp.concatenate([left, right], axis=1), jnp.concatenate(sides, axis=0))

    def ready(at, blocks, many, first, step, heads):
        of_a, of_b, links = [], [], []
        for a in (first, first + 2 * step):
            b = a + step
            lefts = [
                jnp.concatenate(heads(k) + [blocks[k].reshape(many * width, width)], axis=0)
                for k in (a, b)
            ]
            both = apart(*lefts, inverse[a], inverse[b])
            of_a.append(both[:, :width])
            of_b.append(both[:, width:])
            tail = both[both.shape[0] - many * width :, width:]
            links.append(narrow(named(at, b, a, tail, many)))
        narrow_a = [narrow(value) for value in of_a]
        both = apart(*narrow_a, *links)
        through = [both[:, :width], both[:, width:]]
        return of_a, narrow_a, of_b, through, links

    def ready_down(p):
        of_a, narrow_a, of_b, through, _ = ready(
            lower_at, lower, slots, 2 * p, 1, lambda k: [narrow(rhs[k])]
        )
        for i in range(2):
            a, b = 2 * (p + i), 2 * (p + i) + 1
            exact[a, :count] = of_a[i][:count]
            exact[a, count:] = -of_a[i][count:near]
            exact[b, :count] = of_b[i][:count] - through[i][:count]
            exact[b, count:] = through[i][count:near] - of_b[i][count:near]
            if p + i == 0:
                inner = sum(piece(of_a[i][count:], m) for m in range(1, slots))
                exact[a, count:] += -inner
                inner = sum(piece(through[i][count:], m) for m in range(1, slots))
                exact[b, count:] += inner - named(lower_at, b, b, of_b[i][count:], slots)
            else:
                low_pair[p + i, :, :width] = narrow_a[i][near:]
                low_pair[p + i, :, width:] = narrow(through[i][near:])
                low_second[p + i] = narrow(of_b[i][near:])

    def go_down(p):
        a, b = 2 * p, 2 * p + 1
        if p > 0:
            first = mul(sources(down, lower_at, a, None, slots), low_pair[p])
            second = mul(sources(down, lower_at, b, a, slots), low_second[p])
            exact[a] -= first[:, :width]
            exact[b] += first[:, width:] - second
        down[a] = narrow(exact[a])
        down[b] = narrow(exact[b])

    def ready_up(p):
        of_a, narrow_a, of_b, through, links = ready(
            upper_at, upper, upper_slots, last - 2 * p, -1, lambda k: []
        )
        for i in range(2):
            a = last - 2 * (p + i)
            b = a - 1
            fixed[a] = -of_a[i][:width]
            fixed[b] = through[i][:width] - of_b[i][:width]
            if p + i == 0:
                fixed[a] += -sum(piece(of_a[i], m) for m in range(1, upper_slots))
                inner = sum(piece(through[i], m) for m in range(1, upper_slots))
                fixed[b] += inner - named(upper_at, b, b, of_b[i], upper_slots)
            else:
                upp_pair[p + i, :, :width] = narrow_a[i][width:]
                upp_pair[p + i, :, width:] = narrow(through[i][width:])
                upp_second[p + i] = narrow(of_b[i][width:])
        return links

    def go_up(p, passed):
        a = last - 2 * p
        b = a - 1
        of_a = exact[a]
        of_b = exact[b] - passed
        free_a = fixed[a]
        free_b = fixed[b]
        if p > 0:
            first = mul(sources(response, upper_at, a, None, upper_slots), upp_pair[p])
            second = mul(sources(response, upper_at, b, a, upper_slots), upp_second[p])
            of_a = of_a - first[:near, :width]
            of_b = of_b + first[:near, width:] - second[:near]
            free_a = free_a - first[near:, :width]
            free_b = free_b + first[near:, width:] - second[near:]
        for k, value, free in ((a, of_a, free_a), (b, of_b, free_b)):
            base[k] = value[:count]
            response[k, :near] = narrow(value)
            response[k, near:] = narrow(free)

    pairs = rows // 2
    for copy in copies[:4]:
        copy.wait()
    ready_down(0)
    go_down(0)
    for copy in copies[4:]:
        copy.wait()
    links = []
    for p in range(1, pairs):
        if p % 2 == 1 and p + 1 < pairs:
            ready_down(p + 1)
        go_down(p)
        if p % 2 == 1:
            links += ready_up(p - 1)
    for p in range(0, pairs, 2):
        a = last - 2 * p
        passed = apart(down[a], down[a - 2], links[p], links[p + 1])
        go_up(p, passed[:, :width])
        go_up(p + 1, passed[:, width:])

    far = near + width
    payload[:near] = down[last]
    payload[near : near + far] = response[0]
    payload[near + far :] = response[last, near:]


def compose_kernel(axis, bit, final, mine, theirs, *refs):
    prior, sent, inner, prior_out = refs[:4] if bit > 1 else (None, *refs[:3])
    pair = refs[-1]
    width = mine.shape[1]
    count = (mine.shape[0] - 4 * width) // 2
    near = count + width
    me = lax.axis_index(axis)
    place = lax.rem(lax.div(me, bit), 2)
    mid = near + count
    far = near + near + width

    pair[place] = mine[...]
    pair[1 - place] = theirs[...]
    a = pair[0]
    b = pair[1]
    across = mul(a[:near], jnp.concatenate([b[count:near], b[mid : mid + width]], axis=1))
    ahead = b[:near].astype(jnp.float32)
    joined = across[:, :width] + jnp.concatenate(
        [ahead[:count], jnp.zeros((width, width), jnp.float32)], axis=0
    )
    between = across[:, width:] + jnp.concatenate(
        [b[near:mid].astype(jnp.float32), jnp.zeros((width, width), jnp.float32)], axis=0
    )
    between = jnp.concatenate([narrow(between), b[mid + width : far]], axis=0)
    first = mul(between, a[mid + width : far])
    first = narrow(first[:near] + a[near : 2 * near].astype(jnp.float32)), narrow(first[near:])
    joined = narrow(joined)
    inner[:near] = a[:near]
    inner[near:] = between
    prior_out[...] = a[far:]
    if prior is not None:
        lowest = jnp.logical_and(place == 1, lax.rem(me, bit) == 0)

        @pl.when(jnp.logical_not(lowest))
        def _():
            prior_out[...] = prior[...]

    if final:
        refs[-2][...] = joined[:count]
        above = lax.rem(lax.div(me, 2 * bit), 2) == 1

        @pl.when(above)
        def _():
            sent[...] = first[0]

        @pl.when(jnp.logical_not(above))
        def _():
            sent[:count] = joined[:count]
            sent[count:] = b[far:]

    else:
        sent[:near] = joined
        sent[near : 2 * near] = first[0]
        sent[2 * near : far] = first[1]
        sent[far:] = b[far:]


def chain_kernel(axes, levels, *refs):
    own, theirs, base, response, prior = refs[:5]
    inner = refs[5 : 4 + levels]
    solution, rounded, prior_out, near_rows, far_rows = refs[4 + levels :]
    rows, count, width = base.shape
    near = count + width
    me = lax.axis_index(axes[0])
    side = lax.rem(lax.axis_index(axes[1]), 2)

    bit = 1 << (levels - 1)
    upper = lax.div(me, bit) == 1
    down = theirs[:count].astype(jnp.float32)
    up = down + mul(own[...], theirs[count:])
    inflow = narrow(jnp.where(upper, down, 0.0))
    outflow = narrow(jnp.where(upper, 0.0, up))
    prior_out[...] = prior[...]

    @pl.when(me == bit)
    def _():
        prior_out[...] = theirs[count:]

    for level in range(levels - 2, -1, -1):
        part = inner[level]
        upper = lax.rem(lax.div(me, 1 << level), 2) == 1
        down = part[:count].astype(jnp.float32) + mul(inflow, part[count:near])
        both = jnp.concatenate([inflow, outflow], axis=1)
        up = part[near : near + count].astype(jnp.float32) + mul(both, part[near + count :])
        inflow, outflow = (
            narrow(jnp.where(upper, down, inflow.astype(jnp.float32))),
            narrow(jnp.where(upper, outflow.astype(jnp.float32), up)),
        )

    both = jnp.concatenate([inflow, outflow], axis=1)
    for k in range(rows):
        value = base[k] + mul(both, response[k, count:])
        solution[k] = value
        rounded[k] = narrow(value)
    rounded[rows] = inflow
    rounded[rows + 1] = outflow
    rim = near_rows.shape[0]
    for e in range(rim):
        near_rows[e] = rounded[(1 - side) * (rows - rim) + e]
        far_rows[e] = rounded[side * (rows - rim) + e]


def local_kernel(
    axes,
    rounded,
    prior,
    solved,
    diagonal,
    lower,
    upper,
    lower_at,
    upper_at,
    halo_at,
    partial,
    solution,
    masks,
    held,
    out,
):
    copy = pltpu.make_async_copy(solved, solution, out)
    copy.start()
    rows, slots, width, _ = lower.shape
    upper_slots = upper.shape[1]
    before = rounded[rows].astype(jnp.float32) + mul(rounded[0], prior[...])
    held[...] = rounded[...]
    held[rows] = narrow(jnp.where(lax.axis_index(axes[0]) > 0, before, 0.0))
    for k in range(rows):
        total = mul(rounded[k], diagonal[k])
        source = [held[rows]]
        for m in range(1, slots):
            at = lower_at[m, k]
            source.append(held[jnp.where(at == k, rows, at)])
        total = total + mul(
            jnp.concatenate(source, axis=1), lower[k].reshape(slots * width, width)
        )
        source = [rounded[rows + 1]]
        for m in range(1, upper_slots):
            at = upper_at[m, k]
            source.append(rounded[jnp.where(at == k, rows + 1, at)])
        total = total + mul(
            jnp.concatenate(source, axis=1), upper[k].reshape(upper_slots * width, width)
        )
        partial[k] = total
    _, picked, places, count, _ = masks.shape
    turn = places // 2 * (1 - lax.rem(lax.axis_index(axes[1]), 2))
    for k in range(rows):
        for m in range(picked):
            at = lax.rem(halo_at[m + 1, k] + turn, places)
            for j in range(places):
                mask = jnp.where(at == j, 1.0, 0.0)
                masks[k, m, j] = narrow(jnp.full((count, width), mask, jnp.float32))
    copy.wait()


def halo_kernel(axis, partial, outer, inner, halo, masks, product, rim_rows):
    rows, slots, width, _ = halo.shape
    rim = inner.shape[0]
    turn = rim * (1 - lax.rem(lax.axis_index(axis), 2))
    place = lax.axis_index(axis)
    lone = jnp.logical_or(place == 0, place == lax.axis_size(axis) - 1)
    rim_rows[:rim] = inner[...]
    rim_rows[rim:] = narrow(jnp.where(lone, 0.0, outer[...].astype(jnp.float32)))
    for k in range(rows):
        source = [rim_rows[lax.rem(k + turn, 2 * rim)]]
        for m in range(1, slots):
            source.append(sum(masks[k, m - 1, j] * rim_rows[j] for j in range(2 * rim)))
        product[k] = partial[k] + mul(
            jnp.concatenate(source, axis=1), halo[k].reshape(slots * width, width)
        )


def trade(block, axis, bit):
    count = lax.axis_size(axis)
    return lax.ppermute(block, axis, [(i, i ^ bit) for i in range(count)])


def swaps(block, axis, first):
    count = lax.axis_size(axis)
    partner = list(range(count))
    for low in range(first, count - 1, 2):
        partner[low], partner[low + 1] = low + 1, low
    return lax.ppermute(block, axis, list(enumerate(partner)))


def on_device(
    right_sides,
    diag_inverse,
    diag_blocks,
    lower_blocks,
    upper_blocks,
    halo_blocks,
    lower_index,
    upper_index,
    halo_index,
):
    rows, count, width = right_sides.shape
    lower_at, upper_at, halo_at = lower_index.T, upper_index.T, halo_index.T
    slots = lower_blocks.shape[1]
    upper_slots = upper_blocks.shape[1]
    groups = lax.axis_size("section")
    near = count + width
    far = near + width
    wide = jax.ShapeDtypeStruct((rows, count, width), jnp.float32)

    indices = (lower_at, upper_at, halo_at)
    base, response, payload, *indices = pl.pallas_call(
        sweep_kernel,
        out_shape=(
            wide,
            jax.ShapeDtypeStruct((rows + 1, far, width), jnp.bfloat16),
            jax.ShapeDtypeStruct((near + far + width, width), jnp.bfloat16),
        )
        + tuple(jax.ShapeDtypeStruct(a.shape, a.dtype) for a in indices),
        in_specs=[HBM] * 7,
        out_specs=(VMEM,) * 6,
        scratch_shapes=[
            pltpu.VMEM(right_sides.shape, right_sides.dtype),
            pltpu.VMEM(diag_inverse.shape, diag_inverse.dtype),
            pltpu.VMEM(lower_blocks.shape, lower_blocks.dtype),
            pltpu.VMEM(upper_blocks.shape, upper_blocks.dtype),
            pltpu.SMEM(lower_at.shape, jnp.int32),
            pltpu.SMEM(upper_at.shape, jnp.int32),
            pltpu.VMEM((rows // 2, (slots - 1) * width, 2 * width), jnp.bfloat16),
            pltpu.VMEM((rows // 2, (slots - 1) * width, width), jnp.bfloat16),
            pltpu.VMEM((rows // 2, (upper_slots - 1) * width, 2 * width), jnp.bfloat16),
            pltpu.VMEM((rows // 2, (upper_slots - 1) * width, width), jnp.bfloat16),
            pltpu.VMEM((rows + 1, near, width), jnp.bfloat16),
            pltpu.VMEM((rows, near, width), jnp.float32),
            pltpu.VMEM((rows, width, width), jnp.float32),
            pltpu.SemaphoreType.DMA((10,)),
        ],
        compiler_params=SMALL,
        name="sweeps",
    )(
        *(
            pltpu.with_memory_space_constraint(a, pltpu.HBM)
            for a in (right_sides, diag_inverse, lower_blocks, upper_blocks, *indices)
        )
    )

    levels = groups.bit_length() - 1
    segment = payload.shape[0]
    bits = jnp.bfloat16
    prior = []
    inner = []
    for level in range(levels - 1):
        theirs = trade(payload, "section", 1 << level)
        final = level == levels - 2

        def compose(*refs, bit=1 << level, final=final):
            compose_kernel("section", bit, final, *refs)

        payload, between, *prior = pl.pallas_call(
            compose,
            out_shape=(
                jax.ShapeDtypeStruct((near if final else segment, width), bits),
                jax.ShapeDtypeStruct((near + far, width), bits),
                jax.ShapeDtypeStruct((width, width), bits),
            )
            + (jax.ShapeDtypeStruct((count, width), bits),) * final,
            in_specs=[VMEM] * (2 + len(prior)),
            out_specs=(VMEM,) * (3 + final),
            scratch_shapes=[pltpu.VMEM((2, segment, width), bits)],
            compiler_params=SMALL,
            name="compose",
        )(payload, theirs, *prior)
        inner.append(between)
    prior, own = prior
    theirs = trade(payload, "section", 1 << (levels - 1))

    def chain(*refs):
        chain_kernel(("section", "dom"), levels, *refs)

    solved, rounded, prior, inner, outer = pl.pallas_call(
        chain,
        out_shape=(
            wide,
            jax.ShapeDtypeStruct((rows + 2, count, width), bits),
            jax.ShapeDtypeStruct((width, width), bits),
            jax.ShapeDtypeStruct((RIM, count, width), bits),
            jax.ShapeDtypeStruct((RIM, count, width), bits),
        ),
        in_specs=[VMEM] * (4 + levels),
        out_specs=(VMEM,) * 5,
        compiler_params=SMALL,
        name="chain",
    )(own, theirs, base, response, prior, *inner)

    outer = swaps(outer, "dom", 1)
    inner = swaps(inner, "dom", 0)

    def local(*refs):
        local_kernel(("section", "dom"), *refs)

    masks = (rows, halo_blocks.shape[1] - 1, 2 * RIM, count, width)
    partial, solution, masks = pl.pallas_call(
        local,
        out_shape=(wide, wide, jax.ShapeDtypeStruct(masks, bits)),
        in_specs=[VMEM] * 6 + [SMEM] * 3,
        out_specs=(VMEM, HBM, VMEM),
        scratch_shapes=[
            pltpu.VMEM((rows + 2, count, width), bits),
            pltpu.SemaphoreType.DMA(()),
        ],
        compiler_params=SMALL,
        name="local_product",
    )(rounded, prior, solved, diag_blocks, lower_blocks, upper_blocks, *indices)

    def halo(*refs):
        halo_kernel("dom", *refs)

    product = pl.pallas_call(
        halo,
        out_shape=wide,
        in_specs=[VMEM] * 5,
        out_specs=VMEM,
        scratch_shapes=[pltpu.VMEM((2 * RIM, count, width), bits)],
        compiler_params=SMALL,
        name="halo_product",
    )(partial, outer, inner, halo_blocks, masks)
    return (solution, product)


def solution(mesh):
    in_specs = (
        P(("section", "dom"), None, None),
        P(("section", "dom"), None, None),
        P(("section", "dom"), None, None),
        P(("section", "dom"), None, None, None),
        P(("section", "dom"), None, None, None),
        P(("section", "dom"), None, None, None),
        P(("section", "dom"), None),
        P(("section", "dom"), None),
        P(("section", "dom"), None),
    )
    out_specs = (P(("section", "dom"), None, None), P(("section", "dom"), None, None))
    return jax.shard_map(
        on_device, mesh=mesh, in_specs=in_specs, out_specs=out_specs, check_vma=False
    )
```

```python
import jax
import jax.numpy as jnp
from jax import lax
from jax.experimental import pallas as pl
from jax.experimental.pallas import tpu as pltpu
from jax.sharding import PartitionSpec as P

RIM = 4

VMEM = pl.BlockSpec(memory_space=pltpu.VMEM)
SMEM = pl.BlockSpec(memory_space=pltpu.SMEM)
HBM = pl.BlockSpec(memory_space=pltpu.HBM)
ANY = pl.BlockSpec(memory_space=pl.ANY)
SMALL = pltpu.CompilerParams(vmem_limit_bytes=16 * 1024 * 1024)


def mul(a, b):
    return jnp.dot(a, b, preferred_element_type=jnp.float32)


def narrow(a):
    return a.astype(jnp.bfloat16)


def sweep_kernel(
    rhs_far,
    inverse_far,
    lower_far,
    upper_far,
    lower_at_far,
    upper_at_far,
    halo_at_far,
    base,
    response,
    payload,
    lower_at_kept,
    upper_at_kept,
    halo_at_kept,
    rhs,
    inverse,
    lower,
    upper,
    lower_at,
    upper_at,
    low_pair,
    low_second,
    upp_pair,
    upp_second,
    down,
    exact,
    fixed,
    arrived,
):
    rows, count, width = rhs.shape
    slots = lower.shape[1]
    upper_slots = upper.shape[1]
    near = count + width
    last = rows - 1
    half = rows // 2
    parts = [
        (inverse_far, inverse),
        (rhs_far, rhs),
        (lower_far.at[:half], lower.at[:half]),
        (lower_at_far, lower_at),
        (lower_far.at[half:], lower.at[half:]),
        (upper_far, upper),
        (upper_at_far, upper_at),
        (lower_at_far, lower_at_kept),
        (upper_at_far, upper_at_kept),
        (halo_at_far, halo_at_kept),
    ]
    copies = [
        pltpu.make_async_copy(far, here, arrived.at[i]) for i, (far, here) in enumerate(parts)
    ]
    for copy in copies:
        copy.start()
    eye = narrow(
        lax.broadcasted_iota(jnp.int32, (width, width), 0)
        == lax.broadcasted_iota(jnp.int32, (width, width), 1)
    )
    down[:, :count] = jnp.zeros((rows + 1, count, width), jnp.bfloat16)
    response[:, :near] = jnp.zeros((rows + 1, near, width), jnp.bfloat16)
    for k in range(rows):
        down[k, count:] = eye
        response[k, near:] = eye
    down[rows, count:] = jnp.zeros_like(eye)
    response[rows, near:] = jnp.zeros_like(eye)

    def piece(blocks, m):
        return blocks[m * width : (m + 1) * width]

    def named(at, k, row, blocks, many):
        return sum(
            jnp.where(at[m, k] == row, piece(blocks, m), 0.0) for m in range(1, many)
        )

    def sources(held, at, k, skipped, many):
        picked = []
        for m in range(1, many):
            row = at[m, k]
            picked.append(held[row if skipped is None else jnp.where(row == skipped, rows, row)])
        return jnp.concatenate(picked, axis=1)

    def apart(left, right, own, other):
        zero = jnp.zeros_like(own)
        sides = [jnp.concatenate([own, zero], axis=1), jnp.concatenate([zero, other], axis=1)]
        return mul(jnp.concatenate([left, right], axis=1), jnp.concatenate(sides, axis=0))

    def ready(at, blocks, many, first, step, heads):
        of_a, of_b, links = [], [], []
        for a in (first, first + 2 * step):
            b = a + step
            lefts = [
                jnp.concatenate(heads(k) + [blocks[k].reshape(many * width, width)], axis=0)
                for k in (a, b)
            ]
            both = apart(*lefts, inverse[a], inverse[b])
            of_a.append(both[:, :width])
            of_b.append(both[:, width:])
            tail = both[both.shape[0] - many * width :, width:]
            links.append(narrow(named(at, b, a, tail, many)))
        narrow_a = [narrow(value) for value in of_a]
        both = apart(*narrow_a, *links)
        through = [both[:, :width], both[:, width:]]
        return of_a, narrow_a, of_b, through, links

    def ready_down(p):
        of_a, narrow_a, of_b, through, _ = ready(
            lower_at, lower, slots, 2 * p, 1, lambda k: [narrow(rhs[k])]
        )
        for i in range(2):
            a, b = 2 * (p + i), 2 * (p + i) + 1
            exact[a, :count] = of_a[i][:count]
            exact[a, count:] = -of_a[i][count:near]
            exact[b, :count] = of_b[i][:count] - through[i][:count]
            exact[b, count:] = through[i][count:near] - of_b[i][count:near]
            if p + i == 0:
                inner = sum(piece(of_a[i][count:], m) for m in range(1, slots))
                exact[a, count:] += -inner
                inner = sum(piece(through[i][count:], m) for m in range(1, slots))
                exact[b, count:] += inner - named(lower_at, b, b, of_b[i][count:], slots)
            else:
                low_pair[p + i, :, :width] = narrow_a[i][near:]
                low_pair[p + i, :, width:] = narrow(through[i][near:])
                low_second[p + i] = narrow(of_b[i][near:])

    def go_down(p):
        a, b = 2 * p, 2 * p + 1
        if p > 0:
            first = mul(sources(down, lower_at, a, None, slots), low_pair[p])
            second = mul(sources(down, lower_at, b, a, slots), low_second[p])
            exact[a] -= first[:, :width]
            exact[b] += first[:, width:] - second
        down[a] = narrow(exact[a])
        down[b] = narrow(exact[b])

    def ready_up(p):
        of_a, narrow_a, of_b, through, links = ready(
            upper_at, upper, upper_slots, last - 2 * p, -1, lambda k: []
        )
        for i in range(2):
            a = last - 2 * (p + i)
            b = a - 1
            fixed[a] = -of_a[i][:width]
            fixed[b] = through[i][:width] - of_b[i][:width]
            if p + i == 0:
                fixed[a] += -sum(piece(of_a[i], m) for m in range(1, upper_slots))
                inner = sum(piece(through[i], m) for m in range(1, upper_slots))
                fixed[b] += inner - named(upper_at, b, b, of_b[i], upper_slots)
            else:
                upp_pair[p + i, :, :width] = narrow_a[i][width:]
                upp_pair[p + i, :, width:] = narrow(through[i][width:])
                upp_second[p + i] = narrow(of_b[i][width:])
        return links

    def go_up(p, passed):
        a = last - 2 * p
        b = a - 1
        of_a = exact[a]
        of_b = exact[b] - passed
        free_a = fixed[a]
        free_b = fixed[b]
        if p > 0:
            first = mul(sources(response, upper_at, a, None, upper_slots), upp_pair[p])
            second = mul(sources(response, upper_at, b, a, upper_slots), upp_second[p])
            of_a = of_a - first[:near, :width]
            of_b = of_b + first[:near, width:] - second[:near]
            free_a = free_a - first[near:, :width]
            free_b = free_b + first[near:, width:] - second[near:]
        for k, value, free in ((a, of_a, free_a), (b, of_b, free_b)):
            base[k] = value[:count]
            response[k, :near] = narrow(value)
            response[k, near:] = narrow(free)

    pairs = rows // 2
    for copy in copies[:4]:
        copy.wait()
    ready_down(0)
    go_down(0)
    for copy in copies[4:]:
        copy.wait()
    links = []
    for p in range(1, pairs):
        if p % 2 == 1 and p + 1 < pairs:
            ready_down(p + 1)
        go_down(p)
        if p % 2 == 1:
            links += ready_up(p - 1)
    for p in range(0, pairs, 2):
        a = last - 2 * p
        passed = apart(down[a], down[a - 2], links[p], links[p + 1])
        go_up(p, passed[:, :width])
        go_up(p + 1, passed[:, width:])

    far = near + width
    payload[:near] = down[last]
    payload[near : near + far] = response[0]
    payload[near + far :] = response[last, near:]


def compose_kernel(axis, bit, final, mine, theirs, *refs):
    prior, sent, inner, prior_out = refs[:4] if bit > 1 else (None, *refs[:3])
    pair = refs[-1]
    width = mine.shape[1]
    count = (mine.shape[0] - 4 * width) // 2
    near = count + width
    me = lax.axis_index(axis)
    place = lax.rem(lax.div(me, bit), 2)
    mid = near + count
    far = near + near + width

    pair[place] = mine[...]
    pair[1 - place] = theirs[...]
    a = pair[0]
    b = pair[1]
    across = mul(a[:near], jnp.concatenate([b[count:near], b[mid : mid + width]], axis=1))
    ahead = b[:near].astype(jnp.float32)
    joined = across[:, :width] + jnp.concatenate(
        [ahead[:count], jnp.zeros((width, width), jnp.float32)], axis=0
    )
    between = across[:, width:] + jnp.concatenate(
        [b[near:mid].astype(jnp.float32), jnp.zeros((width, width), jnp.float32)], axis=0
    )
    between = jnp.concatenate([narrow(between), b[mid + width : far]], axis=0)
    first = mul(between, a[mid + width : far])
    first = narrow(first[:near] + a[near : 2 * near].astype(jnp.float32)), narrow(first[near:])
    joined = narrow(joined)
    inner[:near] = a[:near]
    inner[near:] = between
    prior_out[...] = a[far:]
    if prior is not None:
        lowest = jnp.logical_and(place == 1, lax.rem(me, bit) == 0)

        @pl.when(jnp.logical_not(lowest))
        def _():
            prior_out[...] = prior[...]

    if final:
        refs[-2][...] = joined[:count]
        above = lax.rem(lax.div(me, 2 * bit), 2) == 1

        @pl.when(above)
        def _():
            sent[...] = first[0]

        @pl.when(jnp.logical_not(above))
        def _():
            sent[:count] = joined[:count]
            sent[count:] = b[far:]

    else:
        sent[:near] = joined
        sent[near : 2 * near] = first[0]
        sent[2 * near : far] = first[1]
        sent[far:] = b[far:]


def chain_kernel(axes, levels, *refs):
    own, theirs, base, response, prior = refs[:5]
    inner = refs[5 : 4 + levels]
    solution, rounded, prior_out, near_rows, far_rows = refs[4 + levels :]
    rows, count, width = base.shape
    near = count + width
    me = lax.axis_index(axes[0])
    side = lax.rem(lax.axis_index(axes[1]), 2)

    bit = 1 << (levels - 1)
    upper = lax.div(me, bit) == 1
    down = theirs[:count].astype(jnp.float32)
    up = down + mul(own[...], theirs[count:])
    inflow = narrow(jnp.where(upper, down, 0.0))
    outflow = narrow(jnp.where(upper, 0.0, up))
    prior_out[...] = prior[...]

    @pl.when(me == bit)
    def _():
        prior_out[...] = theirs[count:]

    for level in range(levels - 2, -1, -1):
        part = inner[level]
        upper = lax.rem(lax.div(me, 1 << level), 2) == 1
        down = part[:count].astype(jnp.float32) + mul(inflow, part[count:near])
        both = jnp.concatenate([inflow, outflow], axis=1)
        up = part[near : near + count].astype(jnp.float32) + mul(both, part[near + count :])
        inflow, outflow = (
            narrow(jnp.where(upper, down, inflow.astype(jnp.float32))),
            narrow(jnp.where(upper, outflow.astype(jnp.float32), up)),
        )

    both = jnp.concatenate([inflow, outflow], axis=1)
    for k in range(rows):
        value = base[k] + mul(both, response[k, count:])
        solution[k] = value
        rounded[k] = narrow(value)
    rounded[rows] = inflow
    rounded[rows + 1] = outflow
    rim = near_rows.shape[0]
    for e in range(rim):
        near_rows[e] = rounded[(1 - side) * (rows - rim) + e]
        far_rows[e] = rounded[side * (rows - rim) + e]


def local_kernel(
    axes,
    rounded,
    prior,
    solved,
    diagonal,
    lower,
    upper,
    lower_at,
    upper_at,
    halo_at,
    relayed,
    partial,
    solution,
    masks,
    held,
    out,
):
    copy = pltpu.make_async_copy(solved, solution, out)
    copy.start()
    rows, slots, width, _ = lower.shape
    upper_slots = upper.shape[1]
    before = rounded[rows].astype(jnp.float32) + mul(rounded[0], prior[...])
    held[...] = rounded[...]
    held[rows] = narrow(jnp.where(lax.axis_index(axes[0]) > 0, before, 0.0))
    for k in range(rows):
        total = mul(rounded[k], diagonal[k])
        source = [held[rows]]
        for m in range(1, slots):
            at = lower_at[m, k]
            source.append(held[jnp.where(at == k, rows, at)])
        total = total + mul(
            jnp.concatenate(source, axis=1), lower[k].reshape(slots * width, width)
        )
        source = [rounded[rows + 1]]
        for m in range(1, upper_slots):
            at = upper_at[m, k]
            source.append(rounded[jnp.where(at == k, rows + 1, at)])
        total = total + mul(
            jnp.concatenate(source, axis=1), upper[k].reshape(upper_slots * width, width)
        )
        partial[k] = total
    _, picked, places, count, _ = masks.shape
    turn = places // 2 * (1 - lax.rem(lax.axis_index(axes[1]), 2))
    for k in range(rows):
        for m in range(picked):
            at = lax.rem(halo_at[m + 1, k] + turn, places)
            for j in range(places):
                mask = jnp.where(at == j, 1.0, 0.0)
                masks[k, m, j] = narrow(jnp.full((count, width), mask, jnp.float32))
    copy.wait()


def halo_kernel(axis, partial, outer, inner, halo, masks, product, rim_rows):
    rows, slots, width, _ = halo.shape
    rim = inner.shape[0]
    turn = rim * (1 - lax.rem(lax.axis_index(axis), 2))
    rim_rows[:rim] = inner[...]
    rim_rows[rim:] = outer[...]
    for k in range(rows):
        source = [rim_rows[lax.rem(k + turn, 2 * rim)]]
        for m in range(1, slots):
            source.append(sum(masks[k, m - 1, j] * rim_rows[j] for j in range(2 * rim)))
        product[k] = partial[k] + mul(
            jnp.concatenate(source, axis=1), halo[k].reshape(slots * width, width)
        )


def trade(block, axis, bit):
    count = lax.axis_size(axis)
    return lax.ppermute(block, axis, [(i, i ^ bit) for i in range(count)])


def swaps(block, axis):
    count = lax.axis_size(axis)
    return lax.ppermute(block, axis, [(i, i ^ 1) for i in range(count)])


def relay(block, axis):
    count = lax.axis_size(axis)
    pairs = [(i, i + 2 if i % 2 else i - 2) for i in range(count)]
    return lax.ppermute(block, axis, [(i, j) for i, j in pairs if 0 <= j < count])


def on_device(
    right_sides,
    diag_inverse,
    diag_blocks,
    lower_blocks,
    upper_blocks,
    halo_blocks,
    lower_index,
    upper_index,
    halo_index,
):
    rows, count, width = right_sides.shape
    lower_at, upper_at, halo_at = lower_index.T, upper_index.T, halo_index.T
    slots = lower_blocks.shape[1]
    upper_slots = upper_blocks.shape[1]
    groups = lax.axis_size("section")
    near = count + width
    far = near + width
    wide = jax.ShapeDtypeStruct((rows, count, width), jnp.float32)

    indices = (lower_at, upper_at, halo_at)
    base, response, payload, *indices = pl.pallas_call(
        sweep_kernel,
        out_shape=(
            wide,
            jax.ShapeDtypeStruct((rows + 1, far, width), jnp.bfloat16),
            jax.ShapeDtypeStruct((near + far + width, width), jnp.bfloat16),
        )
        + tuple(jax.ShapeDtypeStruct(a.shape, a.dtype) for a in indices),
        in_specs=[HBM] * 7,
        out_specs=(VMEM,) * 6,
        scratch_shapes=[
            pltpu.VMEM(right_sides.shape, right_sides.dtype),
            pltpu.VMEM(diag_inverse.shape, diag_inverse.dtype),
            pltpu.VMEM(lower_blocks.shape, lower_blocks.dtype),
            pltpu.VMEM(upper_blocks.shape, upper_blocks.dtype),
            pltpu.SMEM(lower_at.shape, jnp.int32),
            pltpu.SMEM(upper_at.shape, jnp.int32),
            pltpu.VMEM((rows // 2, (slots - 1) * width, 2 * width), jnp.bfloat16),
            pltpu.VMEM((rows // 2, (slots - 1) * width, width), jnp.bfloat16),
            pltpu.VMEM((rows // 2, (upper_slots - 1) * width, 2 * width), jnp.bfloat16),
            pltpu.VMEM((rows // 2, (upper_slots - 1) * width, width), jnp.bfloat16),
            pltpu.VMEM((rows + 1, near, width), jnp.bfloat16),
            pltpu.VMEM((rows, near, width), jnp.float32),
            pltpu.VMEM((rows, width, width), jnp.float32),
            pltpu.SemaphoreType.DMA((10,)),
        ],
        compiler_params=SMALL,
        name="sweeps",
    )(
        *(
            pltpu.with_memory_space_constraint(a, pltpu.HBM)
            for a in (right_sides, diag_inverse, lower_blocks, upper_blocks, *indices)
        )
    )

    levels = groups.bit_length() - 1
    segment = payload.shape[0]
    bits = jnp.bfloat16
    prior = []
    inner = []
    for level in range(levels - 1):
        theirs = trade(payload, "section", 1 << level)
        final = level == levels - 2

        def compose(*refs, bit=1 << level, final=final):
            compose_kernel("section", bit, final, *refs)

        payload, between, *prior = pl.pallas_call(
            compose,
            out_shape=(
                jax.ShapeDtypeStruct((near if final else segment, width), bits),
                jax.ShapeDtypeStruct((near + far, width), bits),
                jax.ShapeDtypeStruct((width, width), bits),
            )
            + (jax.ShapeDtypeStruct((count, width), bits),) * final,
            in_specs=[VMEM] * (2 + len(prior)),
            out_specs=(VMEM,) * (3 + final),
            scratch_shapes=[pltpu.VMEM((2, segment, width), bits)],
            compiler_params=SMALL,
            name="compose",
        )(payload, theirs, *prior)
        inner.append(between)
    prior, own = prior
    theirs = trade(payload, "section", 1 << (levels - 1))

    def chain(*refs):
        chain_kernel(("section", "dom"), levels, *refs)

    solved, rounded, prior, inner, outer = pl.pallas_call(
        chain,
        out_shape=(
            wide,
            jax.ShapeDtypeStruct((rows + 2, count, width), bits),
            jax.ShapeDtypeStruct((width, width), bits),
            jax.ShapeDtypeStruct((RIM, count, width), bits),
            jax.ShapeDtypeStruct((RIM, count, width), bits),
        ),
        in_specs=[VMEM] * (4 + levels),
        out_specs=(VMEM,) * 5,
        compiler_params=SMALL,
        name="chain",
    )(own, theirs, base, response, prior, *inner)

    relayed = relay(outer, "dom")
    inner = swaps(inner, "dom")
    outer = swaps(relayed, "dom")

    def local(*refs):
        local_kernel(("section", "dom"), *refs)

    masks = (rows, halo_blocks.shape[1] - 1, 2 * RIM, count, width)
    partial, solution, masks = pl.pallas_call(
        local,
        out_shape=(wide, wide, jax.ShapeDtypeStruct(masks, bits)),
        in_specs=[VMEM] * 6 + [SMEM] * 3 + [ANY],
        out_specs=(VMEM, HBM, VMEM),
        scratch_shapes=[
            pltpu.VMEM((rows + 2, count, width), bits),
            pltpu.SemaphoreType.DMA(()),
        ],
        compiler_params=SMALL,
        name="local_product",
    )(rounded, prior, solved, diag_blocks, lower_blocks, upper_blocks, *indices, relayed)

    def halo(*refs):
        halo_kernel("dom", *refs)

    product = pl.pallas_call(
        halo,
        out_shape=wide,
        in_specs=[VMEM] * 5,
        out_specs=VMEM,
        scratch_shapes=[pltpu.VMEM((2 * RIM, count, width), bits)],
        compiler_params=SMALL,
        name="halo_product",
    )(partial, outer, inner, halo_blocks, masks)
    return (solution, product)


def solution(mesh):
    in_specs = (
        P(("section", "dom"), None, None),
        P(("section", "dom"), None, None),
        P(("section", "dom"), None, None),
        P(("section", "dom"), None, None, None),
        P(("section", "dom"), None, None, None),
        P(("section", "dom"), None, None, None),
        P(("section", "dom"), None),
        P(("section", "dom"), None),
        P(("section", "dom"), None),
    )
    out_specs = (P(("section", "dom"), None, None), P(("section", "dom"), None, None))
    return jax.shard_map(
        on_device, mesh=mesh, in_specs=in_specs, out_specs=out_specs, check_vma=False
    )
```

```python
import jax
import jax.numpy as jnp
from jax import lax
from jax.experimental import pallas as pl
from jax.experimental.pallas import tpu as pltpu
from jax.sharding import PartitionSpec as P

RIM = 4

VMEM = pl.BlockSpec(memory_space=pltpu.VMEM)
SMEM = pl.BlockSpec(memory_space=pltpu.SMEM)
HBM = pl.BlockSpec(memory_space=pltpu.HBM)
SMALL = pltpu.CompilerParams(vmem_limit_bytes=16 * 1024 * 1024)


def mul(a, b):
    return jnp.dot(a, b, preferred_element_type=jnp.float32)


def narrow(a):
    return a.astype(jnp.bfloat16)


def sweep_kernel(
    rhs_far,
    inverse_far,
    lower_far,
    upper_far,
    lower_at_far,
    upper_at_far,
    halo_at_far,
    base,
    response,
    payload,
    lower_at_kept,
    upper_at_kept,
    halo_at_kept,
    rhs,
    inverse,
    lower,
    upper,
    lower_at,
    upper_at,
    low_pair,
    low_second,
    upp_pair,
    upp_second,
    down,
    exact,
    fixed,
    arrived,
):
    rows, count, width = rhs.shape
    slots = lower.shape[1]
    upper_slots = upper.shape[1]
    near = count + width
    last = rows - 1
    half = rows // 2
    parts = [
        (inverse_far, inverse),
        (rhs_far, rhs),
        (lower_far.at[:half], lower.at[:half]),
        (lower_at_far, lower_at),
        (lower_far.at[half:], lower.at[half:]),
        (upper_far, upper),
        (upper_at_far, upper_at),
        (lower_at_far, lower_at_kept),
        (upper_at_far, upper_at_kept),
        (halo_at_far, halo_at_kept),
    ]
    copies = [
        pltpu.make_async_copy(far, here, arrived.at[i]) for i, (far, here) in enumerate(parts)
    ]
    for copy in copies[:5]:
        copy.start()
    eye = narrow(
        lax.broadcasted_iota(jnp.int32, (width, width), 0)
        == lax.broadcasted_iota(jnp.int32, (width, width), 1)
    )
    down[:, :count] = jnp.zeros((rows + 1, count, width), jnp.bfloat16)
    response[:, :near] = jnp.zeros((rows + 1, near, width), jnp.bfloat16)
    for k in range(rows):
        down[k, count:] = eye
        response[k, near:] = eye
    down[rows, count:] = jnp.zeros_like(eye)
    response[rows, near:] = jnp.zeros_like(eye)

    def piece(blocks, m):
        return blocks[m * width : (m + 1) * width]

    def named(at, k, row, blocks, many):
        return sum(
            jnp.where(at[m, k] == row, piece(blocks, m), 0.0) for m in range(1, many)
        )

    def sources(held, at, k, skipped, many):
        picked = []
        for m in range(1, many):
            row = at[m, k]
            picked.append(held[row if skipped is None else jnp.where(row == skipped, rows, row)])
        return jnp.concatenate(picked, axis=1)

    def apart(left, right, own, other):
        zero = jnp.zeros_like(own)
        sides = [jnp.concatenate([own, zero], axis=1), jnp.concatenate([zero, other], axis=1)]
        return mul(jnp.concatenate([left, right], axis=1), jnp.concatenate(sides, axis=0))

    def ready(at, blocks, many, first, step, heads):
        of_a, of_b, links = [], [], []
        for a in (first, first + 2 * step):
            b = a + step
            lefts = [
                jnp.concatenate(heads(k) + [blocks[k].reshape(many * width, width)], axis=0)
                for k in (a, b)
            ]
            both = apart(*lefts, inverse[a], inverse[b])
            of_a.append(both[:, :width])
            of_b.append(both[:, width:])
            tail = both[both.shape[0] - many * width :, width:]
            links.append(narrow(named(at, b, a, tail, many)))
        narrow_a = [narrow(value) for value in of_a]
        both = apart(*narrow_a, *links)
        through = [both[:, :width], both[:, width:]]
        return of_a, narrow_a, of_b, through, links

    def ready_down(p):
        of_a, narrow_a, of_b, through, _ = ready(
            lower_at, lower, slots, 2 * p, 1, lambda k: [narrow(rhs[k])]
        )
        for i in range(2):
            a, b = 2 * (p + i), 2 * (p + i) + 1
            exact[a, :count] = of_a[i][:count]
            exact[a, count:] = -of_a[i][count:near]
            exact[b, :count] = of_b[i][:count] - through[i][:count]
            exact[b, count:] = through[i][count:near] - of_b[i][count:near]
            if p + i == 0:
                inner = sum(piece(of_a[i][count:], m) for m in range(1, slots))
                exact[a, count:] += -inner
                inner = sum(piece(through[i][count:], m) for m in range(1, slots))
                exact[b, count:] += inner - named(lower_at, b, b, of_b[i][count:], slots)
            else:
                low_pair[p + i, :, :width] = narrow_a[i][near:]
                low_pair[p + i, :, width:] = narrow(through[i][near:])
                low_second[p + i] = narrow(of_b[i][near:])

    def go_down(p):
        a, b = 2 * p, 2 * p + 1
        if p > 0:
            first = mul(sources(down, lower_at, a, None, slots), low_pair[p])
            second = mul(sources(down, lower_at, b, a, slots), low_second[p])
            exact[a] -= first[:, :width]
            exact[b] += first[:, width:] - second
        down[a] = narrow(exact[a])
        down[b] = narrow(exact[b])

    def ready_up(p):
        of_a, narrow_a, of_b, through, links = ready(
            upper_at, upper, upper_slots, last - 2 * p, -1, lambda k: []
        )
        for i in range(2):
            a = last - 2 * (p + i)
            b = a - 1
            fixed[a] = -of_a[i][:width]
            fixed[b] = through[i][:width] - of_b[i][:width]
            if p + i == 0:
                fixed[a] += -sum(piece(of_a[i], m) for m in range(1, upper_slots))
                inner = sum(piece(through[i], m) for m in range(1, upper_slots))
                fixed[b] += inner - named(upper_at, b, b, of_b[i], upper_slots)
            else:
                upp_pair[p + i, :, :width] = narrow_a[i][width:]
                upp_pair[p + i, :, width:] = narrow(through[i][width:])
                upp_second[p + i] = narrow(of_b[i][width:])
        return links

    def go_up(p, passed):
        a = last - 2 * p
        b = a - 1
        of_a = exact[a]
        of_b = exact[b] - passed
        free_a = fixed[a]
        free_b = fixed[b]
        if p > 0:
            first = mul(sources(response, upper_at, a, None, upper_slots), upp_pair[p])
            second = mul(sources(response, upper_at, b, a, upper_slots), upp_second[p])
            of_a = of_a - first[:near, :width]
            of_b = of_b + first[:near, width:] - second[:near]
            free_a = free_a - first[near:, :width]
            free_b = free_b + first[near:, width:] - second[near:]
        for k, value, free in ((a, of_a, free_a), (b, of_b, free_b)):
            base[k] = value[:count]
            response[k, :near] = narrow(value)
            response[k, near:] = narrow(free)

    pairs = rows // 2
    for copy in copies[:4]:
        copy.wait()
    for copy in copies[5:]:
        copy.start()
    ready_down(0)
    go_down(0)
    for copy in copies[4:]:
        copy.wait()
    links = []
    for p in range(1, pairs):
        if p % 2 == 1 and p + 1 < pairs:
            ready_down(p + 1)
        go_down(p)
        if p % 2 == 1:
            links += ready_up(p - 1)
    for p in range(0, pairs, 2):
        a = last - 2 * p
        passed = apart(down[a], down[a - 2], links[p], links[p + 1])
        go_up(p, passed[:, :width])
        go_up(p + 1, passed[:, width:])

    far = near + width
    payload[:near] = down[last]
    payload[near : near + far] = response[0]
    payload[near + far :] = response[last, near:]


def compose_kernel(axis, bit, final, mine, theirs, *refs):
    prior, sent, inner, prior_out = refs[:4] if bit > 1 else (None, *refs[:3])
    pair = refs[-1]
    width = mine.shape[1]
    count = (mine.shape[0] - 4 * width) // 2
    near = count + width
    me = lax.axis_index(axis)
    place = lax.rem(lax.div(me, bit), 2)
    mid = near + count
    far = near + near + width

    pair[place] = mine[...]
    pair[1 - place] = theirs[...]
    a = pair[0]
    b = pair[1]
    across = mul(a[:near], jnp.concatenate([b[count:near], b[mid : mid + width]], axis=1))
    ahead = b[:near].astype(jnp.float32)
    joined = across[:, :width] + jnp.concatenate(
        [ahead[:count], jnp.zeros((width, width), jnp.float32)], axis=0
    )
    between = across[:, width:] + jnp.concatenate(
        [b[near:mid].astype(jnp.float32), jnp.zeros((width, width), jnp.float32)], axis=0
    )
    between = jnp.concatenate([narrow(between), b[mid + width : far]], axis=0)
    first = mul(between, a[mid + width : far])
    first = narrow(first[:near] + a[near : 2 * near].astype(jnp.float32)), narrow(first[near:])
    joined = narrow(joined)
    inner[:near] = a[:near]
    inner[near:] = between
    prior_out[...] = a[far:]
    if prior is not None:
        lowest = jnp.logical_and(place == 1, lax.rem(me, bit) == 0)

        @pl.when(jnp.logical_not(lowest))
        def _():
            prior_out[...] = prior[...]

    if final:
        refs[-2][...] = joined[:count]
        above = lax.rem(lax.div(me, 2 * bit), 2) == 1

        @pl.when(above)
        def _():
            sent[...] = first[0]

        @pl.when(jnp.logical_not(above))
        def _():
            sent[:count] = joined[:count]
            sent[count:] = b[far:]

    else:
        sent[:near] = joined
        sent[near : 2 * near] = first[0]
        sent[2 * near : far] = first[1]
        sent[far:] = b[far:]


def fold_kernel(axis, levels, *refs):
    base, response = refs[:2]
    inner = refs[2 : 1 + levels]
    folded, folded_response, inflow_map, outflow_map = refs[1 + levels :]
    rows, count, width = base.shape
    near = count + width
    me = lax.axis_index(axis)

    upper = lax.div(me, 1 << (levels - 1)) == 1
    across = lax.broadcasted_iota(jnp.int32, (near, width), 1) + count
    unit = jnp.where(lax.broadcasted_iota(jnp.int32, (near, width), 0) == across, 1.0, 0.0)
    inflow = jnp.where(upper, unit, 0.0)
    outflow = jnp.where(upper, 0.0, unit)
    blank = jnp.zeros((width, width), jnp.float32)
    for level in range(levels - 2, -1, -1):
        part = inner[level]
        upper = lax.rem(lax.div(me, 1 << level), 2) == 1
        known = jnp.concatenate([part[:count].astype(jnp.float32), blank], axis=0)
        down = known + mul(narrow(inflow), part[count:near])
        both = narrow(jnp.concatenate([inflow, outflow], axis=1))
        known = jnp.concatenate([part[near : near + count].astype(jnp.float32), blank], axis=0)
        up = known + mul(both, part[near + count :])
        inflow, outflow = jnp.where(upper, down, inflow), jnp.where(upper, outflow, up)

    inflow_map[...] = narrow(inflow)
    outflow_map[...] = narrow(outflow)
    both = narrow(jnp.concatenate([inflow, outflow], axis=1))
    for k in range(rows):
        value = mul(both, response[k, count:])
        folded[k] = base[k] + value[:count]
        folded_response[k] = narrow(value[count:])


def chain_kernel(
    axes, levels, own, theirs, base, response, solution, rounded, brought, near_rows, far_rows
):
    rows, count, width = base.shape
    side = lax.rem(lax.axis_index(axes[1]), 2)
    upper = lax.div(lax.axis_index(axes[0]), 1 << (levels - 1)) == 1
    down = theirs[:count].astype(jnp.float32)
    up = down + mul(own[...], theirs[count:])
    z = narrow(jnp.where(upper, down, up))
    brought[...] = z
    for k in range(rows):
        value = base[k] + mul(z, response[k])
        solution[k] = value
        rounded[k] = narrow(value)
    rim = near_rows.shape[0]
    for e in range(rim):
        near_rows[e] = rounded[(1 - side) * (rows - rim) + e]
        far_rows[e] = rounded[side * (rows - rim) + e]


def local_kernel(
    axes,
    levels,
    rounded,
    brought,
    inflow_map,
    outflow_map,
    prior,
    theirs,
    solved,
    diagonal,
    lower,
    upper,
    lower_at_far,
    upper_at_far,
    halo_at_far,
    partial,
    solution,
    masks,
    held,
    last_block,
    lower_at,
    upper_at,
    halo_at,
    arrived,
):
    parts = [
        (lower_at_far, lower_at),
        (upper_at_far, upper_at),
        (halo_at_far, halo_at),
        (solved, solution),
    ]
    copies = [
        pltpu.make_async_copy(source, target, arrived.at[i])
        for i, (source, target) in enumerate(parts)
    ]
    for copy in copies:
        copy.start()
    rows, slots, width, _ = lower.shape
    upper_slots = upper.shape[1]
    count = brought.shape[0]
    me = lax.axis_index(axes[0])
    last_block[...] = prior[...]

    @pl.when(me == 1 << (levels - 1))
    def _():
        last_block[...] = theirs[count:]

    z = brought[...]
    after = narrow(outflow_map[:count].astype(jnp.float32) + mul(z, outflow_map[count:]))
    before = inflow_map[:count].astype(jnp.float32) + mul(z, inflow_map[count:])
    before = narrow(before).astype(jnp.float32) + mul(rounded[0], last_block[...])
    before = narrow(jnp.where(me > 0, before, 0.0))
    held[:rows] = rounded[...]
    held[rows] = before
    held[rows + 1] = after
    for k in range(rows):
        source = jnp.concatenate([rounded[k], after], axis=1)
        total = mul(source, jnp.concatenate([diagonal[k], upper[k, 0]], axis=0))
        partial[k] = total + mul(before, lower[k, 0])
    for copy in copies[:3]:
        copy.wait()
    for k in range(rows):
        source = []
        for m in range(1, slots):
            at = lower_at[m, k]
            source.append(held[jnp.where(at == k, rows, at)])
        total = mul(
            jnp.concatenate(source, axis=1), lower[k, 1:].reshape((slots - 1) * width, width)
        )
        source = []
        for m in range(1, upper_slots):
            at = upper_at[m, k]
            source.append(held[jnp.where(at == k, rows + 1, at)])
        partial[k] += total + mul(
            jnp.concatenate(source, axis=1),
            upper[k, 1:].reshape((upper_slots - 1) * width, width),
        )
    _, picked, places, _, _ = masks.shape
    turn = places // 2 * (1 - lax.rem(lax.axis_index(axes[1]), 2))
    for k in range(rows):
        for m in range(picked):
            at = lax.rem(halo_at[m + 1, k] + turn, places)
            for j in range(places):
                mask = jnp.where(at == j, 1.0, 0.0)
                masks[k, m, j] = narrow(jnp.full((count, width), mask, jnp.float32))
    copies[3].wait()


def halo_kernel(axis, partial, outer, inner, halo, masks, product, rim_rows):
    rows, slots, width, _ = halo.shape
    rim = inner.shape[0]
    turn = rim * (1 - lax.rem(lax.axis_index(axis), 2))
    rim_rows[:rim] = inner[...]
    rim_rows[rim:] = outer[...]
    for k in range(rows):
        source = [rim_rows[lax.rem(k + turn, 2 * rim)]]
        for m in range(1, slots):
            source.append(sum(masks[k, m - 1, j] * rim_rows[j] for j in range(2 * rim)))
        product[k] = partial[k] + mul(
            jnp.concatenate(source, axis=1), halo[k].reshape(slots * width, width)
        )


def trade(block, axis, bit):
    count = lax.axis_size(axis)
    return lax.ppermute(block, axis, [(i, i ^ bit) for i in range(count)])


def swaps(block, axis, first):
    count = lax.axis_size(axis)
    pairs = []
    for low in range(first, count - 1, 2):
        pairs += [(low, low + 1), (low + 1, low)]
    return lax.ppermute(block, axis, pairs)


def on_device(
    right_sides,
    diag_inverse,
    diag_blocks,
    lower_blocks,
    upper_blocks,
    halo_blocks,
    lower_index,
    upper_index,
    halo_index,
):
    rows, count, width = right_sides.shape
    lower_at, upper_at, halo_at = lower_index.T, upper_index.T, halo_index.T
    slots = lower_blocks.shape[1]
    upper_slots = upper_blocks.shape[1]
    groups = lax.axis_size("section")
    near = count + width
    far = near + width
    wide = jax.ShapeDtypeStruct((rows, count, width), jnp.float32)

    indices = (lower_at, upper_at, halo_at)
    base, response, payload, *indices = pl.pallas_call(
        sweep_kernel,
        out_shape=(
            wide,
            jax.ShapeDtypeStruct((rows + 1, far, width), jnp.bfloat16),
            jax.ShapeDtypeStruct((near + far + width, width), jnp.bfloat16),
        )
        + tuple(jax.ShapeDtypeStruct(a.shape, a.dtype) for a in indices),
        in_specs=[HBM] * 7,
        out_specs=(VMEM,) * 6,
        scratch_shapes=[
            pltpu.VMEM(right_sides.shape, right_sides.dtype),
            pltpu.VMEM(diag_inverse.shape, diag_inverse.dtype),
            pltpu.VMEM(lower_blocks.shape, lower_blocks.dtype),
            pltpu.VMEM(upper_blocks.shape, upper_blocks.dtype),
            pltpu.SMEM(lower_at.shape, jnp.int32),
            pltpu.SMEM(upper_at.shape, jnp.int32),
            pltpu.VMEM((rows // 2, (slots - 1) * width, 2 * width), jnp.bfloat16),
            pltpu.VMEM((rows // 2, (slots - 1) * width, width), jnp.bfloat16),
            pltpu.VMEM((rows // 2, (upper_slots - 1) * width, 2 * width), jnp.bfloat16),
            pltpu.VMEM((rows // 2, (upper_slots - 1) * width, width), jnp.bfloat16),
            pltpu.VMEM((rows + 1, near, width), jnp.bfloat16),
            pltpu.VMEM((rows, near, width), jnp.float32),
            pltpu.VMEM((rows, width, width), jnp.float32),
            pltpu.SemaphoreType.DMA((10,)),
        ],
        compiler_params=SMALL,
        name="sweeps",
    )(
        *(
            pltpu.with_memory_space_constraint(a, pltpu.HBM)
            for a in (right_sides, diag_inverse, lower_blocks, upper_blocks, *indices)
        )
    )

    levels = groups.bit_length() - 1
    segment = payload.shape[0]
    bits = jnp.bfloat16
    prior = []
    inner = []
    for level in range(levels - 1):
        theirs = trade(payload, "section", 1 << level)
        final = level == levels - 2

        def compose(*refs, bit=1 << level, final=final):
            compose_kernel("section", bit, final, *refs)

        payload, between, *prior = pl.pallas_call(
            compose,
            out_shape=(
                jax.ShapeDtypeStruct((near if final else segment, width), bits),
                jax.ShapeDtypeStruct((near + far, width), bits),
                jax.ShapeDtypeStruct((width, width), bits),
            )
            + (jax.ShapeDtypeStruct((count, width), bits),) * final,
            in_specs=[VMEM] * (2 + len(prior)),
            out_specs=(VMEM,) * (3 + final),
            scratch_shapes=[pltpu.VMEM((2, segment, width), bits)],
            compiler_params=SMALL,
            name="compose",
        )(payload, theirs, *prior)
        inner.append(between)
    prior, own = prior
    theirs = trade(payload, "section", 1 << (levels - 1))

    def fold(*refs):
        fold_kernel("section", levels, *refs)

    base, response, inflow_map, outflow_map = pl.pallas_call(
        fold,
        out_shape=(
            wide,
            jax.ShapeDtypeStruct((rows, width, width), bits),
            jax.ShapeDtypeStruct((near, width), bits),
            jax.ShapeDtypeStruct((near, width), bits),
        ),
        in_specs=[VMEM] * (1 + levels),
        out_specs=(VMEM,) * 4,
        compiler_params=SMALL,
        name="fold",
    )(base, response, *inner)

    def chain(*refs):
        chain_kernel(("section", "dom"), levels, *refs)

    solved, rounded, brought, inner, outer = pl.pallas_call(
        chain,
        out_shape=(
            wide,
            jax.ShapeDtypeStruct((rows, count, width), bits),
            jax.ShapeDtypeStruct((count, width), bits),
            jax.ShapeDtypeStruct((RIM, count, width), bits),
            jax.ShapeDtypeStruct((RIM, count, width), bits),
        ),
        in_specs=[VMEM] * 4,
        out_specs=(VMEM,) * 5,
        compiler_params=SMALL,
        name="chain",
    )(own, theirs, base, response)

    outer = swaps(outer, "dom", 1)
    inner = swaps(inner, "dom", 0)

    def local(*refs):
        local_kernel(("section", "dom"), levels, *refs)

    masks = (rows, halo_blocks.shape[1] - 1, 2 * RIM, count, width)
    partial, solution, masks = pl.pallas_call(
        local,
        out_shape=(wide, wide, jax.ShapeDtypeStruct(masks, bits)),
        in_specs=[VMEM] * 13,
        out_specs=(VMEM, HBM, VMEM),
        scratch_shapes=[
            pltpu.VMEM((rows + 2, count, width), bits),
            pltpu.VMEM((width, width), bits),
        ]
        + [pltpu.SMEM(a.shape, jnp.int32) for a in indices]
        + [pltpu.SemaphoreType.DMA((4,))],
        compiler_params=SMALL,
        name="local_product",
    )(
        rounded,
        brought,
        inflow_map,
        outflow_map,
        prior,
        theirs,
        solved,
        diag_blocks,
        lower_blocks,
        upper_blocks,
        *indices,
    )

    def halo(*refs):
        halo_kernel("dom", *refs)

    product = pl.pallas_call(
        halo,
        out_shape=wide,
        in_specs=[VMEM] * 5,
        out_specs=VMEM,
        scratch_shapes=[pltpu.VMEM((2 * RIM, count, width), bits)],
        compiler_params=SMALL,
        name="halo_product",
    )(partial, outer, inner, halo_blocks, masks)
    return (solution, product)


def solution(mesh):
    in_specs = (
        P(("section", "dom"), None, None),
        P(("section", "dom"), None, None),
        P(("section", "dom"), None, None),
        P(("section", "dom"), None, None, None),
        P(("section", "dom"), None, None, None),
        P(("section", "dom"), None, None, None),
        P(("section", "dom"), None),
        P(("section", "dom"), None),
        P(("section", "dom"), None),
    )
    out_specs = (P(("section", "dom"), None, None), P(("section", "dom"), None, None))
    return jax.shard_map(
        on_device, mesh=mesh, in_specs=in_specs, out_specs=out_specs, check_vma=False
    )
```

```python
import jax
import jax.numpy as jnp
from jax import lax
from jax.experimental import pallas as pl
from jax.experimental.pallas import tpu as pltpu
from jax.sharding import PartitionSpec as P

RIM = 4

VMEM = pl.BlockSpec(memory_space=pltpu.VMEM)
SMEM = pl.BlockSpec(memory_space=pltpu.SMEM)
HBM = pl.BlockSpec(memory_space=pltpu.HBM)
SMALL = pltpu.CompilerParams(vmem_limit_bytes=16 * 1024 * 1024)


def mul(a, b):
    return jnp.dot(a, b, preferred_element_type=jnp.float32)


def narrow(a):
    return a.astype(jnp.bfloat16)


def sweep_kernel(
    rhs_far,
    inverse_far,
    lower_far,
    upper_far,
    lower_at_far,
    upper_at_far,
    halo_at_far,
    base,
    response,
    payload,
    lower_at_kept,
    upper_at_kept,
    halo_at_kept,
    rhs,
    inverse,
    lower,
    upper,
    lower_at,
    upper_at,
    low_pair,
    low_second,
    upp_pair,
    upp_second,
    down,
    exact,
    fixed,
    arrived,
):
    rows, count, width = rhs.shape
    slots = lower.shape[1]
    upper_slots = upper.shape[1]
    near = count + width
    last = rows - 1
    half = rows // 2
    parts = [
        (inverse_far.at[:2], inverse.at[:2]),
        (lower_far.at[:2], lower.at[:2]),
        (rhs_far, rhs),
        (lower_at_far, lower_at),
        (inverse_far.at[2:], inverse.at[2:]),
        (lower_far.at[2:half], lower.at[2:half]),
        (lower_far.at[half:], lower.at[half:]),
        (upper_far, upper),
        (upper_at_far, upper_at),
        (lower_at_far, lower_at_kept),
        (upper_at_far, upper_at_kept),
        (halo_at_far, halo_at_kept),
    ]
    copies = [
        pltpu.make_async_copy(far, here, arrived.at[i]) for i, (far, here) in enumerate(parts)
    ]
    for copy in copies[:9]:
        copy.start()
    eye = narrow(
        lax.broadcasted_iota(jnp.int32, (width, width), 0)
        == lax.broadcasted_iota(jnp.int32, (width, width), 1)
    )
    down[:, :count] = jnp.zeros((rows + 1, count, width), jnp.bfloat16)
    response[:, :near] = jnp.zeros((rows + 1, near, width), jnp.bfloat16)
    for k in range(rows):
        down[k, count:] = eye
        response[k, near:] = eye
    down[rows, count:] = jnp.zeros_like(eye)
    response[rows, near:] = jnp.zeros_like(eye)

    def piece(blocks, m):
        return blocks[m * width : (m + 1) * width]

    def named(at, k, row, blocks, many):
        return sum(
            jnp.where(at[m, k] == row, piece(blocks, m), 0.0) for m in range(1, many)
        )

    def sources(held, at, k, skipped, many):
        picked = []
        for m in range(1, many):
            row = at[m, k]
            picked.append(held[row if skipped is None else jnp.where(row == skipped, rows, row)])
        return jnp.concatenate(picked, axis=1)

    def apart(left, right, own, other):
        zero = jnp.zeros_like(own)
        sides = [jnp.concatenate([own, zero], axis=1), jnp.concatenate([zero, other], axis=1)]
        return mul(jnp.concatenate([left, right], axis=1), jnp.concatenate(sides, axis=0))

    def ready(at, blocks, many, first, step, heads, later=()):
        of_a, of_b, links = [], [], []
        for a in (first, first + 2 * step):
            if a != first:
                for copy in later:
                    copy.wait()
            b = a + step
            lefts = [
                jnp.concatenate(heads(k) + [blocks[k].reshape(many * width, width)], axis=0)
                for k in (a, b)
            ]
            both = apart(*lefts, inverse[a], inverse[b])
            of_a.append(both[:, :width])
            of_b.append(both[:, width:])
            tail = both[both.shape[0] - many * width :, width:]
            links.append(narrow(named(at, b, a, tail, many)))
        narrow_a = [narrow(value) for value in of_a]
        both = apart(*narrow_a, *links)
        through = [both[:, :width], both[:, width:]]
        return of_a, narrow_a, of_b, through, links

    def ready_down(p, later=()):
        of_a, narrow_a, of_b, through, _ = ready(
            lower_at, lower, slots, 2 * p, 1, lambda k: [narrow(rhs[k])], later
        )
        for i in range(2):
            a, b = 2 * (p + i), 2 * (p + i) + 1
            exact[a, :count] = of_a[i][:count]
            exact[a, count:] = -of_a[i][count:near]
            exact[b, :count] = of_b[i][:count] - through[i][:count]
            exact[b, count:] = through[i][count:near] - of_b[i][count:near]
            if p + i == 0:
                inner = sum(piece(of_a[i][count:], m) for m in range(1, slots))
                exact[a, count:] += -inner
                inner = sum(piece(through[i][count:], m) for m in range(1, slots))
                exact[b, count:] += inner - named(lower_at, b, b, of_b[i][count:], slots)
            else:
                low_pair[p + i, :, :width] = narrow_a[i][near:]
                low_pair[p + i, :, width:] = narrow(through[i][near:])
                low_second[p + i] = narrow(of_b[i][near:])

    def go_down(p):
        a, b = 2 * p, 2 * p + 1
        if p > 0:
            first = mul(sources(down, lower_at, a, None, slots), low_pair[p])
            second = mul(sources(down, lower_at, b, a, slots), low_second[p])
            exact[a] -= first[:, :width]
            exact[b] += first[:, width:] - second
        down[a] = narrow(exact[a])
        down[b] = narrow(exact[b])

    def ready_up(p):
        of_a, narrow_a, of_b, through, links = ready(
            upper_at, upper, upper_slots, last - 2 * p, -1, lambda k: []
        )
        for i in range(2):
            a = last - 2 * (p + i)
            b = a - 1
            fixed[a] = -of_a[i][:width]
            fixed[b] = through[i][:width] - of_b[i][:width]
            if p + i == 0:
                fixed[a] += -sum(piece(of_a[i], m) for m in range(1, upper_slots))
                inner = sum(piece(through[i], m) for m in range(1, upper_slots))
                fixed[b] += inner - named(upper_at, b, b, of_b[i], upper_slots)
            else:
                upp_pair[p + i, :, :width] = narrow_a[i][width:]
                upp_pair[p + i, :, width:] = narrow(through[i][width:])
                upp_second[p + i] = narrow(of_b[i][width:])
        return links

    def go_up(p, passed):
        a = last - 2 * p
        b = a - 1
        of_a = exact[a]
        of_b = exact[b] - passed
        free_a = fixed[a]
        free_b = fixed[b]
        if p > 0:
            first = mul(sources(response, upper_at, a, None, upper_slots), upp_pair[p])
            second = mul(sources(response, upper_at, b, a, upper_slots), upp_second[p])
            of_a = of_a - first[:near, :width]
            of_b = of_b + first[:near, width:] - second[:near]
            free_a = free_a - first[near:, :width]
            free_b = free_b + first[near:, width:] - second[near:]
        for k, value, free in ((a, of_a, free_a), (b, of_b, free_b)):
            base[k] = value[:count]
            response[k, :near] = narrow(value)
            response[k, near:] = narrow(free)

    pairs = rows // 2
    for copy in copies[:4]:
        copy.wait()
    for copy in copies[9:]:
        copy.start()
    ready_down(0, copies[4:6])
    go_down(0)
    for copy in copies[6:9]:
        copy.wait()
    links = []
    for p in range(1, pairs):
        if p % 2 == 1 and p + 1 < pairs:
            ready_down(p + 1)
        go_down(p)
        if p % 2 == 1:
            links += ready_up(p - 1)
    for p in range(0, pairs, 2):
        a = last - 2 * p
        passed = apart(down[a], down[a - 2], links[p], links[p + 1])
        go_up(p, passed[:, :width])
        go_up(p + 1, passed[:, width:])

    far = near + width
    payload[:near] = down[last]
    payload[near : near + far] = response[0]
    payload[near + far :] = response[last, near:]
    for copy in copies[9:]:
        copy.wait()


def compose_kernel(axis, bit, final, mine, theirs, *refs):
    prior, sent, inner, prior_out = refs[:4] if bit > 1 else (None, *refs[:3])
    pair = refs[-1]
    width = mine.shape[1]
    count = (mine.shape[0] - 4 * width) // 2
    near = count + width
    me = lax.axis_index(axis)
    place = lax.rem(lax.div(me, bit), 2)
    mid = near + count
    far = near + near + width

    pair[place] = mine[...]
    pair[1 - place] = theirs[...]
    a = pair[0]
    b = pair[1]
    across = mul(a[:near], jnp.concatenate([b[count:near], b[mid : mid + width]], axis=1))
    ahead = b[:near].astype(jnp.float32)
    joined = across[:, :width] + jnp.concatenate(
        [ahead[:count], jnp.zeros((width, width), jnp.float32)], axis=0
    )
    between = across[:, width:] + jnp.concatenate(
        [b[near:mid].astype(jnp.float32), jnp.zeros((width, width), jnp.float32)], axis=0
    )
    between = jnp.concatenate([narrow(between), b[mid + width : far]], axis=0)
    first = mul(between, a[mid + width : far])
    first = narrow(first[:near] + a[near : 2 * near].astype(jnp.float32)), narrow(first[near:])
    joined = narrow(joined)
    inner[:near] = a[:near]
    inner[near:] = between
    prior_out[...] = a[far:]
    if prior is not None:
        lowest = jnp.logical_and(place == 1, lax.rem(me, bit) == 0)

        @pl.when(jnp.logical_not(lowest))
        def _():
            prior_out[...] = prior[...]

    if final:
        refs[-2][...] = joined[:count]
        above = lax.rem(lax.div(me, 2 * bit), 2) == 1

        @pl.when(above)
        def _():
            sent[...] = first[0]

        @pl.when(jnp.logical_not(above))
        def _():
            sent[:count] = joined[:count]
            sent[count:] = b[far:]

    else:
        sent[:near] = joined
        sent[near : 2 * near] = first[0]
        sent[2 * near : far] = first[1]
        sent[far:] = b[far:]


def fold_kernel(axis, levels, *refs):
    base, response = refs[:2]
    inner = refs[2 : 1 + levels]
    folded, folded_response, inflow_map, outflow_map = refs[1 + levels :]
    rows, count, width = base.shape
    near = count + width
    me = lax.axis_index(axis)

    upper = lax.div(me, 1 << (levels - 1)) == 1
    across = lax.broadcasted_iota(jnp.int32, (near, width), 1) + count
    unit = jnp.where(lax.broadcasted_iota(jnp.int32, (near, width), 0) == across, 1.0, 0.0)
    inflow = jnp.where(upper, unit, 0.0)
    outflow = jnp.where(upper, 0.0, unit)
    blank = jnp.zeros((width, width), jnp.float32)
    for level in range(levels - 2, -1, -1):
        part = inner[level]
        upper = lax.rem(lax.div(me, 1 << level), 2) == 1
        known = jnp.concatenate([part[:count].astype(jnp.float32), blank], axis=0)
        down = known + mul(narrow(inflow), part[count:near])
        both = narrow(jnp.concatenate([inflow, outflow], axis=1))
        known = jnp.concatenate([part[near : near + count].astype(jnp.float32), blank], axis=0)
        up = known + mul(both, part[near + count :])
        inflow, outflow = jnp.where(upper, down, inflow), jnp.where(upper, outflow, up)

    inflow_map[...] = narrow(inflow)
    outflow_map[...] = narrow(outflow)
    both = narrow(jnp.concatenate([inflow, outflow], axis=1))
    for k in range(rows):
        value = mul(both, response[k, count:])
        folded[k] = base[k] + value[:count]
        folded_response[k] = narrow(value[count:])


def chain_kernel(
    axes, levels, own, theirs, base, response, solution, rounded, brought, near_rows, far_rows
):
    rows, count, width = base.shape
    side = lax.rem(lax.axis_index(axes[1]), 2)
    upper = lax.div(lax.axis_index(axes[0]), 1 << (levels - 1)) == 1
    down = theirs[:count].astype(jnp.float32)
    up = down + mul(own[...], theirs[count:])
    z = narrow(jnp.where(upper, down, up))
    brought[...] = z
    for k in range(rows):
        value = base[k] + mul(z, response[k])
        solution[k] = value
        rounded[k] = narrow(value)
    rim = near_rows.shape[0]
    for e in range(rim):
        near_rows[e] = rounded[(1 - side) * (rows - rim) + e]
        far_rows[e] = rounded[side * (rows - rim) + e]


def local_kernel(
    axes,
    levels,
    rounded,
    brought,
    inflow_map,
    outflow_map,
    prior,
    theirs,
    solved,
    diagonal,
    lower,
    upper,
    lower_at_far,
    upper_at_far,
    halo_at_far,
    partial,
    solution,
    masks,
    held,
    last_block,
    lower_at,
    upper_at,
    halo_at,
    arrived,
):
    parts = [
        (lower_at_far, lower_at),
        (upper_at_far, upper_at),
        (halo_at_far, halo_at),
        (solved, solution),
    ]
    copies = [
        pltpu.make_async_copy(source, target, arrived.at[i])
        for i, (source, target) in enumerate(parts)
    ]
    for copy in copies:
        copy.start()
    rows, slots, width, _ = lower.shape
    upper_slots = upper.shape[1]
    count = brought.shape[0]
    me = lax.axis_index(axes[0])
    last_block[...] = prior[...]

    @pl.when(me == 1 << (levels - 1))
    def _():
        last_block[...] = theirs[count:]

    z = brought[...]
    after = narrow(outflow_map[:count].astype(jnp.float32) + mul(z, outflow_map[count:]))
    before = inflow_map[:count].astype(jnp.float32) + mul(z, inflow_map[count:])
    before = narrow(before).astype(jnp.float32) + mul(rounded[0], last_block[...])
    before = narrow(jnp.where(me > 0, before, 0.0))
    held[:rows] = rounded[...]
    held[rows] = before
    held[rows + 1] = after
    for k in range(rows):
        source = jnp.concatenate([rounded[k], after], axis=1)
        total = mul(source, jnp.concatenate([diagonal[k], upper[k, 0]], axis=0))
        partial[k] = total + mul(before, lower[k, 0])
    for copy in copies[:3]:
        copy.wait()
    for k in range(rows):
        source = []
        for m in range(1, slots):
            at = lower_at[m, k]
            source.append(held[jnp.where(at == k, rows, at)])
        total = mul(
            jnp.concatenate(source, axis=1), lower[k, 1:].reshape((slots - 1) * width, width)
        )
        source = []
        for m in range(1, upper_slots):
            at = upper_at[m, k]
            source.append(held[jnp.where(at == k, rows + 1, at)])
        partial[k] += total + mul(
            jnp.concatenate(source, axis=1),
            upper[k, 1:].reshape((upper_slots - 1) * width, width),
        )
    _, picked, places, _, _ = masks.shape
    turn = places // 2 * (1 - lax.rem(lax.axis_index(axes[1]), 2))
    for k in range(rows):
        for m in range(picked):
            at = lax.rem(halo_at[m + 1, k] + turn, places)
            for j in range(places):
                mask = jnp.where(at == j, 1.0, 0.0)
                masks[k, m, j] = narrow(jnp.full((count, width), mask, jnp.float32))
    copies[3].wait()


def halo_kernel(axis, partial, outer, inner, halo, masks, product, rim_rows):
    rows, slots, width, _ = halo.shape
    rim = inner.shape[0]
    turn = rim * (1 - lax.rem(lax.axis_index(axis), 2))
    rim_rows[:rim] = inner[...]
    rim_rows[rim:] = outer[...]
    for k in range(rows):
        source = [rim_rows[lax.rem(k + turn, 2 * rim)]]
        for m in range(1, slots):
            source.append(sum(masks[k, m - 1, j] * rim_rows[j] for j in range(2 * rim)))
        product[k] = partial[k] + mul(
            jnp.concatenate(source, axis=1), halo[k].reshape(slots * width, width)
        )


def trade(block, axis, bit):
    count = lax.axis_size(axis)
    return lax.ppermute(block, axis, [(i, i ^ bit) for i in range(count)])


def swaps(block, axis, first):
    count = lax.axis_size(axis)
    pairs = []
    for low in range(first, count - 1, 2):
        pairs += [(low, low + 1), (low + 1, low)]
    return lax.ppermute(block, axis, pairs)


def on_device(
    right_sides,
    diag_inverse,
    diag_blocks,
    lower_blocks,
    upper_blocks,
    halo_blocks,
    lower_index,
    upper_index,
    halo_index,
):
    rows, count, width = right_sides.shape
    lower_at, upper_at, halo_at = lower_index.T, upper_index.T, halo_index.T
    slots = lower_blocks.shape[1]
    upper_slots = upper_blocks.shape[1]
    groups = lax.axis_size("section")
    near = count + width
    far = near + width
    wide = jax.ShapeDtypeStruct((rows, count, width), jnp.float32)

    indices = (lower_at, upper_at, halo_at)
    base, response, payload, *indices = pl.pallas_call(
        sweep_kernel,
        out_shape=(
            wide,
            jax.ShapeDtypeStruct((rows + 1, far, width), jnp.bfloat16),
            jax.ShapeDtypeStruct((near + far + width, width), jnp.bfloat16),
        )
        + tuple(jax.ShapeDtypeStruct(a.shape, a.dtype) for a in indices),
        in_specs=[HBM] * 7,
        out_specs=(VMEM,) * 6,
        scratch_shapes=[
            pltpu.VMEM(right_sides.shape, right_sides.dtype),
            pltpu.VMEM(diag_inverse.shape, diag_inverse.dtype),
            pltpu.VMEM(lower_blocks.shape, lower_blocks.dtype),
            pltpu.VMEM(upper_blocks.shape, upper_blocks.dtype),
            pltpu.SMEM(lower_at.shape, jnp.int32),
            pltpu.SMEM(upper_at.shape, jnp.int32),
            pltpu.VMEM((rows // 2, (slots - 1) * width, 2 * width), jnp.bfloat16),
            pltpu.VMEM((rows // 2, (slots - 1) * width, width), jnp.bfloat16),
            pltpu.VMEM((rows // 2, (upper_slots - 1) * width, 2 * width), jnp.bfloat16),
            pltpu.VMEM((rows // 2, (upper_slots - 1) * width, width), jnp.bfloat16),
            pltpu.VMEM((rows + 1, near, width), jnp.bfloat16),
            pltpu.VMEM((rows, near, width), jnp.float32),
            pltpu.VMEM((rows, width, width), jnp.float32),
            pltpu.SemaphoreType.DMA((12,)),
        ],
        compiler_params=SMALL,
        name="sweeps",
    )(
        *(
            pltpu.with_memory_space_constraint(a, pltpu.HBM)
            for a in (right_sides, diag_inverse, lower_blocks, upper_blocks, *indices)
        )
    )

    levels = groups.bit_length() - 1
    segment = payload.shape[0]
    bits = jnp.bfloat16
    prior = []
    inner = []
    for level in range(levels - 1):
        theirs = trade(payload, "section", 1 << level)
        final = level == levels - 2

        def compose(*refs, bit=1 << level, final=final):
            compose_kernel("section", bit, final, *refs)

        payload, between, *prior = pl.pallas_call(
            compose,
            out_shape=(
                jax.ShapeDtypeStruct((near if final else segment, width), bits),
                jax.ShapeDtypeStruct((near + far, width), bits),
                jax.ShapeDtypeStruct((width, width), bits),
            )
            + (jax.ShapeDtypeStruct((count, width), bits),) * final,
            in_specs=[VMEM] * (2 + len(prior)),
            out_specs=(VMEM,) * (3 + final),
            scratch_shapes=[pltpu.VMEM((2, segment, width), bits)],
            compiler_params=SMALL,
            name="compose",
        )(payload, theirs, *prior)
        inner.append(between)
    prior, own = prior
    theirs = trade(payload, "section", 1 << (levels - 1))

    def fold(*refs):
        fold_kernel("section", levels, *refs)

    base, response, inflow_map, outflow_map = pl.pallas_call(
        fold,
        out_shape=(
            wide,
            jax.ShapeDtypeStruct((rows, width, width), bits),
            jax.ShapeDtypeStruct((near, width), bits),
            jax.ShapeDtypeStruct((near, width), bits),
        ),
        in_specs=[VMEM] * (1 + levels),
        out_specs=(VMEM,) * 4,
        compiler_params=SMALL,
        name="fold",
    )(base, response, *inner)

    def chain(*refs):
        chain_kernel(("section", "dom"), levels, *refs)

    solved, rounded, brought, inner, outer = pl.pallas_call(
        chain,
        out_shape=(
            wide,
            jax.ShapeDtypeStruct((rows, count, width), bits),
            jax.ShapeDtypeStruct((count, width), bits),
            jax.ShapeDtypeStruct((RIM, count, width), bits),
            jax.ShapeDtypeStruct((RIM, count, width), bits),
        ),
        in_specs=[VMEM] * 4,
        out_specs=(VMEM,) * 5,
        compiler_params=SMALL,
        name="chain",
    )(own, theirs, base, response)

    outer = swaps(outer, "dom", 1)
    inner = swaps(inner, "dom", 0)

    def local(*refs):
        local_kernel(("section", "dom"), levels, *refs)

    masks = (rows, halo_blocks.shape[1] - 1, 2 * RIM, count, width)
    partial, solution, masks = pl.pallas_call(
        local,
        out_shape=(wide, wide, jax.ShapeDtypeStruct(masks, bits)),
        in_specs=[VMEM] * 13,
        out_specs=(VMEM, HBM, VMEM),
        scratch_shapes=[
            pltpu.VMEM((rows + 2, count, width), bits),
            pltpu.VMEM((width, width), bits),
        ]
        + [pltpu.SMEM(a.shape, jnp.int32) for a in indices]
        + [pltpu.SemaphoreType.DMA((4,))],
        compiler_params=SMALL,
        name="local_product",
    )(
        rounded,
        brought,
        inflow_map,
        outflow_map,
        prior,
        theirs,
        solved,
        diag_blocks,
        lower_blocks,
        upper_blocks,
        *indices,
    )

    def halo(*refs):
        halo_kernel("dom", *refs)

    product = pl.pallas_call(
        halo,
        out_shape=wide,
        in_specs=[VMEM] * 5,
        out_specs=VMEM,
        scratch_shapes=[pltpu.VMEM((2 * RIM, count, width), bits)],
        compiler_params=SMALL,
        name="halo_product",
    )(partial, outer, inner, halo_blocks, masks)
    return (solution, product)


def solution(mesh):
    in_specs = (
        P(("section", "dom"), None, None),
        P(("section", "dom"), None, None),
        P(("section", "dom"), None, None),
        P(("section", "dom"), None, None, None),
        P(("section", "dom"), None, None, None),
        P(("section", "dom"), None, None, None),
        P(("section", "dom"), None),
        P(("section", "dom"), None),
        P(("section", "dom"), None),
    )
    out_specs = (P(("section", "dom"), None, None), P(("section", "dom"), None, None))
    return jax.shard_map(
        on_device, mesh=mesh, in_specs=in_specs, out_specs=out_specs, check_vma=False
    )
```

```python
import jax
import jax.numpy as jnp
from jax import lax
from jax.experimental import pallas as pl
from jax.experimental.pallas import tpu as pltpu
from jax.sharding import PartitionSpec as P

RIM = 4

VMEM = pl.BlockSpec(memory_space=pltpu.VMEM)
SMEM = pl.BlockSpec(memory_space=pltpu.SMEM)
HBM = pl.BlockSpec(memory_space=pltpu.HBM)
SMALL = pltpu.CompilerParams(vmem_limit_bytes=16 * 1024 * 1024)


def mul(a, b):
    return jnp.dot(a, b, preferred_element_type=jnp.float32)


def narrow(a):
    return a.astype(jnp.bfloat16)


def sweep_kernel(
    rhs_far,
    inverse_far,
    lower_far,
    upper_far,
    lower_at_far,
    upper_at_far,
    base,
    response,
    payload,
    rhs,
    inverse,
    lower,
    upper,
    lower_at,
    upper_at,
    low_pair,
    low_second,
    upp_pair,
    upp_second,
    down,
    exact,
    fixed,
    arrived,
):
    rows, count, width = rhs.shape
    slots = lower.shape[1]
    upper_slots = upper.shape[1]
    near = count + width
    last = rows - 1
    half = rows // 2
    parts = [
        (inverse_far, inverse),
        (rhs_far, rhs),
        (lower_far.at[:half], lower.at[:half]),
        (lower_at_far, lower_at),
        (lower_far.at[half:], lower.at[half:]),
        (upper_far, upper),
        (upper_at_far, upper_at),
    ]
    copies = [
        pltpu.make_async_copy(far, here, arrived.at[i]) for i, (far, here) in enumerate(parts)
    ]
    for copy in copies:
        copy.start()
    eye = narrow(
        lax.broadcasted_iota(jnp.int32, (width, width), 0)
        == lax.broadcasted_iota(jnp.int32, (width, width), 1)
    )
    down[:, :count] = jnp.zeros((rows + 1, count, width), jnp.bfloat16)
    response[:, :near] = jnp.zeros((rows + 1, near, width), jnp.bfloat16)
    for k in range(rows):
        down[k, count:] = eye
        response[k, near:] = eye
    down[rows, count:] = jnp.zeros_like(eye)
    response[rows, near:] = jnp.zeros_like(eye)

    def piece(blocks, m):
        return blocks[m * width : (m + 1) * width]

    def named(at, k, row, blocks, many):
        return sum(
            jnp.where(at[m, k] == row, piece(blocks, m), 0.0) for m in range(1, many)
        )

    def sources(held, at, k, skipped, many):
        picked = []
        for m in range(1, many):
            row = at[m, k]
            picked.append(held[row if skipped is None else jnp.where(row == skipped, rows, row)])
        return jnp.concatenate(picked, axis=1)

    def apart(left, right, own, other):
        zero = jnp.zeros_like(own)
        sides = [jnp.concatenate([own, zero], axis=1), jnp.concatenate([zero, other], axis=1)]
        return mul(jnp.concatenate([left, right], axis=1), jnp.concatenate(sides, axis=0))

    def ready(at, blocks, many, first, step, heads):
        of_a, of_b, links = [], [], []
        for a in (first, first + 2 * step):
            b = a + step
            lefts = [
                jnp.concatenate(heads(k) + [blocks[k].reshape(many * width, width)], axis=0)
                for k in (a, b)
            ]
            both = apart(*lefts, inverse[a], inverse[b])
            of_a.append(both[:, :width])
            of_b.append(both[:, width:])
            tail = both[both.shape[0] - many * width :, width:]
            links.append(narrow(named(at, b, a, tail, many)))
        narrow_a = [narrow(value) for value in of_a]
        both = apart(*narrow_a, *links)
        through = [both[:, :width], both[:, width:]]
        return of_a, narrow_a, of_b, through, links

    def ready_down(p):
        of_a, narrow_a, of_b, through, _ = ready(
            lower_at, lower, slots, 2 * p, 1, lambda k: [narrow(rhs[k])]
        )
        for i in range(2):
            a, b = 2 * (p + i), 2 * (p + i) + 1
            free_a = -of_a[i][count:near]
            free_b = through[i][count:near] - of_b[i][count:near]
            if p + i == 0:
                inner = sum(piece(of_a[i][count:], m) for m in range(1, slots))
                free_a = free_a - inner
                inner = sum(piece(through[i][count:], m) for m in range(1, slots))
                free_b = free_b + inner - named(lower_at, b, b, of_b[i][count:], slots)
            else:
                low_pair[p + i, :, :width] = narrow_a[i][near:]
                low_pair[p + i, :, width:] = narrow(through[i][near:])
                low_second[p + i] = narrow(of_b[i][near:])
            exact[a, :count] = of_a[i][:count]
            exact[a, count:] = free_a
            exact[b, :count] = of_b[i][:count] - through[i][:count]
            exact[b, count:] = free_b

    def go_down(p):
        a, b = 2 * p, 2 * p + 1
        of_a, of_b = exact[a], exact[b]
        if p > 0:
            first = mul(sources(down, lower_at, a, None, slots), low_pair[p])
            second = mul(sources(down, lower_at, b, a, slots), low_second[p])
            of_a = of_a - first[:, :width]
            of_b = of_b + first[:, width:] - second
            exact[a] = of_a
            exact[b] = of_b
        down[a] = narrow(of_a)
        down[b] = narrow(of_b)

    def ready_up(p):
        of_a, narrow_a, of_b, through, links = ready(
            upper_at, upper, upper_slots, last - 2 * p, -1, lambda k: []
        )
        for i in range(2):
            a = last - 2 * (p + i)
            b = a - 1
            free_a = -of_a[i][:width]
            free_b = through[i][:width] - of_b[i][:width]
            if p + i == 0:
                free_a = free_a - sum(piece(of_a[i], m) for m in range(1, upper_slots))
                inner = sum(piece(through[i], m) for m in range(1, upper_slots))
                free_b = free_b + inner - named(upper_at, b, b, of_b[i], upper_slots)
            else:
                upp_pair[p + i, :, :width] = narrow_a[i][width:]
                upp_pair[p + i, :, width:] = narrow(through[i][width:])
                upp_second[p + i] = narrow(of_b[i][width:])
            fixed[a] = free_a
            fixed[b] = free_b
        return links

    def go_up(p, passed):
        a = last - 2 * p
        b = a - 1
        of_a = exact[a]
        of_b = exact[b] - passed
        free_a = fixed[a]
        free_b = fixed[b]
        if p > 0:
            first = mul(sources(response, upper_at, a, None, upper_slots), upp_pair[p])
            second = mul(sources(response, upper_at, b, a, upper_slots), upp_second[p])
            of_a = of_a - first[:near, :width]
            of_b = of_b + first[:near, width:] - second[:near]
            free_a = free_a - first[near:, :width]
            free_b = free_b + first[near:, width:] - second[near:]
        for k, value, free in ((a, of_a, free_a), (b, of_b, free_b)):
            base[k] = value[:count]
            response[k, :near] = narrow(value)
            response[k, near:] = narrow(free)

    pairs = rows // 2
    for copy in copies[:4]:
        copy.wait()
    ready_down(0)
    go_down(0)
    for copy in copies[4:]:
        copy.wait()
    links = []
    for p in range(1, pairs):
        if p % 2 == 1 and p + 1 < pairs:
            ready_down(p + 1)
        go_down(p)
        if p % 2 == 1:
            links += ready_up(p - 1)
    far = near + width
    payload[:near] = down[last]
    for p in range(0, pairs, 2):
        a = last - 2 * p
        passed = apart(down[a], down[a - 2], links[p], links[p + 1])
        go_up(p, passed[:, :width])
        go_up(p + 1, passed[:, width:])

    payload[near + far :] = response[last, near:]
    payload[near : near + far] = response[0]


def compose_kernel(axis, bit, final, mine, theirs, *refs):
    prior, sent, inner, prior_out = refs[:4] if bit > 1 else (None, *refs[:3])
    pair = refs[-1]
    width = mine.shape[1]
    count = (mine.shape[0] - 4 * width) // 2
    near = count + width
    me = lax.axis_index(axis)
    place = lax.rem(lax.div(me, bit), 2)
    mid = near + count
    far = near + near + width

    pair[place] = mine[...]
    pair[1 - place] = theirs[...]
    a = pair[0]
    b = pair[1]
    across = mul(a[:near], jnp.concatenate([b[count:near], b[mid : mid + width]], axis=1))
    ahead = b[:near].astype(jnp.float32)
    joined = across[:, :width] + jnp.concatenate(
        [ahead[:count], jnp.zeros((width, width), jnp.float32)], axis=0
    )
    between = across[:, width:] + jnp.concatenate(
        [b[near:mid].astype(jnp.float32), jnp.zeros((width, width), jnp.float32)], axis=0
    )
    between = jnp.concatenate([narrow(between), b[mid + width : far]], axis=0)
    first = mul(between, a[mid + width : far])
    first = narrow(first[:near] + a[near : 2 * near].astype(jnp.float32)), narrow(first[near:])
    joined = narrow(joined)
    inner[:near] = a[:near]
    inner[near:] = between
    prior_out[...] = a[far:]
    if prior is not None:
        lowest = jnp.logical_and(place == 1, lax.rem(me, bit) == 0)

        @pl.when(jnp.logical_not(lowest))
        def _():
            prior_out[...] = prior[...]

    if final:
        refs[-2][...] = joined[:count]
        above = lax.rem(lax.div(me, 2 * bit), 2) == 1

        @pl.when(above)
        def _():
            sent[...] = first[0]

        @pl.when(jnp.logical_not(above))
        def _():
            sent[:count] = joined[:count]
            sent[count:] = b[far:]

    else:
        sent[:near] = joined
        sent[near : 2 * near] = first[0]
        sent[2 * near : far] = first[1]
        sent[far:] = b[far:]


def fold_kernel(axis, levels, *refs):
    base, response = refs[:2]
    inner = refs[2 : 1 + levels]
    folded, folded_response, inflow_map, outflow_map = refs[1 + levels :]
    rows, count, width = base.shape
    near = count + width
    me = lax.axis_index(axis)

    upper = lax.div(me, 1 << (levels - 1)) == 1
    across = lax.broadcasted_iota(jnp.int32, (near, width), 1) + count
    unit = jnp.where(lax.broadcasted_iota(jnp.int32, (near, width), 0) == across, 1.0, 0.0)
    inflow = jnp.where(upper, unit, 0.0)
    outflow = jnp.where(upper, 0.0, unit)
    blank = jnp.zeros((width, width), jnp.float32)
    for level in range(levels - 2, -1, -1):
        part = inner[level]
        upper = lax.rem(lax.div(me, 1 << level), 2) == 1
        known = jnp.concatenate([part[:count].astype(jnp.float32), blank], axis=0)
        down = known + mul(narrow(inflow), part[count:near])
        both = narrow(jnp.concatenate([inflow, outflow], axis=1))
        known = jnp.concatenate([part[near : near + count].astype(jnp.float32), blank], axis=0)
        up = known + mul(both, part[near + count :])
        inflow, outflow = jnp.where(upper, down, inflow), jnp.where(upper, outflow, up)

    inflow_map[...] = narrow(inflow)
    outflow_map[...] = narrow(outflow)
    both = narrow(jnp.concatenate([inflow, outflow], axis=1))
    for k in range(rows):
        value = mul(both, response[k, count:])
        folded[k] = base[k] + value[:count]
        folded_response[k] = narrow(value[count:])


def chain_kernel(
    axes, levels, own, theirs, base, response, solution, rounded, brought, near_rows, far_rows
):
    rows, count, width = base.shape
    side = lax.rem(lax.axis_index(axes[1]), 2)
    upper = lax.div(lax.axis_index(axes[0]), 1 << (levels - 1)) == 1
    down = theirs[:count].astype(jnp.float32)
    up = down + mul(own[...], theirs[count:])
    z = narrow(jnp.where(upper, down, up))
    brought[...] = z
    for k in range(rows):
        value = base[k] + mul(z, response[k])
        solution[k] = value
        rounded[k] = narrow(value)
    rim = near_rows.shape[0]
    for e in range(rim):
        near_rows[e] = rounded[(1 - side) * (rows - rim) + e]
        far_rows[e] = rounded[side * (rows - rim) + e]


def local_kernel(
    axes,
    levels,
    rounded,
    brought,
    inflow_map,
    outflow_map,
    prior,
    theirs,
    solved,
    diagonal,
    lower,
    upper,
    lower_at_far,
    upper_at_far,
    halo_at_far,
    partial,
    solution,
    masks,
    held,
    last_block,
    lower_at,
    upper_at,
    halo_at,
    arrived,
):
    parts = [
        (lower_at_far, lower_at),
        (upper_at_far, upper_at),
        (halo_at_far, halo_at),
        (solved, solution),
    ]
    copies = [
        pltpu.make_async_copy(source, target, arrived.at[i])
        for i, (source, target) in enumerate(parts)
    ]
    for copy in copies:
        copy.start()
    rows, slots, width, _ = lower.shape
    upper_slots = upper.shape[1]
    count = brought.shape[0]
    me = lax.axis_index(axes[0])
    last_block[...] = prior[...]

    @pl.when(me == 1 << (levels - 1))
    def _():
        last_block[...] = theirs[count:]

    z = brought[...]
    after = narrow(outflow_map[:count].astype(jnp.float32) + mul(z, outflow_map[count:]))
    before = inflow_map[:count].astype(jnp.float32) + mul(z, inflow_map[count:])
    before = narrow(before).astype(jnp.float32) + mul(rounded[0], last_block[...])
    before = narrow(jnp.where(me > 0, before, 0.0))
    held[:rows] = rounded[...]
    held[rows] = before
    held[rows + 1] = after
    for k in range(rows):
        source = jnp.concatenate([rounded[k], after], axis=1)
        total = mul(source, jnp.concatenate([diagonal[k], upper[k, 0]], axis=0))
        partial[k] = total + mul(before, lower[k, 0])
    for copy in copies[:3]:
        copy.wait()
    for k in range(rows):
        source = []
        for m in range(1, slots):
            at = lower_at[m, k]
            source.append(held[jnp.where(at == k, rows, at)])
        total = mul(
            jnp.concatenate(source, axis=1), lower[k, 1:].reshape((slots - 1) * width, width)
        )
        source = []
        for m in range(1, upper_slots):
            at = upper_at[m, k]
            source.append(held[jnp.where(at == k, rows + 1, at)])
        partial[k] += total + mul(
            jnp.concatenate(source, axis=1),
            upper[k, 1:].reshape((upper_slots - 1) * width, width),
        )
    _, picked, places, _, _ = masks.shape
    turn = places // 2 * (1 - lax.rem(lax.axis_index(axes[1]), 2))
    for k in range(rows):
        for m in range(picked):
            at = lax.rem(halo_at[m + 1, k] + turn, places)
            for j in range(places):
                mask = jnp.where(at == j, 1.0, 0.0)
                masks[k, m, j] = narrow(jnp.full((count, width), mask, jnp.float32))
    copies[3].wait()


def halo_kernel(axis, partial, outer, inner, halo, masks, product, rim_rows):
    rows, slots, width, _ = halo.shape
    rim = inner.shape[0]
    turn = rim * (1 - lax.rem(lax.axis_index(axis), 2))
    rim_rows[:rim] = inner[...]
    rim_rows[rim:] = outer[...]
    for k in range(rows):
        source = [rim_rows[lax.rem(k + turn, 2 * rim)]]
        for m in range(1, slots):
            source.append(sum(masks[k, m - 1, j] * rim_rows[j] for j in range(2 * rim)))
        product[k] = partial[k] + mul(
            jnp.concatenate(source, axis=1), halo[k].reshape(slots * width, width)
        )


def trade(block, axis, bit):
    count = lax.axis_size(axis)
    return lax.ppermute(block, axis, [(i, i ^ bit) for i in range(count)])


def swaps(block, axis, first):
    count = lax.axis_size(axis)
    pairs = []
    for low in range(first, count - 1, 2):
        pairs += [(low, low + 1), (low + 1, low)]
    return lax.ppermute(block, axis, pairs)


def on_device(
    right_sides,
    diag_inverse,
    diag_blocks,
    lower_blocks,
    upper_blocks,
    halo_blocks,
    lower_index,
    upper_index,
    halo_index,
):
    rows, count, width = right_sides.shape
    lower_at, upper_at, halo_at = lower_index.T, upper_index.T, halo_index.T
    slots = lower_blocks.shape[1]
    upper_slots = upper_blocks.shape[1]
    groups = lax.axis_size("section")
    near = count + width
    far = near + width
    wide = jax.ShapeDtypeStruct((rows, count, width), jnp.float32)

    indices = [
        pltpu.with_memory_space_constraint(a, pltpu.HBM) for a in (lower_at, upper_at, halo_at)
    ]
    base, response, payload = pl.pallas_call(
        sweep_kernel,
        out_shape=(
            wide,
            jax.ShapeDtypeStruct((rows + 1, far, width), jnp.bfloat16),
            jax.ShapeDtypeStruct((near + far + width, width), jnp.bfloat16),
        ),
        in_specs=[HBM] * 6,
        out_specs=(VMEM,) * 3,
        scratch_shapes=[
            pltpu.VMEM(right_sides.shape, right_sides.dtype),
            pltpu.VMEM(diag_inverse.shape, diag_inverse.dtype),
            pltpu.VMEM(lower_blocks.shape, lower_blocks.dtype),
            pltpu.VMEM(upper_blocks.shape, upper_blocks.dtype),
            pltpu.SMEM(lower_at.shape, jnp.int32),
            pltpu.SMEM(upper_at.shape, jnp.int32),
            pltpu.VMEM((rows // 2, (slots - 1) * width, 2 * width), jnp.bfloat16),
            pltpu.VMEM((rows // 2, (slots - 1) * width, width), jnp.bfloat16),
            pltpu.VMEM((rows // 2, (upper_slots - 1) * width, 2 * width), jnp.bfloat16),
            pltpu.VMEM((rows // 2, (upper_slots - 1) * width, width), jnp.bfloat16),
            pltpu.VMEM((rows + 1, near, width), jnp.bfloat16),
            pltpu.VMEM((rows, near, width), jnp.float32),
            pltpu.VMEM((rows, width, width), jnp.float32),
            pltpu.SemaphoreType.DMA((7,)),
        ],
        compiler_params=SMALL,
        name="sweeps",
    )(
        *(
            pltpu.with_memory_space_constraint(a, pltpu.HBM)
            for a in (right_sides, diag_inverse, lower_blocks, upper_blocks)
        ),
        *indices[:2],
    )

    levels = groups.bit_length() - 1
    segment = payload.shape[0]
    bits = jnp.bfloat16
    prior = []
    inner = []
    for level in range(levels - 1):
        theirs = trade(payload, "section", 1 << level)
        final = level == levels - 2

        def compose(*refs, bit=1 << level, final=final):
            compose_kernel("section", bit, final, *refs)

        payload, between, *prior = pl.pallas_call(
            compose,
            out_shape=(
                jax.ShapeDtypeStruct((near if final else segment, width), bits),
                jax.ShapeDtypeStruct((near + far, width), bits),
                jax.ShapeDtypeStruct((width, width), bits),
            )
            + (jax.ShapeDtypeStruct((count, width), bits),) * final,
            in_specs=[VMEM] * (2 + len(prior)),
            out_specs=(VMEM,) * (3 + final),
            scratch_shapes=[pltpu.VMEM((2, segment, width), bits)],
            compiler_params=SMALL,
            name="compose",
        )(payload, theirs, *prior)
        inner.append(between)
    prior, own = prior
    theirs = trade(payload, "section", 1 << (levels - 1))

    def fold(*refs):
        fold_kernel("section", levels, *refs)

    base, response, inflow_map, outflow_map = pl.pallas_call(
        fold,
        out_shape=(
            wide,
            jax.ShapeDtypeStruct((rows, width, width), bits),
            jax.ShapeDtypeStruct((near, width), bits),
            jax.ShapeDtypeStruct((near, width), bits),
        ),
        in_specs=[VMEM] * (1 + levels),
        out_specs=(VMEM,) * 4,
        compiler_params=SMALL,
        name="fold",
    )(base, response, *inner)

    def chain(*refs):
        chain_kernel(("section", "dom"), levels, *refs)

    solved, rounded, brought, inner, outer = pl.pallas_call(
        chain,
        out_shape=(
            wide,
            jax.ShapeDtypeStruct((rows, count, width), bits),
            jax.ShapeDtypeStruct((count, width), bits),
            jax.ShapeDtypeStruct((RIM, count, width), bits),
            jax.ShapeDtypeStruct((RIM, count, width), bits),
        ),
        in_specs=[VMEM] * 4,
        out_specs=(VMEM,) * 5,
        compiler_params=SMALL,
        name="chain",
    )(own, theirs, base, response)

    outer = swaps(outer, "dom", 1)
    inner = swaps(inner, "dom", 0)

    def local(*refs):
        local_kernel(("section", "dom"), levels, *refs)

    masks = (rows, halo_blocks.shape[1] - 1, 2 * RIM, count, width)
    partial, solution, masks = pl.pallas_call(
        local,
        out_shape=(wide, wide, jax.ShapeDtypeStruct(masks, bits)),
        in_specs=[VMEM] * 10 + [HBM] * 3,
        out_specs=(VMEM, HBM, VMEM),
        scratch_shapes=[
            pltpu.VMEM((rows + 2, count, width), bits),
            pltpu.VMEM((width, width), bits),
        ]
        + [pltpu.SMEM(a.shape, jnp.int32) for a in indices]
        + [pltpu.SemaphoreType.DMA((4,))],
        compiler_params=SMALL,
        name="local_product",
    )(
        rounded,
        brought,
        inflow_map,
        outflow_map,
        prior,
        theirs,
        solved,
        diag_blocks,
        lower_blocks,
        upper_blocks,
        *indices,
    )

    def halo(*refs):
        halo_kernel("dom", *refs)

    product = pl.pallas_call(
        halo,
        out_shape=wide,
        in_specs=[VMEM] * 5,
        out_specs=VMEM,
        scratch_shapes=[pltpu.VMEM((2 * RIM, count, width), bits)],
        compiler_params=SMALL,
        name="halo_product",
    )(partial, outer, inner, halo_blocks, masks)
    return (solution, product)


def solution(mesh):
    in_specs = (
        P(("section", "dom"), None, None),
        P(("section", "dom"), None, None),
        P(("section", "dom"), None, None),
        P(("section", "dom"), None, None, None),
        P(("section", "dom"), None, None, None),
        P(("section", "dom"), None, None, None),
        P(("section", "dom"), None),
        P(("section", "dom"), None),
        P(("section", "dom"), None),
    )
    out_specs = (P(("section", "dom"), None, None), P(("section", "dom"), None, None))
    return jax.shard_map(
        on_device, mesh=mesh, in_specs=in_specs, out_specs=out_specs, check_vma=False
    )
```

```python
import jax
import jax.numpy as jnp
from jax import lax
from jax.experimental import pallas as pl
from jax.experimental.pallas import tpu as pltpu
from jax.sharding import PartitionSpec as P

RIM = 4

VMEM = pl.BlockSpec(memory_space=pltpu.VMEM)
SMEM = pl.BlockSpec(memory_space=pltpu.SMEM)
HBM = pl.BlockSpec(memory_space=pltpu.HBM)
SMALL = pltpu.CompilerParams(vmem_limit_bytes=16 * 1024 * 1024)


def mul(a, b):
    return jnp.dot(a, b, preferred_element_type=jnp.float32)


def narrow(a):
    return a.astype(jnp.bfloat16)


def sweep_kernel(
    rhs_far,
    inverse_far,
    lower_far,
    upper_far,
    lower_at_far,
    upper_at_far,
    base,
    response,
    payload,
    rhs,
    inverse,
    lower,
    upper,
    lower_at,
    upper_at,
    low_pair,
    low_second,
    upp_pair,
    upp_second,
    down,
    exact,
    fixed,
    arrived,
):
    rows, count, width = rhs.shape
    slots = lower.shape[1]
    upper_slots = upper.shape[1]
    near = count + width
    last = rows - 1
    half = rows // 2
    parts = [
        (inverse_far, inverse),
        (rhs_far, rhs),
        (lower_far.at[:half], lower.at[:half]),
        (lower_at_far, lower_at),
        (lower_far.at[half:], lower.at[half:]),
        (upper_far, upper),
        (upper_at_far, upper_at),
    ]
    copies = [
        pltpu.make_async_copy(far, here, arrived.at[i]) for i, (far, here) in enumerate(parts)
    ]
    for copy in copies:
        copy.start()
    eye = narrow(
        lax.broadcasted_iota(jnp.int32, (width, width), 0)
        == lax.broadcasted_iota(jnp.int32, (width, width), 1)
    )
    down[:, :count] = jnp.zeros((rows + 1, count, width), jnp.bfloat16)
    response[:, :near] = jnp.zeros((rows + 1, near, width), jnp.bfloat16)
    for k in range(rows):
        down[k, count:] = eye
        response[k, near:] = eye
    down[rows, count:] = jnp.zeros_like(eye)
    response[rows, near:] = jnp.zeros_like(eye)

    def piece(blocks, m):
        return blocks[m * width : (m + 1) * width]

    def named(at, k, row, blocks, many):
        return sum(
            jnp.where(at[m, k] == row, piece(blocks, m), 0.0) for m in range(1, many)
        )

    def sources(held, at, k, skipped, many):
        picked = []
        for m in range(1, many):
            row = at[m, k]
            picked.append(held[row if skipped is None else jnp.where(row == skipped, rows, row)])
        return jnp.concatenate(picked, axis=1)

    def apart(left, right, own, other):
        zero = jnp.zeros_like(own)
        sides = [jnp.concatenate([own, zero], axis=1), jnp.concatenate([zero, other], axis=1)]
        return mul(jnp.concatenate([left, right], axis=1), jnp.concatenate(sides, axis=0))

    def ready(at, blocks, many, first, step, heads):
        of_a, of_b, links = [], [], []
        for a in (first, first + 2 * step):
            b = a + step
            lefts = [
                jnp.concatenate(heads(k) + [blocks[k].reshape(many * width, width)], axis=0)
                for k in (a, b)
            ]
            both = apart(*lefts, inverse[a], inverse[b])
            of_a.append(both[:, :width])
            of_b.append(both[:, width:])
            tail = both[both.shape[0] - many * width :, width:]
            links.append(narrow(named(at, b, a, tail, many)))
        narrow_a = [narrow(value) for value in of_a]
        both = apart(*narrow_a, *links)
        through = [both[:, :width], both[:, width:]]
        return of_a, narrow_a, of_b, through, links

    def ready_down(p):
        of_a, narrow_a, of_b, through, _ = ready(
            lower_at, lower, slots, 2 * p, 1, lambda k: [narrow(rhs[k])]
        )
        for i in range(2):
            a, b = 2 * (p + i), 2 * (p + i) + 1
            free_a = -of_a[i][count:near]
            free_b = through[i][count:near] - of_b[i][count:near]
            if p + i == 0:
                inner = sum(piece(of_a[i][count:], m) for m in range(1, slots))
                free_a = free_a - inner
                inner = sum(piece(through[i][count:], m) for m in range(1, slots))
                free_b = free_b + inner - named(lower_at, b, b, of_b[i][count:], slots)
            else:
                low_pair[p + i, :, :width] = narrow_a[i][near:]
                low_pair[p + i, :, width:] = narrow(through[i][near:])
                low_second[p + i] = narrow(of_b[i][near:])
            exact[a, :count] = of_a[i][:count]
            exact[a, count:] = free_a
            exact[b, :count] = of_b[i][:count] - through[i][:count]
            exact[b, count:] = free_b

    def ready_turn(link):
        p = rows // 2 - 1
        both = narrow(apart(low_pair[p, :, width:], low_second[p], link, link))
        return both[:, :width], both[:, width:], mul(narrow(exact[last]), link)

    def go_down(p, turn=None):
        a, b = 2 * p, 2 * p + 1
        of_a, of_b = exact[a], exact[b]
        if p > 0:
            right = [low_pair[p], low_second[p]]
            if turn is not None:
                right = [jnp.concatenate(both, axis=1) for both in zip(right, turn)]
            first = mul(sources(down, lower_at, a, None, slots), right[0])
            second = mul(sources(down, lower_at, b, a, slots), right[1])
            of_a = of_a - first[:, :width]
            of_b = of_b + first[:, width : 2 * width] - second[:, :width]
            exact[a] = of_a
            exact[b] = of_b
        down[a] = narrow(of_a)
        down[b] = narrow(of_b)
        return None if turn is None else turn[2] + first[:, 2 * width :] - second[:, width:]

    def ready_up(p):
        of_a, narrow_a, of_b, through, links = ready(
            upper_at, upper, upper_slots, last - 2 * p, -1, lambda k: []
        )
        for i in range(2):
            a = last - 2 * (p + i)
            b = a - 1
            free_a = -of_a[i][:width]
            free_b = through[i][:width] - of_b[i][:width]
            if p + i == 0:
                free_a = free_a - sum(piece(of_a[i], m) for m in range(1, upper_slots))
                inner = sum(piece(through[i], m) for m in range(1, upper_slots))
                free_b = free_b + inner - named(upper_at, b, b, of_b[i], upper_slots)
            else:
                upp_pair[p + i, :, :width] = narrow_a[i][width:]
                upp_pair[p + i, :, width:] = narrow(through[i][width:])
                upp_second[p + i] = narrow(of_b[i][width:])
            fixed[a] = free_a
            fixed[b] = free_b
        return links

    def go_up(p, passed):
        a = last - 2 * p
        b = a - 1
        of_a = exact[a]
        of_b = exact[b] - passed
        free_a = fixed[a]
        free_b = fixed[b]
        if p > 0:
            first = mul(sources(response, upper_at, a, None, upper_slots), upp_pair[p])
            second = mul(sources(response, upper_at, b, a, upper_slots), upp_second[p])
            of_a = of_a - first[:near, :width]
            of_b = of_b + first[:near, width:] - second[:near]
            free_a = free_a - first[near:, :width]
            free_b = free_b + first[near:, width:] - second[near:]
        for k, value, free in ((a, of_a, free_a), (b, of_b, free_b)):
            base[k] = value[:count]
            response[k, :near] = narrow(value)
            response[k, near:] = narrow(free)

    pairs = rows // 2
    for copy in copies[:4]:
        copy.wait()
    ready_down(0)
    go_down(0)
    for copy in copies[4:]:
        copy.wait()
    links = []
    turn = None
    for p in range(1, pairs):
        if p % 2 == 1 and p + 1 < pairs:
            ready_down(p + 1)
        if p + 1 < pairs:
            go_down(p)
        else:
            passed = [go_down(p, turn), mul(down[last - 2], links[1])]
        if p % 2 == 1:
            links += ready_up(p - 1)
        if turn is None:
            turn = ready_turn(links[0])
    far = near + width
    payload[:near] = down[last]
    for p in range(0, pairs, 2):
        if p > 0:
            a = last - 2 * p
            both = apart(down[a], down[a - 2], links[p], links[p + 1])
            passed = [both[:, :width], both[:, width:]]
        go_up(p, passed[0])
        go_up(p + 1, passed[1])

    payload[near + far :] = response[last, near:]
    payload[near : near + far] = response[0]


def compose_kernel(axis, bit, final, mine, theirs, *refs):
    prior, sent, inner, prior_out = refs[:4] if bit > 1 else (None, *refs[:3])
    pair = refs[-1]
    width = mine.shape[1]
    count = (mine.shape[0] - 4 * width) // 2
    near = count + width
    me = lax.axis_index(axis)
    place = lax.rem(lax.div(me, bit), 2)
    mid = near + count
    far = near + near + width

    pair[place] = mine[...]
    pair[1 - place] = theirs[...]
    a = pair[0]
    b = pair[1]
    across = mul(a[:near], jnp.concatenate([b[count:near], b[mid : mid + width]], axis=1))
    ahead = b[:near].astype(jnp.float32)
    joined = across[:, :width] + jnp.concatenate(
        [ahead[:count], jnp.zeros((width, width), jnp.float32)], axis=0
    )
    between = across[:, width:] + jnp.concatenate(
        [b[near:mid].astype(jnp.float32), jnp.zeros((width, width), jnp.float32)], axis=0
    )
    between = jnp.concatenate([narrow(between), b[mid + width : far]], axis=0)
    first = mul(between, a[mid + width : far])
    first = narrow(first[:near] + a[near : 2 * near].astype(jnp.float32)), narrow(first[near:])
    joined = narrow(joined)
    inner[:near] = a[:near]
    inner[near:] = between
    prior_out[...] = a[far:]
    if prior is not None:
        lowest = jnp.logical_and(place == 1, lax.rem(me, bit) == 0)

        @pl.when(jnp.logical_not(lowest))
        def _():
            prior_out[...] = prior[...]

    if final:
        refs[-2][...] = joined[:count]
        above = lax.rem(lax.div(me, 2 * bit), 2) == 1

        @pl.when(above)
        def _():
            sent[...] = first[0]

        @pl.when(jnp.logical_not(above))
        def _():
            sent[:count] = joined[:count]
            sent[count:] = b[far:]

    else:
        sent[:near] = joined
        sent[near : 2 * near] = first[0]
        sent[2 * near : far] = first[1]
        sent[far:] = b[far:]


def fold_kernel(axis, levels, *refs):
    base, response = refs[:2]
    inner = refs[2 : 1 + levels]
    folded, folded_response, inflow_map, outflow_map = refs[1 + levels :]
    rows, count, width = base.shape
    near = count + width
    me = lax.axis_index(axis)

    upper = lax.div(me, 1 << (levels - 1)) == 1
    across = lax.broadcasted_iota(jnp.int32, (near, width), 1) + count
    unit = jnp.where(lax.broadcasted_iota(jnp.int32, (near, width), 0) == across, 1.0, 0.0)
    inflow = jnp.where(upper, unit, 0.0)
    outflow = jnp.where(upper, 0.0, unit)
    blank = jnp.zeros((width, width), jnp.float32)
    for level in range(levels - 2, -1, -1):
        part = inner[level]
        upper = lax.rem(lax.div(me, 1 << level), 2) == 1
        known = jnp.concatenate([part[:count].astype(jnp.float32), blank], axis=0)
        down = known + mul(narrow(inflow), part[count:near])
        both = narrow(jnp.concatenate([inflow, outflow], axis=1))
        known = jnp.concatenate([part[near : near + count].astype(jnp.float32), blank], axis=0)
        up = known + mul(both, part[near + count :])
        inflow, outflow = jnp.where(upper, down, inflow), jnp.where(upper, outflow, up)

    inflow_map[...] = narrow(inflow)
    outflow_map[...] = narrow(outflow)
    both = narrow(jnp.concatenate([inflow, outflow], axis=1))
    for k in range(rows):
        value = mul(both, response[k, count:])
        folded[k] = base[k] + value[:count]
        folded_response[k] = narrow(value[count:])


def chain_kernel(
    axes, levels, own, theirs, base, response, solution, rounded, brought, near_rows, far_rows
):
    rows, count, width = base.shape
    side = lax.rem(lax.axis_index(axes[1]), 2)
    upper = lax.div(lax.axis_index(axes[0]), 1 << (levels - 1)) == 1
    down = theirs[:count].astype(jnp.float32)
    up = down + mul(own[...], theirs[count:])
    z = narrow(jnp.where(upper, down, up))
    brought[...] = z
    for k in range(rows):
        value = base[k] + mul(z, response[k])
        solution[k] = value
        rounded[k] = narrow(value)
    rim = near_rows.shape[0]
    for e in range(rim):
        near_rows[e] = rounded[(1 - side) * (rows - rim) + e]
        far_rows[e] = rounded[side * (rows - rim) + e]


def local_kernel(
    axes,
    levels,
    rounded,
    brought,
    inflow_map,
    outflow_map,
    prior,
    theirs,
    solved,
    diagonal,
    lower,
    upper,
    lower_at_far,
    upper_at_far,
    halo_at_far,
    partial,
    solution,
    masks,
    held,
    last_block,
    lower_at,
    upper_at,
    halo_at,
    arrived,
):
    parts = [
        (lower_at_far, lower_at),
        (upper_at_far, upper_at),
        (halo_at_far, halo_at),
        (solved, solution),
    ]
    copies = [
        pltpu.make_async_copy(source, target, arrived.at[i])
        for i, (source, target) in enumerate(parts)
    ]
    for copy in copies:
        copy.start()
    rows, slots, width, _ = lower.shape
    upper_slots = upper.shape[1]
    count = brought.shape[0]
    me = lax.axis_index(axes[0])
    last_block[...] = prior[...]

    @pl.when(me == 1 << (levels - 1))
    def _():
        last_block[...] = theirs[count:]

    z = brought[...]
    after = narrow(outflow_map[:count].astype(jnp.float32) + mul(z, outflow_map[count:]))
    before = inflow_map[:count].astype(jnp.float32) + mul(z, inflow_map[count:])
    before = narrow(before).astype(jnp.float32) + mul(rounded[0], last_block[...])
    before = narrow(jnp.where(me > 0, before, 0.0))
    held[:rows] = rounded[...]
    held[rows] = before
    held[rows + 1] = after
    for k in range(rows):
        source = jnp.concatenate([rounded[k], after], axis=1)
        total = mul(source, jnp.concatenate([diagonal[k], upper[k, 0]], axis=0))
        partial[k] = total + mul(before, lower[k, 0])
    for copy in copies[:3]:
        copy.wait()
    for k in range(rows):
        source = []
        for m in range(1, slots):
            at = lower_at[m, k]
            source.append(held[jnp.where(at == k, rows, at)])
        total = mul(
            jnp.concatenate(source, axis=1), lower[k, 1:].reshape((slots - 1) * width, width)
        )
        source = []
        for m in range(1, upper_slots):
            at = upper_at[m, k]
            source.append(held[jnp.where(at == k, rows + 1, at)])
        partial[k] += total + mul(
            jnp.concatenate(source, axis=1),
            upper[k, 1:].reshape((upper_slots - 1) * width, width),
        )
    _, picked, places, _, _ = masks.shape
    turn = places // 2 * (1 - lax.rem(lax.axis_index(axes[1]), 2))
    for k in range(rows):
        for m in range(picked):
            at = lax.rem(halo_at[m + 1, k] + turn, places)
            for j in range(places):
                mask = jnp.where(at == j, 1.0, 0.0)
                masks[k, m, j] = narrow(jnp.full((count, width), mask, jnp.float32))
    copies[3].wait()


def halo_kernel(axis, partial, outer, inner, halo, masks, product, rim_rows):
    rows, slots, width, _ = halo.shape
    rim = inner.shape[0]
    turn = rim * (1 - lax.rem(lax.axis_index(axis), 2))
    rim_rows[:rim] = inner[...]
    rim_rows[rim:] = outer[...]
    for k in range(rows):
        source = [rim_rows[lax.rem(k + turn, 2 * rim)]]
        for m in range(1, slots):
            source.append(sum(masks[k, m - 1, j] * rim_rows[j] for j in range(2 * rim)))
        product[k] = partial[k] + mul(
            jnp.concatenate(source, axis=1), halo[k].reshape(slots * width, width)
        )


def trade(block, axis, bit):
    count = lax.axis_size(axis)
    return lax.ppermute(block, axis, [(i, i ^ bit) for i in range(count)])


def swaps(block, axis, first):
    count = lax.axis_size(axis)
    pairs = []
    for low in range(first, count - 1, 2):
        pairs += [(low, low + 1), (low + 1, low)]
    return lax.ppermute(block, axis, pairs)


def on_device(
    right_sides,
    diag_inverse,
    diag_blocks,
    lower_blocks,
    upper_blocks,
    halo_blocks,
    lower_index,
    upper_index,
    halo_index,
):
    rows, count, width = right_sides.shape
    lower_at, upper_at, halo_at = lower_index.T, upper_index.T, halo_index.T
    slots = lower_blocks.shape[1]
    upper_slots = upper_blocks.shape[1]
    groups = lax.axis_size("section")
    near = count + width
    far = near + width
    wide = jax.ShapeDtypeStruct((rows, count, width), jnp.float32)

    indices = [
        pltpu.with_memory_space_constraint(a, pltpu.HBM) for a in (lower_at, upper_at, halo_at)
    ]
    base, response, payload = pl.pallas_call(
        sweep_kernel,
        out_shape=(
            wide,
            jax.ShapeDtypeStruct((rows + 1, far, width), jnp.bfloat16),
            jax.ShapeDtypeStruct((near + far + width, width), jnp.bfloat16),
        ),
        in_specs=[HBM] * 6,
        out_specs=(VMEM,) * 3,
        scratch_shapes=[
            pltpu.VMEM(right_sides.shape, right_sides.dtype),
            pltpu.VMEM(diag_inverse.shape, diag_inverse.dtype),
            pltpu.VMEM(lower_blocks.shape, lower_blocks.dtype),
            pltpu.VMEM(upper_blocks.shape, upper_blocks.dtype),
            pltpu.SMEM(lower_at.shape, jnp.int32),
            pltpu.SMEM(upper_at.shape, jnp.int32),
            pltpu.VMEM((rows // 2, (slots - 1) * width, 2 * width), jnp.bfloat16),
            pltpu.VMEM((rows // 2, (slots - 1) * width, width), jnp.bfloat16),
            pltpu.VMEM((rows // 2, (upper_slots - 1) * width, 2 * width), jnp.bfloat16),
            pltpu.VMEM((rows // 2, (upper_slots - 1) * width, width), jnp.bfloat16),
            pltpu.VMEM((rows + 1, near, width), jnp.bfloat16),
            pltpu.VMEM((rows, near, width), jnp.float32),
            pltpu.VMEM((rows, width, width), jnp.float32),
            pltpu.SemaphoreType.DMA((7,)),
        ],
        compiler_params=SMALL,
        name="sweeps",
    )(
        *(
            pltpu.with_memory_space_constraint(a, pltpu.HBM)
            for a in (right_sides, diag_inverse, lower_blocks, upper_blocks)
        ),
        *indices[:2],
    )

    levels = groups.bit_length() - 1
    segment = payload.shape[0]
    bits = jnp.bfloat16
    prior = []
    inner = []
    for level in range(levels - 1):
        theirs = trade(payload, "section", 1 << level)
        final = level == levels - 2

        def compose(*refs, bit=1 << level, final=final):
            compose_kernel("section", bit, final, *refs)

        payload, between, *prior = pl.pallas_call(
            compose,
            out_shape=(
                jax.ShapeDtypeStruct((near if final else segment, width), bits),
                jax.ShapeDtypeStruct((near + far, width), bits),
                jax.ShapeDtypeStruct((width, width), bits),
            )
            + (jax.ShapeDtypeStruct((count, width), bits),) * final,
            in_specs=[VMEM] * (2 + len(prior)),
            out_specs=(VMEM,) * (3 + final),
            scratch_shapes=[pltpu.VMEM((2, segment, width), bits)],
            compiler_params=SMALL,
            name="compose",
        )(payload, theirs, *prior)
        inner.append(between)
    prior, own = prior
    theirs = trade(payload, "section", 1 << (levels - 1))

    def fold(*refs):
        fold_kernel("section", levels, *refs)

    base, response, inflow_map, outflow_map = pl.pallas_call(
        fold,
        out_shape=(
            wide,
            jax.ShapeDtypeStruct((rows, width, width), bits),
            jax.ShapeDtypeStruct((near, width), bits),
            jax.ShapeDtypeStruct((near, width), bits),
        ),
        in_specs=[VMEM] * (1 + levels),
        out_specs=(VMEM,) * 4,
        compiler_params=SMALL,
        name="fold",
    )(base, response, *inner)

    def chain(*refs):
        chain_kernel(("section", "dom"), levels, *refs)

    solved, rounded, brought, inner, outer = pl.pallas_call(
        chain,
        out_shape=(
            wide,
            jax.ShapeDtypeStruct((rows, count, width), bits),
            jax.ShapeDtypeStruct((count, width), bits),
            jax.ShapeDtypeStruct((RIM, count, width), bits),
            jax.ShapeDtypeStruct((RIM, count, width), bits),
        ),
        in_specs=[VMEM] * 4,
        out_specs=(VMEM,) * 5,
        compiler_params=SMALL,
        name="chain",
    )(own, theirs, base, response)

    outer = swaps(outer, "dom", 1)
    inner = swaps(inner, "dom", 0)

    def local(*refs):
        local_kernel(("section", "dom"), levels, *refs)

    masks = (rows, halo_blocks.shape[1] - 1, 2 * RIM, count, width)
    partial, solution, masks = pl.pallas_call(
        local,
        out_shape=(wide, wide, jax.ShapeDtypeStruct(masks, bits)),
        in_specs=[VMEM] * 10 + [HBM] * 3,
        out_specs=(VMEM, HBM, VMEM),
        scratch_shapes=[
            pltpu.VMEM((rows + 2, count, width), bits),
            pltpu.VMEM((width, width), bits),
        ]
        + [pltpu.SMEM(a.shape, jnp.int32) for a in indices]
        + [pltpu.SemaphoreType.DMA((4,))],
        compiler_params=SMALL,
        name="local_product",
    )(
        rounded,
        brought,
        inflow_map,
        outflow_map,
        prior,
        theirs,
        solved,
        diag_blocks,
        lower_blocks,
        upper_blocks,
        *indices,
    )

    def halo(*refs):
        halo_kernel("dom", *refs)

    product = pl.pallas_call(
        halo,
        out_shape=wide,
        in_specs=[VMEM] * 5,
        out_specs=VMEM,
        scratch_shapes=[pltpu.VMEM((2 * RIM, count, width), bits)],
        compiler_params=SMALL,
        name="halo_product",
    )(partial, outer, inner, halo_blocks, masks)
    return (solution, product)


def solution(mesh):
    in_specs = (
        P(("section", "dom"), None, None),
        P(("section", "dom"), None, None),
        P(("section", "dom"), None, None),
        P(("section", "dom"), None, None, None),
        P(("section", "dom"), None, None, None),
        P(("section", "dom"), None, None, None),
        P(("section", "dom"), None),
        P(("section", "dom"), None),
        P(("section", "dom"), None),
    )
    out_specs = (P(("section", "dom"), None, None), P(("section", "dom"), None, None))
    return jax.shard_map(
        on_device, mesh=mesh, in_specs=in_specs, out_specs=out_specs, check_vma=False
    )
```

```python
import jax
import jax.numpy as jnp
from jax import lax
from jax.experimental import pallas as pl
from jax.experimental.pallas import tpu as pltpu
from jax.sharding import PartitionSpec as P

RIM = 4

VMEM = pl.BlockSpec(memory_space=pltpu.VMEM)
SMEM = pl.BlockSpec(memory_space=pltpu.SMEM)
HBM = pl.BlockSpec(memory_space=pltpu.HBM)
SMALL = pltpu.CompilerParams(vmem_limit_bytes=16 * 1024 * 1024)


def mul(a, b):
    return jnp.dot(a, b, preferred_element_type=jnp.float32)


def narrow(a):
    return a.astype(jnp.bfloat16)


def sweep_kernel(
    rhs_far,
    inverse_far,
    lower_far,
    upper_far,
    lower_at_far,
    upper_at_far,
    base,
    response,
    payload,
    rhs,
    inverse,
    lower,
    upper,
    lower_at,
    upper_at,
    low_pair,
    low_second,
    upp_pair,
    upp_second,
    down,
    exact,
    fixed,
    arrived,
):
    rows, count, width = rhs.shape
    slots = lower.shape[1]
    upper_slots = upper.shape[1]
    near = count + width
    last = rows - 1
    half = rows // 2
    parts = [
        (inverse_far, inverse),
        (rhs_far, rhs),
        (lower_far.at[:half], lower.at[:half]),
        (lower_at_far, lower_at),
        (lower_far.at[half:], lower.at[half:]),
        (upper_far, upper),
        (upper_at_far, upper_at),
    ]
    copies = [
        pltpu.make_async_copy(far, here, arrived.at[i]) for i, (far, here) in enumerate(parts)
    ]
    for copy in copies:
        copy.start()
    eye = narrow(
        lax.broadcasted_iota(jnp.int32, (width, width), 0)
        == lax.broadcasted_iota(jnp.int32, (width, width), 1)
    )
    down[:, :count] = jnp.zeros((rows + 1, count, width), jnp.bfloat16)
    response[:, :near] = jnp.zeros((rows + 1, near, width), jnp.bfloat16)
    for k in range(rows):
        down[k, count:] = eye
        response[k, near:] = eye
    down[rows, count:] = jnp.zeros_like(eye)
    response[rows, near:] = jnp.zeros_like(eye)

    def piece(blocks, m):
        return blocks[m * width : (m + 1) * width]

    def named(at, k, row, blocks, many):
        return sum(
            jnp.where(at[m, k] == row, piece(blocks, m), 0.0) for m in range(1, many)
        )

    def sources(held, at, k, skipped, many):
        picked = []
        for m in range(1, many):
            row = at[m, k]
            picked.append(held[row if skipped is None else jnp.where(row == skipped, rows, row)])
        return jnp.concatenate(picked, axis=1)

    def apart(left, right, own, other):
        zero = jnp.zeros_like(own)
        sides = [jnp.concatenate([own, zero], axis=1), jnp.concatenate([zero, other], axis=1)]
        return mul(jnp.concatenate([left, right], axis=1), jnp.concatenate(sides, axis=0))

    def ready(at, blocks, many, first, step, heads):
        of_a, of_b, links = [], [], []
        for a in (first, first + 2 * step):
            b = a + step
            lefts = [
                jnp.concatenate(heads(k) + [blocks[k].reshape(many * width, width)], axis=0)
                for k in (a, b)
            ]
            both = apart(*lefts, inverse[a], inverse[b])
            of_a.append(both[:, :width])
            of_b.append(both[:, width:])
            tail = both[both.shape[0] - many * width :, width:]
            links.append(narrow(named(at, b, a, tail, many)))
        narrow_a = [narrow(value) for value in of_a]
        both = apart(*narrow_a, *links)
        through = [both[:, :width], both[:, width:]]
        return of_a, narrow_a, of_b, through, links

    def ready_down(p):
        of_a, narrow_a, of_b, through, _ = ready(
            lower_at, lower, slots, 2 * p, 1, lambda k: [narrow(rhs[k])]
        )
        for i in range(2):
            a, b = 2 * (p + i), 2 * (p + i) + 1
            free_a = -of_a[i][count:near]
            free_b = through[i][count:near] - of_b[i][count:near]
            if p + i == 0:
                inner = sum(piece(of_a[i][count:], m) for m in range(1, slots))
                free_a = free_a - inner
                inner = sum(piece(through[i][count:], m) for m in range(1, slots))
                free_b = free_b + inner - named(lower_at, b, b, of_b[i][count:], slots)
            else:
                low_pair[p + i, :, :width] = narrow_a[i][near:]
                low_pair[p + i, :, width:] = narrow(through[i][near:])
                low_second[p + i] = narrow(of_b[i][near:])
            exact[a, :count] = of_a[i][:count]
            exact[a, count:] = free_a
            exact[b, :count] = of_b[i][:count] - through[i][:count]
            exact[b, count:] = free_b

    def go_down(p):
        a, b = 2 * p, 2 * p + 1
        of_a, of_b = exact[a], exact[b]
        if p > 0:
            first = mul(sources(down, lower_at, a, None, slots), low_pair[p])
            second = mul(sources(down, lower_at, b, a, slots), low_second[p])
            of_a = of_a - first[:, :width]
            of_b = of_b + first[:, width:] - second
            exact[a] = of_a
            exact[b] = of_b
        down[a] = narrow(of_a)
        down[b] = narrow(of_b)

    def ready_up(p):
        of_a, narrow_a, of_b, through, links = ready(
            upper_at, upper, upper_slots, last - 2 * p, -1, lambda k: []
        )
        for i in range(2):
            a = last - 2 * (p + i)
            b = a - 1
            free_a = -of_a[i][:width]
            free_b = through[i][:width] - of_b[i][:width]
            if p + i == 0:
                free_a = free_a - sum(piece(of_a[i], m) for m in range(1, upper_slots))
                inner = sum(piece(through[i], m) for m in range(1, upper_slots))
                free_b = free_b + inner - named(upper_at, b, b, of_b[i], upper_slots)
            else:
                upp_pair[p + i, :, :width] = narrow_a[i][width:]
                upp_pair[p + i, :, width:] = narrow(through[i][width:])
                upp_second[p + i] = narrow(of_b[i][width:])
            fixed[a] = free_a
            fixed[b] = free_b
        return links

    def go_up(p, passed):
        a = last - 2 * p
        b = a - 1
        of_a = exact[a]
        of_b = exact[b] - passed
        free_a = fixed[a]
        free_b = fixed[b]
        if p > 0:
            first = mul(sources(response, upper_at, a, None, upper_slots), upp_pair[p])
            second = mul(sources(response, upper_at, b, a, upper_slots), upp_second[p])
            of_a = of_a - first[:near, :width]
            of_b = of_b + first[:near, width:] - second[:near]
            free_a = free_a - first[near:, :width]
            free_b = free_b + first[near:, width:] - second[near:]
        for k, value, free in ((a, of_a, free_a), (b, of_b, free_b)):
            base[k] = value[:count]
            response[k, :near] = narrow(value)
            response[k, near:] = narrow(free)

    pairs = rows // 2
    for copy in copies[:4]:
        copy.wait()
    ready_down(0)
    go_down(0)
    for copy in copies[4:]:
        copy.wait()
    links = []
    for p in range(1, pairs):
        if p % 2 == 1 and p + 1 < pairs:
            ready_down(p + 1)
        go_down(p)
        if p % 2 == 1:
            links += ready_up(p - 1)
    far = near + width
    payload[:near] = down[last]
    for p in range(0, pairs, 2):
        a = last - 2 * p
        passed = apart(down[a], down[a - 2], links[p], links[p + 1])
        go_up(p, passed[:, :width])
        go_up(p + 1, passed[:, width:])

    payload[near + far :] = response[last, near:]
    payload[near : near + far] = response[0]


def compose_kernel(axis, bit, final, mine, theirs, *refs):
    prior, sent, inner, prior_out = refs[:4] if bit > 1 else (None, *refs[:3])
    width = mine.shape[1]
    count = (mine.shape[0] - 4 * width) // 2
    near = count + width
    me = lax.axis_index(axis)
    place = lax.rem(lax.div(me, bit), 2)
    mid = near + count
    far = near + near + width
    blank = jnp.zeros((width, width), jnp.float32)

    def join(a, b):
        sides = [b[count:near], b[mid : mid + width]]
        across = mul(a[:near], jnp.concatenate(sides, axis=1))
        ahead = jnp.concatenate([b[:count].astype(jnp.float32), blank], axis=0)
        joined = narrow(across[:, :width] + ahead)
        ahead = jnp.concatenate([b[near:mid].astype(jnp.float32), blank], axis=0)
        between = narrow(across[:, width:] + ahead)
        first = mul(between, a[mid + width : far]) + a[near : 2 * near].astype(jnp.float32)
        inner[:near] = a[:near]
        inner[near : 2 * near] = between
        inner[2 * near :] = b[mid + width : far]
        prior_out[...] = a[far:]
        if final:
            refs[-1][...] = joined[:count]
            above = lax.rem(lax.div(me, 2 * bit), 2) == 1

            @pl.when(above)
            def _():
                sent[...] = narrow(first)

            @pl.when(jnp.logical_not(above))
            def _():
                sent[:count] = joined[:count]
                sent[count:] = b[far:]

        else:
            sent[:near] = joined
            sent[near : 2 * near] = narrow(first)
            sent[2 * near : far] = narrow(mul(b[mid + width : far], a[mid + width : far]))
            sent[far:] = b[far:]

    @pl.when(place == 0)
    def _():
        join(mine, theirs)

    @pl.when(place == 1)
    def _():
        join(theirs, mine)

    if prior is not None:
        lowest = jnp.logical_and(place == 1, lax.rem(me, bit) == 0)

        @pl.when(jnp.logical_not(lowest))
        def _():
            prior_out[...] = prior[...]


def fold_kernel(axis, levels, *refs):
    base, response = refs[:2]
    inner = refs[2 : 1 + levels]
    folded, folded_response, inflow_map, outflow_map = refs[1 + levels :]
    rows, count, width = base.shape
    near = count + width
    me = lax.axis_index(axis)

    upper = lax.div(me, 1 << (levels - 1)) == 1
    across = lax.broadcasted_iota(jnp.int32, (near, width), 1) + count
    unit = jnp.where(lax.broadcasted_iota(jnp.int32, (near, width), 0) == across, 1.0, 0.0)
    inflow = jnp.where(upper, unit, 0.0)
    outflow = jnp.where(upper, 0.0, unit)
    blank = jnp.zeros((width, width), jnp.float32)
    for level in range(levels - 2, -1, -1):
        part = inner[level]
        upper = lax.rem(lax.div(me, 1 << level), 2) == 1
        known = jnp.concatenate([part[:count].astype(jnp.float32), blank], axis=0)
        down = known + mul(narrow(inflow), part[count:near])
        both = narrow(jnp.concatenate([inflow, outflow], axis=1))
        known = jnp.concatenate([part[near : near + count].astype(jnp.float32), blank], axis=0)
        up = known + mul(both, part[near + count :])
        inflow, outflow = jnp.where(upper, down, inflow), jnp.where(upper, outflow, up)

    inflow_map[...] = narrow(inflow)
    outflow_map[...] = narrow(outflow)
    both = narrow(jnp.concatenate([inflow, outflow], axis=1))
    for k in range(rows):
        value = mul(both, response[k, count:])
        folded[k] = base[k] + value[:count]
        folded_response[k] = narrow(value[count:])


def chain_kernel(
    axes, levels, own, theirs, base, response, solution, rounded, brought, near_rows, far_rows
):
    rows, count, width = base.shape
    side = lax.rem(lax.axis_index(axes[1]), 2)
    upper = lax.div(lax.axis_index(axes[0]), 1 << (levels - 1)) == 1
    down = theirs[:count].astype(jnp.float32)
    up = down + mul(own[...], theirs[count:])
    z = narrow(jnp.where(upper, down, up))
    brought[...] = z
    values = []
    for k in range(rows):
        value = base[k] + mul(z, response[k])
        solution[k] = value
        values.append(narrow(value))
        rounded[k] = values[k]
    rim = near_rows.shape[0]
    for odd, to_low, to_high in ((0, far_rows, near_rows), (1, near_rows, far_rows)):

        @pl.when(side == odd)
        def _(to_low=to_low, to_high=to_high):
            for e in range(rim):
                to_low[e] = values[e]
                to_high[e] = values[rows - rim + e]


def local_kernel(
    axes,
    levels,
    rounded,
    brought,
    inflow_map,
    outflow_map,
    prior,
    theirs,
    solved,
    diagonal,
    lower,
    upper,
    lower_at_far,
    upper_at_far,
    halo_at_far,
    partial,
    solution,
    masks,
    held,
    last_block,
    lower_at,
    upper_at,
    halo_at,
    arrived,
):
    parts = [
        (lower_at_far, lower_at),
        (upper_at_far, upper_at),
        (halo_at_far, halo_at),
        (solved, solution),
    ]
    copies = [
        pltpu.make_async_copy(source, target, arrived.at[i])
        for i, (source, target) in enumerate(parts)
    ]
    for copy in copies:
        copy.start()
    rows, slots, width, _ = lower.shape
    upper_slots = upper.shape[1]
    count = brought.shape[0]
    me = lax.axis_index(axes[0])
    last_block[...] = prior[...]

    @pl.when(me == 1 << (levels - 1))
    def _():
        last_block[...] = theirs[count:]

    z = brought[...]
    after = narrow(outflow_map[:count].astype(jnp.float32) + mul(z, outflow_map[count:]))
    before = inflow_map[:count].astype(jnp.float32) + mul(z, inflow_map[count:])
    before = narrow(before).astype(jnp.float32) + mul(rounded[0], last_block[...])
    before = narrow(jnp.where(me > 0, before, 0.0))
    held[:rows] = rounded[...]
    held[rows] = before
    held[rows + 1] = after
    for k in range(rows):
        source = jnp.concatenate([rounded[k], after], axis=1)
        total = mul(source, jnp.concatenate([diagonal[k], upper[k, 0]], axis=0))
        partial[k] = total + mul(before, lower[k, 0])
    for copy in copies[:3]:
        copy.wait()
    for k in range(rows):
        source = []
        for m in range(1, slots):
            at = lower_at[m, k]
            source.append(held[jnp.where(at == k, rows, at)])
        total = mul(
            jnp.concatenate(source, axis=1), lower[k, 1:].reshape((slots - 1) * width, width)
        )
        source = []
        for m in range(1, upper_slots):
            at = upper_at[m, k]
            source.append(held[jnp.where(at == k, rows + 1, at)])
        partial[k] += total + mul(
            jnp.concatenate(source, axis=1),
            upper[k, 1:].reshape((upper_slots - 1) * width, width),
        )
    _, picked, places, _, _ = masks.shape
    for k in range(rows):
        for m in range(picked):
            at = halo_at[m + 1, k]
            for j in range(places):
                mask = jnp.where(at == j, 1.0, 0.0)
                masks[k, m, j] = narrow(jnp.full((count, width), mask, jnp.float32))
    copies[3].wait()


def halo_kernel(axis, partial, outer, inner, halo, masks, product):
    rows, slots, width, _ = halo.shape
    rim = inner.shape[0]
    side = lax.rem(lax.axis_index(axis), 2)

    def add(left, right):
        rim_rows = [left[e] for e in range(rim)] + [right[e] for e in range(rim)]
        for k in range(rows):
            source = [rim_rows[k % (2 * rim)]]
            for m in range(1, slots):
                source.append(sum(masks[k, m - 1, j] * rim_rows[j] for j in range(2 * rim)))
            product[k] = partial[k] + mul(
                jnp.concatenate(source, axis=1), halo[k].reshape(slots * width, width)
            )

    @pl.when(side == 0)
    def _():
        add(outer, inner)

    @pl.when(side == 1)
    def _():
        add(inner, outer)


def trade(block, axis, bit):
    count = lax.axis_size(axis)
    return lax.ppermute(block, axis, [(i, i ^ bit) for i in range(count)])


def swaps(block, axis, first):
    count = lax.axis_size(axis)
    pairs = []
    for low in range(first, count - 1, 2):
        pairs += [(low, low + 1), (low + 1, low)]
    return lax.ppermute(block, axis, pairs)


def on_device(
    right_sides,
    diag_inverse,
    diag_blocks,
    lower_blocks,
    upper_blocks,
    halo_blocks,
    lower_index,
    upper_index,
    halo_index,
):
    rows, count, width = right_sides.shape
    lower_at, upper_at, halo_at = lower_index.T, upper_index.T, halo_index.T
    slots = lower_blocks.shape[1]
    upper_slots = upper_blocks.shape[1]
    groups = lax.axis_size("section")
    near = count + width
    far = near + width
    wide = jax.ShapeDtypeStruct((rows, count, width), jnp.float32)

    indices = [
        pltpu.with_memory_space_constraint(a, pltpu.HBM) for a in (lower_at, upper_at, halo_at)
    ]
    base, response, payload = pl.pallas_call(
        sweep_kernel,
        out_shape=(
            wide,
            jax.ShapeDtypeStruct((rows + 1, far, width), jnp.bfloat16),
            jax.ShapeDtypeStruct((near + far + width, width), jnp.bfloat16),
        ),
        in_specs=[HBM] * 6,
        out_specs=(VMEM,) * 3,
        scratch_shapes=[
            pltpu.VMEM(right_sides.shape, right_sides.dtype),
            pltpu.VMEM(diag_inverse.shape, diag_inverse.dtype),
            pltpu.VMEM(lower_blocks.shape, lower_blocks.dtype),
            pltpu.VMEM(upper_blocks.shape, upper_blocks.dtype),
            pltpu.SMEM(lower_at.shape, jnp.int32),
            pltpu.SMEM(upper_at.shape, jnp.int32),
            pltpu.VMEM((rows // 2, (slots - 1) * width, 2 * width), jnp.bfloat16),
            pltpu.VMEM((rows // 2, (slots - 1) * width, width), jnp.bfloat16),
            pltpu.VMEM((rows // 2, (upper_slots - 1) * width, 2 * width), jnp.bfloat16),
            pltpu.VMEM((rows // 2, (upper_slots - 1) * width, width), jnp.bfloat16),
            pltpu.VMEM((rows + 1, near, width), jnp.bfloat16),
            pltpu.VMEM((rows, near, width), jnp.float32),
            pltpu.VMEM((rows, width, width), jnp.float32),
            pltpu.SemaphoreType.DMA((7,)),
        ],
        compiler_params=SMALL,
        name="sweeps",
    )(
        *(
            pltpu.with_memory_space_constraint(a, pltpu.HBM)
            for a in (right_sides, diag_inverse, lower_blocks, upper_blocks)
        ),
        *indices[:2],
    )

    levels = groups.bit_length() - 1
    segment = payload.shape[0]
    bits = jnp.bfloat16
    prior = []
    inner = []
    for level in range(levels - 1):
        theirs = trade(payload, "section", 1 << level)
        final = level == levels - 2

        def compose(*refs, bit=1 << level, final=final):
            compose_kernel("section", bit, final, *refs)

        payload, between, *prior = pl.pallas_call(
            compose,
            out_shape=(
                jax.ShapeDtypeStruct((near if final else segment, width), bits),
                jax.ShapeDtypeStruct((near + far, width), bits),
                jax.ShapeDtypeStruct((width, width), bits),
            )
            + (jax.ShapeDtypeStruct((count, width), bits),) * final,
            in_specs=[VMEM] * (2 + len(prior)),
            out_specs=(VMEM,) * (3 + final),
            compiler_params=SMALL,
            name="compose",
        )(payload, theirs, *prior)
        inner.append(between)
    prior, own = prior
    theirs = trade(payload, "section", 1 << (levels - 1))

    def fold(*refs):
        fold_kernel("section", levels, *refs)

    base, response, inflow_map, outflow_map = pl.pallas_call(
        fold,
        out_shape=(
            wide,
            jax.ShapeDtypeStruct((rows, width, width), bits),
            jax.ShapeDtypeStruct((near, width), bits),
            jax.ShapeDtypeStruct((near, width), bits),
        ),
        in_specs=[VMEM] * (1 + levels),
        out_specs=(VMEM,) * 4,
        compiler_params=SMALL,
        name="fold",
    )(base, response, *inner)

    def chain(*refs):
        chain_kernel(("section", "dom"), levels, *refs)

    solved, rounded, brought, inner, outer = pl.pallas_call(
        chain,
        out_shape=(
            wide,
            jax.ShapeDtypeStruct((rows, count, width), bits),
            jax.ShapeDtypeStruct((count, width), bits),
            jax.ShapeDtypeStruct((RIM, count, width), bits),
            jax.ShapeDtypeStruct((RIM, count, width), bits),
        ),
        in_specs=[VMEM] * 4,
        out_specs=(VMEM,) * 5,
        compiler_params=SMALL,
        name="chain",
    )(own, theirs, base, response)

    outer = swaps(outer, "dom", 1)
    inner = swaps(inner, "dom", 0)

    def local(*refs):
        local_kernel(("section", "dom"), levels, *refs)

    masks = (rows, halo_blocks.shape[1] - 1, 2 * RIM, count, width)
    partial, solution, masks = pl.pallas_call(
        local,
        out_shape=(wide, wide, jax.ShapeDtypeStruct(masks, bits)),
        in_specs=[VMEM] * 10 + [HBM] * 3,
        out_specs=(VMEM, HBM, VMEM),
        scratch_shapes=[
            pltpu.VMEM((rows + 2, count, width), bits),
            pltpu.VMEM((width, width), bits),
        ]
        + [pltpu.SMEM(a.shape, jnp.int32) for a in indices]
        + [pltpu.SemaphoreType.DMA((4,))],
        compiler_params=SMALL,
        name="local_product",
    )(
        rounded,
        brought,
        inflow_map,
        outflow_map,
        prior,
        theirs,
        solved,
        diag_blocks,
        lower_blocks,
        upper_blocks,
        *indices,
    )

    def halo(*refs):
        halo_kernel("dom", *refs)

    product = pl.pallas_call(
        halo,
        out_shape=wide,
        in_specs=[VMEM] * 5,
        out_specs=VMEM,
        compiler_params=SMALL,
        name="halo_product",
    )(partial, outer, inner, halo_blocks, masks)
    return (solution, product)


def solution(mesh):
    in_specs = (
        P(("section", "dom"), None, None),
        P(("section", "dom"), None, None),
        P(("section", "dom"), None, None),
        P(("section", "dom"), None, None, None),
        P(("section", "dom"), None, None, None),
        P(("section", "dom"), None, None, None),
        P(("section", "dom"), None),
        P(("section", "dom"), None),
        P(("section", "dom"), None),
    )
    out_specs = (P(("section", "dom"), None, None), P(("section", "dom"), None, None))
    return jax.shard_map(
        on_device, mesh=mesh, in_specs=in_specs, out_specs=out_specs, check_vma=False
    )
```

```python
import jax
import jax.numpy as jnp
from jax import lax
from jax.experimental import pallas as pl
from jax.experimental.pallas import tpu as pltpu
from jax.sharding import PartitionSpec as P

RIM = 4

VMEM = pl.BlockSpec(memory_space=pltpu.VMEM)
SMEM = pl.BlockSpec(memory_space=pltpu.SMEM)
HBM = pl.BlockSpec(memory_space=pltpu.HBM)
SMALL = pltpu.CompilerParams(vmem_limit_bytes=16 * 1024 * 1024)


def mul(a, b):
    return jnp.dot(a, b, preferred_element_type=jnp.float32)


def narrow(a):
    return a.astype(jnp.bfloat16)


def sweep_kernel(
    rhs_far,
    inverse_far,
    lower_far,
    upper_far,
    lower_at_far,
    upper_at_far,
    base,
    response,
    payload,
    rhs,
    inverse,
    lower,
    upper,
    lower_at,
    upper_at,
    low_pair,
    low_second,
    upp_pair,
    upp_second,
    down,
    exact,
    fixed,
    arrived,
):
    rows, count, width = rhs.shape
    slots = lower.shape[1]
    upper_slots = upper.shape[1]
    near = count + width
    last = rows - 1
    half = rows // 2
    parts = [
        (inverse_far, inverse),
        (rhs_far, rhs),
        (lower_far.at[:half], lower.at[:half]),
        (lower_at_far, lower_at),
        (lower_far.at[half:], lower.at[half:]),
        (upper_far, upper),
        (upper_at_far, upper_at),
    ]
    copies = [
        pltpu.make_async_copy(far, here, arrived.at[i]) for i, (far, here) in enumerate(parts)
    ]
    for copy in copies:
        copy.start()
    eye = narrow(
        lax.broadcasted_iota(jnp.int32, (width, width), 0)
        == lax.broadcasted_iota(jnp.int32, (width, width), 1)
    )
    down[:, :count] = jnp.zeros((rows + 1, count, width), jnp.bfloat16)
    response[:, :near] = jnp.zeros((rows + 1, near, width), jnp.bfloat16)
    for k in range(rows):
        down[k, count:] = eye
        response[k, near:] = eye
    down[rows, count:] = jnp.zeros_like(eye)
    response[rows, near:] = jnp.zeros_like(eye)

    def piece(blocks, m):
        return blocks[m * width : (m + 1) * width]

    def named(at, k, row, blocks, many):
        return sum(
            jnp.where(at[m, k] == row, piece(blocks, m), 0.0) for m in range(1, many)
        )

    def sources(held, at, k, skipped, many):
        picked = []
        for m in range(1, many):
            row = at[m, k]
            picked.append(held[row if skipped is None else jnp.where(row == skipped, rows, row)])
        return jnp.concatenate(picked, axis=1)

    def apart(left, right, own, other):
        zero = jnp.zeros_like(own)
        sides = [jnp.concatenate([own, zero], axis=1), jnp.concatenate([zero, other], axis=1)]
        return mul(jnp.concatenate([left, right], axis=1), jnp.concatenate(sides, axis=0))

    def ready(at, blocks, many, first, step, heads):
        of_a, of_b, links = [], [], []
        for a in (first, first + 2 * step):
            b = a + step
            lefts = [
                jnp.concatenate(heads(k) + [blocks[k].reshape(many * width, width)], axis=0)
                for k in (a, b)
            ]
            both = apart(*lefts, inverse[a], inverse[b])
            of_a.append(both[:, :width])
            of_b.append(both[:, width:])
            tail = both[both.shape[0] - many * width :, width:]
            links.append(narrow(named(at, b, a, tail, many)))
        narrow_a = [narrow(value) for value in of_a]
        both = apart(*narrow_a, *links)
        through = [both[:, :width], both[:, width:]]
        return of_a, narrow_a, of_b, through, links

    def ready_down(p):
        of_a, narrow_a, of_b, through, _ = ready(
            lower_at, lower, slots, 2 * p, 1, lambda k: [narrow(rhs[k])]
        )
        for i in range(2):
            a, b = 2 * (p + i), 2 * (p + i) + 1
            free_a = -of_a[i][count:near]
            free_b = through[i][count:near] - of_b[i][count:near]
            if p + i == 0:
                inner = sum(piece(of_a[i][count:], m) for m in range(1, slots))
                free_a = free_a - inner
                inner = sum(piece(through[i][count:], m) for m in range(1, slots))
                free_b = free_b + inner - named(lower_at, b, b, of_b[i][count:], slots)
            else:
                low_pair[p + i, :, :width] = narrow_a[i][near:]
                low_pair[p + i, :, width:] = narrow(through[i][near:])
                low_second[p + i] = narrow(of_b[i][near:])
            exact[a, :count] = of_a[i][:count]
            exact[a, count:] = free_a
            exact[b, :count] = of_b[i][:count] - through[i][:count]
            exact[b, count:] = free_b

    def go_down(p):
        a, b = 2 * p, 2 * p + 1
        of_a, of_b = exact[a], exact[b]
        if p > 0:
            first = mul(sources(down, lower_at, a, None, slots), low_pair[p])
            second = mul(sources(down, lower_at, b, a, slots), low_second[p])
            of_a = of_a - first[:, :width]
            of_b = of_b + first[:, width:] - second
            exact[a] = of_a
            exact[b] = of_b
        down[a] = narrow(of_a)
        down[b] = narrow(of_b)

    def ready_up(p):
        of_a, narrow_a, of_b, through, links = ready(
            upper_at, upper, upper_slots, last - 2 * p, -1, lambda k: []
        )
        for i in range(2):
            a = last - 2 * (p + i)
            b = a - 1
            free_a = -of_a[i][:width]
            free_b = through[i][:width] - of_b[i][:width]
            if p + i == 0:
                free_a = free_a - sum(piece(of_a[i], m) for m in range(1, upper_slots))
                inner = sum(piece(through[i], m) for m in range(1, upper_slots))
                free_b = free_b + inner - named(upper_at, b, b, of_b[i], upper_slots)
            else:
                upp_pair[p + i, :, :width] = narrow_a[i][width:]
                upp_pair[p + i, :, width:] = narrow(through[i][width:])
                upp_second[p + i] = narrow(of_b[i][width:])
            fixed[a] = free_a
            fixed[b] = free_b
        return links

    def go_up(p, passed):
        a = last - 2 * p
        b = a - 1
        of_a = exact[a]
        of_b = exact[b] - passed
        free_a = fixed[a]
        free_b = fixed[b]
        if p > 0:
            first = mul(sources(response, upper_at, a, None, upper_slots), upp_pair[p])
            second = mul(sources(response, upper_at, b, a, upper_slots), upp_second[p])
            of_a = of_a - first[:near, :width]
            of_b = of_b + first[:near, width:] - second[:near]
            free_a = free_a - first[near:, :width]
            free_b = free_b + first[near:, width:] - second[near:]
        for k, value, free in ((a, of_a, free_a), (b, of_b, free_b)):
            base[k] = value[:count]
            response[k, :near] = narrow(value)
            response[k, near:] = narrow(free)

    pairs = rows // 2
    for copy in copies[:4]:
        copy.wait()
    ready_down(0)
    go_down(0)
    for copy in copies[4:]:
        copy.wait()
    links = []
    for p in range(1, pairs):
        if p % 2 == 1 and p + 1 < pairs:
            ready_down(p + 1)
        go_down(p)
        if p % 2 == 1:
            links += ready_up(p - 1)
    far = near + width
    payload[:near] = down[last]
    for p in range(0, pairs, 2):
        a = last - 2 * p
        passed = apart(down[a], down[a - 2], links[p], links[p + 1])
        go_up(p, passed[:, :width])
        go_up(p + 1, passed[:, width:])

    payload[near + far :] = response[last, near:]
    payload[near : near + far] = response[0]


def compose_kernel(axis, bit, final, mine, theirs, *refs):
    prior, sent, inner, prior_out = refs[:4] if bit > 1 else (None, *refs[:3])
    width = mine.shape[1]
    count = (mine.shape[0] - 4 * width) // 2
    near = count + width
    me = lax.axis_index(axis)
    place = lax.rem(lax.div(me, bit), 2)
    mid = near + count
    far = near + near + width
    blank = jnp.zeros((width, width), jnp.float32)

    def join(a, b):
        sides = [b[count:near], b[mid : mid + width]]
        across = mul(a[:near], jnp.concatenate(sides, axis=1))
        ahead = jnp.concatenate([b[:count].astype(jnp.float32), blank], axis=0)
        joined = narrow(across[:, :width] + ahead)
        ahead = jnp.concatenate([b[near:mid].astype(jnp.float32), blank], axis=0)
        between = narrow(across[:, width:] + ahead)
        first = mul(between, a[mid + width : far]) + a[near : 2 * near].astype(jnp.float32)
        inner[:near] = a[:near]
        inner[near : 2 * near] = between
        inner[2 * near :] = b[mid + width : far]
        prior_out[...] = a[far:]
        if final:
            refs[-1][...] = joined[:count]
            above = lax.rem(lax.div(me, 2 * bit), 2) == 1

            @pl.when(above)
            def _():
                sent[...] = narrow(first)

            @pl.when(jnp.logical_not(above))
            def _():
                sent[:count] = joined[:count]
                sent[count:] = b[far:]

        else:
            sent[:near] = joined
            sent[near : 2 * near] = narrow(first)
            sent[2 * near : far] = narrow(mul(b[mid + width : far], a[mid + width : far]))
            sent[far:] = b[far:]

    @pl.when(place == 0)
    def _():
        join(mine, theirs)

    @pl.when(place == 1)
    def _():
        join(theirs, mine)

    if prior is not None:
        lowest = jnp.logical_and(place == 1, lax.rem(me, bit) == 0)

        @pl.when(jnp.logical_not(lowest))
        def _():
            prior_out[...] = prior[...]


def fold_kernel(axis, levels, *refs):
    base, response = refs[:2]
    inner = refs[2 : 1 + levels]
    diagonal_far, folded, folded_response, inflow_map, outflow_map = refs[1 + levels : 6 + levels]
    diagonal, arrived = refs[6 + levels :]
    copy = pltpu.make_async_copy(diagonal_far, diagonal, arrived)
    copy.start()
    rows, count, width = base.shape
    near = count + width
    me = lax.axis_index(axis)

    upper = lax.div(me, 1 << (levels - 1)) == 1
    across = lax.broadcasted_iota(jnp.int32, (near, width), 1) + count
    unit = jnp.where(lax.broadcasted_iota(jnp.int32, (near, width), 0) == across, 1.0, 0.0)
    inflow = jnp.where(upper, unit, 0.0)
    outflow = jnp.where(upper, 0.0, unit)
    blank = jnp.zeros((width, width), jnp.float32)
    for level in range(levels - 2, -1, -1):
        part = inner[level]
        upper = lax.rem(lax.div(me, 1 << level), 2) == 1
        known = jnp.concatenate([part[:count].astype(jnp.float32), blank], axis=0)
        down = known + mul(narrow(inflow), part[count:near])
        both = narrow(jnp.concatenate([inflow, outflow], axis=1))
        known = jnp.concatenate([part[near : near + count].astype(jnp.float32), blank], axis=0)
        up = known + mul(both, part[near + count :])
        inflow, outflow = jnp.where(upper, down, inflow), jnp.where(upper, outflow, up)

    inflow_map[...] = narrow(inflow)
    outflow_map[...] = narrow(outflow)
    both = narrow(jnp.concatenate([inflow, outflow], axis=1))
    for k in range(rows):
        value = mul(both, response[k, count:])
        folded[k] = base[k] + value[:count]
        folded_response[k] = narrow(value[count:])
    copy.wait()


def chain_kernel(
    axes, levels, own, theirs, base, response, solution, rounded, brought, near_rows, far_rows
):
    rows, count, width = base.shape
    side = lax.rem(lax.axis_index(axes[1]), 2)
    upper = lax.div(lax.axis_index(axes[0]), 1 << (levels - 1)) == 1
    down = theirs[:count].astype(jnp.float32)
    up = down + mul(own[...], theirs[count:])
    z = narrow(jnp.where(upper, down, up))
    brought[...] = z
    values = []
    for k in range(rows):
        value = base[k] + mul(z, response[k])
        solution[k] = value
        values.append(narrow(value))
        rounded[k] = values[k]
    rim = near_rows.shape[0]
    for odd, to_low, to_high in ((0, far_rows, near_rows), (1, near_rows, far_rows)):

        @pl.when(side == odd)
        def _(to_low=to_low, to_high=to_high):
            for e in range(rim):
                to_low[e] = values[e]
                to_high[e] = values[rows - rim + e]


def local_kernel(
    axes,
    levels,
    rounded,
    brought,
    inflow_map,
    outflow_map,
    prior,
    theirs,
    solved,
    diagonal,
    lower,
    upper,
    lower_at_far,
    upper_at_far,
    halo_at_far,
    partial,
    solution,
    masks,
    held,
    last_block,
    lower_at,
    upper_at,
    halo_at,
    arrived,
):
    parts = [
        (lower_at_far, lower_at),
        (upper_at_far, upper_at),
        (halo_at_far, halo_at),
        (solved, solution),
    ]
    copies = [
        pltpu.make_async_copy(source, target, arrived.at[i])
        for i, (source, target) in enumerate(parts)
    ]
    for copy in copies:
        copy.start()
    rows, slots, width, _ = lower.shape
    upper_slots = upper.shape[1]
    count = brought.shape[0]
    me = lax.axis_index(axes[0])
    last_block[...] = prior[...]

    @pl.when(me == 1 << (levels - 1))
    def _():
        last_block[...] = theirs[count:]

    z = brought[...]
    after = narrow(outflow_map[:count].astype(jnp.float32) + mul(z, outflow_map[count:]))
    before = inflow_map[:count].astype(jnp.float32) + mul(z, inflow_map[count:])
    before = narrow(before).astype(jnp.float32) + mul(rounded[0], last_block[...])
    before = narrow(jnp.where(me > 0, before, 0.0))
    held[:rows] = rounded[...]
    held[rows] = before
    held[rows + 1] = after
    for k in range(rows):
        source = jnp.concatenate([rounded[k], after], axis=1)
        total = mul(source, jnp.concatenate([diagonal[k], upper[k, 0]], axis=0))
        partial[k] = total + mul(before, lower[k, 0])
    for copy in copies[:3]:
        copy.wait()
    for k in range(rows):
        source = []
        for m in range(1, slots):
            at = lower_at[m, k]
            source.append(held[jnp.where(at == k, rows, at)])
        total = mul(
            jnp.concatenate(source, axis=1), lower[k, 1:].reshape((slots - 1) * width, width)
        )
        source = []
        for m in range(1, upper_slots):
            at = upper_at[m, k]
            source.append(held[jnp.where(at == k, rows + 1, at)])
        partial[k] += total + mul(
            jnp.concatenate(source, axis=1),
            upper[k, 1:].reshape((upper_slots - 1) * width, width),
        )
    _, picked, places, _, _ = masks.shape
    for k in range(rows):
        for m in range(picked):
            at = halo_at[m + 1, k]
            for j in range(places):
                mask = jnp.where(at == j, 1.0, 0.0)
                masks[k, m, j] = narrow(jnp.full((count, width), mask, jnp.float32))
    copies[3].wait()


def halo_kernel(axis, partial, outer, inner, halo, masks, product):
    rows, slots, width, _ = halo.shape
    rim = inner.shape[0]
    side = lax.rem(lax.axis_index(axis), 2)

    def add(left, right):
        rim_rows = [left[e] for e in range(rim)] + [right[e] for e in range(rim)]
        for k in range(rows):
            source = [rim_rows[k % (2 * rim)]]
            for m in range(1, slots):
                source.append(sum(masks[k, m - 1, j] * rim_rows[j] for j in range(2 * rim)))
            product[k] = partial[k] + mul(
                jnp.concatenate(source, axis=1), halo[k].reshape(slots * width, width)
            )

    @pl.when(side == 0)
    def _():
        add(outer, inner)

    @pl.when(side == 1)
    def _():
        add(inner, outer)


def trade(block, axis, bit):
    count = lax.axis_size(axis)
    return lax.ppermute(block, axis, [(i, i ^ bit) for i in range(count)])


def swaps(block, axis, first):
    count = lax.axis_size(axis)
    pairs = []
    for low in range(first, count - 1, 2):
        pairs += [(low, low + 1), (low + 1, low)]
    return lax.ppermute(block, axis, pairs)


def on_device(
    right_sides,
    diag_inverse,
    diag_blocks,
    lower_blocks,
    upper_blocks,
    halo_blocks,
    lower_index,
    upper_index,
    halo_index,
):
    rows, count, width = right_sides.shape
    lower_at, upper_at, halo_at = lower_index.T, upper_index.T, halo_index.T
    slots = lower_blocks.shape[1]
    upper_slots = upper_blocks.shape[1]
    groups = lax.axis_size("section")
    near = count + width
    far = near + width
    wide = jax.ShapeDtypeStruct((rows, count, width), jnp.float32)

    indices = [
        pltpu.with_memory_space_constraint(a, pltpu.HBM) for a in (lower_at, upper_at, halo_at)
    ]
    base, response, payload = pl.pallas_call(
        sweep_kernel,
        out_shape=(
            wide,
            jax.ShapeDtypeStruct((rows + 1, far, width), jnp.bfloat16),
            jax.ShapeDtypeStruct((near + far + width, width), jnp.bfloat16),
        ),
        in_specs=[HBM] * 6,
        out_specs=(VMEM,) * 3,
        scratch_shapes=[
            pltpu.VMEM(right_sides.shape, right_sides.dtype),
            pltpu.VMEM(diag_inverse.shape, diag_inverse.dtype),
            pltpu.VMEM(lower_blocks.shape, lower_blocks.dtype),
            pltpu.VMEM(upper_blocks.shape, upper_blocks.dtype),
            pltpu.SMEM(lower_at.shape, jnp.int32),
            pltpu.SMEM(upper_at.shape, jnp.int32),
            pltpu.VMEM((rows // 2, (slots - 1) * width, 2 * width), jnp.bfloat16),
            pltpu.VMEM((rows // 2, (slots - 1) * width, width), jnp.bfloat16),
            pltpu.VMEM((rows // 2, (upper_slots - 1) * width, 2 * width), jnp.bfloat16),
            pltpu.VMEM((rows // 2, (upper_slots - 1) * width, width), jnp.bfloat16),
            pltpu.VMEM((rows + 1, near, width), jnp.bfloat16),
            pltpu.VMEM((rows, near, width), jnp.float32),
            pltpu.VMEM((rows, width, width), jnp.float32),
            pltpu.SemaphoreType.DMA((7,)),
        ],
        compiler_params=SMALL,
        name="sweeps",
    )(
        *(
            pltpu.with_memory_space_constraint(a, pltpu.HBM)
            for a in (right_sides, diag_inverse, lower_blocks, upper_blocks)
        ),
        *indices[:2],
    )

    levels = groups.bit_length() - 1
    segment = payload.shape[0]
    bits = jnp.bfloat16
    prior = []
    inner = []
    for level in range(levels - 1):
        theirs = trade(payload, "section", 1 << level)
        final = level == levels - 2

        def compose(*refs, bit=1 << level, final=final):
            compose_kernel("section", bit, final, *refs)

        payload, between, *prior = pl.pallas_call(
            compose,
            out_shape=(
                jax.ShapeDtypeStruct((near if final else segment, width), bits),
                jax.ShapeDtypeStruct((near + far, width), bits),
                jax.ShapeDtypeStruct((width, width), bits),
            )
            + (jax.ShapeDtypeStruct((count, width), bits),) * final,
            in_specs=[VMEM] * (2 + len(prior)),
            out_specs=(VMEM,) * (3 + final),
            compiler_params=SMALL,
            name="compose",
        )(payload, theirs, *prior)
        inner.append(between)
    prior, own = prior
    theirs = trade(payload, "section", 1 << (levels - 1))

    def fold(*refs):
        fold_kernel("section", levels, *refs)

    base, response, inflow_map, outflow_map, diagonal = pl.pallas_call(
        fold,
        out_shape=(
            wide,
            jax.ShapeDtypeStruct((rows, width, width), bits),
            jax.ShapeDtypeStruct((near, width), bits),
            jax.ShapeDtypeStruct((near, width), bits),
            jax.ShapeDtypeStruct(diag_blocks.shape, diag_blocks.dtype),
        ),
        in_specs=[VMEM] * (1 + levels) + [HBM],
        out_specs=(VMEM,) * 5,
        scratch_shapes=[pltpu.SemaphoreType.DMA(())],
        compiler_params=SMALL,
        name="fold",
    )(base, response, *inner, pltpu.with_memory_space_constraint(diag_blocks, pltpu.HBM))

    def chain(*refs):
        chain_kernel(("section", "dom"), levels, *refs)

    solved, rounded, brought, inner, outer = pl.pallas_call(
        chain,
        out_shape=(
            wide,
            jax.ShapeDtypeStruct((rows, count, width), bits),
            jax.ShapeDtypeStruct((count, width), bits),
            jax.ShapeDtypeStruct((RIM, count, width), bits),
            jax.ShapeDtypeStruct((RIM, count, width), bits),
        ),
        in_specs=[VMEM] * 4,
        out_specs=(VMEM,) * 5,
        compiler_params=SMALL,
        name="chain",
    )(own, theirs, base, response)

    outer = swaps(outer, "dom", 1)
    inner = swaps(inner, "dom", 0)

    def local(*refs):
        local_kernel(("section", "dom"), levels, *refs)

    masks = (rows, halo_blocks.shape[1] - 1, 2 * RIM, count, width)
    partial, solution, masks = pl.pallas_call(
        local,
        out_shape=(wide, wide, jax.ShapeDtypeStruct(masks, bits)),
        in_specs=[VMEM] * 10 + [HBM] * 3,
        out_specs=(VMEM, HBM, VMEM),
        scratch_shapes=[
            pltpu.VMEM((rows + 2, count, width), bits),
            pltpu.VMEM((width, width), bits),
        ]
        + [pltpu.SMEM(a.shape, jnp.int32) for a in indices]
        + [pltpu.SemaphoreType.DMA((4,))],
        compiler_params=SMALL,
        name="local_product",
    )(
        rounded,
        brought,
        inflow_map,
        outflow_map,
        prior,
        theirs,
        solved,
        diagonal,
        lower_blocks,
        upper_blocks,
        *indices,
    )

    def halo(*refs):
        halo_kernel("dom", *refs)

    product = pl.pallas_call(
        halo,
        out_shape=wide,
        in_specs=[VMEM] * 5,
        out_specs=VMEM,
        compiler_params=SMALL,
        name="halo_product",
    )(partial, outer, inner, halo_blocks, masks)
    return (solution, product)


def solution(mesh):
    in_specs = (
        P(("section", "dom"), None, None),
        P(("section", "dom"), None, None),
        P(("section", "dom"), None, None),
        P(("section", "dom"), None, None, None),
        P(("section", "dom"), None, None, None),
        P(("section", "dom"), None, None, None),
        P(("section", "dom"), None),
        P(("section", "dom"), None),
        P(("section", "dom"), None),
    )
    out_specs = (P(("section", "dom"), None, None), P(("section", "dom"), None, None))
    return jax.shard_map(
        on_device, mesh=mesh, in_specs=in_specs, out_specs=out_specs, check_vma=False
    )
```

```python
import jax
import jax.numpy as jnp
from jax import lax
from jax.experimental import pallas as pl
from jax.experimental.pallas import tpu as pltpu
from jax.sharding import PartitionSpec as P

RIM = 4

VMEM = pl.BlockSpec(memory_space=pltpu.VMEM)
SMEM = pl.BlockSpec(memory_space=pltpu.SMEM)
HBM = pl.BlockSpec(memory_space=pltpu.HBM)
SMALL = pltpu.CompilerParams(vmem_limit_bytes=16 * 1024 * 1024)


def mul(a, b):
    return jnp.dot(a, b, preferred_element_type=jnp.float32)


def narrow(a):
    return a.astype(jnp.bfloat16)


def sweep_kernel(
    rhs_far,
    inverse_far,
    lower_far,
    upper_far,
    lower_at_far,
    upper_at_far,
    base,
    response,
    free,
    payload,
    rhs,
    inverse,
    lower,
    upper,
    lower_at,
    upper_at,
    low_pair,
    low_second,
    upp_pair,
    upp_second,
    down,
    exact,
    fixed,
    arrived,
):
    rows, count, width = rhs.shape
    slots = lower.shape[1]
    upper_slots = upper.shape[1]
    near = count + width
    last = rows - 1
    half = rows // 2
    parts = [
        (inverse_far, inverse),
        (rhs_far, rhs),
        (lower_far.at[:half], lower.at[:half]),
        (lower_at_far, lower_at),
        (lower_far.at[half:], lower.at[half:]),
        (upper_far, upper),
        (upper_at_far, upper_at),
    ]
    copies = [
        pltpu.make_async_copy(far, here, arrived.at[i]) for i, (far, here) in enumerate(parts)
    ]
    for copy in copies:
        copy.start()
    eye = narrow(
        lax.broadcasted_iota(jnp.int32, (width, width), 0)
        == lax.broadcasted_iota(jnp.int32, (width, width), 1)
    )
    down[:, :count] = jnp.zeros((rows + 1, count, width), jnp.bfloat16)
    response[...] = jnp.zeros(response.shape, jnp.bfloat16)
    for k in range(rows):
        down[k, count:] = eye
        free[k] = eye
    down[rows, count:] = jnp.zeros_like(eye)
    free[rows] = jnp.zeros_like(eye)

    def piece(blocks, m):
        return blocks[m * width : (m + 1) * width]

    def named(at, k, row, blocks, many):
        return sum(
            jnp.where(at[m, k] == row, piece(blocks, m), 0.0) for m in range(1, many)
        )

    def sources(held, at, k, skipped, many):
        picked = []
        for m in range(1, many):
            row = at[m, k]
            picked.append(held[row if skipped is None else jnp.where(row == skipped, rows, row)])
        return jnp.concatenate(picked, axis=1)

    def apart(left, right, own, other):
        zero = jnp.zeros_like(own)
        sides = [jnp.concatenate([own, zero], axis=1), jnp.concatenate([zero, other], axis=1)]
        return mul(jnp.concatenate([left, right], axis=1), jnp.concatenate(sides, axis=0))

    def ready(at, blocks, many, first, step, heads):
        of_a, of_b, links = [], [], []
        for a in (first, first + 2 * step):
            b = a + step
            lefts = [
                jnp.concatenate(heads(k) + [blocks[k].reshape(many * width, width)], axis=0)
                for k in (a, b)
            ]
            both = apart(*lefts, inverse[a], inverse[b])
            of_a.append(both[:, :width])
            of_b.append(both[:, width:])
            tail = both[both.shape[0] - many * width :, width:]
            links.append(narrow(named(at, b, a, tail, many)))
        narrow_a = [narrow(value) for value in of_a]
        both = apart(*narrow_a, *links)
        through = [both[:, :width], both[:, width:]]
        return of_a, narrow_a, of_b, through, links

    def ready_down(p):
        of_a, narrow_a, of_b, through, _ = ready(
            lower_at, lower, slots, 2 * p, 1, lambda k: [narrow(rhs[k])]
        )
        for i in range(2):
            a, b = 2 * (p + i), 2 * (p + i) + 1
            free_a = -of_a[i][count:near]
            free_b = through[i][count:near] - of_b[i][count:near]
            if p + i == 0:
                inner = sum(piece(of_a[i][count:], m) for m in range(1, slots))
                free_a = free_a - inner
                inner = sum(piece(through[i][count:], m) for m in range(1, slots))
                free_b = free_b + inner - named(lower_at, b, b, of_b[i][count:], slots)
            else:
                low_pair[p + i, :, :width] = narrow_a[i][near:]
                low_pair[p + i, :, width:] = narrow(through[i][near:])
                low_second[p + i] = narrow(of_b[i][near:])
            exact[a, :count] = of_a[i][:count]
            exact[a, count:] = free_a
            exact[b, :count] = of_b[i][:count] - through[i][:count]
            exact[b, count:] = free_b

    def go_down(p):
        a, b = 2 * p, 2 * p + 1
        of_a, of_b = exact[a], exact[b]
        if p > 0:
            first = mul(sources(down, lower_at, a, None, slots), low_pair[p])
            second = mul(sources(down, lower_at, b, a, slots), low_second[p])
            of_a = of_a - first[:, :width]
            of_b = of_b + first[:, width:] - second
            exact[a] = of_a
            exact[b] = of_b
        down[a] = narrow(of_a)
        down[b] = narrow(of_b)

    def ready_up(p):
        of_a, narrow_a, of_b, through, links = ready(
            upper_at, upper, upper_slots, last - 2 * p, -1, lambda k: []
        )
        for i in range(2):
            a = last - 2 * (p + i)
            b = a - 1
            free_a = -of_a[i][:width]
            free_b = through[i][:width] - of_b[i][:width]
            if p + i == 0:
                free_a = free_a - sum(piece(of_a[i], m) for m in range(1, upper_slots))
                inner = sum(piece(through[i], m) for m in range(1, upper_slots))
                free_b = free_b + inner - named(upper_at, b, b, of_b[i], upper_slots)
            else:
                upp_pair[p + i, :, :width] = narrow_a[i][width:]
                upp_pair[p + i, :, width:] = narrow(through[i][width:])
                upp_second[p + i] = narrow(of_b[i][width:])
            fixed[a] = free_a
            fixed[b] = free_b
        return links

    def step_up(p, held, of_a, of_b):
        a = last - 2 * p
        b = a - 1
        if p > 0:
            first = mul(sources(held, upper_at, a, None, upper_slots), upp_pair[p])
            second = mul(sources(held, upper_at, b, a, upper_slots), upp_second[p])
            of_a = of_a - first[:, :width]
            of_b = of_b + first[:, width:] - second
        held[a] = narrow(of_a)
        held[b] = narrow(of_b)
        return of_a, of_b

    def go_free(p):
        a = last - 2 * p
        step_up(p, free, fixed[a], fixed[a - 1])

    def go_up(p, passed):
        a = last - 2 * p
        of_a, of_b = step_up(p, response, exact[a], exact[a - 1] - passed)
        base[a] = of_a[:count]
        base[a - 1] = of_b[:count]

    pairs = rows // 2
    for copy in copies[:4]:
        copy.wait()
    ready_down(0)
    go_down(0)
    for copy in copies[4:]:
        copy.wait()
    links = []
    freed = 0
    for p in range(1, pairs):
        if p % 2 == 1 and p + 1 < pairs:
            ready_down(p + 1)
        go_down(p)
        while freed < len(links):
            go_free(freed)
            freed += 1
        if p % 2 == 1:
            links += ready_up(p - 1)
    far = near + width
    payload[:near] = down[last]
    for p in range(pairs):
        a = last - 2 * p
        if p % 2 == 0:
            passed = apart(down[a], down[a - 2], links[p], links[p + 1])
        go_up(p, passed[:, width * (p % 2) : width * (p % 2 + 1)])
        if freed < pairs:
            go_free(freed)
            freed += 1

    payload[near + far :] = free[last]
    payload[2 * near : near + far] = free[0]
    payload[near : 2 * near] = response[0]


def compose_kernel(axis, bit, final, mine, theirs, *refs):
    prior, sent, inner, prior_out = refs[:4] if bit > 1 else (None, *refs[:3])
    width = mine.shape[1]
    count = (mine.shape[0] - 4 * width) // 2
    near = count + width
    me = lax.axis_index(axis)
    place = lax.rem(lax.div(me, bit), 2)
    mid = near + count
    far = near + near + width
    blank = jnp.zeros((width, width), jnp.float32)

    def join(a, b):
        sides = [b[count:near], b[mid : mid + width]]
        across = mul(a[:near], jnp.concatenate(sides, axis=1))
        ahead = jnp.concatenate([b[:count].astype(jnp.float32), blank], axis=0)
        joined = narrow(across[:, :width] + ahead)
        ahead = jnp.concatenate([b[near:mid].astype(jnp.float32), blank], axis=0)
        between = narrow(across[:, width:] + ahead)
        first = mul(between, a[mid + width : far]) + a[near : 2 * near].astype(jnp.float32)
        inner[:near] = a[:near]
        inner[near : 2 * near] = between
        inner[2 * near :] = b[mid + width : far]
        prior_out[...] = a[far:]
        if final:
            refs[-1][...] = joined[:count]
            above = lax.rem(lax.div(me, 2 * bit), 2) == 1

            @pl.when(above)
            def _():
                sent[...] = narrow(first)

            @pl.when(jnp.logical_not(above))
            def _():
                sent[:count] = joined[:count]
                sent[count:] = b[far:]

        else:
            sent[:near] = joined
            sent[near : 2 * near] = narrow(first)
            sent[2 * near : far] = narrow(mul(b[mid + width : far], a[mid + width : far]))
            sent[far:] = b[far:]

    @pl.when(place == 0)
    def _():
        join(mine, theirs)

    @pl.when(place == 1)
    def _():
        join(theirs, mine)

    if prior is not None:
        lowest = jnp.logical_and(place == 1, lax.rem(me, bit) == 0)

        @pl.when(jnp.logical_not(lowest))
        def _():
            prior_out[...] = prior[...]


def fold_kernel(axis, levels, *refs):
    base, response, free = refs[:3]
    inner = refs[3 : 2 + levels]
    diagonal_far, folded, folded_response, inflow_map, outflow_map = refs[2 + levels : 7 + levels]
    diagonal, arrived = refs[7 + levels :]
    copy = pltpu.make_async_copy(diagonal_far, diagonal, arrived)
    copy.start()
    rows, count, width = base.shape
    near = count + width
    me = lax.axis_index(axis)

    upper = lax.div(me, 1 << (levels - 1)) == 1
    across = lax.broadcasted_iota(jnp.int32, (near, width), 1) + count
    unit = jnp.where(lax.broadcasted_iota(jnp.int32, (near, width), 0) == across, 1.0, 0.0)
    inflow = jnp.where(upper, unit, 0.0)
    outflow = jnp.where(upper, 0.0, unit)
    blank = jnp.zeros((width, width), jnp.float32)
    for level in range(levels - 2, -1, -1):
        part = inner[level]
        upper = lax.rem(lax.div(me, 1 << level), 2) == 1
        known = jnp.concatenate([part[:count].astype(jnp.float32), blank], axis=0)
        down = known + mul(narrow(inflow), part[count:near])
        both = narrow(jnp.concatenate([inflow, outflow], axis=1))
        known = jnp.concatenate([part[near : near + count].astype(jnp.float32), blank], axis=0)
        up = known + mul(both, part[near + count :])
        inflow, outflow = jnp.where(upper, down, inflow), jnp.where(upper, outflow, up)

    inflow_map[...] = narrow(inflow)
    outflow_map[...] = narrow(outflow)
    both = narrow(jnp.concatenate([inflow, outflow], axis=1))
    for k in range(rows):
        value = mul(both, jnp.concatenate([response[k, count:], free[k]], axis=0))
        folded[k] = base[k] + value[:count]
        folded_response[k] = narrow(value[count:])
    copy.wait()


def chain_kernel(
    axes, levels, own, theirs, base, response, solution, rounded, brought, near_rows, far_rows
):
    rows, count, width = base.shape
    side = lax.rem(lax.axis_index(axes[1]), 2)
    upper = lax.div(lax.axis_index(axes[0]), 1 << (levels - 1)) == 1
    down = theirs[:count].astype(jnp.float32)
    up = down + mul(own[...], theirs[count:])
    z = narrow(jnp.where(upper, down, up))
    brought[...] = z
    values = []
    for k in range(rows):
        value = base[k] + mul(z, response[k])
        solution[k] = value
        values.append(narrow(value))
        rounded[k] = values[k]
    rim = near_rows.shape[0]
    for odd, to_low, to_high in ((0, far_rows, near_rows), (1, near_rows, far_rows)):

        @pl.when(side == odd)
        def _(to_low=to_low, to_high=to_high):
            for e in range(rim):
                to_low[e] = values[e]
                to_high[e] = values[rows - rim + e]


def local_kernel(
    axes,
    levels,
    rounded,
    brought,
    inflow_map,
    outflow_map,
    prior,
    theirs,
    solved,
    diagonal,
    lower,
    upper,
    lower_at_far,
    upper_at_far,
    halo_at_far,
    partial,
    solution,
    masks,
    held,
    last_block,
    lower_at,
    upper_at,
    halo_at,
    arrived,
):
    parts = [
        (lower_at_far, lower_at),
        (upper_at_far, upper_at),
        (halo_at_far, halo_at),
        (solved, solution),
    ]
    copies = [
        pltpu.make_async_copy(source, target, arrived.at[i])
        for i, (source, target) in enumerate(parts)
    ]
    for copy in copies:
        copy.start()
    rows, slots, width, _ = lower.shape
    upper_slots = upper.shape[1]
    count = brought.shape[0]
    me = lax.axis_index(axes[0])
    last_block[...] = prior[...]

    @pl.when(me == 1 << (levels - 1))
    def _():
        last_block[...] = theirs[count:]

    z = brought[...]
    after = narrow(outflow_map[:count].astype(jnp.float32) + mul(z, outflow_map[count:]))
    before = inflow_map[:count].astype(jnp.float32) + mul(z, inflow_map[count:])
    before = narrow(before).astype(jnp.float32) + mul(rounded[0], last_block[...])
    before = narrow(jnp.where(me > 0, before, 0.0))
    held[:rows] = rounded[...]
    held[rows] = before
    held[rows + 1] = after
    for k in range(rows):
        source = jnp.concatenate([rounded[k], after], axis=1)
        total = mul(source, jnp.concatenate([diagonal[k], upper[k, 0]], axis=0))
        partial[k] = total + mul(before, lower[k, 0])
    for copy in copies[:3]:
        copy.wait()
    for k in range(rows):
        source = []
        for m in range(1, slots):
            at = lower_at[m, k]
            source.append(held[jnp.where(at == k, rows, at)])
        total = mul(
            jnp.concatenate(source, axis=1), lower[k, 1:].reshape((slots - 1) * width, width)
        )
        source = []
        for m in range(1, upper_slots):
            at = upper_at[m, k]
            source.append(held[jnp.where(at == k, rows + 1, at)])
        partial[k] += total + mul(
            jnp.concatenate(source, axis=1),
            upper[k, 1:].reshape((upper_slots - 1) * width, width),
        )
    _, picked, places, _, _ = masks.shape
    for k in range(rows):
        for m in range(picked):
            at = halo_at[m + 1, k]
            for j in range(places):
                mask = jnp.where(at == j, 1.0, 0.0)
                masks[k, m, j] = narrow(jnp.full((count, width), mask, jnp.float32))
    copies[3].wait()


def halo_kernel(axis, partial, outer, inner, halo, masks, product):
    rows, slots, width, _ = halo.shape
    rim = inner.shape[0]
    side = lax.rem(lax.axis_index(axis), 2)

    def add(left, right):
        rim_rows = [left[e] for e in range(rim)] + [right[e] for e in range(rim)]
        for k in range(rows):
            source = [rim_rows[k % (2 * rim)]]
            for m in range(1, slots):
                source.append(sum(masks[k, m - 1, j] * rim_rows[j] for j in range(2 * rim)))
            product[k] = partial[k] + mul(
                jnp.concatenate(source, axis=1), halo[k].reshape(slots * width, width)
            )

    @pl.when(side == 0)
    def _():
        add(outer, inner)

    @pl.when(side == 1)
    def _():
        add(inner, outer)


def trade(block, axis, bit):
    count = lax.axis_size(axis)
    return lax.ppermute(block, axis, [(i, i ^ bit) for i in range(count)])


def swaps(block, axis, first):
    count = lax.axis_size(axis)
    pairs = []
    for low in range(first, count - 1, 2):
        pairs += [(low, low + 1), (low + 1, low)]
    return lax.ppermute(block, axis, pairs)


def on_device(
    right_sides,
    diag_inverse,
    diag_blocks,
    lower_blocks,
    upper_blocks,
    halo_blocks,
    lower_index,
    upper_index,
    halo_index,
):
    rows, count, width = right_sides.shape
    lower_at, upper_at, halo_at = lower_index.T, upper_index.T, halo_index.T
    slots = lower_blocks.shape[1]
    upper_slots = upper_blocks.shape[1]
    groups = lax.axis_size("section")
    near = count + width
    far = near + width
    wide = jax.ShapeDtypeStruct((rows, count, width), jnp.float32)

    indices = [
        pltpu.with_memory_space_constraint(a, pltpu.HBM) for a in (lower_at, upper_at, halo_at)
    ]
    base, response, free, payload = pl.pallas_call(
        sweep_kernel,
        out_shape=(
            wide,
            jax.ShapeDtypeStruct((rows + 1, near, width), jnp.bfloat16),
            jax.ShapeDtypeStruct((rows + 1, width, width), jnp.bfloat16),
            jax.ShapeDtypeStruct((near + far + width, width), jnp.bfloat16),
        ),
        in_specs=[HBM] * 6,
        out_specs=(VMEM,) * 4,
        scratch_shapes=[
            pltpu.VMEM(right_sides.shape, right_sides.dtype),
            pltpu.VMEM(diag_inverse.shape, diag_inverse.dtype),
            pltpu.VMEM(lower_blocks.shape, lower_blocks.dtype),
            pltpu.VMEM(upper_blocks.shape, upper_blocks.dtype),
            pltpu.SMEM(lower_at.shape, jnp.int32),
            pltpu.SMEM(upper_at.shape, jnp.int32),
            pltpu.VMEM((rows // 2, (slots - 1) * width, 2 * width), jnp.bfloat16),
            pltpu.VMEM((rows // 2, (slots - 1) * width, width), jnp.bfloat16),
            pltpu.VMEM((rows // 2, (upper_slots - 1) * width, 2 * width), jnp.bfloat16),
            pltpu.VMEM((rows // 2, (upper_slots - 1) * width, width), jnp.bfloat16),
            pltpu.VMEM((rows + 1, near, width), jnp.bfloat16),
            pltpu.VMEM((rows, near, width), jnp.float32),
            pltpu.VMEM((rows, width, width), jnp.float32),
            pltpu.SemaphoreType.DMA((7,)),
        ],
        compiler_params=SMALL,
        name="sweeps",
    )(
        *(
            pltpu.with_memory_space_constraint(a, pltpu.HBM)
            for a in (right_sides, diag_inverse, lower_blocks, upper_blocks)
        ),
        *indices[:2],
    )

    levels = groups.bit_length() - 1
    segment = payload.shape[0]
    bits = jnp.bfloat16
    prior = []
    inner = []
    for level in range(levels - 1):
        theirs = trade(payload, "section", 1 << level)
        final = level == levels - 2

        def compose(*refs, bit=1 << level, final=final):
            compose_kernel("section", bit, final, *refs)

        payload, between, *prior = pl.pallas_call(
            compose,
            out_shape=(
                jax.ShapeDtypeStruct((near if final else segment, width), bits),
                jax.ShapeDtypeStruct((near + far, width), bits),
                jax.ShapeDtypeStruct((width, width), bits),
            )
            + (jax.ShapeDtypeStruct((count, width), bits),) * final,
            in_specs=[VMEM] * (2 + len(prior)),
            out_specs=(VMEM,) * (3 + final),
            compiler_params=SMALL,
            name="compose",
        )(payload, theirs, *prior)
        inner.append(between)
    prior, own = prior
    theirs = trade(payload, "section", 1 << (levels - 1))

    def fold(*refs):
        fold_kernel("section", levels, *refs)

    base, response, inflow_map, outflow_map, diagonal = pl.pallas_call(
        fold,
        out_shape=(
            wide,
            jax.ShapeDtypeStruct((rows, width, width), bits),
            jax.ShapeDtypeStruct((near, width), bits),
            jax.ShapeDtypeStruct((near, width), bits),
            jax.ShapeDtypeStruct(diag_blocks.shape, diag_blocks.dtype),
        ),
        in_specs=[VMEM] * (2 + levels) + [HBM],
        out_specs=(VMEM,) * 5,
        scratch_shapes=[pltpu.SemaphoreType.DMA(())],
        compiler_params=SMALL,
        name="fold",
    )(base, response, free, *inner, pltpu.with_memory_space_constraint(diag_blocks, pltpu.HBM))

    def chain(*refs):
        chain_kernel(("section", "dom"), levels, *refs)

    solved, rounded, brought, inner, outer = pl.pallas_call(
        chain,
        out_shape=(
            wide,
            jax.ShapeDtypeStruct((rows, count, width), bits),
            jax.ShapeDtypeStruct((count, width), bits),
            jax.ShapeDtypeStruct((RIM, count, width), bits),
            jax.ShapeDtypeStruct((RIM, count, width), bits),
        ),
        in_specs=[VMEM] * 4,
        out_specs=(VMEM,) * 5,
        compiler_params=SMALL,
        name="chain",
    )(own, theirs, base, response)

    outer = swaps(outer, "dom", 1)
    inner = swaps(inner, "dom", 0)

    def local(*refs):
        local_kernel(("section", "dom"), levels, *refs)

    masks = (rows, halo_blocks.shape[1] - 1, 2 * RIM, count, width)
    partial, solution, masks = pl.pallas_call(
        local,
        out_shape=(wide, wide, jax.ShapeDtypeStruct(masks, bits)),
        in_specs=[VMEM] * 10 + [HBM] * 3,
        out_specs=(VMEM, HBM, VMEM),
        scratch_shapes=[
            pltpu.VMEM((rows + 2, count, width), bits),
            pltpu.VMEM((width, width), bits),
        ]
        + [pltpu.SMEM(a.shape, jnp.int32) for a in indices]
        + [pltpu.SemaphoreType.DMA((4,))],
        compiler_params=SMALL,
        name="local_product",
    )(
        rounded,
        brought,
        inflow_map,
        outflow_map,
        prior,
        theirs,
        solved,
        diagonal,
        lower_blocks,
        upper_blocks,
        *indices,
    )

    def halo(*refs):
        halo_kernel("dom", *refs)

    product = pl.pallas_call(
        halo,
        out_shape=wide,
        in_specs=[VMEM] * 5,
        out_specs=VMEM,
        compiler_params=SMALL,
        name="halo_product",
    )(partial, outer, inner, halo_blocks, masks)
    return (solution, product)


def solution(mesh):
    in_specs = (
        P(("section", "dom"), None, None),
        P(("section", "dom"), None, None),
        P(("section", "dom"), None, None),
        P(("section", "dom"), None, None, None),
        P(("section", "dom"), None, None, None),
        P(("section", "dom"), None, None, None),
        P(("section", "dom"), None),
        P(("section", "dom"), None),
        P(("section", "dom"), None),
    )
    out_specs = (P(("section", "dom"), None, None), P(("section", "dom"), None, None))
    return jax.shard_map(
        on_device, mesh=mesh, in_specs=in_specs, out_specs=out_specs, check_vma=False
    )
```

```python
import jax
import jax.numpy as jnp
from jax import lax
from jax.experimental import pallas as pl
from jax.experimental.pallas import tpu as pltpu
from jax.sharding import PartitionSpec as P

RIM = 4

VMEM = pl.BlockSpec(memory_space=pltpu.VMEM)
SMEM = pl.BlockSpec(memory_space=pltpu.SMEM)
HBM = pl.BlockSpec(memory_space=pltpu.HBM)
SMALL = pltpu.CompilerParams(vmem_limit_bytes=16 * 1024 * 1024)


def mul(a, b):
    return jnp.dot(a, b, preferred_element_type=jnp.float32)


def narrow(a):
    return a.astype(jnp.bfloat16)


def sweep_kernel(
    rhs_far,
    inverse_far,
    lower_far,
    upper_far,
    lower_at_far,
    upper_at_far,
    base,
    response,
    payload,
    rhs,
    inverse,
    lower,
    upper,
    lower_at,
    upper_at,
    low_pair,
    low_second,
    upp_pair,
    upp_second,
    down,
    exact,
    fixed,
    arrived,
):
    rows, count, width = rhs.shape
    slots = lower.shape[1]
    upper_slots = upper.shape[1]
    near = count + width
    last = rows - 1
    half = rows // 2
    parts = [
        (inverse_far, inverse),
        (rhs_far, rhs),
        (lower_far.at[:half], lower.at[:half]),
        (lower_at_far, lower_at),
        (lower_far.at[half:], lower.at[half:]),
        (upper_far, upper),
        (upper_at_far, upper_at),
    ]
    copies = [
        pltpu.make_async_copy(far, here, arrived.at[i]) for i, (far, here) in enumerate(parts)
    ]
    for copy in copies:
        copy.start()
    eye = narrow(
        lax.broadcasted_iota(jnp.int32, (width, width), 0)
        == lax.broadcasted_iota(jnp.int32, (width, width), 1)
    )
    down[:, :count] = jnp.zeros((rows + 1, count, width), jnp.bfloat16)
    response[:, :near] = jnp.zeros((rows + 1, near, width), jnp.bfloat16)
    for k in range(rows):
        down[k, count:] = eye
        response[k, near:] = eye
    down[rows, count:] = jnp.zeros_like(eye)
    response[rows, near:] = jnp.zeros_like(eye)

    def piece(blocks, m):
        return blocks[m * width : (m + 1) * width]

    def named(at, k, row, blocks, many):
        return sum(
            jnp.where(at[m, k] == row, piece(blocks, m), 0.0) for m in range(1, many)
        )

    def sources(held, at, k, skipped, many):
        picked = []
        for m in range(1, many):
            row = at[m, k]
            picked.append(held[row if skipped is None else jnp.where(row == skipped, rows, row)])
        return jnp.concatenate(picked, axis=1)

    def apart(left, right, own, other):
        zero = jnp.zeros_like(own)
        sides = [jnp.concatenate([own, zero], axis=1), jnp.concatenate([zero, other], axis=1)]
        return mul(jnp.concatenate([left, right], axis=1), jnp.concatenate(sides, axis=0))

    def scaled(k, parts):
        lefts = [jnp.concatenate(parts(j), axis=0) for j in (k, k + 1)]
        both = apart(*lefts, inverse[k], inverse[k + 1])
        return {k: both[:, :width], k + 1: both[:, width:]}

    def ready(at, many, places, of, extra=()):
        links = []
        for a, b in places:
            tail = of[b][of[b].shape[0] - many * width :]
            links.append(narrow(named(at, b, a, tail, many)))
        narrow_a = [narrow(of[a]) for a, _ in places]
        lefts = narrow_a
        if extra:
            lefts = [jnp.concatenate(both, axis=0) for both in zip(narrow_a, extra)]
        both = apart(*lefts, *links)
        return narrow_a, [both[:, :width], both[:, width:]], links

    def ready_down(p, of):
        places = [(2 * p, 2 * p + 1), (2 * p + 2, 2 * p + 3)]
        narrow_a, through, _ = ready(lower_at, slots, places, of)
        for i, (a, b) in enumerate(places):
            free_a = -of[a][count:near]
            free_b = through[i][count:near] - of[b][count:near]
            if p + i == 0:
                inner = sum(piece(of[a][count:], m) for m in range(1, slots))
                free_a = free_a - inner
                inner = sum(piece(through[i][count:], m) for m in range(1, slots))
                free_b = free_b + inner - named(lower_at, b, b, of[b][count:], slots)
            else:
                low_pair[p + i, :, :width] = narrow_a[i][near:]
                low_pair[p + i, :, width:] = narrow(through[i][near:])
                low_second[p + i] = narrow(of[b][near:])
            exact[a, :count] = of[a][:count]
            exact[a, count:] = free_a
            exact[b, :count] = of[b][:count] - through[i][:count]
            exact[b, count:] = free_b

    def go_down(p):
        a, b = 2 * p, 2 * p + 1
        of_a, of_b = exact[a], exact[b]
        if p > 0:
            first = mul(sources(down, lower_at, a, None, slots), low_pair[p])
            second = mul(sources(down, lower_at, b, a, slots), low_second[p])
            of_a = of_a - first[:, :width]
            of_b = of_b + first[:, width:] - second
            exact[a] = of_a
            exact[b] = of_b
        down[a] = narrow(of_a)
        down[b] = narrow(of_b)

    def ready_up(p, of, extra=()):
        places = [(last - 2 * (p + i), last - 2 * (p + i) - 1) for i in range(2)]
        narrow_a, through, links = ready(upper_at, upper_slots, places, of, extra)
        size = upper_slots * width
        for i, (a, b) in enumerate(places):
            free_a = -of[a][:width]
            free_b = through[i][:width] - of[b][:width]
            if p + i == 0:
                free_a = free_a - sum(piece(of[a], m) for m in range(1, upper_slots))
                inner = sum(piece(through[i], m) for m in range(1, upper_slots))
                free_b = free_b + inner - named(upper_at, b, b, of[b], upper_slots)
            else:
                upp_pair[p + i, :, :width] = narrow_a[i][width:]
                upp_pair[p + i, :, width:] = narrow(through[i][width:size])
                upp_second[p + i] = narrow(of[b][width:])
            fixed[a] = free_a
            fixed[b] = free_b
        return links, [value[size:] for value in through]

    def go_up(p, passed):
        a = last - 2 * p
        b = a - 1
        of_a = exact[a]
        of_b = exact[b] - passed
        free_a = fixed[a]
        free_b = fixed[b]
        if p > 0:
            first = mul(sources(response, upper_at, a, None, upper_slots), upp_pair[p])
            second = mul(sources(response, upper_at, b, a, upper_slots), upp_second[p])
            of_a = of_a - first[:near, :width]
            of_b = of_b + first[:near, width:] - second[:near]
            free_a = free_a - first[near:, :width]
            free_b = free_b + first[near:, width:] - second[near:]
        for k, value, free in ((a, of_a, free_a), (b, of_b, free_b)):
            base[k] = value[:count]
            response[k, :near] = narrow(value)
            response[k, near:] = narrow(free)

    pairs = rows // 2
    middle = pairs // 2

    def lower_part(k):
        return [narrow(rhs[k]), lower[k].reshape(slots * width, width)]

    def upper_part(k):
        return [upper[k].reshape(upper_slots * width, width)]

    for copy in copies[:4]:
        copy.wait()
    for p in range(0, middle, 2):
        ready_down(p, scaled(2 * p, lower_part) | scaled(2 * p + 2, lower_part))
    go_down(0)
    for copy in copies[4:]:
        copy.wait()
    of_low, of_upp = {}, {}
    for k in range(half, rows, 2):
        for j, value in scaled(k, lambda j: lower_part(j) + upper_part(j)).items():
            of_low[j] = value[: count + slots * width]
            of_upp[j] = value[count + slots * width :]
    for p in range(middle, pairs, 2):
        ready_down(p, of_low)
    links = []
    for p in range(1, pairs):
        go_down(p)
        if p % 2 == 1 and p - 1 < middle:
            links += ready_up(p - 1, of_upp)[0]
    far = near + width
    payload[:near] = down[last]
    passed = []
    for p in range(middle, pairs, 2):
        a = last - 2 * p
        of_upp = scaled(a - 1, upper_part) | scaled(a - 3, upper_part)
        passed += ready_up(p, of_upp, (down[a], down[a - 2]))[1]
    early = []
    for p in range(0, middle, 2):
        a = last - 2 * p
        both = apart(down[a], down[a - 2], links[p], links[p + 1])
        early += [both[:, :width], both[:, width:]]
    for p, value in enumerate(early + passed):
        go_up(p, value)

    payload[near + far :] = response[last, near:]
    payload[near : near + far] = response[0]


def compose_kernel(axis, bit, final, mine, theirs, *refs):
    prior, sent, inner, prior_out = refs[:4] if bit > 1 else (None, *refs[:3])
    width = mine.shape[1]
    count = (mine.shape[0] - 4 * width) // 2
    near = count + width
    me = lax.axis_index(axis)
    place = lax.rem(lax.div(me, bit), 2)
    mid = near + count
    far = near + near + width
    blank = jnp.zeros((width, width), jnp.float32)

    def join(a, b):
        sides = [b[count:near], b[mid : mid + width]]
        across = mul(a[:near], jnp.concatenate(sides, axis=1))
        ahead = jnp.concatenate([b[:count].astype(jnp.float32), blank], axis=0)
        joined = narrow(across[:, :width] + ahead)
        ahead = jnp.concatenate([b[near:mid].astype(jnp.float32), blank], axis=0)
        between = narrow(across[:, width:] + ahead)
        first = mul(between, a[mid + width : far]) + a[near : 2 * near].astype(jnp.float32)
        inner[:near] = a[:near]
        inner[near : 2 * near] = between
        inner[2 * near :] = b[mid + width : far]
        prior_out[...] = a[far:]
        if final:
            refs[-1][...] = joined[:count]
            above = lax.rem(lax.div(me, 2 * bit), 2) == 1

            @pl.when(above)
            def _():
                sent[...] = narrow(first)

            @pl.when(jnp.logical_not(above))
            def _():
                sent[:count] = joined[:count]
                sent[count:] = b[far:]

        else:
            sent[:near] = joined
            sent[near : 2 * near] = narrow(first)
            sent[2 * near : far] = narrow(mul(b[mid + width : far], a[mid + width : far]))
            sent[far:] = b[far:]

    @pl.when(place == 0)
    def _():
        join(mine, theirs)

    @pl.when(place == 1)
    def _():
        join(theirs, mine)

    if prior is not None:
        lowest = jnp.logical_and(place == 1, lax.rem(me, bit) == 0)

        @pl.when(jnp.logical_not(lowest))
        def _():
            prior_out[...] = prior[...]


def fold_kernel(axis, levels, *refs):
    base, response = refs[:2]
    inner = refs[2 : 1 + levels]
    diagonal_far, folded, folded_response, inflow_map, outflow_map = refs[1 + levels : 6 + levels]
    diagonal, arrived = refs[6 + levels :]
    copy = pltpu.make_async_copy(diagonal_far, diagonal, arrived)
    copy.start()
    rows, count, width = base.shape
    near = count + width
    me = lax.axis_index(axis)

    upper = lax.div(me, 1 << (levels - 1)) == 1
    across = lax.broadcasted_iota(jnp.int32, (near, width), 1) + count
    unit = jnp.where(lax.broadcasted_iota(jnp.int32, (near, width), 0) == across, 1.0, 0.0)
    inflow = jnp.where(upper, unit, 0.0)
    outflow = jnp.where(upper, 0.0, unit)
    blank = jnp.zeros((width, width), jnp.float32)
    for level in range(levels - 2, -1, -1):
        part = inner[level]
        upper = lax.rem(lax.div(me, 1 << level), 2) == 1
        known = jnp.concatenate([part[:count].astype(jnp.float32), blank], axis=0)
        down = known + mul(narrow(inflow), part[count:near])
        both = narrow(jnp.concatenate([inflow, outflow], axis=1))
        known = jnp.concatenate([part[near : near + count].astype(jnp.float32), blank], axis=0)
        up = known + mul(both, part[near + count :])
        inflow, outflow = jnp.where(upper, down, inflow), jnp.where(upper, outflow, up)

    inflow_map[...] = narrow(inflow)
    outflow_map[...] = narrow(outflow)
    both = narrow(jnp.concatenate([inflow, outflow], axis=1))
    for k in range(rows):
        value = mul(both, response[k, count:])
        folded[k] = base[k] + value[:count]
        folded_response[k] = narrow(value[count:])
    copy.wait()


def chain_kernel(
    axes, levels, own, theirs, base, response, solution, rounded, brought, near_rows, far_rows
):
    rows, count, width = base.shape
    side = lax.rem(lax.axis_index(axes[1]), 2)
    upper = lax.div(lax.axis_index(axes[0]), 1 << (levels - 1)) == 1
    down = theirs[:count].astype(jnp.float32)
    up = down + mul(own[...], theirs[count:])
    z = narrow(jnp.where(upper, down, up))
    brought[...] = z
    values = []
    for k in range(rows):
        value = base[k] + mul(z, response[k])
        solution[k] = value
        values.append(narrow(value))
        rounded[k] = values[k]
    rim = near_rows.shape[0]
    for odd, to_low, to_high in ((0, far_rows, near_rows), (1, near_rows, far_rows)):

        @pl.when(side == odd)
        def _(to_low=to_low, to_high=to_high):
            for e in range(rim):
                to_low[e] = values[e]
                to_high[e] = values[rows - rim + e]


def local_kernel(
    axes,
    levels,
    rounded,
    brought,
    inflow_map,
    outflow_map,
    prior,
    theirs,
    solved,
    diagonal,
    lower,
    upper,
    lower_at_far,
    upper_at_far,
    halo_at_far,
    partial,
    solution,
    masks,
    held,
    last_block,
    lower_at,
    upper_at,
    halo_at,
    arrived,
):
    parts = [
        (lower_at_far, lower_at),
        (upper_at_far, upper_at),
        (halo_at_far, halo_at),
        (solved, solution),
    ]
    copies = [
        pltpu.make_async_copy(source, target, arrived.at[i])
        for i, (source, target) in enumerate(parts)
    ]
    for copy in copies:
        copy.start()
    rows, slots, width, _ = lower.shape
    upper_slots = upper.shape[1]
    count = brought.shape[0]
    me = lax.axis_index(axes[0])
    last_block[...] = prior[...]

    @pl.when(me == 1 << (levels - 1))
    def _():
        last_block[...] = theirs[count:]

    z = brought[...]
    after = narrow(outflow_map[:count].astype(jnp.float32) + mul(z, outflow_map[count:]))
    before = inflow_map[:count].astype(jnp.float32) + mul(z, inflow_map[count:])
    before = narrow(before).astype(jnp.float32) + mul(rounded[0], last_block[...])
    before = narrow(jnp.where(me > 0, before, 0.0))
    held[:rows] = rounded[...]
    held[rows] = before
    held[rows + 1] = after
    for k in range(rows):
        source = jnp.concatenate([rounded[k], after], axis=1)
        total = mul(source, jnp.concatenate([diagonal[k], upper[k, 0]], axis=0))
        partial[k] = total + mul(before, lower[k, 0])
    for copy in copies[:3]:
        copy.wait()
    for k in range(rows):
        source = []
        for m in range(1, slots):
            at = lower_at[m, k]
            source.append(held[jnp.where(at == k, rows, at)])
        total = mul(
            jnp.concatenate(source, axis=1), lower[k, 1:].reshape((slots - 1) * width, width)
        )
        source = []
        for m in range(1, upper_slots):
            at = upper_at[m, k]
            source.append(held[jnp.where(at == k, rows + 1, at)])
        partial[k] += total + mul(
            jnp.concatenate(source, axis=1),
            upper[k, 1:].reshape((upper_slots - 1) * width, width),
        )
    _, picked, places, _, _ = masks.shape
    for k in range(rows):
        for m in range(picked):
            at = halo_at[m + 1, k]
            for j in range(places):
                mask = jnp.where(at == j, 1.0, 0.0)
                masks[k, m, j] = narrow(jnp.full((count, width), mask, jnp.float32))
    copies[3].wait()


def halo_kernel(axis, partial, outer, inner, halo, masks, product):
    rows, slots, width, _ = halo.shape
    rim = inner.shape[0]
    side = lax.rem(lax.axis_index(axis), 2)

    def add(left, right):
        rim_rows = [left[e] for e in range(rim)] + [right[e] for e in range(rim)]
        for k in range(rows):
            source = [rim_rows[k % (2 * rim)]]
            for m in range(1, slots):
                source.append(sum(masks[k, m - 1, j] * rim_rows[j] for j in range(2 * rim)))
            product[k] = partial[k] + mul(
                jnp.concatenate(source, axis=1), halo[k].reshape(slots * width, width)
            )

    @pl.when(side == 0)
    def _():
        add(outer, inner)

    @pl.when(side == 1)
    def _():
        add(inner, outer)


def trade(block, axis, bit):
    count = lax.axis_size(axis)
    return lax.ppermute(block, axis, [(i, i ^ bit) for i in range(count)])


def swaps(block, axis, first):
    count = lax.axis_size(axis)
    pairs = []
    for low in range(first, count - 1, 2):
        pairs += [(low, low + 1), (low + 1, low)]
    return lax.ppermute(block, axis, pairs)


def on_device(
    right_sides,
    diag_inverse,
    diag_blocks,
    lower_blocks,
    upper_blocks,
    halo_blocks,
    lower_index,
    upper_index,
    halo_index,
):
    rows, count, width = right_sides.shape
    lower_at, upper_at, halo_at = lower_index.T, upper_index.T, halo_index.T
    slots = lower_blocks.shape[1]
    upper_slots = upper_blocks.shape[1]
    groups = lax.axis_size("section")
    near = count + width
    far = near + width
    wide = jax.ShapeDtypeStruct((rows, count, width), jnp.float32)

    indices = [
        pltpu.with_memory_space_constraint(a, pltpu.HBM) for a in (lower_at, upper_at, halo_at)
    ]
    base, response, payload = pl.pallas_call(
        sweep_kernel,
        out_shape=(
            wide,
            jax.ShapeDtypeStruct((rows + 1, far, width), jnp.bfloat16),
            jax.ShapeDtypeStruct((near + far + width, width), jnp.bfloat16),
        ),
        in_specs=[HBM] * 6,
        out_specs=(VMEM,) * 3,
        scratch_shapes=[
            pltpu.VMEM(right_sides.shape, right_sides.dtype),
            pltpu.VMEM(diag_inverse.shape, diag_inverse.dtype),
            pltpu.VMEM(lower_blocks.shape, lower_blocks.dtype),
            pltpu.VMEM(upper_blocks.shape, upper_blocks.dtype),
            pltpu.SMEM(lower_at.shape, jnp.int32),
            pltpu.SMEM(upper_at.shape, jnp.int32),
            pltpu.VMEM((rows // 2, (slots - 1) * width, 2 * width), jnp.bfloat16),
            pltpu.VMEM((rows // 2, (slots - 1) * width, width), jnp.bfloat16),
            pltpu.VMEM((rows // 2, (upper_slots - 1) * width, 2 * width), jnp.bfloat16),
            pltpu.VMEM((rows // 2, (upper_slots - 1) * width, width), jnp.bfloat16),
            pltpu.VMEM((rows + 1, near, width), jnp.bfloat16),
            pltpu.VMEM((rows, near, width), jnp.float32),
            pltpu.VMEM((rows, width, width), jnp.float32),
            pltpu.SemaphoreType.DMA((7,)),
        ],
        compiler_params=SMALL,
        name="sweeps",
    )(
        *(
            pltpu.with_memory_space_constraint(a, pltpu.HBM)
            for a in (right_sides, diag_inverse, lower_blocks, upper_blocks)
        ),
        *indices[:2],
    )

    levels = groups.bit_length() - 1
    segment = payload.shape[0]
    bits = jnp.bfloat16
    prior = []
    inner = []
    for level in range(levels - 1):
        theirs = trade(payload, "section", 1 << level)
        final = level == levels - 2

        def compose(*refs, bit=1 << level, final=final):
            compose_kernel("section", bit, final, *refs)

        payload, between, *prior = pl.pallas_call(
            compose,
            out_shape=(
                jax.ShapeDtypeStruct((near if final else segment, width), bits),
                jax.ShapeDtypeStruct((near + far, width), bits),
                jax.ShapeDtypeStruct((width, width), bits),
            )
            + (jax.ShapeDtypeStruct((count, width), bits),) * final,
            in_specs=[VMEM] * (2 + len(prior)),
            out_specs=(VMEM,) * (3 + final),
            compiler_params=SMALL,
            name="compose",
        )(payload, theirs, *prior)
        inner.append(between)
    prior, own = prior
    theirs = trade(payload, "section", 1 << (levels - 1))

    def fold(*refs):
        fold_kernel("section", levels, *refs)

    base, response, inflow_map, outflow_map, diagonal = pl.pallas_call(
        fold,
        out_shape=(
            wide,
            jax.ShapeDtypeStruct((rows, width, width), bits),
            jax.ShapeDtypeStruct((near, width), bits),
            jax.ShapeDtypeStruct((near, width), bits),
            jax.ShapeDtypeStruct(diag_blocks.shape, diag_blocks.dtype),
        ),
        in_specs=[VMEM] * (1 + levels) + [HBM],
        out_specs=(VMEM,) * 5,
        scratch_shapes=[pltpu.SemaphoreType.DMA(())],
        compiler_params=SMALL,
        name="fold",
    )(base, response, *inner, pltpu.with_memory_space_constraint(diag_blocks, pltpu.HBM))

    def chain(*refs):
        chain_kernel(("section", "dom"), levels, *refs)

    solved, rounded, brought, inner, outer = pl.pallas_call(
        chain,
        out_shape=(
            wide,
            jax.ShapeDtypeStruct((rows, count, width), bits),
            jax.ShapeDtypeStruct((count, width), bits),
            jax.ShapeDtypeStruct((RIM, count, width), bits),
            jax.ShapeDtypeStruct((RIM, count, width), bits),
        ),
        in_specs=[VMEM] * 4,
        out_specs=(VMEM,) * 5,
        compiler_params=SMALL,
        name="chain",
    )(own, theirs, base, response)

    outer = swaps(outer, "dom", 1)
    inner = swaps(inner, "dom", 0)

    def local(*refs):
        local_kernel(("section", "dom"), levels, *refs)

    masks = (rows, halo_blocks.shape[1] - 1, 2 * RIM, count, width)
    partial, solution, masks = pl.pallas_call(
        local,
        out_shape=(wide, wide, jax.ShapeDtypeStruct(masks, bits)),
        in_specs=[VMEM] * 10 + [HBM] * 3,
        out_specs=(VMEM, HBM, VMEM),
        scratch_shapes=[
            pltpu.VMEM((rows + 2, count, width), bits),
            pltpu.VMEM((width, width), bits),
        ]
        + [pltpu.SMEM(a.shape, jnp.int32) for a in indices]
        + [pltpu.SemaphoreType.DMA((4,))],
        compiler_params=SMALL,
        name="local_product",
    )(
        rounded,
        brought,
        inflow_map,
        outflow_map,
        prior,
        theirs,
        solved,
        diagonal,
        lower_blocks,
        upper_blocks,
        *indices,
    )

    def halo(*refs):
        halo_kernel("dom", *refs)

    product = pl.pallas_call(
        halo,
        out_shape=wide,
        in_specs=[VMEM] * 5,
        out_specs=VMEM,
        compiler_params=SMALL,
        name="halo_product",
    )(partial, outer, inner, halo_blocks, masks)
    return (solution, product)


def solution(mesh):
    in_specs = (
        P(("section", "dom"), None, None),
        P(("section", "dom"), None, None),
        P(("section", "dom"), None, None),
        P(("section", "dom"), None, None, None),
        P(("section", "dom"), None, None, None),
        P(("section", "dom"), None, None, None),
        P(("section", "dom"), None),
        P(("section", "dom"), None),
        P(("section", "dom"), None),
    )
    out_specs = (P(("section", "dom"), None, None), P(("section", "dom"), None, None))
    return jax.shard_map(
        on_device, mesh=mesh, in_specs=in_specs, out_specs=out_specs, check_vma=False
    )
```

```python
import jax
import jax.numpy as jnp
from jax import lax
from jax.experimental import pallas as pl
from jax.experimental.pallas import tpu as pltpu
from jax.sharding import PartitionSpec as P

RIM = 4

VMEM = pl.BlockSpec(memory_space=pltpu.VMEM)
SMEM = pl.BlockSpec(memory_space=pltpu.SMEM)
HBM = pl.BlockSpec(memory_space=pltpu.HBM)
SMALL = pltpu.CompilerParams(vmem_limit_bytes=16 * 1024 * 1024)


def mul(a, b):
    return jnp.dot(a, b, preferred_element_type=jnp.float32)


def narrow(a):
    return a.astype(jnp.bfloat16)


def sweep_kernel(
    rhs_far,
    inverse_far,
    lower_far,
    upper_far,
    lower_at_far,
    upper_at_far,
    base,
    response,
    payload,
    rhs,
    inverse,
    lower,
    upper,
    lower_at,
    upper_at,
    low_pair,
    low_second,
    upp_pair,
    upp_second,
    down,
    exact,
    fixed,
    arrived,
):
    rows, count, width = rhs.shape
    slots = lower.shape[1]
    upper_slots = upper.shape[1]
    near = count + width
    last = rows - 1
    half = rows // 2
    parts = [
        (inverse_far, inverse),
        (rhs_far, rhs),
        (lower_far.at[:half], lower.at[:half]),
        (lower_at_far, lower_at),
        (lower_far.at[half:], lower.at[half:]),
        (upper_far, upper),
        (upper_at_far, upper_at),
    ]
    copies = [
        pltpu.make_async_copy(far, here, arrived.at[i]) for i, (far, here) in enumerate(parts)
    ]
    for copy in copies:
        copy.start()
    eye = narrow(
        lax.broadcasted_iota(jnp.int32, (width, width), 0)
        == lax.broadcasted_iota(jnp.int32, (width, width), 1)
    )
    down[:, :count] = jnp.zeros((rows + 1, count, width), jnp.bfloat16)
    response[:, :near] = jnp.zeros((rows + 1, near, width), jnp.bfloat16)
    for k in range(rows):
        down[k, count:] = eye
        response[k, near:] = eye
    down[rows, count:] = jnp.zeros_like(eye)
    response[rows, near:] = jnp.zeros_like(eye)

    def piece(blocks, m):
        return blocks[m * width : (m + 1) * width]

    def named(at, k, row, blocks, many):
        return sum(
            jnp.where(at[m, k] == row, piece(blocks, m), 0.0) for m in range(1, many)
        )

    def sources(held, at, k, skipped, many):
        picked = []
        for m in range(1, many):
            row = at[m, k]
            picked.append(held[row if skipped is None else jnp.where(row == skipped, rows, row)])
        return jnp.concatenate(picked, axis=1)

    def apart(left, right, own, other):
        zero = jnp.zeros_like(own)
        sides = [jnp.concatenate([own, zero], axis=1), jnp.concatenate([zero, other], axis=1)]
        return mul(jnp.concatenate([left, right], axis=1), jnp.concatenate(sides, axis=0))

    def scaled(k, parts):
        lefts = [jnp.concatenate(parts(j), axis=0) for j in (k, k + 1)]
        both = apart(*lefts, inverse[k], inverse[k + 1])
        return {k: both[:, :width], k + 1: both[:, width:]}

    def ready(at, many, places, of):
        links = []
        for a, b in places:
            tail = of[b][of[b].shape[0] - many * width :]
            links.append(narrow(named(at, b, a, tail, many)))
        narrow_a = [narrow(of[a]) for a, _ in places]
        both = apart(*narrow_a, *links)
        return narrow_a, [both[:, :width], both[:, width:]], links

    def ready_down(p, of):
        places = [(2 * p, 2 * p + 1), (2 * p + 2, 2 * p + 3)]
        narrow_a, through, _ = ready(lower_at, slots, places, of)
        for i, (a, b) in enumerate(places):
            free_a = -of[a][count:near]
            free_b = through[i][count:near] - of[b][count:near]
            if p + i == 0:
                inner = sum(piece(of[a][count:], m) for m in range(1, slots))
                free_a = free_a - inner
                inner = sum(piece(through[i][count:], m) for m in range(1, slots))
                free_b = free_b + inner - named(lower_at, b, b, of[b][count:], slots)
            else:
                low_pair[p + i, :, :width] = narrow_a[i][near:]
                low_pair[p + i, :, width:] = narrow(through[i][near:])
                low_second[p + i] = narrow(of[b][near:])
            exact[a, :count] = of[a][:count]
            exact[a, count:] = free_a
            exact[b, :count] = of[b][:count] - through[i][:count]
            exact[b, count:] = free_b

    def go_down(p):
        a, b = 2 * p, 2 * p + 1
        of_a, of_b = exact[a], exact[b]
        if p > 0:
            first = mul(sources(down, lower_at, a, None, slots), low_pair[p])
            second = mul(sources(down, lower_at, b, a, slots), low_second[p])
            of_a = of_a - first[:, :width]
            of_b = of_b + first[:, width:] - second
            exact[a] = of_a
            exact[b] = of_b
        down[a] = narrow(of_a)
        down[b] = narrow(of_b)

    def ready_up(p, of):
        places = [(last - 2 * (p + i), last - 2 * (p + i) - 1) for i in range(2)]
        narrow_a, through, links = ready(upper_at, upper_slots, places, of)
        for i, (a, b) in enumerate(places):
            free_a = -of[a][:width]
            free_b = through[i][:width] - of[b][:width]
            if p + i == 0:
                free_a = free_a - sum(piece(of[a], m) for m in range(1, upper_slots))
                inner = sum(piece(through[i], m) for m in range(1, upper_slots))
                free_b = free_b + inner - named(upper_at, b, b, of[b], upper_slots)
            else:
                upp_pair[p + i, :, :width] = narrow_a[i][width:]
                upp_pair[p + i, :, width:] = narrow(through[i][width:])
                upp_second[p + i] = narrow(of[b][width:])
            fixed[a] = free_a
            fixed[b] = free_b
        return links

    def go_up(p, passed):
        a = last - 2 * p
        b = a - 1
        of_a = exact[a]
        of_b = exact[b] - passed
        free_a = fixed[a]
        free_b = fixed[b]
        if p > 0:
            first = mul(sources(response, upper_at, a, None, upper_slots), upp_pair[p])
            second = mul(sources(response, upper_at, b, a, upper_slots), upp_second[p])
            of_a = of_a - first[:near, :width]
            of_b = of_b + first[:near, width:] - second[:near]
            free_a = free_a - first[near:, :width]
            free_b = free_b + first[near:, width:] - second[near:]
        for k, value, free in ((a, of_a, free_a), (b, of_b, free_b)):
            base[k] = value[:count]
            response[k, :near] = narrow(value)
            response[k, near:] = narrow(free)

    pairs = rows // 2
    middle = pairs // 2

    def lower_part(k):
        return [narrow(rhs[k]), lower[k].reshape(slots * width, width)]

    def upper_part(k):
        return [upper[k].reshape(upper_slots * width, width)]

    for copy in copies[:4]:
        copy.wait()
    for p in range(0, middle, 2):
        ready_down(p, scaled(2 * p, lower_part) | scaled(2 * p + 2, lower_part))
    go_down(0)
    for copy in copies[4:]:
        copy.wait()
    of_low, of_upp = {}, {}
    for k in range(half, rows, 2):
        for j, value in scaled(k, lambda j: lower_part(j) + upper_part(j)).items():
            of_low[j] = value[: count + slots * width]
            of_upp[j] = value[count + slots * width :]
    for p in range(middle, pairs, 2):
        ready_down(p, of_low)
    links = []
    for p in range(1, pairs):
        go_down(p)
        if p % 2 == 1 and p - 1 < middle:
            links += ready_up(p - 1, of_upp)
    far = near + width
    payload[:near] = down[last]
    for p in range(middle, pairs, 2):
        a = last - 2 * p
        links += ready_up(p, scaled(a - 1, upper_part) | scaled(a - 3, upper_part))
    for p in range(0, pairs, 2):
        a = last - 2 * p
        passed = apart(down[a], down[a - 2], links[p], links[p + 1])
        go_up(p, passed[:, :width])
        go_up(p + 1, passed[:, width:])

    payload[near + far :] = response[last, near:]
    payload[near : near + far] = response[0]


def compose_kernel(axis, bit, final, mine, theirs, *refs):
    prior, sent, inner, prior_out = refs[:4] if bit > 1 else (None, *refs[:3])
    width = mine.shape[1]
    count = (mine.shape[0] - 4 * width) // 2
    near = count + width
    me = lax.axis_index(axis)
    place = lax.rem(lax.div(me, bit), 2)
    mid = near + count
    far = near + near + width
    blank = jnp.zeros((width, width), jnp.float32)

    def join(a, b):
        sides = [b[count:near], b[mid : mid + width]]
        across = mul(a[:near], jnp.concatenate(sides, axis=1))
        ahead = jnp.concatenate([b[:count].astype(jnp.float32), blank], axis=0)
        joined = narrow(across[:, :width] + ahead)
        ahead = jnp.concatenate([b[near:mid].astype(jnp.float32), blank], axis=0)
        between = narrow(across[:, width:] + ahead)
        first = mul(between, a[mid + width : far]) + a[near : 2 * near].astype(jnp.float32)
        inner[:near] = a[:near]
        inner[near : 2 * near] = between
        inner[2 * near :] = b[mid + width : far]
        prior_out[...] = a[far:]
        if final:
            refs[-1][...] = joined[:count]
            above = lax.rem(lax.div(me, 2 * bit), 2) == 1

            @pl.when(above)
            def _():
                sent[...] = narrow(first)

            @pl.when(jnp.logical_not(above))
            def _():
                sent[:count] = joined[:count]
                sent[count:] = b[far:]

        else:
            sent[:near] = joined
            sent[near : 2 * near] = narrow(first)
            sent[2 * near : far] = narrow(mul(b[mid + width : far], a[mid + width : far]))
            sent[far:] = b[far:]

    @pl.when(place == 0)
    def _():
        join(mine, theirs)

    @pl.when(place == 1)
    def _():
        join(theirs, mine)

    if prior is not None:
        lowest = jnp.logical_and(place == 1, lax.rem(me, bit) == 0)

        @pl.when(jnp.logical_not(lowest))
        def _():
            prior_out[...] = prior[...]


def fold_kernel(axis, levels, *refs):
    base, response = refs[:2]
    inner = refs[2 : 1 + levels]
    diagonal_far, folded, folded_response, inflow_map, outflow_map = refs[1 + levels : 6 + levels]
    diagonal, arrived = refs[6 + levels :]
    copy = pltpu.make_async_copy(diagonal_far, diagonal, arrived)
    copy.start()
    rows, count, width = base.shape
    near = count + width
    me = lax.axis_index(axis)

    upper = lax.div(me, 1 << (levels - 1)) == 1
    across = lax.broadcasted_iota(jnp.int32, (near, width), 1) + count
    unit = jnp.where(lax.broadcasted_iota(jnp.int32, (near, width), 0) == across, 1.0, 0.0)
    inflow = jnp.where(upper, unit, 0.0)
    outflow = jnp.where(upper, 0.0, unit)
    blank = jnp.zeros((width, width), jnp.float32)
    for level in range(levels - 2, -1, -1):
        part = inner[level]
        upper = lax.rem(lax.div(me, 1 << level), 2) == 1
        known = jnp.concatenate([part[:count].astype(jnp.float32), blank], axis=0)
        down = known + mul(narrow(inflow), part[count:near])
        both = narrow(jnp.concatenate([inflow, outflow], axis=1))
        known = jnp.concatenate([part[near : near + count].astype(jnp.float32), blank], axis=0)
        up = known + mul(both, part[near + count :])
        inflow, outflow = jnp.where(upper, down, inflow), jnp.where(upper, outflow, up)

    inflow_map[...] = narrow(inflow)
    outflow_map[...] = narrow(outflow)
    both = narrow(jnp.concatenate([inflow, outflow], axis=1))
    for k in range(rows):
        value = mul(both, response[k, count:])
        folded[k] = base[k] + value[:count]
        folded_response[k] = narrow(value[count:])
    copy.wait()


def chain_kernel(
    axes, levels, own, theirs, base, response, solution, rounded, brought, near_rows, far_rows
):
    rows, count, width = base.shape
    side = lax.rem(lax.axis_index(axes[1]), 2)
    upper = lax.div(lax.axis_index(axes[0]), 1 << (levels - 1)) == 1
    down = theirs[:count].astype(jnp.float32)
    up = down + mul(own[...], theirs[count:])
    z = narrow(jnp.where(upper, down, up))
    brought[...] = z
    values = []
    for k in range(rows):
        value = base[k] + mul(z, response[k])
        solution[k] = value
        values.append(narrow(value))
        rounded[k] = values[k]
    rim = near_rows.shape[0]
    for odd, to_low, to_high in ((0, far_rows, near_rows), (1, near_rows, far_rows)):

        @pl.when(side == odd)
        def _(to_low=to_low, to_high=to_high):
            for e in range(rim):
                to_low[e] = values[e]
                to_high[e] = values[rows - rim + e]


def local_kernel(
    axes,
    levels,
    rounded,
    brought,
    inflow_map,
    outflow_map,
    prior,
    theirs,
    solved,
    diagonal,
    lower,
    upper,
    lower_at_far,
    upper_at_far,
    halo_at_far,
    partial,
    solution,
    masks,
    held,
    last_block,
    lower_at,
    upper_at,
    halo_at,
    arrived,
):
    parts = [
        (lower_at_far, lower_at),
        (upper_at_far, upper_at),
        (halo_at_far, halo_at),
        (solved, solution),
    ]
    copies = [
        pltpu.make_async_copy(source, target, arrived.at[i])
        for i, (source, target) in enumerate(parts)
    ]
    for copy in copies:
        copy.start()
    rows, slots, width, _ = lower.shape
    upper_slots = upper.shape[1]
    count = brought.shape[0]
    me = lax.axis_index(axes[0])
    last_block[...] = prior[...]

    @pl.when(me == 1 << (levels - 1))
    def _():
        last_block[...] = theirs[count:]

    z = brought[...]
    after = narrow(outflow_map[:count].astype(jnp.float32) + mul(z, outflow_map[count:]))
    before = inflow_map[:count].astype(jnp.float32) + mul(z, inflow_map[count:])
    before = narrow(before).astype(jnp.float32) + mul(rounded[0], last_block[...])
    before = narrow(jnp.where(me > 0, before, 0.0))
    held[:rows] = rounded[...]
    held[rows] = before
    held[rows + 1] = after
    for k in range(rows):
        source = jnp.concatenate([rounded[k], after], axis=1)
        total = mul(source, jnp.concatenate([diagonal[k], upper[k, 0]], axis=0))
        partial[k] = total + mul(before, lower[k, 0])
    for copy in copies[:3]:
        copy.wait()
    for k in range(rows):
        source = []
        for m in range(1, slots):
            at = lower_at[m, k]
            source.append(held[jnp.where(at == k, rows, at)])
        total = mul(
            jnp.concatenate(source, axis=1), lower[k, 1:].reshape((slots - 1) * width, width)
        )
        source = []
        for m in range(1, upper_slots):
            at = upper_at[m, k]
            source.append(held[jnp.where(at == k, rows + 1, at)])
        partial[k] += total + mul(
            jnp.concatenate(source, axis=1),
            upper[k, 1:].reshape((upper_slots - 1) * width, width),
        )
    _, picked, places, _, _ = masks.shape
    for k in range(rows):
        for m in range(picked):
            at = halo_at[m + 1, k]
            for j in range(places):
                mask = jnp.where(at == j, 1.0, 0.0)
                masks[k, m, j] = narrow(jnp.full((count, width), mask, jnp.float32))
    copies[3].wait()


def halo_kernel(axis, partial, outer, inner, halo, masks, product):
    rows, slots, width, _ = halo.shape
    rim = inner.shape[0]
    side = lax.rem(lax.axis_index(axis), 2)

    def add(left, right):
        rim_rows = [left[e] for e in range(rim)] + [right[e] for e in range(rim)]
        for k in range(rows):
            source = [rim_rows[k % (2 * rim)]]
            for m in range(1, slots):
                source.append(sum(masks[k, m - 1, j] * rim_rows[j] for j in range(2 * rim)))
            product[k] = partial[k] + mul(
                jnp.concatenate(source, axis=1), halo[k].reshape(slots * width, width)
            )

    @pl.when(side == 0)
    def _():
        add(outer, inner)

    @pl.when(side == 1)
    def _():
        add(inner, outer)


def trade(block, axis, bit):
    count = lax.axis_size(axis)
    return lax.ppermute(block, axis, [(i, i ^ bit) for i in range(count)])


def swaps(block, axis, first):
    count = lax.axis_size(axis)
    pairs = []
    for low in range(first, count - 1, 2):
        pairs += [(low, low + 1), (low + 1, low)]
    return lax.ppermute(block, axis, pairs)


def on_device(
    right_sides,
    diag_inverse,
    diag_blocks,
    lower_blocks,
    upper_blocks,
    halo_blocks,
    lower_index,
    upper_index,
    halo_index,
):
    rows, count, width = right_sides.shape
    lower_at, upper_at, halo_at = lower_index.T, upper_index.T, halo_index.T
    slots = lower_blocks.shape[1]
    upper_slots = upper_blocks.shape[1]
    groups = lax.axis_size("section")
    near = count + width
    far = near + width
    wide = jax.ShapeDtypeStruct((rows, count, width), jnp.float32)

    indices = [
        pltpu.with_memory_space_constraint(a, pltpu.HBM) for a in (lower_at, upper_at, halo_at)
    ]
    base, response, payload = pl.pallas_call(
        sweep_kernel,
        out_shape=(
            wide,
            jax.ShapeDtypeStruct((rows + 1, far, width), jnp.bfloat16),
            jax.ShapeDtypeStruct((near + far + width, width), jnp.bfloat16),
        ),
        in_specs=[HBM] * 6,
        out_specs=(VMEM,) * 3,
        scratch_shapes=[
            pltpu.VMEM(right_sides.shape, right_sides.dtype),
            pltpu.VMEM(diag_inverse.shape, diag_inverse.dtype),
            pltpu.VMEM(lower_blocks.shape, lower_blocks.dtype),
            pltpu.VMEM(upper_blocks.shape, upper_blocks.dtype),
            pltpu.SMEM(lower_at.shape, jnp.int32),
            pltpu.SMEM(upper_at.shape, jnp.int32),
            pltpu.VMEM((rows // 2, (slots - 1) * width, 2 * width), jnp.bfloat16),
            pltpu.VMEM((rows // 2, (slots - 1) * width, width), jnp.bfloat16),
            pltpu.VMEM((rows // 2, (upper_slots - 1) * width, 2 * width), jnp.bfloat16),
            pltpu.VMEM((rows // 2, (upper_slots - 1) * width, width), jnp.bfloat16),
            pltpu.VMEM((rows + 1, near, width), jnp.bfloat16),
            pltpu.VMEM((rows, near, width), jnp.float32),
            pltpu.VMEM((rows, width, width), jnp.float32),
            pltpu.SemaphoreType.DMA((7,)),
        ],
        compiler_params=SMALL,
        name="sweeps",
    )(
        *(
            pltpu.with_memory_space_constraint(a, pltpu.HBM)
            for a in (right_sides, diag_inverse, lower_blocks, upper_blocks)
        ),
        *indices[:2],
    )

    levels = groups.bit_length() - 1
    segment = payload.shape[0]
    bits = jnp.bfloat16
    prior = []
    inner = []
    for level in range(levels - 1):
        theirs = trade(payload, "section", 1 << level)
        final = level == levels - 2

        def compose(*refs, bit=1 << level, final=final):
            compose_kernel("section", bit, final, *refs)

        payload, between, *prior = pl.pallas_call(
            compose,
            out_shape=(
                jax.ShapeDtypeStruct((near if final else segment, width), bits),
                jax.ShapeDtypeStruct((near + far, width), bits),
                jax.ShapeDtypeStruct((width, width), bits),
            )
            + (jax.ShapeDtypeStruct((count, width), bits),) * final,
            in_specs=[VMEM] * (2 + len(prior)),
            out_specs=(VMEM,) * (3 + final),
            compiler_params=SMALL,
            name="compose",
        )(payload, theirs, *prior)
        inner.append(between)
    prior, own = prior
    theirs = trade(payload, "section", 1 << (levels - 1))

    def fold(*refs):
        fold_kernel("section", levels, *refs)

    base, response, inflow_map, outflow_map, diagonal = pl.pallas_call(
        fold,
        out_shape=(
            wide,
            jax.ShapeDtypeStruct((rows, width, width), bits),
            jax.ShapeDtypeStruct((near, width), bits),
            jax.ShapeDtypeStruct((near, width), bits),
            jax.ShapeDtypeStruct(diag_blocks.shape, diag_blocks.dtype),
        ),
        in_specs=[VMEM] * (1 + levels) + [HBM],
        out_specs=(VMEM,) * 5,
        scratch_shapes=[pltpu.SemaphoreType.DMA(())],
        compiler_params=SMALL,
        name="fold",
    )(base, response, *inner, pltpu.with_memory_space_constraint(diag_blocks, pltpu.HBM))

    def chain(*refs):
        chain_kernel(("section", "dom"), levels, *refs)

    solved, rounded, brought, inner, outer = pl.pallas_call(
        chain,
        out_shape=(
            wide,
            jax.ShapeDtypeStruct((rows, count, width), bits),
            jax.ShapeDtypeStruct((count, width), bits),
            jax.ShapeDtypeStruct((RIM, count, width), bits),
            jax.ShapeDtypeStruct((RIM, count, width), bits),
        ),
        in_specs=[VMEM] * 4,
        out_specs=(VMEM,) * 5,
        compiler_params=SMALL,
        name="chain",
    )(own, theirs, base, response)

    outer = swaps(outer, "dom", 1)
    inner = swaps(inner, "dom", 0)

    def local(*refs):
        local_kernel(("section", "dom"), levels, *refs)

    masks = (rows, halo_blocks.shape[1] - 1, 2 * RIM, count, width)
    partial, solution, masks = pl.pallas_call(
        local,
        out_shape=(wide, wide, jax.ShapeDtypeStruct(masks, bits)),
        in_specs=[VMEM] * 10 + [HBM] * 3,
        out_specs=(VMEM, HBM, VMEM),
        scratch_shapes=[
            pltpu.VMEM((rows + 2, count, width), bits),
            pltpu.VMEM((width, width), bits),
        ]
        + [pltpu.SMEM(a.shape, jnp.int32) for a in indices]
        + [pltpu.SemaphoreType.DMA((4,))],
        compiler_params=SMALL,
        name="local_product",
    )(
        rounded,
        brought,
        inflow_map,
        outflow_map,
        prior,
        theirs,
        solved,
        diagonal,
        lower_blocks,
        upper_blocks,
        *indices,
    )

    def halo(*refs):
        halo_kernel("dom", *refs)

    product = pl.pallas_call(
        halo,
        out_shape=wide,
        in_specs=[VMEM] * 5,
        out_specs=VMEM,
        compiler_params=SMALL,
        name="halo_product",
    )(partial, outer, inner, halo_blocks, masks)
    return (solution, product)


def solution(mesh):
    in_specs = (
        P(("section", "dom"), None, None),
        P(("section", "dom"), None, None),
        P(("section", "dom"), None, None),
        P(("section", "dom"), None, None, None),
        P(("section", "dom"), None, None, None),
        P(("section", "dom"), None, None, None),
        P(("section", "dom"), None),
        P(("section", "dom"), None),
        P(("section", "dom"), None),
    )
    out_specs = (P(("section", "dom"), None, None), P(("section", "dom"), None, None))
    return jax.shard_map(
        on_device, mesh=mesh, in_specs=in_specs, out_specs=out_specs, check_vma=False
    )
```

```python
import jax
import jax.numpy as jnp
from jax import lax
from jax.experimental import pallas as pl
from jax.experimental.pallas import tpu as pltpu
from jax.sharding import PartitionSpec as P

RIM = 4

VMEM = pl.BlockSpec(memory_space=pltpu.VMEM)
SMEM = pl.BlockSpec(memory_space=pltpu.SMEM)
HBM = pl.BlockSpec(memory_space=pltpu.HBM)
SMALL = pltpu.CompilerParams(vmem_limit_bytes=16 * 1024 * 1024)


def mul(a, b):
    return jnp.dot(a, b, preferred_element_type=jnp.float32)


def narrow(a):
    return a.astype(jnp.bfloat16)


def sweep_kernel(
    rhs_far,
    inverse_far,
    lower_far,
    upper_far,
    lower_at_far,
    upper_at_far,
    base,
    response,
    payload,
    rhs,
    inverse,
    lower,
    upper,
    lower_at,
    upper_at,
    low_pair,
    low_second,
    upp_pair,
    upp_second,
    down,
    exact,
    fixed,
    arrived,
):
    rows, count, width = rhs.shape
    slots = lower.shape[1]
    upper_slots = upper.shape[1]
    near = count + width
    last = rows - 1
    half = rows // 2
    parts = [
        (lower_far.at[:half], lower.at[:half]),
        (inverse_far.at[:half], inverse.at[:half]),
        (rhs_far.at[:half], rhs.at[:half]),
        (lower_at_far, lower_at),
        (inverse_far.at[half:], inverse.at[half:]),
        (rhs_far.at[half:], rhs.at[half:]),
        (lower_far.at[half:], lower.at[half:]),
        (upper_far, upper),
        (upper_at_far, upper_at),
    ]
    copies = [
        pltpu.make_async_copy(far, here, arrived.at[i]) for i, (far, here) in enumerate(parts)
    ]
    for copy in copies:
        copy.start()
    eye = narrow(
        lax.broadcasted_iota(jnp.int32, (width, width), 0)
        == lax.broadcasted_iota(jnp.int32, (width, width), 1)
    )
    down[:, :count] = jnp.zeros((rows + 1, count, width), jnp.bfloat16)
    response[:, :near] = jnp.zeros((rows + 1, near, width), jnp.bfloat16)
    for k in range(rows):
        down[k, count:] = eye
        response[k, near:] = eye
    down[rows, count:] = jnp.zeros_like(eye)
    response[rows, near:] = jnp.zeros_like(eye)

    def piece(blocks, m):
        return blocks[m * width : (m + 1) * width]

    def named(at, k, row, blocks, many):
        return sum(
            jnp.where(at[m, k] == row, piece(blocks, m), 0.0) for m in range(1, many)
        )

    def sources(held, at, k, skipped, many):
        picked = []
        for m in range(1, many):
            row = at[m, k]
            picked.append(held[row if skipped is None else jnp.where(row == skipped, rows, row)])
        return jnp.concatenate(picked, axis=1)

    def apart(left, right, own, other):
        zero = jnp.zeros_like(own)
        sides = [jnp.concatenate([own, zero], axis=1), jnp.concatenate([zero, other], axis=1)]
        return mul(jnp.concatenate([left, right], axis=1), jnp.concatenate(sides, axis=0))

    def ready(at, blocks, many, first, step, heads):
        of_a, of_b, links = [], [], []
        for a in (first, first + 2 * step):
            b = a + step
            lefts = [
                jnp.concatenate(heads(k) + [blocks[k].reshape(many * width, width)], axis=0)
                for k in (a, b)
            ]
            both = apart(*lefts, inverse[a], inverse[b])
            of_a.append(both[:, :width])
            of_b.append(both[:, width:])
            tail = both[both.shape[0] - many * width :, width:]
            links.append(narrow(named(at, b, a, tail, many)))
        narrow_a = [narrow(value) for value in of_a]
        both = apart(*narrow_a, *links)
        through = [both[:, :width], both[:, width:]]
        return of_a, narrow_a, of_b, through, links

    def ready_down(p):
        of_a, narrow_a, of_b, through, _ = ready(
            lower_at, lower, slots, 2 * p, 1, lambda k: [narrow(rhs[k])]
        )
        for i in range(2):
            a, b = 2 * (p + i), 2 * (p + i) + 1
            free_a = -of_a[i][count:near]
            free_b = through[i][count:near] - of_b[i][count:near]
            if p + i == 0:
                inner = sum(piece(of_a[i][count:], m) for m in range(1, slots))
                free_a = free_a - inner
                inner = sum(piece(through[i][count:], m) for m in range(1, slots))
                free_b = free_b + inner - named(lower_at, b, b, of_b[i][count:], slots)
            else:
                low_pair[p + i, :, :width] = narrow_a[i][near:]
                low_pair[p + i, :, width:] = narrow(through[i][near:])
                low_second[p + i] = narrow(of_b[i][near:])
            exact[a, :count] = of_a[i][:count]
            exact[a, count:] = free_a
            exact[b, :count] = of_b[i][:count] - through[i][:count]
            exact[b, count:] = free_b

    def go_down(p):
        a, b = 2 * p, 2 * p + 1
        of_a, of_b = exact[a], exact[b]
        if p > 0:
            first = mul(sources(down, lower_at, a, None, slots), low_pair[p])
            second = mul(sources(down, lower_at, b, a, slots), low_second[p])
            of_a = of_a - first[:, :width]
            of_b = of_b + first[:, width:] - second
            exact[a] = of_a
            exact[b] = of_b
        down[a] = narrow(of_a)
        down[b] = narrow(of_b)

    def ready_up(p):
        of_a, narrow_a, of_b, through, links = ready(
            upper_at, upper, upper_slots, last - 2 * p, -1, lambda k: []
        )
        for i in range(2):
            a = last - 2 * (p + i)
            b = a - 1
            free_a = -of_a[i][:width]
            free_b = through[i][:width] - of_b[i][:width]
            if p + i == 0:
                free_a = free_a - sum(piece(of_a[i], m) for m in range(1, upper_slots))
                inner = sum(piece(through[i], m) for m in range(1, upper_slots))
                free_b = free_b + inner - named(upper_at, b, b, of_b[i], upper_slots)
            else:
                upp_pair[p + i, :, :width] = narrow_a[i][width:]
                upp_pair[p + i, :, width:] = narrow(through[i][width:])
                upp_second[p + i] = narrow(of_b[i][width:])
            fixed[a] = free_a
            fixed[b] = free_b
        return links

    def go_up(p, passed):
        a = last - 2 * p
        b = a - 1
        of_a = exact[a]
        of_b = exact[b] - passed
        free_a = fixed[a]
        free_b = fixed[b]
        if p > 0:
            first = mul(sources(response, upper_at, a, None, upper_slots), upp_pair[p])
            second = mul(sources(response, upper_at, b, a, upper_slots), upp_second[p])
            of_a = of_a - first[:near, :width]
            of_b = of_b + first[:near, width:] - second[:near]
            free_a = free_a - first[near:, :width]
            free_b = free_b + first[near:, width:] - second[near:]
        for k, value, free in ((a, of_a, free_a), (b, of_b, free_b)):
            base[k] = value[:count]
            response[k, :near] = narrow(value)
            response[k, near:] = narrow(free)

    pairs = rows // 2
    for copy in copies[:4]:
        copy.wait()
    ready_down(0)
    go_down(0)
    for copy in copies[4:]:
        copy.wait()
    links = []
    for p in range(1, pairs):
        if p % 2 == 1 and p + 1 < pairs:
            ready_down(p + 1)
        go_down(p)
        if p % 2 == 1:
            links += ready_up(p - 1)
    far = near + width
    payload[:near] = down[last]
    for p in range(0, pairs, 2):
        a = last - 2 * p
        passed = apart(down[a], down[a - 2], links[p], links[p + 1])
        go_up(p, passed[:, :width])
        go_up(p + 1, passed[:, width:])

    payload[near + far :] = response[last, near:]
    payload[near : near + far] = response[0]


def compose_kernel(axis, bit, final, mine, theirs, *refs):
    prior, sent, inner, prior_out = refs[:4] if bit > 1 else (None, *refs[:3])
    width = mine.shape[1]
    count = (mine.shape[0] - 4 * width) // 2
    near = count + width
    me = lax.axis_index(axis)
    place = lax.rem(lax.div(me, bit), 2)
    mid = near + count
    far = near + near + width
    blank = jnp.zeros((width, width), jnp.float32)

    def join(a, b):
        sides = [b[count:near], b[mid : mid + width]]
        across = mul(a[:near], jnp.concatenate(sides, axis=1))
        ahead = jnp.concatenate([b[:count].astype(jnp.float32), blank], axis=0)
        joined = narrow(across[:, :width] + ahead)
        ahead = jnp.concatenate([b[near:mid].astype(jnp.float32), blank], axis=0)
        between = narrow(across[:, width:] + ahead)
        first = mul(between, a[mid + width : far]) + a[near : 2 * near].astype(jnp.float32)
        inner[:near] = a[:near]
        inner[near : 2 * near] = between
        inner[2 * near :] = b[mid + width : far]
        prior_out[...] = a[far:]
        if final:
            refs[-1][...] = joined[:count]
            above = lax.rem(lax.div(me, 2 * bit), 2) == 1

            @pl.when(above)
            def _():
                sent[...] = narrow(first)

            @pl.when(jnp.logical_not(above))
            def _():
                sent[:count] = joined[:count]
                sent[count:] = b[far:]

        else:
            sent[:near] = joined
            sent[near : 2 * near] = narrow(first)
            sent[2 * near : far] = narrow(mul(b[mid + width : far], a[mid + width : far]))
            sent[far:] = b[far:]

    @pl.when(place == 0)
    def _():
        join(mine, theirs)

    @pl.when(place == 1)
    def _():
        join(theirs, mine)

    if prior is not None:
        lowest = jnp.logical_and(place == 1, lax.rem(me, bit) == 0)

        @pl.when(jnp.logical_not(lowest))
        def _():
            prior_out[...] = prior[...]


def fold_kernel(axis, levels, *refs):
    base, response = refs[:2]
    inner = refs[2 : 1 + levels]
    diagonal_far, folded, folded_response, inflow_map, outflow_map = refs[1 + levels : 6 + levels]
    diagonal, arrived = refs[6 + levels :]
    copy = pltpu.make_async_copy(diagonal_far, diagonal, arrived)
    copy.start()
    rows, count, width = base.shape
    near = count + width
    me = lax.axis_index(axis)

    upper = lax.div(me, 1 << (levels - 1)) == 1
    across = lax.broadcasted_iota(jnp.int32, (near, width), 1) + count
    unit = jnp.where(lax.broadcasted_iota(jnp.int32, (near, width), 0) == across, 1.0, 0.0)
    inflow = jnp.where(upper, unit, 0.0)
    outflow = jnp.where(upper, 0.0, unit)
    blank = jnp.zeros((width, width), jnp.float32)
    for level in range(levels - 2, -1, -1):
        part = inner[level]
        upper = lax.rem(lax.div(me, 1 << level), 2) == 1
        known = jnp.concatenate([part[:count].astype(jnp.float32), blank], axis=0)
        down = known + mul(narrow(inflow), part[count:near])
        both = narrow(jnp.concatenate([inflow, outflow], axis=1))
        known = jnp.concatenate([part[near : near + count].astype(jnp.float32), blank], axis=0)
        up = known + mul(both, part[near + count :])
        inflow, outflow = jnp.where(upper, down, inflow), jnp.where(upper, outflow, up)

    inflow_map[...] = narrow(inflow)
    outflow_map[...] = narrow(outflow)
    both = narrow(jnp.concatenate([inflow, outflow], axis=1))
    for k in range(rows):
        value = mul(both, response[k, count:])
        folded[k] = base[k] + value[:count]
        folded_response[k] = narrow(value[count:])
    copy.wait()


def chain_kernel(
    axes, levels, own, theirs, base, response, solution, rounded, brought, near_rows, far_rows
):
    rows, count, width = base.shape
    side = lax.rem(lax.axis_index(axes[1]), 2)
    upper = lax.div(lax.axis_index(axes[0]), 1 << (levels - 1)) == 1
    down = theirs[:count].astype(jnp.float32)
    up = down + mul(own[...], theirs[count:])
    z = narrow(jnp.where(upper, down, up))
    brought[...] = z
    values = []
    for k in range(rows):
        value = base[k] + mul(z, response[k])
        solution[k] = value
        values.append(narrow(value))
        rounded[k] = values[k]
    rim = near_rows.shape[0]
    for odd, to_low, to_high in ((0, far_rows, near_rows), (1, near_rows, far_rows)):

        @pl.when(side == odd)
        def _(to_low=to_low, to_high=to_high):
            for e in range(rim):
                to_low[e] = values[e]
                to_high[e] = values[rows - rim + e]


def local_kernel(
    axes,
    levels,
    rounded,
    brought,
    inflow_map,
    outflow_map,
    prior,
    theirs,
    solved,
    diagonal,
    lower,
    upper,
    lower_at_far,
    upper_at_far,
    halo_at_far,
    partial,
    solution,
    masks,
    held,
    last_block,
    lower_at,
    upper_at,
    halo_at,
    arrived,
):
    parts = [
        (lower_at_far, lower_at),
        (upper_at_far, upper_at),
        (halo_at_far, halo_at),
        (solved, solution),
    ]
    copies = [
        pltpu.make_async_copy(source, target, arrived.at[i])
        for i, (source, target) in enumerate(parts)
    ]
    for copy in copies:
        copy.start()
    rows, slots, width, _ = lower.shape
    upper_slots = upper.shape[1]
    count = brought.shape[0]
    me = lax.axis_index(axes[0])
    last_block[...] = prior[...]

    @pl.when(me == 1 << (levels - 1))
    def _():
        last_block[...] = theirs[count:]

    z = brought[...]
    after = narrow(outflow_map[:count].astype(jnp.float32) + mul(z, outflow_map[count:]))
    before = inflow_map[:count].astype(jnp.float32) + mul(z, inflow_map[count:])
    before = narrow(before).astype(jnp.float32) + mul(rounded[0], last_block[...])
    before = narrow(jnp.where(me > 0, before, 0.0))
    held[:rows] = rounded[...]
    held[rows] = before
    held[rows + 1] = after
    for k in range(rows):
        source = jnp.concatenate([rounded[k], after], axis=1)
        total = mul(source, jnp.concatenate([diagonal[k], upper[k, 0]], axis=0))
        partial[k] = total + mul(before, lower[k, 0])
    for copy in copies[:3]:
        copy.wait()
    for k in range(rows):
        source = []
        for m in range(1, slots):
            at = lower_at[m, k]
            source.append(held[jnp.where(at == k, rows, at)])
        total = mul(
            jnp.concatenate(source, axis=1), lower[k, 1:].reshape((slots - 1) * width, width)
        )
        source = []
        for m in range(1, upper_slots):
            at = upper_at[m, k]
            source.append(held[jnp.where(at == k, rows + 1, at)])
        partial[k] += total + mul(
            jnp.concatenate(source, axis=1),
            upper[k, 1:].reshape((upper_slots - 1) * width, width),
        )
    _, picked, places, _, _ = masks.shape
    for k in range(rows):
        for m in range(picked):
            at = halo_at[m + 1, k]
            for j in range(places):
                mask = jnp.where(at == j, 1.0, 0.0)
                masks[k, m, j] = narrow(jnp.full((count, width), mask, jnp.float32))
    copies[3].wait()


def halo_kernel(axis, partial, outer, inner, halo, masks, product):
    rows, slots, width, _ = halo.shape
    rim = inner.shape[0]
    side = lax.rem(lax.axis_index(axis), 2)

    def add(left, right):
        rim_rows = [left[e] for e in range(rim)] + [right[e] for e in range(rim)]
        for k in range(rows):
            source = [rim_rows[k % (2 * rim)]]
            for m in range(1, slots):
                source.append(sum(masks[k, m - 1, j] * rim_rows[j] for j in range(2 * rim)))
            product[k] = partial[k] + mul(
                jnp.concatenate(source, axis=1), halo[k].reshape(slots * width, width)
            )

    @pl.when(side == 0)
    def _():
        add(outer, inner)

    @pl.when(side == 1)
    def _():
        add(inner, outer)


def trade(block, axis, bit):
    count = lax.axis_size(axis)
    return lax.ppermute(block, axis, [(i, i ^ bit) for i in range(count)])


def swaps(block, axis, first):
    count = lax.axis_size(axis)
    pairs = []
    for low in range(first, count - 1, 2):
        pairs += [(low, low + 1), (low + 1, low)]
    return lax.ppermute(block, axis, pairs)


def on_device(
    right_sides,
    diag_inverse,
    diag_blocks,
    lower_blocks,
    upper_blocks,
    halo_blocks,
    lower_index,
    upper_index,
    halo_index,
):
    rows, count, width = right_sides.shape
    lower_at, upper_at, halo_at = lower_index.T, upper_index.T, halo_index.T
    slots = lower_blocks.shape[1]
    upper_slots = upper_blocks.shape[1]
    groups = lax.axis_size("section")
    near = count + width
    far = near + width
    wide = jax.ShapeDtypeStruct((rows, count, width), jnp.float32)

    indices = [
        pltpu.with_memory_space_constraint(a, pltpu.HBM) for a in (lower_at, upper_at, halo_at)
    ]
    base, response, payload = pl.pallas_call(
        sweep_kernel,
        out_shape=(
            wide,
            jax.ShapeDtypeStruct((rows + 1, far, width), jnp.bfloat16),
            jax.ShapeDtypeStruct((near + far + width, width), jnp.bfloat16),
        ),
        in_specs=[HBM] * 6,
        out_specs=(VMEM,) * 3,
        scratch_shapes=[
            pltpu.VMEM(right_sides.shape, right_sides.dtype),
            pltpu.VMEM(diag_inverse.shape, diag_inverse.dtype),
            pltpu.VMEM(lower_blocks.shape, lower_blocks.dtype),
            pltpu.VMEM(upper_blocks.shape, upper_blocks.dtype),
            pltpu.SMEM(lower_at.shape, jnp.int32),
            pltpu.SMEM(upper_at.shape, jnp.int32),
            pltpu.VMEM((rows // 2, (slots - 1) * width, 2 * width), jnp.bfloat16),
            pltpu.VMEM((rows // 2, (slots - 1) * width, width), jnp.bfloat16),
            pltpu.VMEM((rows // 2, (upper_slots - 1) * width, 2 * width), jnp.bfloat16),
            pltpu.VMEM((rows // 2, (upper_slots - 1) * width, width), jnp.bfloat16),
            pltpu.VMEM((rows + 1, near, width), jnp.bfloat16),
            pltpu.VMEM((rows, near, width), jnp.float32),
            pltpu.VMEM((rows, width, width), jnp.float32),
            pltpu.SemaphoreType.DMA((9,)),
        ],
        compiler_params=SMALL,
        name="sweeps",
    )(
        *(
            pltpu.with_memory_space_constraint(a, pltpu.HBM)
            for a in (right_sides, diag_inverse, lower_blocks, upper_blocks)
        ),
        *indices[:2],
    )

    levels = groups.bit_length() - 1
    segment = payload.shape[0]
    bits = jnp.bfloat16
    prior = []
    inner = []
    for level in range(levels - 1):
        theirs = trade(payload, "section", 1 << level)
        final = level == levels - 2

        def compose(*refs, bit=1 << level, final=final):
            compose_kernel("section", bit, final, *refs)

        payload, between, *prior = pl.pallas_call(
            compose,
            out_shape=(
                jax.ShapeDtypeStruct((near if final else segment, width), bits),
                jax.ShapeDtypeStruct((near + far, width), bits),
                jax.ShapeDtypeStruct((width, width), bits),
            )
            + (jax.ShapeDtypeStruct((count, width), bits),) * final,
            in_specs=[VMEM] * (2 + len(prior)),
            out_specs=(VMEM,) * (3 + final),
            compiler_params=SMALL,
            name="compose",
        )(payload, theirs, *prior)
        inner.append(between)
    prior, own = prior
    theirs = trade(payload, "section", 1 << (levels - 1))

    def fold(*refs):
        fold_kernel("section", levels, *refs)

    base, response, inflow_map, outflow_map, diagonal = pl.pallas_call(
        fold,
        out_shape=(
            wide,
            jax.ShapeDtypeStruct((rows, width, width), bits),
            jax.ShapeDtypeStruct((near, width), bits),
            jax.ShapeDtypeStruct((near, width), bits),
            jax.ShapeDtypeStruct(diag_blocks.shape, diag_blocks.dtype),
        ),
        in_specs=[VMEM] * (1 + levels) + [HBM],
        out_specs=(VMEM,) * 5,
        scratch_shapes=[pltpu.SemaphoreType.DMA(())],
        compiler_params=SMALL,
        name="fold",
    )(base, response, *inner, pltpu.with_memory_space_constraint(diag_blocks, pltpu.HBM))

    def chain(*refs):
        chain_kernel(("section", "dom"), levels, *refs)

    solved, rounded, brought, inner, outer = pl.pallas_call(
        chain,
        out_shape=(
            wide,
            jax.ShapeDtypeStruct((rows, count, width), bits),
            jax.ShapeDtypeStruct((count, width), bits),
            jax.ShapeDtypeStruct((RIM, count, width), bits),
            jax.ShapeDtypeStruct((RIM, count, width), bits),
        ),
        in_specs=[VMEM] * 4,
        out_specs=(VMEM,) * 5,
        compiler_params=SMALL,
        name="chain",
    )(own, theirs, base, response)

    outer = swaps(outer, "dom", 1)
    inner = swaps(inner, "dom", 0)

    def local(*refs):
        local_kernel(("section", "dom"), levels, *refs)

    masks = (rows, halo_blocks.shape[1] - 1, 2 * RIM, count, width)
    partial, solution, masks = pl.pallas_call(
        local,
        out_shape=(wide, wide, jax.ShapeDtypeStruct(masks, bits)),
        in_specs=[VMEM] * 10 + [HBM] * 3,
        out_specs=(VMEM, HBM, VMEM),
        scratch_shapes=[
            pltpu.VMEM((rows + 2, count, width), bits),
            pltpu.VMEM((width, width), bits),
        ]
        + [pltpu.SMEM(a.shape, jnp.int32) for a in indices]
        + [pltpu.SemaphoreType.DMA((4,))],
        compiler_params=SMALL,
        name="local_product",
    )(
        rounded,
        brought,
        inflow_map,
        outflow_map,
        prior,
        theirs,
        solved,
        diagonal,
        lower_blocks,
        upper_blocks,
        *indices,
    )

    def halo(*refs):
        halo_kernel("dom", *refs)

    product = pl.pallas_call(
        halo,
        out_shape=wide,
        in_specs=[VMEM] * 5,
        out_specs=VMEM,
        compiler_params=SMALL,
        name="halo_product",
    )(partial, outer, inner, halo_blocks, masks)
    return (solution, product)


def solution(mesh):
    in_specs = (
        P(("section", "dom"), None, None),
        P(("section", "dom"), None, None),
        P(("section", "dom"), None, None),
        P(("section", "dom"), None, None, None),
        P(("section", "dom"), None, None, None),
        P(("section", "dom"), None, None, None),
        P(("section", "dom"), None),
        P(("section", "dom"), None),
        P(("section", "dom"), None),
    )
    out_specs = (P(("section", "dom"), None, None), P(("section", "dom"), None, None))
    return jax.shard_map(
        on_device, mesh=mesh, in_specs=in_specs, out_specs=out_specs, check_vma=False
    )
```

```python
import jax
import jax.numpy as jnp
from jax import lax
from jax.experimental import pallas as pl
from jax.experimental.pallas import tpu as pltpu
from jax.sharding import PartitionSpec as P

RIM = 4

VMEM = pl.BlockSpec(memory_space=pltpu.VMEM)
SMEM = pl.BlockSpec(memory_space=pltpu.SMEM)
HBM = pl.BlockSpec(memory_space=pltpu.HBM)
SMALL = pltpu.CompilerParams(vmem_limit_bytes=16 * 1024 * 1024)


def mul(a, b):
    return jnp.dot(a, b, preferred_element_type=jnp.float32)


def narrow(a):
    return a.astype(jnp.bfloat16)


def sweep_kernel(
    rhs_far,
    inverse_far,
    lower_far,
    upper_far,
    lower_at_far,
    upper_at_far,
    base,
    response,
    payload,
    rhs,
    inverse,
    lower,
    upper,
    lower_at,
    upper_at,
    low_pair,
    low_second,
    upp_pair,
    upp_second,
    down,
    exact,
    fixed,
    arrived,
):
    rows, count, width = rhs.shape
    slots = lower.shape[1]
    upper_slots = upper.shape[1]
    near = count + width
    far = near + width
    last = rows - 1
    half = rows // 2
    parts = [
        (lower_far.at[:half], lower.at[:half]),
        (inverse_far.at[:half], inverse.at[:half]),
        (rhs_far.at[:half], rhs.at[:half]),
        (lower_at_far, lower_at),
        (inverse_far.at[half:], inverse.at[half:]),
        (rhs_far.at[half:], rhs.at[half:]),
        (lower_far.at[half:], lower.at[half:]),
        (upper_far, upper),
        (upper_at_far, upper_at),
    ]
    copies = [
        pltpu.make_async_copy(far, here, arrived.at[i]) for i, (far, here) in enumerate(parts)
    ]
    for copy in copies:
        copy.start()
    eye = narrow(
        lax.broadcasted_iota(jnp.int32, (width, width), 0)
        == lax.broadcasted_iota(jnp.int32, (width, width), 1)
    )
    down[:, :count] = jnp.zeros((rows + 1, count, width), jnp.bfloat16)
    response[:, :near] = jnp.zeros((rows + 1, near, width), jnp.bfloat16)
    for k in range(rows):
        down[k, count:] = eye
        response[k, near:] = eye
    down[rows, count:] = jnp.zeros_like(eye)
    response[rows, near:] = jnp.zeros_like(eye)

    def piece(blocks, m):
        return blocks[m * width : (m + 1) * width]

    def named(at, k, row, blocks, many):
        return sum(
            jnp.where(at[m, k] == row, piece(blocks, m), 0.0) for m in range(1, many)
        )

    def sources(held, at, k, skipped, many):
        picked = []
        for m in range(1, many):
            row = at[m, k]
            picked.append(held[row if skipped is None else jnp.where(row == skipped, rows, row)])
        return jnp.concatenate(picked, axis=1)

    def apart(left, right, own, other):
        zero = jnp.zeros_like(own)
        sides = [jnp.concatenate([own, zero], axis=1), jnp.concatenate([zero, other], axis=1)]
        return mul(jnp.concatenate([left, right], axis=1), jnp.concatenate(sides, axis=0))

    def ready(at, blocks, many, first, step, heads):
        of_a, of_b, links = [], [], []
        for a in (first, first + 2 * step):
            b = a + step
            lefts = [
                jnp.concatenate(heads(k) + [blocks[k].reshape(many * width, width)], axis=0)
                for k in (a, b)
            ]
            both = apart(*lefts, inverse[a], inverse[b])
            of_a.append(both[:, :width])
            of_b.append(both[:, width:])
            tail = both[both.shape[0] - many * width :, width:]
            links.append(narrow(named(at, b, a, tail, many)))
        narrow_a = [narrow(value) for value in of_a]
        both = apart(*narrow_a, *links)
        through = [both[:, :width], both[:, width:]]
        return of_a, narrow_a, of_b, through, links

    def ready_down(p):
        of_a, narrow_a, of_b, through, _ = ready(
            lower_at, lower, slots, 2 * p, 1, lambda k: [narrow(rhs[k])]
        )
        for i in range(2):
            a, b = 2 * (p + i), 2 * (p + i) + 1
            free_a = -of_a[i][count:near]
            free_b = through[i][count:near] - of_b[i][count:near]
            if p + i == 0:
                inner = sum(piece(of_a[i][count:], m) for m in range(1, slots))
                free_a = free_a - inner
                inner = sum(piece(through[i][count:], m) for m in range(1, slots))
                free_b = free_b + inner - named(lower_at, b, b, of_b[i][count:], slots)
            else:
                low_pair[p + i, :, :width] = narrow_a[i][near:]
                low_pair[p + i, :, width:] = narrow(through[i][near:])
                low_second[p + i] = narrow(of_b[i][near:])
            exact[a, :count] = of_a[i][:count]
            exact[a, count:] = free_a
            exact[b, :count] = of_b[i][:count] - through[i][:count]
            exact[b, count:] = free_b

    def go_down(p):
        a, b = 2 * p, 2 * p + 1
        of_a, of_b = exact[a], exact[b]
        if p > 0:
            first = mul(sources(down, lower_at, a, None, slots), low_pair[p])
            second = mul(sources(down, lower_at, b, a, slots), low_second[p])
            of_a = of_a - first[:, :width]
            of_b = of_b + first[:, width:] - second
            exact[a] = of_a
            exact[b] = of_b
        down[a] = narrow(of_a)
        down[b] = narrow(of_b)

    def ready_up(p):
        of_a, narrow_a, of_b, through, links = ready(
            upper_at, upper, upper_slots, last - 2 * p, -1, lambda k: []
        )
        for i in range(2):
            a = last - 2 * (p + i)
            b = a - 1
            free_a = -of_a[i][:width]
            free_b = through[i][:width] - of_b[i][:width]
            if p + i == 0:
                free_a = free_a - sum(piece(of_a[i], m) for m in range(1, upper_slots))
                inner = sum(piece(through[i], m) for m in range(1, upper_slots))
                free_b = free_b + inner - named(upper_at, b, b, of_b[i], upper_slots)
            else:
                upp_pair[p + i, :, :width] = narrow_a[i][width:]
                upp_pair[p + i, :, width:] = narrow(through[i][width:])
                upp_second[p + i] = narrow(of_b[i][width:])
            fixed[a] = free_a
            fixed[b] = free_b
        return links

    def go_up(p, passed):
        a = last - 2 * p
        b = a - 1
        of_a = exact[a]
        of_b = exact[b] - passed
        free_a = fixed[a]
        free_b = fixed[b]
        if p > 0:
            first = mul(sources(response, upper_at, a, None, upper_slots), upp_pair[p])
            second = mul(sources(response, upper_at, b, a, upper_slots), upp_second[p])
            of_a = of_a - first[:near, :width]
            of_b = of_b + first[:near, width:] - second[:near]
            free_a = free_a - first[near:, :width]
            free_b = free_b + first[near:, width:] - second[near:]
        for k, value, free in ((a, of_a, free_a), (b, of_b, free_b)):
            base[k] = value[:count]
            value, free = narrow(value), narrow(free)
            response[k, :near] = value
            response[k, near:] = free
            if k == last:
                payload[far + near :] = free
            if k == 0:
                payload[near : 2 * near] = value
                payload[2 * near : near + far] = free

    pairs = rows // 2
    for copy in copies[:4]:
        copy.wait()
    ready_down(0)
    go_down(0)
    for copy in copies[4:]:
        copy.wait()
    links = []
    for p in range(1, pairs):
        if p % 2 == 1 and p + 1 < pairs:
            ready_down(p + 1)
        go_down(p)
        if p % 2 == 1:
            links += ready_up(p - 1)
    payload[:near] = down[last]
    for p in range(0, pairs, 2):
        a = last - 2 * p
        passed = apart(down[a], down[a - 2], links[p], links[p + 1])
        go_up(p, passed[:, :width])
        go_up(p + 1, passed[:, width:])


def compose_kernel(axis, bit, final, mine, theirs, *refs):
    prior, sent, inner, prior_out = refs[:4] if bit > 1 else (None, *refs[:3])
    width = mine.shape[1]
    count = (mine.shape[0] - 4 * width) // 2
    near = count + width
    me = lax.axis_index(axis)
    place = lax.rem(lax.div(me, bit), 2)
    mid = near + count
    far = near + near + width
    blank = jnp.zeros((width, width), jnp.float32)

    def join(a, b):
        sides = [b[count:near], b[mid : mid + width]]
        across = mul(a[:near], jnp.concatenate(sides, axis=1))
        ahead = jnp.concatenate([b[:count].astype(jnp.float32), blank], axis=0)
        joined = narrow(across[:, :width] + ahead)
        ahead = jnp.concatenate([b[near:mid].astype(jnp.float32), blank], axis=0)
        between = narrow(across[:, width:] + ahead)
        first = mul(between, a[mid + width : far]) + a[near : 2 * near].astype(jnp.float32)
        inner[:near] = a[:near]
        inner[near : 2 * near] = between
        inner[2 * near :] = b[mid + width : far]
        prior_out[...] = a[far:]
        if final:
            refs[-1][...] = joined[:count]
            above = lax.rem(lax.div(me, 2 * bit), 2) == 1

            @pl.when(above)
            def _():
                sent[...] = narrow(first)

            @pl.when(jnp.logical_not(above))
            def _():
                sent[:count] = joined[:count]
                sent[count:] = b[far:]

        else:
            sent[:near] = joined
            sent[near : 2 * near] = narrow(first)
            sent[2 * near : far] = narrow(mul(b[mid + width : far], a[mid + width : far]))
            sent[far:] = b[far:]

    @pl.when(place == 0)
    def _():
        join(mine, theirs)

    @pl.when(place == 1)
    def _():
        join(theirs, mine)

    if prior is not None:
        lowest = jnp.logical_and(place == 1, lax.rem(me, bit) == 0)

        @pl.when(jnp.logical_not(lowest))
        def _():
            prior_out[...] = prior[...]


def fold_kernel(axis, levels, *refs):
    base, response = refs[:2]
    inner = refs[2 : 1 + levels]
    diagonal_far, folded, folded_response, inflow_map, outflow_map = refs[1 + levels : 6 + levels]
    diagonal, arrived = refs[6 + levels :]
    copy = pltpu.make_async_copy(diagonal_far, diagonal, arrived)
    copy.start()
    rows, count, width = base.shape
    near = count + width
    me = lax.axis_index(axis)

    upper = lax.div(me, 1 << (levels - 1)) == 1
    across = lax.broadcasted_iota(jnp.int32, (near, width), 1) + count
    unit = jnp.where(lax.broadcasted_iota(jnp.int32, (near, width), 0) == across, 1.0, 0.0)
    inflow = jnp.where(upper, unit, 0.0)
    outflow = jnp.where(upper, 0.0, unit)
    blank = jnp.zeros((width, width), jnp.float32)
    for level in range(levels - 2, -1, -1):
        part = inner[level]
        upper = lax.rem(lax.div(me, 1 << level), 2) == 1
        known = jnp.concatenate([part[:count].astype(jnp.float32), blank], axis=0)
        down = known + mul(narrow(inflow), part[count:near])
        both = narrow(jnp.concatenate([inflow, outflow], axis=1))
        known = jnp.concatenate([part[near : near + count].astype(jnp.float32), blank], axis=0)
        up = known + mul(both, part[near + count :])
        inflow, outflow = jnp.where(upper, down, inflow), jnp.where(upper, outflow, up)

    inflow_map[...] = narrow(inflow)
    outflow_map[...] = narrow(outflow)
    both = narrow(jnp.concatenate([inflow, outflow], axis=1))
    for k in range(rows):
        value = mul(both, response[k, count:])
        folded[k] = base[k] + value[:count]
        folded_response[k] = narrow(value[count:])
    copy.wait()


def chain_kernel(
    axes, levels, own, theirs, base, response, solution, rounded, brought, near_rows, far_rows
):
    rows, count, width = base.shape
    side = lax.rem(lax.axis_index(axes[1]), 2)
    upper = lax.div(lax.axis_index(axes[0]), 1 << (levels - 1)) == 1
    down = theirs[:count].astype(jnp.float32)
    up = down + mul(own[...], theirs[count:])
    z = narrow(jnp.where(upper, down, up))
    brought[...] = z
    values = []
    for k in range(rows):
        value = base[k] + mul(z, response[k])
        solution[k] = value
        values.append(narrow(value))
        rounded[k] = values[k]
    rim = near_rows.shape[0]
    for odd, to_low, to_high in ((0, far_rows, near_rows), (1, near_rows, far_rows)):

        @pl.when(side == odd)
        def _(to_low=to_low, to_high=to_high):
            for e in range(rim):
                to_low[e] = values[e]
                to_high[e] = values[rows - rim + e]


def local_kernel(
    axes,
    levels,
    rounded,
    brought,
    inflow_map,
    outflow_map,
    prior,
    theirs,
    solved,
    diagonal,
    lower,
    upper,
    lower_at_far,
    upper_at_far,
    halo_at_far,
    partial,
    solution,
    masks,
    held,
    last_block,
    lower_at,
    upper_at,
    halo_at,
    arrived,
):
    parts = [
        (lower_at_far, lower_at),
        (upper_at_far, upper_at),
        (halo_at_far, halo_at),
        (solved, solution),
    ]
    copies = [
        pltpu.make_async_copy(source, target, arrived.at[i])
        for i, (source, target) in enumerate(parts)
    ]
    for copy in copies:
        copy.start()
    rows, slots, width, _ = lower.shape
    upper_slots = upper.shape[1]
    count = brought.shape[0]
    me = lax.axis_index(axes[0])
    last_block[...] = prior[...]

    @pl.when(me == 1 << (levels - 1))
    def _():
        last_block[...] = theirs[count:]

    z = brought[...]
    after = narrow(outflow_map[:count].astype(jnp.float32) + mul(z, outflow_map[count:]))
    before = inflow_map[:count].astype(jnp.float32) + mul(z, inflow_map[count:])
    before = narrow(before).astype(jnp.float32) + mul(rounded[0], last_block[...])
    before = narrow(jnp.where(me > 0, before, 0.0))
    held[:rows] = rounded[...]
    held[rows] = before
    held[rows + 1] = after
    for k in range(rows):
        source = jnp.concatenate([rounded[k], after], axis=1)
        total = mul(source, jnp.concatenate([diagonal[k], upper[k, 0]], axis=0))
        partial[k] = total + mul(before, lower[k, 0])
    for copy in copies[:3]:
        copy.wait()
    for k in range(rows):
        source = []
        for m in range(1, slots):
            at = lower_at[m, k]
            source.append(held[jnp.where(at == k, rows, at)])
        total = mul(
            jnp.concatenate(source, axis=1), lower[k, 1:].reshape((slots - 1) * width, width)
        )
        source = []
        for m in range(1, upper_slots):
            at = upper_at[m, k]
            source.append(held[jnp.where(at == k, rows + 1, at)])
        partial[k] += total + mul(
            jnp.concatenate(source, axis=1),
            upper[k, 1:].reshape((upper_slots - 1) * width, width),
        )
    _, picked, places, _, _ = masks.shape
    for k in range(rows):
        for m in range(picked):
            at = halo_at[m + 1, k]
            for j in range(places):
                mask = jnp.where(at == j, 1.0, 0.0)
                masks[k, m, j] = narrow(jnp.full((count, width), mask, jnp.float32))
    copies[3].wait()


def halo_kernel(axis, partial, outer, inner, halo, masks, product):
    rows, slots, width, _ = halo.shape
    rim = inner.shape[0]
    side = lax.rem(lax.axis_index(axis), 2)

    def add(left, right):
        rim_rows = [left[e] for e in range(rim)] + [right[e] for e in range(rim)]
        for k in range(rows):
            source = [rim_rows[k % (2 * rim)]]
            for m in range(1, slots):
                source.append(sum(masks[k, m - 1, j] * rim_rows[j] for j in range(2 * rim)))
            product[k] = partial[k] + mul(
                jnp.concatenate(source, axis=1), halo[k].reshape(slots * width, width)
            )

    @pl.when(side == 0)
    def _():
        add(outer, inner)

    @pl.when(side == 1)
    def _():
        add(inner, outer)


def trade(block, axis, bit):
    count = lax.axis_size(axis)
    return lax.ppermute(block, axis, [(i, i ^ bit) for i in range(count)])


def swaps(block, axis, first):
    count = lax.axis_size(axis)
    pairs = []
    for low in range(first, count - 1, 2):
        pairs += [(low, low + 1), (low + 1, low)]
    return lax.ppermute(block, axis, pairs)


def on_device(
    right_sides,
    diag_inverse,
    diag_blocks,
    lower_blocks,
    upper_blocks,
    halo_blocks,
    lower_index,
    upper_index,
    halo_index,
):
    rows, count, width = right_sides.shape
    lower_at, upper_at, halo_at = lower_index.T, upper_index.T, halo_index.T
    slots = lower_blocks.shape[1]
    upper_slots = upper_blocks.shape[1]
    groups = lax.axis_size("section")
    near = count + width
    far = near + width
    wide = jax.ShapeDtypeStruct((rows, count, width), jnp.float32)

    indices = [
        pltpu.with_memory_space_constraint(a, pltpu.HBM) for a in (lower_at, upper_at, halo_at)
    ]
    base, response, payload = pl.pallas_call(
        sweep_kernel,
        out_shape=(
            wide,
            jax.ShapeDtypeStruct((rows + 1, far, width), jnp.bfloat16),
            jax.ShapeDtypeStruct((near + far + width, width), jnp.bfloat16),
        ),
        in_specs=[HBM] * 6,
        out_specs=(VMEM,) * 3,
        scratch_shapes=[
            pltpu.VMEM(right_sides.shape, right_sides.dtype),
            pltpu.VMEM(diag_inverse.shape, diag_inverse.dtype),
            pltpu.VMEM(lower_blocks.shape, lower_blocks.dtype),
            pltpu.VMEM(upper_blocks.shape, upper_blocks.dtype),
            pltpu.SMEM(lower_at.shape, jnp.int32),
            pltpu.SMEM(upper_at.shape, jnp.int32),
            pltpu.VMEM((rows // 2, (slots - 1) * width, 2 * width), jnp.bfloat16),
            pltpu.VMEM((rows // 2, (slots - 1) * width, width), jnp.bfloat16),
            pltpu.VMEM((rows // 2, (upper_slots - 1) * width, 2 * width), jnp.bfloat16),
            pltpu.VMEM((rows // 2, (upper_slots - 1) * width, width), jnp.bfloat16),
            pltpu.VMEM((rows + 1, near, width), jnp.bfloat16),
            pltpu.VMEM((rows, near, width), jnp.float32),
            pltpu.VMEM((rows, width, width), jnp.float32),
            pltpu.SemaphoreType.DMA((9,)),
        ],
        compiler_params=SMALL,
        name="sweeps",
    )(
        *(
            pltpu.with_memory_space_constraint(a, pltpu.HBM)
            for a in (right_sides, diag_inverse, lower_blocks, upper_blocks)
        ),
        *indices[:2],
    )

    levels = groups.bit_length() - 1
    segment = payload.shape[0]
    bits = jnp.bfloat16
    prior = []
    inner = []
    for level in range(levels - 1):
        theirs = trade(payload, "section", 1 << level)
        final = level == levels - 2

        def compose(*refs, bit=1 << level, final=final):
            compose_kernel("section", bit, final, *refs)

        payload, between, *prior = pl.pallas_call(
            compose,
            out_shape=(
                jax.ShapeDtypeStruct((near if final else segment, width), bits),
                jax.ShapeDtypeStruct((near + far, width), bits),
                jax.ShapeDtypeStruct((width, width), bits),
            )
            + (jax.ShapeDtypeStruct((count, width), bits),) * final,
            in_specs=[VMEM] * (2 + len(prior)),
            out_specs=(VMEM,) * (3 + final),
            compiler_params=SMALL,
            name="compose",
        )(payload, theirs, *prior)
        inner.append(between)
    prior, own = prior
    theirs = trade(payload, "section", 1 << (levels - 1))

    def fold(*refs):
        fold_kernel("section", levels, *refs)

    base, response, inflow_map, outflow_map, diagonal = pl.pallas_call(
        fold,
        out_shape=(
            wide,
            jax.ShapeDtypeStruct((rows, width, width), bits),
            jax.ShapeDtypeStruct((near, width), bits),
            jax.ShapeDtypeStruct((near, width), bits),
            jax.ShapeDtypeStruct(diag_blocks.shape, diag_blocks.dtype),
        ),
        in_specs=[VMEM] * (1 + levels) + [HBM],
        out_specs=(VMEM,) * 5,
        scratch_shapes=[pltpu.SemaphoreType.DMA(())],
        compiler_params=SMALL,
        name="fold",
    )(base, response, *inner, pltpu.with_memory_space_constraint(diag_blocks, pltpu.HBM))

    def chain(*refs):
        chain_kernel(("section", "dom"), levels, *refs)

    solved, rounded, brought, inner, outer = pl.pallas_call(
        chain,
        out_shape=(
            wide,
            jax.ShapeDtypeStruct((rows, count, width), bits),
            jax.ShapeDtypeStruct((count, width), bits),
            jax.ShapeDtypeStruct((RIM, count, width), bits),
            jax.ShapeDtypeStruct((RIM, count, width), bits),
        ),
        in_specs=[VMEM] * 4,
        out_specs=(VMEM,) * 5,
        compiler_params=SMALL,
        name="chain",
    )(own, theirs, base, response)

    outer = swaps(outer, "dom", 1)
    inner = swaps(inner, "dom", 0)

    def local(*refs):
        local_kernel(("section", "dom"), levels, *refs)

    masks = (rows, halo_blocks.shape[1] - 1, 2 * RIM, count, width)
    partial, solution, masks = pl.pallas_call(
        local,
        out_shape=(wide, wide, jax.ShapeDtypeStruct(masks, bits)),
        in_specs=[VMEM] * 10 + [HBM] * 3,
        out_specs=(VMEM, HBM, VMEM),
        scratch_shapes=[
            pltpu.VMEM((rows + 2, count, width), bits),
            pltpu.VMEM((width, width), bits),
        ]
        + [pltpu.SMEM(a.shape, jnp.int32) for a in indices]
        + [pltpu.SemaphoreType.DMA((4,))],
        compiler_params=SMALL,
        name="local_product",
    )(
        rounded,
        brought,
        inflow_map,
        outflow_map,
        prior,
        theirs,
        solved,
        diagonal,
        lower_blocks,
        upper_blocks,
        *indices,
    )

    def halo(*refs):
        halo_kernel("dom", *refs)

    product = pl.pallas_call(
        halo,
        out_shape=wide,
        in_specs=[VMEM] * 5,
        out_specs=VMEM,
        compiler_params=SMALL,
        name="halo_product",
    )(partial, outer, inner, halo_blocks, masks)
    return (solution, product)


def solution(mesh):
    in_specs = (
        P(("section", "dom"), None, None),
        P(("section", "dom"), None, None),
        P(("section", "dom"), None, None),
        P(("section", "dom"), None, None, None),
        P(("section", "dom"), None, None, None),
        P(("section", "dom"), None, None, None),
        P(("section", "dom"), None),
        P(("section", "dom"), None),
        P(("section", "dom"), None),
    )
    out_specs = (P(("section", "dom"), None, None), P(("section", "dom"), None, None))
    return jax.shard_map(
        on_device, mesh=mesh, in_specs=in_specs, out_specs=out_specs, check_vma=False
    )
```

```python
import jax
import jax.numpy as jnp
from jax import lax
from jax.experimental import pallas as pl
from jax.experimental.pallas import tpu as pltpu
from jax.sharding import PartitionSpec as P

RIM = 4

VMEM = pl.BlockSpec(memory_space=pltpu.VMEM)
SMEM = pl.BlockSpec(memory_space=pltpu.SMEM)
HBM = pl.BlockSpec(memory_space=pltpu.HBM)
SMALL = pltpu.CompilerParams(vmem_limit_bytes=16 * 1024 * 1024)


def mul(a, b):
    return jnp.dot(a, b, preferred_element_type=jnp.float32)


def narrow(a):
    return a.astype(jnp.bfloat16)


def sweep_kernel(
    rhs_far,
    inverse_far,
    lower_far,
    upper_far,
    lower_at_far,
    upper_at_far,
    base,
    response,
    payload,
    rhs,
    inverse,
    lower,
    upper,
    lower_at,
    upper_at,
    low_pair,
    low_second,
    upp_pair,
    upp_second,
    down,
    exact,
    fixed,
    arrived,
):
    rows, count, width = rhs.shape
    slots = lower.shape[1]
    upper_slots = upper.shape[1]
    near = count + width
    far = near + width
    last = rows - 1
    half = rows // 2
    parts = [
        (lower_far.at[:half], lower.at[:half]),
        (inverse_far.at[:half], inverse.at[:half]),
        (rhs_far.at[:half], rhs.at[:half]),
        (lower_at_far, lower_at),
        (inverse_far.at[half:], inverse.at[half:]),
        (rhs_far.at[half:], rhs.at[half:]),
        (lower_far.at[half:], lower.at[half:]),
        (upper_far, upper),
        (upper_at_far, upper_at),
    ]
    copies = [
        pltpu.make_async_copy(far, here, arrived.at[i]) for i, (far, here) in enumerate(parts)
    ]
    for copy in copies:
        copy.start()
    eye = narrow(
        lax.broadcasted_iota(jnp.int32, (width, width), 0)
        == lax.broadcasted_iota(jnp.int32, (width, width), 1)
    )
    down[:, :count] = jnp.zeros((rows + 1, count, width), jnp.bfloat16)
    response[:, :near] = jnp.zeros((rows + 1, near, width), jnp.bfloat16)
    for k in range(rows):
        down[k, count:] = eye
        response[k, near:] = eye
    down[rows, count:] = jnp.zeros_like(eye)
    response[rows, near:] = jnp.zeros_like(eye)

    def piece(blocks, m):
        return blocks[m * width : (m + 1) * width]

    def named(at, k, row, blocks, many):
        return sum(
            jnp.where(at[m, k] == row, piece(blocks, m), 0.0) for m in range(1, many)
        )

    def sources(held, at, k, skipped, many):
        picked = []
        for m in range(1, many):
            row = at[m, k]
            picked.append(held[row if skipped is None else jnp.where(row == skipped, rows, row)])
        return jnp.concatenate(picked, axis=1)

    def apart(left, right, own, other):
        zero = jnp.zeros_like(own)
        sides = [jnp.concatenate([own, zero], axis=1), jnp.concatenate([zero, other], axis=1)]
        return mul(jnp.concatenate([left, right], axis=1), jnp.concatenate(sides, axis=0))

    def ready(at, blocks, many, first, step, heads):
        of_a, of_b, links = [], [], []
        for a in (first, first + 2 * step):
            b = a + step
            lefts = [
                jnp.concatenate(heads(k) + [blocks[k].reshape(many * width, width)], axis=0)
                for k in (a, b)
            ]
            both = apart(*lefts, inverse[a], inverse[b])
            of_a.append(both[:, :width])
            of_b.append(both[:, width:])
            tail = both[both.shape[0] - many * width :, width:]
            links.append(narrow(named(at, b, a, tail, many)))
        narrow_a = [narrow(value) for value in of_a]
        both = apart(*narrow_a, *links)
        through = [both[:, :width], both[:, width:]]
        return of_a, narrow_a, of_b, through, links

    def ready_down(p):
        of_a, narrow_a, of_b, through, _ = ready(
            lower_at, lower, slots, 2 * p, 1, lambda k: [narrow(rhs[k])]
        )
        for i in range(2):
            a, b = 2 * (p + i), 2 * (p + i) + 1
            free_a = -of_a[i][count:near]
            free_b = through[i][count:near] - of_b[i][count:near]
            if p + i == 0:
                inner = sum(piece(of_a[i][count:], m) for m in range(1, slots))
                free_a = free_a - inner
                inner = sum(piece(through[i][count:], m) for m in range(1, slots))
                free_b = free_b + inner - named(lower_at, b, b, of_b[i][count:], slots)
            else:
                low_pair[p + i, :, :width] = narrow_a[i][near:]
                low_pair[p + i, :, width:] = narrow(through[i][near:])
                low_second[p + i] = narrow(of_b[i][near:])
            exact[a, :count] = of_a[i][:count]
            exact[a, count:] = free_a
            exact[b, :count] = of_b[i][:count] - through[i][:count]
            exact[b, count:] = free_b

    def go_down(p):
        a, b = 2 * p, 2 * p + 1
        of_a, of_b = exact[a], exact[b]
        if p > 0:
            first = mul(sources(down, lower_at, a, None, slots), low_pair[p])
            second = mul(sources(down, lower_at, b, a, slots), low_second[p])
            of_a = of_a - first[:, :width]
            of_b = of_b + first[:, width:] - second
            exact[a] = of_a
            exact[b] = of_b
        down[a] = narrow(of_a)
        down[b] = narrow(of_b)
        if b == last:
            payload[:near] = narrow(of_b)

    def ready_up(p):
        of_a, narrow_a, of_b, through, links = ready(
            upper_at, upper, upper_slots, last - 2 * p, -1, lambda k: []
        )
        for i in range(2):
            a = last - 2 * (p + i)
            b = a - 1
            free_a = -of_a[i][:width]
            free_b = through[i][:width] - of_b[i][:width]
            if p + i == 0:
                free_a = free_a - sum(piece(of_a[i], m) for m in range(1, upper_slots))
                inner = sum(piece(through[i], m) for m in range(1, upper_slots))
                free_b = free_b + inner - named(upper_at, b, b, of_b[i], upper_slots)
            else:
                upp_pair[p + i, :, :width] = narrow_a[i][width:]
                upp_pair[p + i, :, width:] = narrow(through[i][width:])
                upp_second[p + i] = narrow(of_b[i][width:])
            fixed[a] = free_a
            fixed[b] = free_b
        return links

    def go_up(p, passed):
        a = last - 2 * p
        b = a - 1
        of_a = exact[a]
        of_b = exact[b] - passed
        free_a = fixed[a]
        free_b = fixed[b]
        if p > 0:
            first = mul(sources(response, upper_at, a, None, upper_slots), upp_pair[p])
            second = mul(sources(response, upper_at, b, a, upper_slots), upp_second[p])
            of_a = of_a - first[:near, :width]
            of_b = of_b + first[:near, width:] - second[:near]
            free_a = free_a - first[near:, :width]
            free_b = free_b + first[near:, width:] - second[near:]
        for k, value, free in ((a, of_a, free_a), (b, of_b, free_b)):
            base[k] = value[:count]
            value, free = narrow(value), narrow(free)
            response[k, :near] = value
            response[k, near:] = free
            if k == last:
                payload[far + near :] = free
            if k == 0:
                payload[near : 2 * near] = value
                payload[2 * near : near + far] = free

    pairs = rows // 2
    for copy in copies[:4]:
        copy.wait()
    ready_down(0)
    go_down(0)
    for copy in copies[4:]:
        copy.wait()
    links = []
    for p in range(1, pairs):
        if p % 2 == 1 and p + 1 < pairs:
            ready_down(p + 1)
        go_down(p)
        if p % 2 == 1:
            links += ready_up(p - 1)
    for p in range(0, pairs, 2):
        a = last - 2 * p
        passed = apart(down[a], down[a - 2], links[p], links[p + 1])
        go_up(p, passed[:, :width])
        go_up(p + 1, passed[:, width:])


def compose_kernel(axis, bit, final, mine, theirs, *refs):
    prior, sent, inner, prior_out = refs[:4] if bit > 1 else (None, *refs[:3])
    width = mine.shape[1]
    count = (mine.shape[0] - 4 * width) // 2
    near = count + width
    me = lax.axis_index(axis)
    place = lax.rem(lax.div(me, bit), 2)
    mid = near + count
    far = near + near + width
    blank = jnp.zeros((width, width), jnp.float32)

    def join(a, b):
        sides = [b[count:near], b[mid : mid + width]]
        across = mul(a[:near], jnp.concatenate(sides, axis=1))
        ahead = jnp.concatenate([b[:count].astype(jnp.float32), blank], axis=0)
        joined = narrow(across[:, :width] + ahead)
        ahead = jnp.concatenate([b[near:mid].astype(jnp.float32), blank], axis=0)
        between = narrow(across[:, width:] + ahead)
        first = mul(between, a[mid + width : far]) + a[near : 2 * near].astype(jnp.float32)
        inner[:near] = a[:near]
        inner[near : 2 * near] = between
        inner[2 * near :] = b[mid + width : far]
        prior_out[...] = a[far:]
        if final:
            refs[-1][...] = joined[:count]
            above = lax.rem(lax.div(me, 2 * bit), 2) == 1

            @pl.when(above)
            def _():
                sent[...] = narrow(first)

            @pl.when(jnp.logical_not(above))
            def _():
                sent[:count] = joined[:count]
                sent[count:] = b[far:]

        else:
            sent[:near] = joined
            sent[near : 2 * near] = narrow(first)
            sent[2 * near : far] = narrow(mul(b[mid + width : far], a[mid + width : far]))
            sent[far:] = b[far:]

    @pl.when(place == 0)
    def _():
        join(mine, theirs)

    @pl.when(place == 1)
    def _():
        join(theirs, mine)

    if prior is not None:
        lowest = jnp.logical_and(place == 1, lax.rem(me, bit) == 0)

        @pl.when(jnp.logical_not(lowest))
        def _():
            prior_out[...] = prior[...]


def fold_kernel(axis, levels, *refs):
    base, response = refs[:2]
    inner = refs[2 : 1 + levels]
    diagonal_far, folded, folded_response, inflow_map, outflow_map = refs[1 + levels : 6 + levels]
    diagonal, arrived = refs[6 + levels :]
    copy = pltpu.make_async_copy(diagonal_far, diagonal, arrived)
    copy.start()
    rows, count, width = base.shape
    near = count + width
    me = lax.axis_index(axis)

    upper = lax.div(me, 1 << (levels - 1)) == 1
    across = lax.broadcasted_iota(jnp.int32, (near, width), 1) + count
    unit = jnp.where(lax.broadcasted_iota(jnp.int32, (near, width), 0) == across, 1.0, 0.0)
    inflow = jnp.where(upper, unit, 0.0)
    outflow = jnp.where(upper, 0.0, unit)
    blank = jnp.zeros((width, width), jnp.float32)
    for level in range(levels - 2, -1, -1):
        part = inner[level]
        upper = lax.rem(lax.div(me, 1 << level), 2) == 1
        known = jnp.concatenate([part[:count].astype(jnp.float32), blank], axis=0)
        down = known + mul(narrow(inflow), part[count:near])
        both = narrow(jnp.concatenate([inflow, outflow], axis=1))
        known = jnp.concatenate([part[near : near + count].astype(jnp.float32), blank], axis=0)
        up = known + mul(both, part[near + count :])
        inflow, outflow = jnp.where(upper, down, inflow), jnp.where(upper, outflow, up)

    inflow_map[...] = narrow(inflow)
    outflow_map[...] = narrow(outflow)
    both = narrow(jnp.concatenate([inflow, outflow], axis=1))
    for k in range(rows):
        value = mul(both, response[k, count:])
        folded[k] = base[k] + value[:count]
        folded_response[k] = narrow(value[count:])
    copy.wait()


def chain_kernel(
    axes, levels, own, theirs, base, response, solution, rounded, brought, near_rows, far_rows
):
    rows, count, width = base.shape
    side = lax.rem(lax.axis_index(axes[1]), 2)
    upper = lax.div(lax.axis_index(axes[0]), 1 << (levels - 1)) == 1
    down = theirs[:count].astype(jnp.float32)
    up = down + mul(own[...], theirs[count:])
    z = narrow(jnp.where(upper, down, up))
    brought[...] = z
    values = []
    for k in range(rows):
        value = base[k] + mul(z, response[k])
        solution[k] = value
        values.append(narrow(value))
        rounded[k] = values[k]
    rim = near_rows.shape[0]
    for odd, to_low, to_high in ((0, far_rows, near_rows), (1, near_rows, far_rows)):

        @pl.when(side == odd)
        def _(to_low=to_low, to_high=to_high):
            for e in range(rim):
                to_low[e] = values[e]
                to_high[e] = values[rows - rim + e]


def local_kernel(
    axes,
    levels,
    rounded,
    brought,
    inflow_map,
    outflow_map,
    prior,
    theirs,
    solved,
    diagonal,
    lower,
    upper,
    lower_at_far,
    upper_at_far,
    halo_at_far,
    partial,
    solution,
    masks,
    held,
    last_block,
    lower_at,
    upper_at,
    halo_at,
    arrived,
):
    parts = [
        (lower_at_far, lower_at),
        (upper_at_far, upper_at),
        (halo_at_far, halo_at),
        (solved, solution),
    ]
    copies = [
        pltpu.make_async_copy(source, target, arrived.at[i])
        for i, (source, target) in enumerate(parts)
    ]
    for copy in copies:
        copy.start()
    rows, slots, width, _ = lower.shape
    upper_slots = upper.shape[1]
    count = brought.shape[0]
    me = lax.axis_index(axes[0])
    last_block[...] = prior[...]

    @pl.when(me == 1 << (levels - 1))
    def _():
        last_block[...] = theirs[count:]

    z = brought[...]
    after = narrow(outflow_map[:count].astype(jnp.float32) + mul(z, outflow_map[count:]))
    before = inflow_map[:count].astype(jnp.float32) + mul(z, inflow_map[count:])
    before = narrow(before).astype(jnp.float32) + mul(rounded[0], last_block[...])
    before = narrow(jnp.where(me > 0, before, 0.0))
    held[:rows] = rounded[...]
    held[rows] = before
    held[rows + 1] = after
    for k in range(rows):
        source = jnp.concatenate([rounded[k], after], axis=1)
        total = mul(source, jnp.concatenate([diagonal[k], upper[k, 0]], axis=0))
        partial[k] = total + mul(before, lower[k, 0])
    for copy in copies[:3]:
        copy.wait()
    for k in range(rows):
        source = []
        for m in range(1, slots):
            at = lower_at[m, k]
            source.append(held[jnp.where(at == k, rows, at)])
        total = mul(
            jnp.concatenate(source, axis=1), lower[k, 1:].reshape((slots - 1) * width, width)
        )
        source = []
        for m in range(1, upper_slots):
            at = upper_at[m, k]
            source.append(held[jnp.where(at == k, rows + 1, at)])
        partial[k] += total + mul(
            jnp.concatenate(source, axis=1),
            upper[k, 1:].reshape((upper_slots - 1) * width, width),
        )
    _, picked, places, _, _ = masks.shape
    for k in range(rows):
        for m in range(picked):
            at = halo_at[m + 1, k]
            for j in range(places):
                mask = jnp.where(at == j, 1.0, 0.0)
                masks[k, m, j] = narrow(jnp.full((count, width), mask, jnp.float32))
    copies[3].wait()


def halo_kernel(axis, partial, outer, inner, halo, masks, product):
    rows, slots, width, _ = halo.shape
    rim = inner.shape[0]
    side = lax.rem(lax.axis_index(axis), 2)

    def add(left, right):
        rim_rows = [left[e] for e in range(rim)] + [right[e] for e in range(rim)]
        for k in range(rows):
            source = [rim_rows[k % (2 * rim)]]
            for m in range(1, slots):
                source.append(sum(masks[k, m - 1, j] * rim_rows[j] for j in range(2 * rim)))
            product[k] = partial[k] + mul(
                jnp.concatenate(source, axis=1), halo[k].reshape(slots * width, width)
            )

    @pl.when(side == 0)
    def _():
        add(outer, inner)

    @pl.when(side == 1)
    def _():
        add(inner, outer)


def trade(block, axis, bit):
    count = lax.axis_size(axis)
    return lax.ppermute(block, axis, [(i, i ^ bit) for i in range(count)])


def swaps(block, axis, first):
    count = lax.axis_size(axis)
    pairs = []
    for low in range(first, count - 1, 2):
        pairs += [(low, low + 1), (low + 1, low)]
    return lax.ppermute(block, axis, pairs)


def on_device(
    right_sides,
    diag_inverse,
    diag_blocks,
    lower_blocks,
    upper_blocks,
    halo_blocks,
    lower_index,
    upper_index,
    halo_index,
):
    rows, count, width = right_sides.shape
    lower_at, upper_at, halo_at = lower_index.T, upper_index.T, halo_index.T
    slots = lower_blocks.shape[1]
    upper_slots = upper_blocks.shape[1]
    groups = lax.axis_size("section")
    near = count + width
    far = near + width
    wide = jax.ShapeDtypeStruct((rows, count, width), jnp.float32)

    indices = [
        pltpu.with_memory_space_constraint(a, pltpu.HBM) for a in (lower_at, upper_at, halo_at)
    ]
    base, response, payload = pl.pallas_call(
        sweep_kernel,
        out_shape=(
            wide,
            jax.ShapeDtypeStruct((rows + 1, far, width), jnp.bfloat16),
            jax.ShapeDtypeStruct((near + far + width, width), jnp.bfloat16),
        ),
        in_specs=[HBM] * 6,
        out_specs=(VMEM,) * 3,
        scratch_shapes=[
            pltpu.VMEM(right_sides.shape, right_sides.dtype),
            pltpu.VMEM(diag_inverse.shape, diag_inverse.dtype),
            pltpu.VMEM(lower_blocks.shape, lower_blocks.dtype),
            pltpu.VMEM(upper_blocks.shape, upper_blocks.dtype),
            pltpu.SMEM(lower_at.shape, jnp.int32),
            pltpu.SMEM(upper_at.shape, jnp.int32),
            pltpu.VMEM((rows // 2, (slots - 1) * width, 2 * width), jnp.bfloat16),
            pltpu.VMEM((rows // 2, (slots - 1) * width, width), jnp.bfloat16),
            pltpu.VMEM((rows // 2, (upper_slots - 1) * width, 2 * width), jnp.bfloat16),
            pltpu.VMEM((rows // 2, (upper_slots - 1) * width, width), jnp.bfloat16),
            pltpu.VMEM((rows + 1, near, width), jnp.bfloat16),
            pltpu.VMEM((rows, near, width), jnp.float32),
            pltpu.VMEM((rows, width, width), jnp.float32),
            pltpu.SemaphoreType.DMA((9,)),
        ],
        compiler_params=SMALL,
        name="sweeps",
    )(
        *(
            pltpu.with_memory_space_constraint(a, pltpu.HBM)
            for a in (right_sides, diag_inverse, lower_blocks, upper_blocks)
        ),
        *indices[:2],
    )

    levels = groups.bit_length() - 1
    segment = payload.shape[0]
    bits = jnp.bfloat16
    prior = []
    inner = []
    for level in range(levels - 1):
        theirs = trade(payload, "section", 1 << level)
        final = level == levels - 2

        def compose(*refs, bit=1 << level, final=final):
            compose_kernel("section", bit, final, *refs)

        payload, between, *prior = pl.pallas_call(
            compose,
            out_shape=(
                jax.ShapeDtypeStruct((near if final else segment, width), bits),
                jax.ShapeDtypeStruct((near + far, width), bits),
                jax.ShapeDtypeStruct((width, width), bits),
            )
            + (jax.ShapeDtypeStruct((count, width), bits),) * final,
            in_specs=[VMEM] * (2 + len(prior)),
            out_specs=(VMEM,) * (3 + final),
            compiler_params=SMALL,
            name="compose",
        )(payload, theirs, *prior)
        inner.append(between)
    prior, own = prior
    theirs = trade(payload, "section", 1 << (levels - 1))

    def fold(*refs):
        fold_kernel("section", levels, *refs)

    base, response, inflow_map, outflow_map, diagonal = pl.pallas_call(
        fold,
        out_shape=(
            wide,
            jax.ShapeDtypeStruct((rows, width, width), bits),
            jax.ShapeDtypeStruct((near, width), bits),
            jax.ShapeDtypeStruct((near, width), bits),
            jax.ShapeDtypeStruct(diag_blocks.shape, diag_blocks.dtype),
        ),
        in_specs=[VMEM] * (1 + levels) + [HBM],
        out_specs=(VMEM,) * 5,
        scratch_shapes=[pltpu.SemaphoreType.DMA(())],
        compiler_params=SMALL,
        name="fold",
    )(base, response, *inner, pltpu.with_memory_space_constraint(diag_blocks, pltpu.HBM))

    def chain(*refs):
        chain_kernel(("section", "dom"), levels, *refs)

    solved, rounded, brought, inner, outer = pl.pallas_call(
        chain,
        out_shape=(
            wide,
            jax.ShapeDtypeStruct((rows, count, width), bits),
            jax.ShapeDtypeStruct((count, width), bits),
            jax.ShapeDtypeStruct((RIM, count, width), bits),
            jax.ShapeDtypeStruct((RIM, count, width), bits),
        ),
        in_specs=[VMEM] * 4,
        out_specs=(VMEM,) * 5,
        compiler_params=SMALL,
        name="chain",
    )(own, theirs, base, response)

    outer = swaps(outer, "dom", 1)
    inner = swaps(inner, "dom", 0)

    def local(*refs):
        local_kernel(("section", "dom"), levels, *refs)

    masks = (rows, halo_blocks.shape[1] - 1, 2 * RIM, count, width)
    partial, solution, masks = pl.pallas_call(
        local,
        out_shape=(wide, wide, jax.ShapeDtypeStruct(masks, bits)),
        in_specs=[VMEM] * 10 + [HBM] * 3,
        out_specs=(VMEM, HBM, VMEM),
        scratch_shapes=[
            pltpu.VMEM((rows + 2, count, width), bits),
            pltpu.VMEM((width, width), bits),
        ]
        + [pltpu.SMEM(a.shape, jnp.int32) for a in indices]
        + [pltpu.SemaphoreType.DMA((4,))],
        compiler_params=SMALL,
        name="local_product",
    )(
        rounded,
        brought,
        inflow_map,
        outflow_map,
        prior,
        theirs,
        solved,
        diagonal,
        lower_blocks,
        upper_blocks,
        *indices,
    )

    def halo(*refs):
        halo_kernel("dom", *refs)

    product = pl.pallas_call(
        halo,
        out_shape=wide,
        in_specs=[VMEM] * 5,
        out_specs=VMEM,
        compiler_params=SMALL,
        name="halo_product",
    )(partial, outer, inner, halo_blocks, masks)
    return (solution, product)


def solution(mesh):
    in_specs = (
        P(("section", "dom"), None, None),
        P(("section", "dom"), None, None),
        P(("section", "dom"), None, None),
        P(("section", "dom"), None, None, None),
        P(("section", "dom"), None, None, None),
        P(("section", "dom"), None, None, None),
        P(("section", "dom"), None),
        P(("section", "dom"), None),
        P(("section", "dom"), None),
    )
    out_specs = (P(("section", "dom"), None, None), P(("section", "dom"), None, None))
    return jax.shard_map(
        on_device, mesh=mesh, in_specs=in_specs, out_specs=out_specs, check_vma=False
    )
```
